32 devices in a mesh: tile: 16 (over z, x, core), depth: 2 (over y).
Axes of the slice: x: 2, y: 2, z: 4, core: 2. Of those that a mesh axis runs over, the one named last changes fastest.
Arguments:
- mask_tiles: float32 [32, 128, 128], P('tile'), may hold values from 0 to 1
- target_tiles: int32 [32, 128, 128], P('tile'), may hold values 0 or 1
- kernels: float32 [2, 2, 6, 25, 25], P(None, 'depth'), may hold values from -0.25 to 0.25
- socs_weights: float32 [2, 6], P('depth'), may hold values from 0.1 to 1
- thresholds: float32 [2], P('depth'), may hold values from 0.8 to 2.4
- partner_table: int32 [32], P('tile'), may hold values from 0 to 31, as said below
- mirror_flags: int32 [32], P('tile'), may hold values from 0 to 1, as said below
Outputs:
- mask_final: float32 [32, 128, 128], P('tile')
- step_gradient: float32 [32, 128, 128], P('tile')
The draws below stay inside these ranges and needn't reach their ends.
Inputs may be any that keep to these rules, and one draw needn't show every extreme that they name: partner_table[t] is t itself or t XOR 2^b for some bit b, and partner_table[partner_table[t]] = t. mirror_flags is equal for the two tiles of a matched pair.
All inputs are finite; a program needn't handle non-finite values. No bound on the sum of `target_tiles` on one device may be relied on, other than what follows from the above.
Results may differ from the reference program's by a relative error of at most 0.0003.
Values sent between devices are 32-bit elements; how exact they have to be, the bound alone decides.
No kernel may reach another device: no remote copies, remote signals or barrier semaphores. Data moves between devices by JAX's collectives and lax.ppermute only.
A program may use at most 128 MiB of HBM per device.

```python
import math
import jax
import jax.numpy as jnp
from jax import lax

HALO = 12
CORE = 128
FRAME = 152
KSIZE = 25
KERN = 6
PLANES = 2
TILES_DEV = 2
TILES = 32
STEPS = 2
N_TILE = 16


def matching(key):
    nbits = TILES.bit_length() - 1
    tile_ids = jnp.arange(TILES, dtype=jnp.int32)
    partner = tile_ids
    for rounds in range(4):
        chosen = jax.random.randint(jax.random.fold_in(key, 11 + rounds), (TILES,), 0, nbits)
        candidate = jnp.bitwise_xor(tile_ids, jnp.left_shift(jnp.int32(1), chosen))
        unmatched = partner == tile_ids
        accept = unmatched & unmatched[candidate] & (chosen[candidate] == chosen)
        partner = jnp.where(accept, candidate, partner)
    flips = jax.random.randint(jax.random.fold_in(key, 29), (TILES,), 0, 2)
    mirror = flips[jnp.minimum(tile_ids, partner)]
    return (partner.astype(jnp.int32), mirror.astype(jnp.int32))


def draw_partner_table(key, part):
    return matching(jax.random.fold_in(key, 5))[0]


def draw_mirror_flags(key, part):
    return matching(jax.random.fold_in(key, 5))[1]


def set_ends(drawn, own_key, least, top_value):
    longest = drawn.shape.index(max(drawn.shape))
    spots = []
    for shift in (0, 1):
        where = [jax.random.randint(jax.random.fold_in(own_key, axis), (), 0, length) for axis, length in enumerate(drawn.shape)]
        where[longest] = (where[longest] + shift) % drawn.shape[longest]
        spots.append(tuple(where))
    return drawn.at[spots[0]].set(least).at[spots[1]].set(top_value)


def block_levels(stream_key, dims, cuts, low, largest):
    factor_of = 1.0
    for axis_at, blocks in cuts:
        steps = jax.random.uniform(jax.random.fold_in(jax.random.fold_in(stream_key, 6), axis_at), (blocks,), jnp.float32, low / len(cuts), largest / len(cuts))
        factor_of = factor_of * jnp.repeat(jnp.exp(steps), dims[axis_at] // blocks).reshape((-1,) + (1,) * (len(dims) - 1 - axis_at))
    return factor_of


def gaussian(own_key, shape, spread, limit, pieces=(), kind=jnp.bfloat16):
    values = jax.random.normal(own_key, shape, jnp.float32) * spread
    if len(pieces) > 0:
        values = block_levels(own_key, shape, pieces, -0.22, 0.18) * values
    return jnp.clip(values, min=-limit, max=limit).astype(kind)


def setup_inputs(seed: int = 0) -> dict:
    streams_of = jax.random.split(jax.random.key(seed), 8)
    mask_tiles = jnp.clip(1.0 * jax.random.uniform(streams_of[0], (TILES, CORE, CORE), jnp.float32) ** block_levels(streams_of[0], (TILES, CORE, CORE), ((0, 16),), -0.2, 0.2), 0.0, 1.0)
    target_tiles = set_ends((jax.random.randint(streams_of[1], (TILES, CORE, CORE), 0, 2) < 1).astype(jnp.int32), jax.random.fold_in(streams_of[1], 1), 0, 1)
    kernels = gaussian(streams_of[2], (2, PLANES, KERN, KSIZE, KSIZE), (KSIZE * KSIZE) ** -0.5, 0.25, ((1, 2),), jnp.float32)
    socs_weights = jnp.clip(jnp.exp(math.log(1.0) - 2.3025851 * jax.random.uniform(streams_of[3], (PLANES, KERN), jnp.float32) ** block_levels(streams_of[3], (PLANES, KERN), ((0, 2),), -0.2, 0.2)), 0.1, 1.0)
    thresholds = jnp.clip(0.8 + 1.6000001 * jax.random.uniform(streams_of[4], (PLANES,), jnp.float32) ** block_levels(streams_of[4], (PLANES,), ((0, 2),), -0.2, 0.2), 0.8, 2.4)
    partner_table = draw_partner_table(jax.random.fold_in(streams_of[7], 71), 0)
    mirror_flags = draw_mirror_flags(jax.random.fold_in(streams_of[7], 71), 0)
    return {"mask_tiles": mask_tiles, "target_tiles": target_tiles, "kernels": kernels, "socs_weights": socs_weights, "thresholds": thresholds, "partner_table": partner_table, "mirror_flags": mirror_flags}


steepness = 3.0
step_rate = 0.05


def kernel_spectra(kernels):
    complex_kern = kernels[0] + 1j * kernels[1]
    padded = jnp.pad(complex_kern, ((0, 0), (0, 0), (0, FRAME - KSIZE), (0, FRAME - KSIZE)))
    rolled = jnp.roll(padded, (-HALO, -HALO), axis=(2, 3))
    return jnp.fft.fft2(rolled)


def frame_gradient(frame_data, target_core, spectra, socs_weights, thresholds):
    spectrum = jnp.fft.fft2(frame_data)
    fields = jnp.fft.ifft2(spectra * spectrum[None, None])
    intensity = jnp.sum(socs_weights[:, :, None, None] * (fields.real ** 2 + fields.imag ** 2), axis=1)
    interior = intensity[:, HALO:HALO + CORE, HALO:HALO + CORE]
    resist = jax.nn.sigmoid(steepness * (interior - thresholds[:, None, None]))
    slope = 2.0 * (resist - target_core[None]) * steepness * resist * (1.0 - resist)
    full_slope = jnp.pad(slope, ((0, 0), (HALO, HALO), (HALO, HALO)))
    factor = 2.0 * socs_weights[:, :, None, None] * full_slope[:, None]
    back = jnp.sum(jnp.conj(spectra) * jnp.fft.fft2(factor * fields), axis=(0, 1))
    return jnp.fft.ifft2(back).real


def reference(mask_tiles, target_tiles, kernels, socs_weights, thresholds, partner_table, mirror_flags):
    spectra = kernel_spectra(kernels)
    target_f = target_tiles.astype(jnp.float32)
    step_gradient = jnp.zeros_like(mask_tiles)
    tile_ids = jnp.arange(TILES, dtype=jnp.int32)
    for step_index in range(STEPS):
        picture = mask_tiles.reshape(N_TILE, TILES_DEV, CORE, CORE).transpose(1, 2, 0, 3)
        picture = picture.reshape(TILES_DEV * CORE, N_TILE * CORE)
        padded = jnp.pad(picture, HALO)

        def accumulate(canvas, inputs):
            tile_index, target_core = inputs
            row_start = ((tile_index % TILES_DEV) * CORE).astype(jnp.int32)
            col_start = ((tile_index // TILES_DEV) * CORE).astype(jnp.int32)
            frame_data = lax.dynamic_slice(padded, (row_start, col_start), (FRAME, FRAME))
            frame_grad = frame_gradient(frame_data, target_core, spectra, socs_weights, thresholds)
            current = lax.dynamic_slice(canvas, (row_start, col_start), (FRAME, FRAME))
            canvas = lax.dynamic_update_slice(canvas, current + frame_grad, (row_start, col_start))
            return canvas, None

        canvas, unused = lax.scan(accumulate, jnp.zeros(padded.shape, jnp.float32), (tile_ids, target_f))
        inner = canvas[HALO:HALO + TILES_DEV * CORE, HALO:HALO + N_TILE * CORE]
        gradient = inner.reshape(TILES_DEV, CORE, N_TILE, CORE).transpose(2, 0, 1, 3).reshape(TILES, CORE, CORE)
        partner_vals = gradient[partner_table]
        flipped = jnp.where((mirror_flags == 1)[:, None, None], partner_vals[:, :, ::-1], partner_vals)
        step_gradient = 0.5 * (gradient + flipped)
        mask_tiles = mask_tiles - step_rate * step_gradient
    return mask_tiles, step_gradient
```

```python
import functools

import jax
import jax.numpy as jnp
import ml_dtypes
import numpy as np
from jax import lax
from jax.experimental import pallas as pl
from jax.experimental.pallas import tpu as pltpu
from jax.sharding import PartitionSpec as P

HALO = 12
KSIZE = 25
STEPS = 2
STEEPNESS = 3.0
STEP_RATE = 0.05

CORE = 128
NY = 152
NX = 176
WIDE = 2 * HALO
XB = 96
YB = 128
NU = NY // 2 + 1
NV = NX // 2 + 1
ROWS = 160
ROW0 = 8
EDGE = 48
SLICE = 4
VMEM_LIMIT = 48 * 1024 * 1024

f32 = jnp.float32
bf16 = jnp.bfloat16


def np_split(a):
    hi = np.asarray(a, np.float32).astype(ml_dtypes.bfloat16)
    lo = (np.asarray(a, np.float64) - hi.astype(np.float64)).astype(ml_dtypes.bfloat16)
    return hi, lo


def x_rows(cols):
    out = np.zeros((2 * XB, len(cols)))
    ang = 2 * np.pi * np.outer(np.arange(NV), cols) / NX
    out[:NV] = np.cos(ang)
    out[XB : XB + NV] = np.sin(ang)
    out[XB] = 0.0
    out[XB + NV - 1] = 0.0
    return out


def y_lanes(rows):
    out = np.zeros((len(rows), 2 * YB))
    ang = 2 * np.pi * np.outer(rows, np.arange(NU)) / NY
    out[:, :NU] = np.cos(ang)
    out[:, YB : YB + NU] = np.sin(ang)
    out[:, YB] = 0.0
    out[:, YB + NU - 1] = 0.0
    return out


def half_weights(bins):
    weights = np.full(bins, 2.0)
    weights[0] = weights[-1] = 1.0
    return weights


def x_back(cols):
    kappa = np.zeros(2 * XB)
    kappa[:NV] = half_weights(NV) / 2
    kappa[XB : XB + NV] = half_weights(NV) / 2
    return x_rows(cols).T * kappa


def y_back(rows):
    weight = np.zeros(2 * YB)
    weight[:NU] = half_weights(NU)
    weight[YB : YB + NU] = -half_weights(NU)
    return (y_lanes(rows) * weight).T / (NX * NY)


def strip_rows(sliced, rows_each):
    idx = np.arange(2 * CORE)
    if not sliced:
        return idx // CORE, idx % CORE
    part, rest = idx // (2 * rows_each), idx % (2 * rows_each)
    return rest // rows_each, part * rows_each + rest % rows_each


def window_rows(sliced, rows_each, tile):
    t, r = strip_rows(sliced, rows_each)
    pos = t * CORE + r - tile * CORE + HALO
    return pos, (pos >= 0) & (pos < NY)


@functools.lru_cache(None)
def tables():
    tb = {}
    core_rows = np.arange(HALO, HALO + CORE)
    field_cols = np.arange(ROW0, ROW0 + ROWS)
    own_cols = np.arange(WIDE, WIDE + CORE)

    def put(name, a):
        tb[name + "_hi"], tb[name + "_lo"] = np_split(a)

    put("cx_own", x_rows(own_cols))
    left = np.zeros((2 * XB, EDGE))
    left[:, :WIDE] = x_rows(np.arange(WIDE))
    right = np.zeros((2 * XB, EDGE))
    right[:, :WIDE] = x_rows(np.arange(WIDE + CORE, NX))
    put("cx_left", left)
    put("cx_right", right)
    both = np.zeros((2 * XB, 256))
    both[:, :CORE] = x_rows(own_cols)
    both[:, 256 - WIDE :] = x_rows(np.arange(WIDE))
    both[:, CORE : CORE + WIDE] = x_rows(np.arange(WIDE + CORE, NX))
    put("cx_both", both)
    for name, sliced in (("by_nat", False), ("by_sl", True)):
        mats = []
        for t in range(2):
            pos, inside = window_rows(sliced, SLICE, t)
            mats.append(y_lanes(pos) * inside[:, None])
        put(name, np.concatenate(mats, axis=1))
    put("x2", x_back(field_cols))
    put("y2", y_back(core_rows))
    tb["y2_cat"] = np.concatenate([tb["y2_hi"], tb["y2_lo"]], axis=1)
    y3 = y_lanes(core_rows)
    put("y3", y3)
    tb["y3_dup"] = np.concatenate([tb["y3_hi"], tb["y3_hi"]], axis=0)
    put("x3", x_rows(field_cols))
    put("x4", x_back(own_cols))
    mats = []
    for t in range(2):
        pos, inside = window_rows(True, SLICE, t)
        mats.append(y_back(pos).T * inside[:, None])
    put("yg", np.stack(mats))
    offs = np.arange(KSIZE) - HALO
    kx = np.zeros((2 * XB, 128))
    kx[:, :KSIZE] = x_rows(offs)
    put("kx", kx)
    ky = np.zeros((4, 128, 2 * YB))
    for m in range(4):
        ky[m, 32 * m : 32 * m + KSIZE] = y_lanes(offs)
    put("ky", ky)
    sel = np.zeros((4, EDGE, 128), np.float32)
    for r in range(WIDE):
        sel[0, r, CORE - WIDE + r] = 1
        sel[2, r, r] = 1
    for r in range(HALO):
        sel[1, WIDE + r, CORE - HALO + r] = 1
        sel[3, WIDE + r, r] = 1
    tb["edge_sel"] = sel.astype(ml_dtypes.bfloat16)
    own = np.zeros((ROWS, CORE), np.float32)
    for c in range(CORE):
        own[WIDE - ROW0 + c, c] = 1
    tb["sel_own"] = own.astype(ml_dtypes.bfloat16)
    halo = np.zeros((2, ROWS, EDGE), np.float32)
    for r in range(HALO):
        halo[0, HALO + r - ROW0, WIDE + r] = 1
        halo[1, WIDE + CORE + r - ROW0, WIDE + r] = 1
    tb["sel_halo"] = halo.astype(ml_dtypes.bfloat16)
    tb["flip"] = np.eye(CORE, dtype=np.float32)[::-1].astype(ml_dtypes.bfloat16)
    return tb


def split(x):
    hi = x.astype(bf16)
    return hi, (x - hi.astype(f32)).astype(bf16)


def dot(a, b):
    return lax.dot_general(a, b, (((1,), (0,)), ((), ())), preferred_element_type=f32)


def dot_nt(a, b):
    return lax.dot_general(a, b, (((1,), (1,)), ((), ())), preferred_element_type=f32)


def dot3(a_hi, a_lo, b_hi, b_lo, mul=dot):
    return mul(a_hi, b_hi) + (mul(a_lo, b_hi) + mul(a_hi, b_lo))


def signed(spec):
    cc, cs = spec[:XB, :YB], spec[:XB, YB:]
    sc, ss = spec[XB:, :YB], spec[XB:, YB:]
    return cc - ss, -(cs + sc), cc + ss, sc - cs


def even_odd(pr, pi, mr, mi):
    top = jnp.concatenate([pr + mr, pi + mi], axis=1)
    low = jnp.concatenate([mi - pi, pr - mr], axis=1)
    return jnp.concatenate([top, low], axis=0)


def call(body, names, args, out_shape, scratch=(), smem=(), flops=0, nbytes=0):
    tb = tables()
    consts = [jnp.asarray(tb[n]) for n in names]
    vm = pl.BlockSpec(memory_space=pltpu.VMEM)
    sm = pl.BlockSpec(memory_space=pltpu.SMEM)
    in_specs = [sm if i in smem else vm for i in range(len(args))] + [vm] * len(consts)
    multi = isinstance(out_shape, (list, tuple))

    def wrapped(*refs):
        n_in = len(args)
        ins = refs[:n_in]
        tabs = dict(zip(names, refs[n_in : n_in + len(names)]))
        body(*ins, tabs, *refs[n_in + len(names) :])

    return pl.pallas_call(
        wrapped,
        out_shape=out_shape,
        in_specs=in_specs,
        out_specs=[vm] * len(out_shape) if multi else vm,
        scratch_shapes=list(scratch),
        compiler_params=pltpu.CompilerParams(vmem_limit_bytes=VMEM_LIMIT),
        cost_estimate=pl.CostEstimate(flops=flops, bytes_accessed=nbytes, transcendentals=0),
    )(*args, *consts)


def edges_kernel(mask_ref, target_ref, tb, a_ref, b_ref):
    even = lax.rem(lax.axis_index("tile"), 2) == 0
    m_hi, m_lo = split(mask_ref[...])
    tgt = target_ref[...].astype(f32).astype(bf16)
    sel = tb["edge_sel"]
    right = dot_nt(sel[0], m_hi) + dot_nt(sel[0], m_lo) + dot_nt(sel[1], tgt)
    left = dot_nt(sel[2], m_hi) + dot_nt(sel[2], m_lo) + dot_nt(sel[3], tgt)
    a_ref[...] = jnp.where(even, right, left)
    b_ref[...] = jnp.where(even, left, right)


def spectra_kernel(kern, ker_ref, tb, h_ref, hs_ref):
    hs_ref[...] = jnp.zeros_like(hs_ref)
    for k in range(kern):
        for part in range(2):
            row = 32 * (2 * k + part)
            hs_ref[row : row + KSIZE, :KSIZE] = ker_ref[part, 0, k]
    s_hi, s_lo = split(hs_ref[...])
    z = dot3(tb["kx_hi"][...], tb["kx_lo"][...], s_hi, s_lo, dot_nt)
    z_hi, z_lo = split(z)
    for c in range(2 * kern):
        lanes = slice(128 * (c // 4), 128 * (c // 4) + 128)
        spec = dot3(
            z_hi[:, lanes], z_lo[:, lanes], tb["ky_hi"][c % 4], tb["ky_lo"][c % 4]
        )
        for j, comp in enumerate(signed(spec)):
            h_ref[c, j] = comp


def to_spectrum(v, by_hi, by_lo, f_ref, base):
    v_hi, v_lo = split(v)
    for t in range(2):
        lanes = slice(256 * t, 256 * t + 256)
        spec = dot3(v_hi, v_lo, by_hi[:, lanes], by_lo[:, lanes])
        for j, comp in enumerate(signed(spec)):
            f_ref[t, j] = comp if base is None else base[t, j] - STEP_RATE * comp


def gradient_body(kern, last, f_ref, tgt_ref, h_ref, w_ref, thr_ref, tb, g_ref, fld, inten, tot):
    inten[...] = jnp.zeros_like(inten)

    @pl.loop(0, kern)
    def _(k):
        for t in range(2):
            parts = []
            for part in range(2):
                hpr, hpi, hmr, hmi = (h_ref[2 * k + part, j] for j in range(4))
                fpr, fpi, fmr, fmi = (f_ref[t, j] for j in range(4))
                pr, pi = hpr * fpr - hpi * fpi, hpr * fpi + hpi * fpr
                mr, mi = hmr * fmr - hmi * fmi, hmr * fmi + hmi * fmr
                r_hi, r_lo = split(even_odd(pr, pi, mr, mi))
                parts.append(dot3(tb["x2_hi"][...], tb["x2_lo"][...], r_hi, r_lo))
            g_hi, g_lo = split(jnp.concatenate(parts, axis=0))
            r = dot(g_hi, tb["y2_cat"][...])
            field = r[:, :CORE] + (r[:, CORE:] + dot(g_lo, tb["y2_hi"][...]))
            fld[t, k] = field
            inten[t] += w_ref[0, k] * (field[:ROWS] * field[:ROWS] + field[ROWS:] * field[ROWS:])

    tile = lax.axis_index("tile")
    first = jnp.where(tile == 0, WIDE, HALO) - ROW0
    end = jnp.where(tile == last, WIDE + CORE, WIDE + CORE + HALO) - ROW0
    row = lax.broadcasted_iota(jnp.int32, (ROWS, CORE), 0)
    inside = (row >= first) & (row < end)
    for t in range(2):
        resist = jax.nn.sigmoid(STEEPNESS * (inten[t] - thr_ref[0]))
        target = tgt_ref[:, CORE * t : CORE * t + CORE]
        slope = 2.0 * (resist - target) * STEEPNESS * resist * (1.0 - resist)
        inten[t] = jnp.where(inside, 2.0 * slope, 0.0)
    tot[...] = jnp.zeros_like(tot)

    @pl.loop(0, kern)
    def _(k):
        for t in range(2):
            scaled = w_ref[0, k] * inten[t]
            field = fld[t, k]
            r_hi, r_lo = split(
                jnp.concatenate([scaled * field[:ROWS], scaled * field[ROWS:]], axis=0)
            )
            w = dot(jnp.concatenate([r_hi, r_lo], axis=1), tb["y3_dup"][...])
            w_hi, w_lo = split(w + dot(r_hi, tb["y3_lo"][...]))
            acc = [tot[t, j] for j in range(4)]
            for part in range(2):
                rows = slice(ROWS * part, ROWS * part + ROWS)
                spec = dot3(tb["x3_hi"][...], tb["x3_lo"][...], w_hi[rows], w_lo[rows])
                bpr, bpi, bmr, bmi = signed(spec)
                hpr, hpi, hmr, hmi = (h_ref[2 * k + part, j] for j in range(4))
                acc[0] = acc[0] + (hpr * bpr + hpi * bpi)
                acc[1] = acc[1] + (hpr * bpi - hpi * bpr)
                acc[2] = acc[2] + (hmr * bmr + hmi * bmi)
                acc[3] = acc[3] + (hmr * bmi - hmi * bmr)
            for j in range(4):
                tot[t, j] = acc[j]

    out = None
    for t in range(2):
        r_hi, r_lo = split(even_odd(*(tot[t, j] for j in range(4))))
        u_hi, u_lo = split(dot3(tb["x4_hi"][...], tb["x4_lo"][...], r_hi, r_lo))
        term = dot3(tb["yg_hi"][t], tb["yg_lo"][t], u_hi, u_lo, dot_nt)
        out = term if out is None else out + term
    g_ref[...] = out


def pairs_of(*names):
    return [n + tail for n in names for tail in ("_hi", "_lo")]


GRAD_TABLES = pairs_of("x2", "x3", "x4", "yg") + ["y2_cat", "y2_hi", "y3_dup", "y3_lo"]
FIRST_TABLES = pairs_of("cx_own", "cx_left", "cx_right", "by_nat") + ["sel_own", "sel_halo"]
LATER_TABLES = pairs_of("cx_both", "by_sl")


def first_kernel(
    kern, last, w_ref, thr_ref, mask_ref, target_ref, a_ref, b_ref, h_ref, tb,
    g_ref, f_ref, tgt_ref, fld, inten, tot,
):
    even = lax.rem(lax.axis_index("tile"), 2) == 0
    from_a, from_b = a_ref[...], b_ref[...]
    left = jnp.where(even, from_b, from_a)
    right = jnp.where(even, from_a, from_b)
    m_hi, m_lo = split(mask_ref[...])
    l_hi, l_lo = split(left)
    r_hi, r_lo = split(right)
    v = dot3(tb["cx_own_hi"][...], tb["cx_own_lo"][...], m_hi, m_lo, dot_nt)
    v = v + dot3(tb["cx_left_hi"][...], tb["cx_left_lo"][...], l_hi, l_lo)
    v = v + dot3(tb["cx_right_hi"][...], tb["cx_right_lo"][...], r_hi, r_lo)
    to_spectrum(v, tb["by_nat_hi"], tb["by_nat_lo"], f_ref, None)
    tgt_ref[...] = (
        dot_nt(tb["sel_own"][...], target_ref[...].astype(f32).astype(bf16))
        + dot(tb["sel_halo"][0], l_hi)
        + dot(tb["sel_halo"][1], r_hi)
    )
    gradient_body(kern, last, f_ref, tgt_ref, h_ref, w_ref, thr_ref, tb, g_ref, fld, inten, tot)


def later_kernel(
    kern, last, w_ref, thr_ref, own_ref, f_in_ref, tgt_ref, h_ref, tb,
    g_ref, f_ref, fld, inten, tot,
):
    step = own_ref[...]
    rows = step.shape[0] * 8
    own = step[:, :8].reshape(rows, CORE)
    edge = step[:, 8:].reshape(rows, CORE)
    s_hi, s_lo = split(jnp.concatenate([own, edge], axis=1))
    v = dot3(tb["cx_both_hi"][...], tb["cx_both_lo"][...], s_hi, s_lo, dot_nt)
    to_spectrum(v, tb["by_sl_hi"], tb["by_sl_lo"], f_ref, f_in_ref)
    gradient_body(kern, last, f_ref, tgt_ref, h_ref, w_ref, thr_ref, tb, g_ref, fld, inten, tot)


def match_kernel(n_tile, copies, edges, table_ref, got_ref, tb, out_ref, src_ref):
    total = []
    for d in range(n_tile):
        s = got_ref[d * copies]
        for c in range(1, copies):
            s = s + got_ref[d * copies + c]
        total.append(s)
        src_ref[d] = s
    flat = jnp.concatenate(total, axis=0)
    hi = flat.astype(bf16)
    rest = flat - hi.astype(f32)
    mid = rest.astype(bf16)
    low = (rest - mid.astype(f32)).astype(bf16)
    flip = tb["flip"][...]
    turned = dot(hi, flip) + (dot(mid, flip) + dot(low, flip))
    for d in range(n_tile):
        src_ref[n_tile + d] = turned[8 * d : 8 * d + 8]
    upper = lax.broadcasted_iota(jnp.int32, (8, CORE), 0) < SLICE
    matched = []
    for d in range(n_tile):
        pick = []
        for t in range(2):
            partner = table_ref[d, t]
            value = src_ref[lax.div(partner, 2) + n_tile * table_ref[d, 2 + t]]
            moved = pltpu.roll(value, SLICE, 0)
            pick.append(jnp.where(lax.rem(partner, 2) == t, value, moved))
        matched.append(0.5 * (total[d] + jnp.where(upper, pick[0], pick[1])))
    lane = lax.broadcasted_iota(jnp.int32, (8, CORE), 1)
    zero = jnp.zeros((8, CORE), f32)
    for d in range(n_tile):
        rim = None
        if edges:
            before = matched[d - 1] if d > 0 else zero
            after = matched[d + 1] if d + 1 < n_tile else zero
            rim = jnp.where(lane >= CORE - WIDE, before, jnp.where(lane < WIDE, after, 0.0))
        for c in range(copies):
            out_ref[d * copies + c, :8] = matched[d]
            if edges:
                out_ref[d * copies + c, 8:] = rim


def final_kernel(slices, mask_ref, one_ref, two_ref, tb, mask_out, grad_out):
    for s in range(slices):
        rows = slice(SLICE * s, SLICE * s + SLICE)
        for t in range(2):
            at = slice(SLICE * t, SLICE * t + SLICE)
            two = two_ref[s, at]
            grad_out[t, rows] = two
            stepped = mask_ref[t, rows] - STEP_RATE * one_ref[s, at]
            mask_out[t, rows] = stepped - STEP_RATE * two


def per_device(
    n_tile, n_depth, mask_tiles, target_tiles, kernels, socs_weights, thresholds,
    partner_table, mirror_flags,
):
    tiles_dev, core, _ = mask_tiles.shape
    kern = kernels.shape[2]
    spread = n_tile * n_depth * SLICE == core
    axes = ("tile", "depth") if spread else ("tile",)
    copies = n_depth if spread else 1
    slices = n_tile * copies
    assert slices * SLICE == core and tiles_dev == 2 and core == CORE

    pairs_a = [(i, i ^ 1) for i in range(n_tile)]
    pairs_b = [p for i in range(1, n_tile - 1, 2) for p in ((i, i + 1), (i + 1, i))]

    mask_rows = mask_tiles.reshape(tiles_dev * core, core)
    target_rows = target_tiles.reshape(tiles_dev * core, core)
    edge = jax.ShapeDtypeStruct((EDGE, tiles_dev * core), f32)
    send_a, send_b = call(edges_kernel, ["edge_sel"], [mask_rows, target_rows], [edge, edge])
    from_a = lax.ppermute(send_a, "tile", pairs_a)
    from_b = lax.ppermute(send_b, "tile", pairs_b)
    mine = jnp.concatenate([partner_table, mirror_flags])[None]
    table = lax.all_gather(mine, "tile", axis=0, tiled=True)

    spectra = call(
        functools.partial(spectra_kernel, kern),
        pairs_of("kx", "ky"),
        [kernels],
        jax.ShapeDtypeStruct((2 * kern, 4, XB, YB), f32),
        [pltpu.VMEM((32 * 2 * kern, 128), f32)],
        flops=3 * 10**9,
        nbytes=4 * 10**6,
    )

    scratch = [
        pltpu.VMEM((2, kern, 2 * ROWS, CORE), f32),
        pltpu.VMEM((2, ROWS, CORE), f32),
        pltpu.VMEM((2, 4, XB, YB), f32),
    ]
    strip = jax.ShapeDtypeStruct((tiles_dev * core, core), f32)
    freq = jax.ShapeDtypeStruct((2, 4, XB, YB), f32)
    goal = jax.ShapeDtypeStruct((ROWS, 2 * CORE), f32)

    def exchange(grad, edges):
        grad = grad.reshape(slices, 8, core)
        if not spread:
            grad = lax.psum(grad, "depth")
        got = lax.all_to_all(grad, axes, 0, 0, tiled=True)
        back = call(
            functools.partial(match_kernel, n_tile, copies, edges),
            ["flip"],
            [table, got],
            jax.ShapeDtypeStruct((slices, 16 if edges else 8, core), f32),
            [pltpu.VMEM((2 * n_tile, 8, core), f32)],
            smem=(0,),
        )
        return lax.all_to_all(back, axes, 0, 0, tiled=True)

    grad, freq_now, goals = call(
        functools.partial(first_kernel, kern, n_tile - 1),
        GRAD_TABLES + FIRST_TABLES,
        [socs_weights, thresholds, mask_rows, target_rows, from_a, from_b, spectra],
        [strip, freq, goal],
        scratch,
        smem=(0, 1),
    )
    moves = [exchange(grad, STEPS > 1)]
    for step in range(1, STEPS):
        grad, freq_now = call(
            functools.partial(later_kernel, kern, n_tile - 1),
            GRAD_TABLES + LATER_TABLES,
            [socs_weights, thresholds, moves[-1], freq_now, goals, spectra],
            [strip, freq],
            scratch,
            smem=(0, 1),
        )
        moves.append(exchange(grad, step + 1 < STEPS))
    tiles = jax.ShapeDtypeStruct((tiles_dev, core, core), f32)
    return tuple(
        call(
            functools.partial(final_kernel, slices),
            [],
            [mask_tiles, *moves],
            [tiles, tiles],
        )
    )


def solution(mesh):
    return jax.shard_map(
        functools.partial(per_device, mesh.shape["tile"], mesh.shape["depth"]),
        mesh=mesh,
        in_specs=(
            P("tile", None, None),
            P("tile", None, None),
            P(None, "depth", None, None, None),
            P("depth", None),
            P("depth"),
            P("tile"),
            P("tile"),
        ),
        out_specs=(P("tile", None, None), P("tile", None, None)),
        check_vma=False,
    )
```

```python
import functools

import jax
import jax.numpy as jnp
import ml_dtypes
import numpy as np
from jax import lax
from jax.experimental import pallas as pl
from jax.experimental.pallas import tpu as pltpu
from jax.sharding import PartitionSpec as P

HALO = 12
KSIZE = 25
STEPS = 2
STEEPNESS = 3.0
STEP_RATE = 0.05

CORE = 128
NY = 152
NX = 176
WIDE = 2 * HALO
XB = 96
YB = 128
NU = NY // 2 + 1
NV = NX // 2 + 1
ROWS = 160
ROW0 = 8
EDGE = 48
WIDE_PAD = 32
VMEM_LIMIT = 24 * 1024 * 1024

f32 = jnp.float32
bf16 = jnp.bfloat16


def np_split(a):
    hi = np.asarray(a, np.float32).astype(ml_dtypes.bfloat16)
    lo = (np.asarray(a, np.float64) - hi.astype(np.float64)).astype(ml_dtypes.bfloat16)
    return hi, lo


def x_rows(cols):
    out = np.zeros((2 * XB, len(cols)))
    ang = 2 * np.pi * np.outer(np.arange(NV), cols) / NX
    out[:NV] = np.cos(ang)
    out[XB : XB + NV] = np.sin(ang)
    out[XB] = 0.0
    out[XB + NV - 1] = 0.0
    return out


def y_lanes(rows):
    out = np.zeros((len(rows), 2 * YB))
    ang = 2 * np.pi * np.outer(rows, np.arange(NU)) / NY
    out[:, :NU] = np.cos(ang)
    out[:, YB : YB + NU] = np.sin(ang)
    out[:, YB] = 0.0
    out[:, YB + NU - 1] = 0.0
    return out


def half_weights(bins):
    weights = np.full(bins, 2.0)
    weights[0] = weights[-1] = 1.0
    return weights


def x_back(cols):
    kappa = np.zeros(2 * XB)
    kappa[:NV] = half_weights(NV) / 2
    kappa[XB : XB + NV] = half_weights(NV) / 2
    return x_rows(cols).T * kappa


def y_back(rows):
    weight = np.zeros(2 * YB)
    weight[:NU] = half_weights(NU)
    weight[YB : YB + NU] = -half_weights(NU)
    return (y_lanes(rows) * weight).T / (NX * NY)


def pack(parts):
    rows, where, at = [], {}, 0
    for name, a in parts:
        height = -(-a.shape[0] // 16) * 16
        block = np.zeros((height, 256), np.float64)
        block[: a.shape[0], : a.shape[1]] = a
        rows.append(block)
        where[name] = (at, a.shape[0], a.shape[1])
        at += height
    return np.concatenate(rows), where


def pack_split(parts):
    both = []
    for name, a in parts:
        hi, lo = np_split(a)
        both += [(name + "_hi", hi.astype(np.float64)), (name + "_lo", lo.astype(np.float64))]
    return both


@functools.lru_cache(None)
def tables():
    core_rows = np.arange(HALO, HALO + CORE)
    field_cols = np.arange(ROW0, ROW0 + ROWS)
    own_cols = np.arange(WIDE, WIDE + CORE)
    sides = np.zeros((2 * XB, 256))
    sides[:, :WIDE] = x_rows(np.arange(WIDE))
    sides[:, CORE : CORE + WIDE] = x_rows(np.arange(WIDE + CORE, NX))
    parts = [("cx_own", x_rows(own_cols)), ("cx_side", sides)]
    for t in range(2):
        pos = np.arange(2 * CORE) - t * CORE + HALO
        inside = (pos >= 0) & (pos < NY)
        parts.append((f"by{t}", y_lanes(pos) * inside[:, None]))
    parts += [("x2", x_back(field_cols)), ("x3", x_rows(field_cols)), ("x4", x_back(own_cols))]
    y2_hi, y2_lo = (a.astype(np.float64) for a in np_split(y_back(core_rows)))
    y3_hi, y3_lo = (a.astype(np.float64) for a in np_split(y_lanes(core_rows)))
    grad = pack_split(parts)
    grad += [("y2", np.concatenate([y2_hi, y2_lo], axis=1))]
    grad += [("y3_dup", np.concatenate([y3_hi, y3_hi])), ("y3_lo", y3_lo)]
    own = np.zeros((ROWS, CORE))
    own[np.arange(CORE) + WIDE - ROW0, np.arange(CORE)] = 1
    halo = np.zeros((ROWS, 256))
    for r in range(HALO):
        halo[HALO + r - ROW0, WIDE + r] = 1
        halo[WIDE + CORE + r - ROW0, CORE + WIDE + r] = 1
    grad += [("sel_own", own), ("sel_halo", halo)]
    offs = np.arange(KSIZE) - HALO
    kx = np.zeros((2 * XB, 128))
    kx[:, :KSIZE] = x_rows(offs)
    spec = [("kx", kx)]
    for m in range(4):
        ky = np.zeros((128, 2 * YB))
        ky[32 * m : 32 * m + KSIZE] = y_lanes(offs)
        spec.append((f"ky{m}", ky))
    sel = np.zeros((4, EDGE, 128))
    for r in range(WIDE):
        sel[0, r, CORE - WIDE + r] = 1
        sel[2, r, r] = 1
    for r in range(HALO):
        sel[1, WIDE + r, CORE - HALO + r] = 1
        sel[3, WIDE + r, r] = 1
    edge = [(f"edge{i}", sel[i]) for i in range(4)]
    edge.append(("flip", np.eye(CORE)[::-1]))
    return {"grad": pack(grad), "spec": pack(pack_split(spec)), "edge": pack(edge)}


def split(x):
    hi = x.astype(bf16)
    return hi, (x - hi.astype(f32)).astype(bf16)


def dot(a, b):
    return lax.dot_general(a, b, (((1,), (0,)), ((), ())), preferred_element_type=f32)


def dot_nt(a, b):
    return lax.dot_general(a, b, (((1,), (1,)), ((), ())), preferred_element_type=f32)


def dot3(a_hi, a_lo, b_hi, b_lo, mul=dot):
    return mul(a_hi, b_hi) + (mul(a_lo, b_hi) + mul(a_hi, b_lo))


def signed(spec):
    cc, cs = spec[:XB, :YB], spec[:XB, YB:]
    sc, ss = spec[XB:, :YB], spec[XB:, YB:]
    return cc - ss, -(cs + sc), cc + ss, sc - cs


def even_odd(pr, pi, mr, mi):
    top = jnp.concatenate([pr + mr, pi + mi], axis=1)
    low = jnp.concatenate([mi - pi, pr - mr], axis=1)
    return jnp.concatenate([top, low], axis=0)


def call(body, group, args, out_shape, scratch=(), smem=(), flops=0, nbytes=0):
    packed, where = tables()[group]
    vm = pl.BlockSpec(memory_space=pltpu.VMEM)
    sm = pl.BlockSpec(memory_space=pltpu.SMEM)
    multi = isinstance(out_shape, (list, tuple))
    n_in = len(args)

    def wrapped(*refs):
        def table(name, half=None):
            at, height, width = where[name]
            lanes = slice(0, width) if half is None else slice(128 * half, 128 * half + 128)
            return refs[n_in][at : at + height, lanes]

        body(*refs[:n_in], table, *refs[n_in + 1 :])

    return pl.pallas_call(
        wrapped,
        out_shape=out_shape,
        in_specs=[sm if i in smem else vm for i in range(n_in)] + [vm],
        out_specs=[vm] * len(out_shape) if multi else vm,
        scratch_shapes=list(scratch),
        compiler_params=pltpu.CompilerParams(vmem_limit_bytes=VMEM_LIMIT),
        cost_estimate=pl.CostEstimate(flops=flops, bytes_accessed=nbytes, transcendentals=0),
    )(*args, jnp.asarray(packed.astype(ml_dtypes.bfloat16)))


def is_even():
    return lax.rem(lax.axis_index("tile"), 2) == 0


def send_edges(right, left, a_ref, b_ref):
    even = is_even()
    a_ref[...] = jnp.where(even, right, left)
    b_ref[...] = jnp.where(even, left, right)


def edges_kernel(mask_ref, target_ref, tb, a_ref, b_ref):
    m_hi, m_lo = split(mask_ref[...])
    tgt = target_ref[...].astype(f32).astype(bf16)
    right = dot_nt(tb("edge0"), m_hi) + dot_nt(tb("edge0"), m_lo) + dot_nt(tb("edge1"), tgt)
    left = dot_nt(tb("edge2"), m_hi) + dot_nt(tb("edge2"), m_lo) + dot_nt(tb("edge3"), tgt)
    send_edges(right, left, a_ref, b_ref)


def spectra_kernel(kern, ker_ref, tb, h_ref, hs_ref):
    hs_ref[...] = jnp.zeros_like(hs_ref)
    for k in range(kern):
        for part in range(2):
            row = 32 * (2 * k + part)
            hs_ref[row : row + KSIZE, :KSIZE] = ker_ref[part, 0, k]
    s_hi, s_lo = split(hs_ref[...])
    z = dot3(tb("kx_hi"), tb("kx_lo"), s_hi, s_lo, dot_nt)
    z_hi, z_lo = split(z)
    for c in range(2 * kern):
        lanes = slice(128 * (c // 4), 128 * (c // 4) + 128)
        spec = dot3(z_hi[:, lanes], z_lo[:, lanes], tb(f"ky{c % 4}_hi"), tb(f"ky{c % 4}_lo"))
        for j, comp in enumerate(signed(spec)):
            h_ref[c, j] = comp


def sides(a_ref, b_ref, tb):
    even = is_even()
    from_a, from_b = a_ref[...], b_ref[...]
    l_hi, l_lo = split(jnp.where(even, from_b, from_a))
    r_hi, r_lo = split(jnp.where(even, from_a, from_b))
    height = l_hi.shape[0]
    v = None
    for half, hi, lo in ((0, l_hi, l_lo), (1, r_hi, r_lo)):
        c_hi, c_lo = tb("cx_side_hi", half), tb("cx_side_lo", half)
        term = dot3(c_hi[:, :height], c_lo[:, :height], hi, lo)
        v = term if v is None else v + term
    return v, l_hi, r_hi


def to_spectrum(v, tb, f_ref, base):
    v_hi, v_lo = split(v)
    for t in range(2):
        spec = dot3(v_hi, v_lo, tb(f"by{t}_hi"), tb(f"by{t}_lo"))
        for j, comp in enumerate(signed(spec)):
            f_ref[t, j] = comp if base is None else base[t, j] - STEP_RATE * comp


def gradient_body(kern, last, f_ref, tgt_ref, h_ref, w_ref, thr_ref, tb, g_ref, fld, inten, tot):
    inten[...] = jnp.zeros_like(inten)

    @pl.loop(0, kern)
    def _(k):
        for t in range(2):
            parts = []
            for part in range(2):
                hpr, hpi, hmr, hmi = (h_ref[2 * k + part, j] for j in range(4))
                fpr, fpi, fmr, fmi = (f_ref[t, j] for j in range(4))
                pr, pi = hpr * fpr - hpi * fpi, hpr * fpi + hpi * fpr
                mr, mi = hmr * fmr - hmi * fmi, hmr * fmi + hmi * fmr
                r_hi, r_lo = split(even_odd(pr, pi, mr, mi))
                parts.append(dot3(tb("x2_hi"), tb("x2_lo"), r_hi, r_lo))
            g_hi, g_lo = split(jnp.concatenate(parts, axis=0))
            r = dot(g_hi, tb("y2"))
            field = r[:, :CORE] + (r[:, CORE:] + dot(g_lo, tb("y2", 0)))
            fld[t, k] = field
            inten[t] += w_ref[0, k] * (field[:ROWS] * field[:ROWS] + field[ROWS:] * field[ROWS:])

    tile = lax.axis_index("tile")
    first = jnp.where(tile == 0, WIDE, HALO) - ROW0
    end = jnp.where(tile == last, WIDE + CORE, WIDE + CORE + HALO) - ROW0
    row = lax.broadcasted_iota(jnp.int32, (ROWS, CORE), 0)
    inside = (row >= first) & (row < end)
    for t in range(2):
        resist = jax.nn.sigmoid(STEEPNESS * (inten[t] - thr_ref[0]))
        target = tgt_ref[:, CORE * t : CORE * t + CORE]
        slope = 2.0 * (resist - target) * STEEPNESS * resist * (1.0 - resist)
        inten[t] = jnp.where(inside, 2.0 * slope, 0.0)
    tot[...] = jnp.zeros_like(tot)

    @pl.loop(0, kern)
    def _(k):
        for t in range(2):
            scaled = w_ref[0, k] * inten[t]
            field = fld[t, k]
            r_hi, r_lo = split(
                jnp.concatenate([scaled * field[:ROWS], scaled * field[ROWS:]], axis=0)
            )
            w = dot(jnp.concatenate([r_hi, r_lo], axis=1), tb("y3_dup"))
            w_hi, w_lo = split(w + dot(r_hi, tb("y3_lo")))
            acc = [tot[t, j] for j in range(4)]
            for part in range(2):
                rows = slice(ROWS * part, ROWS * part + ROWS)
                spec = dot3(tb("x3_hi"), tb("x3_lo"), w_hi[rows], w_lo[rows])
                bpr, bpi, bmr, bmi = signed(spec)
                hpr, hpi, hmr, hmi = (h_ref[2 * k + part, j] for j in range(4))
                acc[0] = acc[0] + (hpr * bpr + hpi * bpi)
                acc[1] = acc[1] + (hpr * bpi - hpi * bpr)
                acc[2] = acc[2] + (hmr * bmr + hmi * bmi)
                acc[3] = acc[3] + (hmr * bmi - hmi * bmr)
            for j in range(4):
                tot[t, j] = acc[j]

    lane = lax.broadcasted_iota(jnp.int32, (1, 2 * YB), 1)
    bin_at = lax.rem(lane, YB)
    weight = jnp.where((bin_at == 0) | (bin_at == NU - 1), 1.0, 2.0) / (NX * NY)
    weight = jnp.where(lane < YB, weight, -weight)
    out = None
    for t in range(2):
        r_hi, r_lo = split(even_odd(*(tot[t, j] for j in range(4))))
        u_hi, u_lo = split(weight * dot3(tb("x4_hi"), tb("x4_lo"), r_hi, r_lo))
        term = dot3(tb(f"by{t}_hi"), tb(f"by{t}_lo"), u_hi, u_lo, dot_nt)
        out = term if out is None else out + term
    g_ref[...] = out


def first_kernel(
    kern, last, w_ref, thr_ref, mask_ref, target_ref, a_ref, b_ref, h_ref, tb,
    g_ref, f_ref, tgt_ref, fld, inten, tot,
):
    m_hi, m_lo = split(mask_ref[...])
    v, left, right = sides(a_ref, b_ref, tb)
    v = v + dot3(tb("cx_own_hi"), tb("cx_own_lo"), m_hi, m_lo, dot_nt)
    to_spectrum(v, tb, f_ref, None)
    tgt_ref[...] = (
        dot_nt(tb("sel_own"), target_ref[...].astype(f32).astype(bf16))
        + dot(tb("sel_halo", 0)[:, :EDGE], left)
        + dot(tb("sel_halo", 1)[:, :EDGE], right)
    )
    gradient_body(kern, last, f_ref, tgt_ref, h_ref, w_ref, thr_ref, tb, g_ref, fld, inten, tot)


def later_kernel(
    kern, last, w_ref, thr_ref, own_ref, a_ref, b_ref, f_in_ref, tgt_ref, h_ref, tb,
    g_ref, f_ref, fld, inten, tot,
):
    s_hi, s_lo = split(own_ref[...])
    v, _, _ = sides(a_ref, b_ref, tb)
    v = v + dot3(tb("cx_own_hi"), tb("cx_own_lo"), s_hi, s_lo, dot_nt)
    to_spectrum(v, tb, f_ref, f_in_ref)
    gradient_body(kern, last, f_ref, tgt_ref, h_ref, w_ref, thr_ref, tb, g_ref, fld, inten, tot)


def match(table_ref, own_ref, got_refs, tb):
    device = lax.axis_index("tile")
    own = own_ref[...]
    flip = tb("flip")
    tiles = []
    for t in range(2):
        rows = slice(CORE * t, CORE * t + CORE)
        mine = own[rows]
        bit = lax.bitwise_xor(table_ref[t], 2 * device + t)
        other = jnp.where(bit == 1, own[CORE * (1 - t) : CORE * (1 - t) + CORE], mine)
        for b, got in enumerate(got_refs):
            other = jnp.where(bit == 2 << b, got[rows], other)
        hi = other.astype(bf16)
        rest = other - hi.astype(f32)
        mid = rest.astype(bf16)
        low = (rest - mid.astype(f32)).astype(bf16)
        turned = dot(hi, flip) + (dot(mid, flip) + dot(low, flip))
        tiles.append(0.5 * (mine + jnp.where(table_ref[2 + t] == 1, turned, other)))
    return tiles


def match_kernel(n_got, table_ref, own_ref, *refs):
    got_refs, (tb, out_ref, a_ref, b_ref) = refs[:n_got], refs[n_got:]
    matched = jnp.concatenate(match(table_ref, own_ref, got_refs, tb), axis=0)
    out_ref[...] = matched
    hi, lo = split(matched)
    right, left = tb("edge0")[:WIDE_PAD], tb("edge2")[:WIDE_PAD]
    send_edges(
        dot_nt(right, hi) + dot_nt(right, lo), dot_nt(left, hi) + dot_nt(left, lo), a_ref, b_ref
    )


def final_kernel(n_got, n_moves, table_ref, own_ref, *refs):
    got_refs, refs = refs[:n_got], refs[n_got:]
    mask_ref, moves, (tb, mask_out, grad_out) = refs[0], refs[1 : 1 + n_moves], refs[1 + n_moves :]
    for t, tile in enumerate(match(table_ref, own_ref, got_refs, tb)):
        grad_out[t] = tile
        now = mask_ref[t]
        for move in moves:
            now = now - STEP_RATE * move[CORE * t : CORE * t + CORE]
        mask_out[t] = now - STEP_RATE * tile


def per_device(
    n_tile, n_depth, mask_tiles, target_tiles, kernels, socs_weights, thresholds,
    partner_table, mirror_flags,
):
    tiles_dev, core, _ = mask_tiles.shape
    kern = kernels.shape[2]
    assert tiles_dev == 2 and core == CORE
    pairs_a = [(i, i ^ 1) for i in range(n_tile)]
    pairs_b = [p for i in range(1, n_tile - 1, 2) for p in ((i, i + 1), (i + 1, i))]

    def swap_edges(send_a, send_b):
        return lax.ppermute(send_b, "tile", pairs_b), lax.ppermute(send_a, "tile", pairs_a)

    def gather_sum(grad):
        bit = 1
        while bit < n_depth:
            pairs = [(i, i ^ bit) for i in range(n_depth)]
            grad = grad + lax.ppermute(grad, "depth", pairs)
            bit *= 2
        bits = [1 << b for b in range(n_tile.bit_length() - 1)]
        got = [
            lax.ppermute(grad, "tile", [(i, i ^ bit) for i in range(n_tile)])
            for bit in reversed(bits)
        ]
        return grad, got[::-1]

    mask_rows = mask_tiles.reshape(tiles_dev * core, core)
    target_rows = target_tiles.reshape(tiles_dev * core, core)
    strip = jax.ShapeDtypeStruct((tiles_dev * core, core), f32)
    edge = jax.ShapeDtypeStruct((EDGE, tiles_dev * core), f32)
    side = jax.ShapeDtypeStruct((WIDE_PAD, tiles_dev * core), f32)
    freq = jax.ShapeDtypeStruct((2, 4, XB, YB), f32)
    goal = jax.ShapeDtypeStruct((ROWS, 2 * CORE), f32)
    tiles = jax.ShapeDtypeStruct((tiles_dev, core, core), f32)
    scratch = [
        pltpu.VMEM((2, kern, 2 * ROWS, CORE), f32),
        pltpu.VMEM((2, ROWS, CORE), f32),
        pltpu.VMEM((2, 4, XB, YB), f32),
    ]

    send_a, send_b = call(edges_kernel, "edge", [mask_rows, target_rows], [edge, edge])
    from_b, from_a = swap_edges(send_a, send_b)
    table = jnp.concatenate([partner_table, mirror_flags])
    spectra = call(
        functools.partial(spectra_kernel, kern),
        "spec",
        [kernels],
        jax.ShapeDtypeStruct((2 * kern, 4, XB, YB), f32),
        [pltpu.VMEM((32 * 2 * kern, 128), f32)],
        flops=3 * 10**9,
        nbytes=4 * 10**6,
    )
    grad, freq_now, goals = call(
        functools.partial(first_kernel, kern, n_tile - 1),
        "grad",
        [socs_weights, thresholds, mask_rows, target_rows, from_a, from_b, spectra],
        [strip, freq, goal],
        scratch,
        smem=(0, 1),
    )
    moves = []
    for step in range(1, STEPS):
        total, got = gather_sum(grad)
        move, send_a, send_b = call(
            functools.partial(match_kernel, len(got)),
            "edge",
            [table, total, *got],
            [strip, side, side],
            smem=(0,),
        )
        from_b, from_a = swap_edges(send_a, send_b)
        moves.append(move)
        grad, freq_now = call(
            functools.partial(later_kernel, kern, n_tile - 1),
            "grad",
            [socs_weights, thresholds, move, from_a, from_b, freq_now, goals, spectra],
            [strip, freq],
            scratch,
            smem=(0, 1),
        )
    total, got = gather_sum(grad)
    return tuple(
        call(
            functools.partial(final_kernel, len(got), len(moves)),
            "edge",
            [table, total, *got, mask_tiles, *moves],
            [tiles, tiles],
            smem=(0,),
        )
    )


def solution(mesh):
    return jax.shard_map(
        functools.partial(per_device, mesh.shape["tile"], mesh.shape["depth"]),
        mesh=mesh,
        in_specs=(
            P("tile", None, None),
            P("tile", None, None),
            P(None, "depth", None, None, None),
            P("depth", None),
            P("depth"),
            P("tile"),
            P("tile"),
        ),
        out_specs=(P("tile", None, None), P("tile", None, None)),
        check_vma=False,
    )
```

```python
import functools

import jax
import jax.numpy as jnp
import ml_dtypes
import numpy as np
from jax import lax
from jax.experimental import pallas as pl
from jax.experimental.pallas import tpu as pltpu
from jax.sharding import PartitionSpec as P

HALO = 12
KSIZE = 25
STEPS = 2
STEEPNESS = 3.0
STEP_RATE = 0.05

CORE = 128
NY = 152
NX = 176
WIDE = 2 * HALO
XB = 96
YB = 128
NU = NY // 2 + 1
NV = NX // 2 + 1
ROWS = 160
ROW0 = 8
EDGE = 48
WIDE_PAD = 32
VMEM_LIMIT = 24 * 1024 * 1024

f32 = jnp.float32
bf16 = jnp.bfloat16


def np_split(a):
    hi = np.asarray(a, np.float32).astype(ml_dtypes.bfloat16)
    lo = (np.asarray(a, np.float64) - hi.astype(np.float64)).astype(ml_dtypes.bfloat16)
    return hi, lo


def x_rows(cols):
    out = np.zeros((2 * XB, len(cols)))
    ang = 2 * np.pi * np.outer(np.arange(NV), cols) / NX
    out[:NV] = np.cos(ang)
    out[XB : XB + NV] = np.sin(ang)
    out[XB] = 0.0
    out[XB + NV - 1] = 0.0
    return out


def y_lanes(rows):
    out = np.zeros((len(rows), 2 * YB))
    ang = 2 * np.pi * np.outer(rows, np.arange(NU)) / NY
    out[:, :NU] = np.cos(ang)
    out[:, YB : YB + NU] = np.sin(ang)
    out[:, YB] = 0.0
    out[:, YB + NU - 1] = 0.0
    return out


def half_weights(bins):
    weights = np.full(bins, 2.0)
    weights[0] = weights[-1] = 1.0
    return weights


def x_back(cols):
    kappa = np.zeros(2 * XB)
    kappa[:NV] = half_weights(NV) / 2
    kappa[XB : XB + NV] = half_weights(NV) / 2
    return x_rows(cols).T * kappa


def y_back(rows):
    weight = np.zeros(2 * YB)
    weight[:NU] = half_weights(NU)
    weight[YB : YB + NU] = -half_weights(NU)
    return (y_lanes(rows) * weight).T / (NX * NY)


def pack(parts):
    rows, where, at = [], {}, 0
    for name, a in parts:
        height = -(-a.shape[0] // 16) * 16
        block = np.zeros((height, 256), np.float64)
        block[: a.shape[0], : a.shape[1]] = a
        rows.append(block)
        where[name] = (at, a.shape[0], a.shape[1])
        at += height
    return np.concatenate(rows), where


def pack_split(parts):
    both = []
    for name, a in parts:
        hi, lo = np_split(a)
        if name in ("x2", "x3", "x4"):
            both.append((name, np.concatenate([hi.astype(np.float64), lo.astype(np.float64)])))
            continue
        both += [(name + "_hi", hi.astype(np.float64)), (name + "_lo", lo.astype(np.float64))]
    return both


@functools.lru_cache(None)
def tables():
    core_rows = np.arange(HALO, HALO + CORE)
    field_cols = np.arange(ROW0, ROW0 + ROWS)
    own_cols = np.arange(WIDE, WIDE + CORE)
    sides = np.zeros((2 * XB, 256))
    sides[:, :WIDE] = x_rows(np.arange(WIDE))
    sides[:, CORE : CORE + WIDE] = x_rows(np.arange(WIDE + CORE, NX))
    parts = [("cx_own", x_rows(own_cols)), ("cx_side", sides)]
    for t in range(2):
        pos = np.arange(2 * CORE) - t * CORE + HALO
        inside = (pos >= 0) & (pos < NY)
        parts.append((f"by{t}", y_lanes(pos) * inside[:, None]))
    parts += [("x2", x_back(field_cols)), ("x3", x_rows(field_cols)), ("x4", x_back(own_cols))]
    y2_hi, y2_lo = (a.astype(np.float64) for a in np_split(y_back(core_rows)))
    y3_hi, y3_lo = (a.astype(np.float64) for a in np_split(y_lanes(core_rows)))
    grad = pack_split(parts)
    grad += [("y2", np.concatenate([y2_hi, y2_lo], axis=1))]
    grad += [("y3_dup", np.concatenate([y3_hi, y3_hi])), ("y3_lo", y3_lo)]
    own = np.zeros((ROWS, CORE))
    own[np.arange(CORE) + WIDE - ROW0, np.arange(CORE)] = 1
    halo = np.zeros((ROWS, 256))
    for r in range(HALO):
        halo[HALO + r - ROW0, WIDE + r] = 1
        halo[WIDE + CORE + r - ROW0, CORE + WIDE + r] = 1
    grad += [("sel_own", own), ("sel_halo", halo)]
    offs = np.arange(KSIZE) - HALO
    kx = np.zeros((2 * XB, 128))
    kx[:, :KSIZE] = x_rows(offs)
    spec = [("kx", kx)]
    for m in range(4):
        ky = np.zeros((128, 2 * YB))
        ky[32 * m : 32 * m + KSIZE] = y_lanes(offs)
        spec.append((f"ky{m}", ky))
    sel = np.zeros((4, EDGE, 128))
    for r in range(WIDE):
        sel[0, r, CORE - WIDE + r] = 1
        sel[2, r, r] = 1
    for r in range(HALO):
        sel[1, WIDE + r, CORE - HALO + r] = 1
        sel[3, WIDE + r, r] = 1
    edge = [(f"edge{i}", sel[i]) for i in range(4)]
    edge.append(("flip", np.eye(CORE)[::-1]))
    return {"grad": pack(grad), "spec": pack(pack_split(spec)), "edge": pack(edge)}


def split(x):
    hi = x.astype(bf16)
    return hi, (x - hi.astype(f32)).astype(bf16)


def dot(a, b):
    return lax.dot_general(a, b, (((1,), (0,)), ((), ())), preferred_element_type=f32)


def dot_nt(a, b):
    return lax.dot_general(a, b, (((1,), (1,)), ((), ())), preferred_element_type=f32)


def dot3(a_hi, a_lo, b_hi, b_lo, mul=dot):
    return mul(a_hi, b_hi) + (mul(a_lo, b_hi) + mul(a_hi, b_lo))


def dot_stacked(table, b_hi, b_lo):
    rows = table.shape[0] // 2
    both = dot(table, b_hi)
    return both[:rows] + (both[rows:] + dot(table[:rows], b_lo))


def signed(spec):
    cc, cs = spec[:XB, :YB], spec[:XB, YB:]
    sc, ss = spec[XB:, :YB], spec[XB:, YB:]
    return cc - ss, -(cs + sc), cc + ss, sc - cs


def even_odd(pr, pi, mr, mi):
    top = jnp.concatenate([pr + mr, pi + mi], axis=1)
    low = jnp.concatenate([mi - pi, pr - mr], axis=1)
    return jnp.concatenate([top, low], axis=0)


def table_array(group):
    return jnp.asarray(tables()[group][0].astype(ml_dtypes.bfloat16))


def table_reader(group, ref):
    where = tables()[group][1]

    def table(name, half=None):
        at, height, width = where[name]
        lanes = slice(0, width) if half is None else slice(128 * half, 128 * half + 128)
        return ref[at : at + height, lanes]

    return table


def call(body, group, args, out_shape, scratch=(), smem=(), flops=0, nbytes=0, given=None):
    vm = pl.BlockSpec(memory_space=pltpu.VMEM)
    sm = pl.BlockSpec(memory_space=pltpu.SMEM)
    multi = isinstance(out_shape, (list, tuple))
    n_in = len(args)

    def wrapped(*refs):
        body(*refs[:n_in], table_reader(group, refs[n_in]), *refs[n_in + 1 :])

    return pl.pallas_call(
        wrapped,
        out_shape=out_shape,
        in_specs=[sm if i in smem else vm for i in range(n_in)] + [vm],
        out_specs=[vm] * len(out_shape) if multi else vm,
        scratch_shapes=list(scratch),
        compiler_params=pltpu.CompilerParams(vmem_limit_bytes=VMEM_LIMIT),
        cost_estimate=pl.CostEstimate(flops=flops, bytes_accessed=nbytes, transcendentals=0),
    )(*args, table_array(group) if given is None else given)


def is_even():
    return lax.rem(lax.axis_index("tile"), 2) == 0


def send_edges(right, left, a_ref, b_ref):
    even = is_even()
    a_ref[...] = jnp.where(even, right, left)
    b_ref[...] = jnp.where(even, left, right)


def edges_kernel(
    mask_hbm, target_hbm, table_hbm, ker_hbm, spec_hbm,
    a_ref, b_ref, ker_ref, spec_ref, mask_ref, target_ref, table_ref, sems,
):
    moves = [
        pltpu.make_async_copy(src, dst, sems.at[i])
        for i, (src, dst) in enumerate(
            (
                (mask_hbm, mask_ref),
                (target_hbm, target_ref),
                (table_hbm, table_ref),
                (ker_hbm, ker_ref),
                (spec_hbm, spec_ref),
            )
        )
    ]
    for move in moves:
        move.start()
    for move in moves[:3]:
        move.wait()
    tb = table_reader("edge", table_ref)
    m_hi, m_lo = split(mask_ref[...])
    tgt = target_ref[...].astype(f32).astype(bf16)
    right = dot_nt(tb("edge0"), m_hi) + dot_nt(tb("edge0"), m_lo) + dot_nt(tb("edge1"), tgt)
    left = dot_nt(tb("edge2"), m_hi) + dot_nt(tb("edge2"), m_lo) + dot_nt(tb("edge3"), tgt)
    send_edges(right, left, a_ref, b_ref)
    for move in moves[3:]:
        move.wait()


def send_first_edges(mask_rows, target_rows, kernels):
    height = mask_rows.shape[0]
    args = [mask_rows, target_rows, table_array("edge"), kernels, table_array("spec")]
    edge = jax.ShapeDtypeStruct((EDGE, height), f32)
    like = lambda x: jax.ShapeDtypeStruct(x.shape, x.dtype)
    vm = pl.BlockSpec(memory_space=pltpu.VMEM)
    return pl.pallas_call(
        edges_kernel,
        out_shape=[edge, edge, like(kernels), like(args[4])],
        in_specs=[pl.BlockSpec(memory_space=pl.ANY)] * 5,
        out_specs=[vm] * 4,
        scratch_shapes=[
            pltpu.VMEM(mask_rows.shape, f32),
            pltpu.VMEM(target_rows.shape, jnp.int32),
            pltpu.VMEM(args[2].shape, bf16),
            pltpu.SemaphoreType.DMA((5,)),
        ],
        compiler_params=pltpu.CompilerParams(vmem_limit_bytes=VMEM_LIMIT),
    )(*args)


def spectra_kernel(kern, ker_ref, tb, h_ref, hs_ref):
    hs_ref[...] = jnp.zeros_like(hs_ref)
    for k in range(kern):
        for part in range(2):
            row = 32 * (2 * k + part)
            hs_ref[row : row + KSIZE, :KSIZE] = ker_ref[part, 0, k]
    s_hi, s_lo = split(hs_ref[...])
    z = dot3(tb("kx_hi"), tb("kx_lo"), s_hi, s_lo, dot_nt)
    z_hi, z_lo = split(z)
    for c in range(2 * kern):
        lanes = slice(128 * (c // 4), 128 * (c // 4) + 128)
        spec = dot3(z_hi[:, lanes], z_lo[:, lanes], tb(f"ky{c % 4}_hi"), tb(f"ky{c % 4}_lo"))
        for j, comp in enumerate(signed(spec)):
            h_ref[c, j] = comp


def sides(a_ref, b_ref, tb):
    even = is_even()
    from_a, from_b = a_ref[...], b_ref[...]
    l_hi, l_lo = split(jnp.where(even, from_b, from_a))
    r_hi, r_lo = split(jnp.where(even, from_a, from_b))
    height = l_hi.shape[0]
    v = None
    for half, hi, lo in ((0, l_hi, l_lo), (1, r_hi, r_lo)):
        c_hi, c_lo = tb("cx_side_hi", half), tb("cx_side_lo", half)
        term = dot3(c_hi[:, :height], c_lo[:, :height], hi, lo)
        v = term if v is None else v + term
    return v, l_hi, r_hi


def to_spectrum(v, tb, f_ref, base):
    v_hi, v_lo = split(v)
    for t in range(2):
        spec = dot3(v_hi, v_lo, tb(f"by{t}_hi"), tb(f"by{t}_lo"))
        for j, comp in enumerate(signed(spec)):
            f_ref[t, j] = comp if base is None else base[t, j] - STEP_RATE * comp


def gradient_body(kern, last, f_ref, tgt_ref, h_ref, w_ref, thr_ref, tb, g_ref, fld, inten, tot):
    inten[...] = jnp.zeros_like(inten)

    @pl.loop(0, kern, unroll=True)
    def _(k):
        parts = [[], []]
        for part in range(2):
            hpr, hpi, hmr, hmi = (h_ref[2 * k + part, j] for j in range(4))
            for t in range(2):
                fpr, fpi, fmr, fmi = (f_ref[t, j] for j in range(4))
                pr, pi = hpr * fpr - hpi * fpi, hpr * fpi + hpi * fpr
                mr, mi = hmr * fmr - hmi * fmi, hmr * fmi + hmi * fmr
                parts[t].append(dot_stacked(tb("x2"), *split(even_odd(pr, pi, mr, mi))))
        for t in range(2):
            g_hi, g_lo = split(jnp.concatenate(parts[t], axis=0))
            r = dot(g_hi, tb("y2"))
            field = r[:, :CORE] + (r[:, CORE:] + dot(g_lo, tb("y2", 0)))
            fld[t, k] = field
            inten[t] += w_ref[0, k] * (field[:ROWS] * field[:ROWS] + field[ROWS:] * field[ROWS:])

    tile = lax.axis_index("tile")
    first = jnp.where(tile == 0, WIDE, HALO) - ROW0
    end = jnp.where(tile == last, WIDE + CORE, WIDE + CORE + HALO) - ROW0
    row = lax.broadcasted_iota(jnp.int32, (ROWS, CORE), 0)
    inside = (row >= first) & (row < end)
    for t in range(2):
        resist = jax.nn.sigmoid(STEEPNESS * (inten[t] - thr_ref[0]))
        target = tgt_ref[:, CORE * t : CORE * t + CORE]
        slope = 2.0 * (resist - target) * STEEPNESS * resist * (1.0 - resist)
        inten[t] = jnp.where(inside, 2.0 * slope, 0.0)
    tot[...] = jnp.zeros_like(tot)

    @pl.loop(0, kern, unroll=True)
    def _(k):
        acc = [[tot[t, j] for j in range(4)] for t in range(2)]
        back = []
        for t in range(2):
            scaled = w_ref[0, k] * inten[t]
            field = fld[t, k]
            r_hi, r_lo = split(
                jnp.concatenate([scaled * field[:ROWS], scaled * field[ROWS:]], axis=0)
            )
            w = dot(jnp.concatenate([r_hi, r_lo], axis=1), tb("y3_dup"))
            back.append(split(w + dot(r_hi, tb("y3_lo"))))
        for part in range(2):
            rows = slice(ROWS * part, ROWS * part + ROWS)
            hpr, hpi, hmr, hmi = (h_ref[2 * k + part, j] for j in range(4))
            for t in range(2):
                w_hi, w_lo = back[t]
                spec = dot_stacked(tb("x3"), w_hi[rows], w_lo[rows])
                bpr, bpi, bmr, bmi = signed(spec)
                acc[t][0] = acc[t][0] + (hpr * bpr + hpi * bpi)
                acc[t][1] = acc[t][1] + (hpr * bpi - hpi * bpr)
                acc[t][2] = acc[t][2] + (hmr * bmr + hmi * bmi)
                acc[t][3] = acc[t][3] + (hmr * bmi - hmi * bmr)
        for t in range(2):
            for j in range(4):
                tot[t, j] = acc[t][j]

    lane = lax.broadcasted_iota(jnp.int32, (1, 2 * YB), 1)
    bin_at = lax.rem(lane, YB)
    weight = jnp.where((bin_at == 0) | (bin_at == NU - 1), 1.0, 2.0) / (NX * NY)
    weight = jnp.where(lane < YB, weight, -weight)
    out = None
    for t in range(2):
        r_hi, r_lo = split(even_odd(*(tot[t, j] for j in range(4))))
        u_hi, u_lo = split(weight * dot_stacked(tb("x4"), r_hi, r_lo))
        term = dot3(tb(f"by{t}_hi"), tb(f"by{t}_lo"), u_hi, u_lo, dot_nt)
        out = term if out is None else out + term
    g_ref[...] = out


def first_kernel(
    kern, last, w_ref, thr_ref, mask_ref, target_ref, a_ref, b_ref, h_ref, tb,
    g_ref, f_ref, tgt_ref, fld, inten, tot,
):
    m_hi, m_lo = split(mask_ref[...])
    v, left, right = sides(a_ref, b_ref, tb)
    v = v + dot3(tb("cx_own_hi"), tb("cx_own_lo"), m_hi, m_lo, dot_nt)
    to_spectrum(v, tb, f_ref, None)
    tgt_ref[...] = (
        dot_nt(tb("sel_own"), target_ref[...].astype(f32).astype(bf16))
        + dot(tb("sel_halo", 0)[:, :EDGE], left)
        + dot(tb("sel_halo", 1)[:, :EDGE], right)
    )
    gradient_body(kern, last, f_ref, tgt_ref, h_ref, w_ref, thr_ref, tb, g_ref, fld, inten, tot)


def later_kernel(
    kern, last, w_ref, thr_ref, own_ref, a_ref, b_ref, f_in_ref, tgt_ref, h_ref, tb,
    g_ref, f_ref, fld, inten, tot,
):
    s_hi, s_lo = split(own_ref[...])
    v, _, _ = sides(a_ref, b_ref, tb)
    v = v + dot3(tb("cx_own_hi"), tb("cx_own_lo"), s_hi, s_lo, dot_nt)
    to_spectrum(v, tb, f_ref, f_in_ref)
    gradient_body(kern, last, f_ref, tgt_ref, h_ref, w_ref, thr_ref, tb, g_ref, fld, inten, tot)


def match(table_ref, own_ref, got_refs, tb):
    device = lax.axis_index("tile")
    own = own_ref[...]
    flip = tb("flip")
    tiles = []
    for t in range(2):
        rows = slice(CORE * t, CORE * t + CORE)
        mine = own[rows]
        bit = lax.bitwise_xor(table_ref[t], 2 * device + t)
        other = jnp.where(bit == 1, own[CORE * (1 - t) : CORE * (1 - t) + CORE], mine)
        for b, got in enumerate(got_refs):
            other = jnp.where(bit == 2 << b, got[rows], other)
        hi = other.astype(bf16)
        rest = other - hi.astype(f32)
        mid = rest.astype(bf16)
        low = (rest - mid.astype(f32)).astype(bf16)
        turned = dot(hi, flip) + (dot(mid, flip) + dot(low, flip))
        tiles.append(0.5 * (mine + jnp.where(table_ref[2 + t] == 1, turned, other)))
    return tiles


def match_kernel(n_got, table_ref, own_ref, *refs):
    got_refs, (tb, out_ref, a_ref, b_ref) = refs[:n_got], refs[n_got:]
    matched = jnp.concatenate(match(table_ref, own_ref, got_refs, tb), axis=0)
    out_ref[...] = matched
    hi, lo = split(matched)
    right, left = tb("edge0")[:WIDE_PAD], tb("edge2")[:WIDE_PAD]
    send_edges(
        dot_nt(right, hi) + dot_nt(right, lo), dot_nt(left, hi) + dot_nt(left, lo), a_ref, b_ref
    )


def final_kernel(n_got, n_moves, table_ref, own_ref, *refs):
    got_refs, refs = refs[:n_got], refs[n_got:]
    mask_ref, moves, (tb, mask_out, grad_out) = refs[0], refs[1 : 1 + n_moves], refs[1 + n_moves :]
    for t, tile in enumerate(match(table_ref, own_ref, got_refs, tb)):
        grad_out[t] = tile
        now = mask_ref[t]
        for move in moves:
            now = now - STEP_RATE * move[CORE * t : CORE * t + CORE]
        mask_out[t] = now - STEP_RATE * tile


def per_device(
    n_tile, n_depth, mask_tiles, target_tiles, kernels, socs_weights, thresholds,
    partner_table, mirror_flags,
):
    tiles_dev, core, _ = mask_tiles.shape
    kern = kernels.shape[2]
    assert tiles_dev == 2 and core == CORE
    pairs_a = [(i, i ^ 1) for i in range(n_tile)]
    pairs_b = [p for i in range(1, n_tile - 1, 2) for p in ((i, i + 1), (i + 1, i))]

    def swap_edges(send_a, send_b):
        return lax.ppermute(send_b, "tile", pairs_b), lax.ppermute(send_a, "tile", pairs_a)

    def gather_sum(grad):
        bit = 1
        while bit < n_depth:
            pairs = [(i, i ^ bit) for i in range(n_depth)]
            grad = grad + lax.ppermute(grad, "depth", pairs)
            bit *= 2
        bits = [1 << b for b in range(n_tile.bit_length() - 1)]
        got = [
            lax.ppermute(grad, "tile", [(i, i ^ bit) for i in range(n_tile)])
            for bit in reversed(bits)
        ]
        return grad, got[::-1]

    mask_rows = mask_tiles.reshape(tiles_dev * core, core)
    target_rows = target_tiles.reshape(tiles_dev * core, core)
    strip = jax.ShapeDtypeStruct((tiles_dev * core, core), f32)
    side = jax.ShapeDtypeStruct((WIDE_PAD, tiles_dev * core), f32)
    freq = jax.ShapeDtypeStruct((2, 4, XB, YB), f32)
    goal = jax.ShapeDtypeStruct((ROWS, 2 * CORE), f32)
    tiles = jax.ShapeDtypeStruct((tiles_dev, core, core), f32)
    scratch = [
        pltpu.VMEM((2, kern, 2 * ROWS, CORE), f32),
        pltpu.VMEM((2, ROWS, CORE), f32),
        pltpu.VMEM((2, 4, XB, YB), f32),
    ]

    send_a, send_b, kernels, spec_table = send_first_edges(mask_rows, target_rows, kernels)
    from_b, from_a = swap_edges(send_a, send_b)
    table = jnp.concatenate([partner_table, mirror_flags])
    spectra = call(
        functools.partial(spectra_kernel, kern),
        "spec",
        [kernels],
        jax.ShapeDtypeStruct((2 * kern, 4, XB, YB), f32),
        [pltpu.VMEM((32 * 2 * kern, 128), f32)],
        flops=3 * 10**9,
        nbytes=4 * 10**6,
        given=spec_table,
    )
    grad, freq_now, goals = call(
        functools.partial(first_kernel, kern, n_tile - 1),
        "grad",
        [socs_weights, thresholds, mask_rows, target_rows, from_a, from_b, spectra],
        [strip, freq, goal],
        scratch,
        smem=(0, 1),
    )
    moves = []
    for step in range(1, STEPS):
        total, got = gather_sum(grad)
        move, send_a, send_b = call(
            functools.partial(match_kernel, len(got)),
            "edge",
            [table, total, *got],
            [strip, side, side],
            smem=(0,),
        )
        from_b, from_a = swap_edges(send_a, send_b)
        moves.append(move)
        grad, freq_now = call(
            functools.partial(later_kernel, kern, n_tile - 1),
            "grad",
            [socs_weights, thresholds, move, from_a, from_b, freq_now, goals, spectra],
            [strip, freq],
            scratch,
            smem=(0, 1),
        )
    total, got = gather_sum(grad)
    return tuple(
        call(
            functools.partial(final_kernel, len(got), len(moves)),
            "edge",
            [table, total, *got, mask_tiles, *moves],
            [tiles, tiles],
            smem=(0,),
        )
    )


def solution(mesh):
    return jax.shard_map(
        functools.partial(per_device, mesh.shape["tile"], mesh.shape["depth"]),
        mesh=mesh,
        in_specs=(
            P("tile", None, None),
            P("tile", None, None),
            P(None, "depth", None, None, None),
            P("depth", None),
            P("depth"),
            P("tile"),
            P("tile"),
        ),
        out_specs=(P("tile", None, None), P("tile", None, None)),
        check_vma=False,
    )
```

```python
import functools

import jax
import jax.numpy as jnp
import ml_dtypes
import numpy as np
from jax import lax
from jax.experimental import pallas as pl
from jax.experimental.pallas import tpu as pltpu
from jax.sharding import PartitionSpec as P

HALO = 12
KSIZE = 25
STEPS = 2
STEEPNESS = 3.0
STEP_RATE = 0.05

CORE = 128
NY = 152
NX = 176
WIDE = 2 * HALO
XB = 96
YB = 128
NU = NY // 2 + 1
NV = NX // 2 + 1
ROWS = 160
ROW0 = 8
EDGE = 48
HALF = CORE // 2
WIDE_PAD = 32
VMEM_LIMIT = 24 * 1024 * 1024

f32 = jnp.float32
bf16 = jnp.bfloat16


def np_split(a):
    hi = np.asarray(a, np.float32).astype(ml_dtypes.bfloat16)
    lo = (np.asarray(a, np.float64) - hi.astype(np.float64)).astype(ml_dtypes.bfloat16)
    return hi, lo


def x_rows(cols):
    out = np.zeros((2 * XB, len(cols)))
    ang = 2 * np.pi * np.outer(np.arange(NV), cols) / NX
    out[:NV] = np.cos(ang)
    out[XB : XB + NV] = np.sin(ang)
    out[XB] = 0.0
    out[XB + NV - 1] = 0.0
    return out


def y_lanes(rows):
    out = np.zeros((len(rows), 2 * YB))
    ang = 2 * np.pi * np.outer(rows, np.arange(NU)) / NY
    out[:, :NU] = np.cos(ang)
    out[:, YB : YB + NU] = np.sin(ang)
    out[:, YB] = 0.0
    out[:, YB + NU - 1] = 0.0
    return out


def half_weights(bins):
    weights = np.full(bins, 2.0)
    weights[0] = weights[-1] = 1.0
    return weights


def x_back(cols):
    kappa = np.zeros(2 * XB)
    kappa[:NV] = half_weights(NV) / 2
    kappa[XB : XB + NV] = half_weights(NV) / 2
    return x_rows(cols).T * kappa


def y_back(rows):
    weight = np.zeros(2 * YB)
    weight[:NU] = half_weights(NU)
    weight[YB : YB + NU] = -half_weights(NU)
    return (y_lanes(rows) * weight).T / (NX * NY)


def pack(parts):
    rows, where, at = [], {}, 0
    for name, a in parts:
        height = -(-a.shape[0] // 16) * 16
        block = np.zeros((height, 256), np.float64)
        block[: a.shape[0], : a.shape[1]] = a
        rows.append(block)
        where[name] = (at, a.shape[0], a.shape[1])
        at += height
    return np.concatenate(rows), where


def pack_split(parts):
    both = []
    for name, a in parts:
        hi, lo = np_split(a)
        if name in ("x2", "x3", "x4"):
            both.append((name, np.concatenate([hi.astype(np.float64), lo.astype(np.float64)])))
            continue
        both += [(name + "_hi", hi.astype(np.float64)), (name + "_lo", lo.astype(np.float64))]
    return both


@functools.lru_cache(None)
def tables():
    core_rows = np.arange(HALO, HALO + CORE)
    field_cols = np.arange(ROW0, ROW0 + ROWS)
    own_cols = np.arange(WIDE, WIDE + CORE)
    sides = np.zeros((2 * XB, 256))
    sides[:, :WIDE] = x_rows(np.arange(WIDE))
    sides[:, CORE : CORE + WIDE] = x_rows(np.arange(WIDE + CORE, NX))
    parts = [("cx_own", x_rows(own_cols)), ("cx_side", sides)]
    for t in range(2):
        pos = np.arange(2 * CORE) - t * CORE + HALO
        inside = (pos >= 0) & (pos < NY)
        parts.append((f"by{t}", y_lanes(pos) * inside[:, None]))
    parts += [("x2", x_back(field_cols)), ("x3", x_rows(field_cols)), ("x4", x_back(own_cols))]
    y2_hi, y2_lo = (a.astype(np.float64) for a in np_split(y_back(core_rows)))
    y3_hi, y3_lo = (a.astype(np.float64) for a in np_split(y_lanes(core_rows)))
    grad = pack_split(parts)
    grad += [("y2", np.concatenate([y2_hi, y2_lo], axis=1))]
    grad += [("y3_dup", np.concatenate([y3_hi, y3_hi])), ("y3_lo", y3_lo)]
    own = np.zeros((ROWS, CORE))
    own[np.arange(CORE) + WIDE - ROW0, np.arange(CORE)] = 1
    halo = np.zeros((ROWS, 256))
    for r in range(HALO):
        halo[HALO + r - ROW0, WIDE + r] = 1
        halo[WIDE + CORE + r - ROW0, CORE + WIDE + r] = 1
    grad += [("sel_own", own), ("sel_halo", halo)]
    offs = np.arange(KSIZE) - HALO
    kx = np.zeros((2 * XB, 128))
    kx[:, :KSIZE] = x_rows(offs)
    spec = [("kx", kx)]
    for m in range(4):
        ky = np.zeros((128, 2 * YB))
        ky[32 * m : 32 * m + KSIZE] = y_lanes(offs)
        spec.append((f"ky{m}", ky))
    sel = np.zeros((4, EDGE, 128))
    for r in range(WIDE):
        sel[0, r, CORE - WIDE + r] = 1
        sel[2, r, r] = 1
    for r in range(HALO):
        sel[1, WIDE + r, CORE - HALO + r] = 1
        sel[3, WIDE + r, r] = 1
    edge = [(f"edge{i}", sel[i]) for i in range(4)]
    edge.append(("flip", np.eye(CORE)[::-1]))
    return {"grad": pack(grad), "spec": pack(pack_split(spec)), "edge": pack(edge)}


def split(x):
    hi = x.astype(bf16)
    return hi, (x - hi.astype(f32)).astype(bf16)


def dot(a, b):
    return lax.dot_general(a, b, (((1,), (0,)), ((), ())), preferred_element_type=f32)


def dot_nt(a, b):
    return lax.dot_general(a, b, (((1,), (1,)), ((), ())), preferred_element_type=f32)


def dot3(a_hi, a_lo, b_hi, b_lo, mul=dot):
    return mul(a_hi, b_hi) + (mul(a_lo, b_hi) + mul(a_hi, b_lo))


def dot_stacked(table, b_hi, b_lo):
    rows = table.shape[0] // 2
    both = dot(table, b_hi)
    return both[:rows] + (both[rows:] + dot(table[:rows], b_lo))


def signed(spec):
    cc, cs = spec[:XB, :YB], spec[:XB, YB:]
    sc, ss = spec[XB:, :YB], spec[XB:, YB:]
    return cc - ss, -(cs + sc), cc + ss, sc - cs


def even_odd(pr, pi, mr, mi):
    top = jnp.concatenate([pr + mr, pi + mi], axis=1)
    low = jnp.concatenate([mi - pi, pr - mr], axis=1)
    return jnp.concatenate([top, low], axis=0)


def table_array(group):
    return jnp.asarray(tables()[group][0].astype(ml_dtypes.bfloat16))


def table_reader(group, ref):
    where = tables()[group][1]

    def table(name, half=None):
        at, height, width = where[name]
        lanes = slice(0, width) if half is None else slice(128 * half, 128 * half + 128)
        return ref[at : at + height, lanes]

    return table


def call(body, group, args, out_shape, scratch=(), smem=(), flops=0, nbytes=0, given=None):
    vm = pl.BlockSpec(memory_space=pltpu.VMEM)
    sm = pl.BlockSpec(memory_space=pltpu.SMEM)
    multi = isinstance(out_shape, (list, tuple))
    n_in = len(args)
    if group is not None:
        args = [*args, table_array(group) if given is None else given]

    def wrapped(*refs):
        if group is not None:
            refs = [*refs[:n_in], table_reader(group, refs[n_in]), *refs[n_in + 1 :]]
        body(*refs)

    return pl.pallas_call(
        wrapped,
        out_shape=out_shape,
        in_specs=[sm if i in smem else vm for i in range(len(args))],
        out_specs=[vm] * len(out_shape) if multi else vm,
        scratch_shapes=list(scratch),
        compiler_params=pltpu.CompilerParams(vmem_limit_bytes=VMEM_LIMIT),
        cost_estimate=pl.CostEstimate(flops=flops, bytes_accessed=nbytes, transcendentals=0),
    )(*args)


def is_upper():
    return lax.rem(lax.axis_index("depth"), 2) == 1


def is_even():
    return lax.rem(lax.axis_index("tile"), 2) == 0


def send_edges(right, left, a_ref, b_ref):
    even = is_even()
    a_ref[...] = jnp.where(even, right, left)
    b_ref[...] = jnp.where(even, left, right)


def edges_kernel(
    mask_hbm, target_hbm, table_hbm, ker_hbm, spec_hbm,
    a_ref, b_ref, ker_ref, spec_ref, mask_ref, target_ref, table_ref, sems,
):
    moves = [
        pltpu.make_async_copy(src, dst, sems.at[i])
        for i, (src, dst) in enumerate(
            (
                (mask_hbm, mask_ref),
                (target_hbm, target_ref),
                (table_hbm, table_ref),
                (ker_hbm, ker_ref),
                (spec_hbm, spec_ref),
            )
        )
    ]
    for move in moves:
        move.start()
    for move in moves[:3]:
        move.wait()
    tb = table_reader("edge", table_ref)
    m_hi, m_lo = split(mask_ref[...])
    tgt = target_ref[...].astype(f32).astype(bf16)
    right = dot_nt(tb("edge0"), m_hi) + dot_nt(tb("edge0"), m_lo) + dot_nt(tb("edge1"), tgt)
    left = dot_nt(tb("edge2"), m_hi) + dot_nt(tb("edge2"), m_lo) + dot_nt(tb("edge3"), tgt)
    send_edges(right, left, a_ref, b_ref)
    for move in moves[3:]:
        move.wait()


def send_first_edges(mask_rows, target_rows, kernels):
    height = mask_rows.shape[0]
    args = [mask_rows, target_rows, table_array("edge"), kernels, table_array("spec")]
    edge = jax.ShapeDtypeStruct((EDGE, height), f32)
    like = lambda x: jax.ShapeDtypeStruct(x.shape, x.dtype)
    vm = pl.BlockSpec(memory_space=pltpu.VMEM)
    return pl.pallas_call(
        edges_kernel,
        out_shape=[edge, edge, like(kernels), like(args[4])],
        in_specs=[pl.BlockSpec(memory_space=pltpu.HBM)] * 5,
        out_specs=[vm] * 4,
        scratch_shapes=[
            pltpu.VMEM(mask_rows.shape, f32),
            pltpu.VMEM(target_rows.shape, jnp.int32),
            pltpu.VMEM(args[2].shape, bf16),
            pltpu.SemaphoreType.DMA((5,)),
        ],
        compiler_params=pltpu.CompilerParams(vmem_limit_bytes=VMEM_LIMIT),
    )(*args)


def spectra_kernel(kern, ker_ref, tb, h_ref, hs_ref):
    hs_ref[...] = jnp.zeros_like(hs_ref)
    for k in range(kern):
        for part in range(2):
            row = 32 * (2 * k + part)
            hs_ref[row : row + KSIZE, :KSIZE] = ker_ref[part, 0, k]
    s_hi, s_lo = split(hs_ref[...])
    z = dot3(tb("kx_hi"), tb("kx_lo"), s_hi, s_lo, dot_nt)
    z_hi, z_lo = split(z)
    for c in range(2 * kern):
        lanes = slice(128 * (c // 4), 128 * (c // 4) + 128)
        spec = dot3(z_hi[:, lanes], z_lo[:, lanes], tb(f"ky{c % 4}_hi"), tb(f"ky{c % 4}_lo"))
        for j, comp in enumerate(signed(spec)):
            h_ref[c, j] = comp


def sides(a_ref, b_ref, tb):
    even = is_even()
    from_a, from_b = a_ref[...], b_ref[...]
    l_hi, l_lo = split(jnp.where(even, from_b, from_a))
    r_hi, r_lo = split(jnp.where(even, from_a, from_b))
    height = l_hi.shape[0]
    v = None
    for half, hi, lo in ((0, l_hi, l_lo), (1, r_hi, r_lo)):
        c_hi, c_lo = tb("cx_side_hi", half), tb("cx_side_lo", half)
        term = dot3(c_hi[:, :height], c_lo[:, :height], hi, lo)
        v = term if v is None else v + term
    return v, l_hi, r_hi


def to_spectrum(v, tb, f_ref, base):
    v_hi, v_lo = split(v)
    for t in range(2):
        spec = dot3(v_hi, v_lo, tb(f"by{t}_hi"), tb(f"by{t}_lo"))
        for j, comp in enumerate(signed(spec)):
            f_ref[t, j] = comp if base is None else base[t, j] - STEP_RATE * comp


def gradient_body(kern, last, f_ref, tgt_ref, h_ref, w_ref, thr_ref, tb, keep_ref, send_ref, fld, inten, tot):
    inten[...] = jnp.zeros_like(inten)

    @pl.loop(0, kern, unroll=True)
    def _(k):
        parts = [[], []]
        for part in range(2):
            hpr, hpi, hmr, hmi = (h_ref[2 * k + part, j] for j in range(4))
            for t in range(2):
                fpr, fpi, fmr, fmi = (f_ref[t, j] for j in range(4))
                pr, pi = hpr * fpr - hpi * fpi, hpr * fpi + hpi * fpr
                mr, mi = hmr * fmr - hmi * fmi, hmr * fmi + hmi * fmr
                parts[t].append(dot_stacked(tb("x2"), *split(even_odd(pr, pi, mr, mi))))
        for t in range(2):
            g_hi, g_lo = split(jnp.concatenate(parts[t], axis=0))
            r = dot(g_hi, tb("y2"))
            field = r[:, :CORE] + (r[:, CORE:] + dot(g_lo, tb("y2", 0)))
            fld[t, k] = field
            inten[t] += w_ref[0, k] * (field[:ROWS] * field[:ROWS] + field[ROWS:] * field[ROWS:])

    tile = lax.axis_index("tile")
    first = jnp.where(tile == 0, WIDE, HALO) - ROW0
    end = jnp.where(tile == last, WIDE + CORE, WIDE + CORE + HALO) - ROW0
    row = lax.broadcasted_iota(jnp.int32, (ROWS, CORE), 0)
    inside = (row >= first) & (row < end)
    for t in range(2):
        resist = jax.nn.sigmoid(STEEPNESS * (inten[t] - thr_ref[0]))
        target = tgt_ref[:, CORE * t : CORE * t + CORE]
        slope = 2.0 * (resist - target) * STEEPNESS * resist * (1.0 - resist)
        inten[t] = jnp.where(inside, 2.0 * slope, 0.0)
    tot[...] = jnp.zeros_like(tot)

    @pl.loop(0, kern, unroll=True)
    def _(k):
        acc = [[tot[t, j] for j in range(4)] for t in range(2)]
        back = []
        for t in range(2):
            scaled = w_ref[0, k] * inten[t]
            field = fld[t, k]
            r_hi, r_lo = split(
                jnp.concatenate([scaled * field[:ROWS], scaled * field[ROWS:]], axis=0)
            )
            w = dot(jnp.concatenate([r_hi, r_lo], axis=1), tb("y3_dup"))
            back.append(split(w + dot(r_hi, tb("y3_lo"))))
        for part in range(2):
            rows = slice(ROWS * part, ROWS * part + ROWS)
            hpr, hpi, hmr, hmi = (h_ref[2 * k + part, j] for j in range(4))
            for t in range(2):
                w_hi, w_lo = back[t]
                spec = dot_stacked(tb("x3"), w_hi[rows], w_lo[rows])
                bpr, bpi, bmr, bmi = signed(spec)
                acc[t][0] = acc[t][0] + (hpr * bpr + hpi * bpi)
                acc[t][1] = acc[t][1] + (hpr * bpi - hpi * bpr)
                acc[t][2] = acc[t][2] + (hmr * bmr + hmi * bmi)
                acc[t][3] = acc[t][3] + (hmr * bmi - hmi * bmr)
        for t in range(2):
            for j in range(4):
                tot[t, j] = acc[t][j]

    lane = lax.broadcasted_iota(jnp.int32, (1, 2 * YB), 1)
    bin_at = lax.rem(lane, YB)
    weight = jnp.where((bin_at == 0) | (bin_at == NU - 1), 1.0, 2.0) / (NX * NY)
    weight = jnp.where(lane < YB, weight, -weight)
    out = None
    for t in range(2):
        r_hi, r_lo = split(even_odd(*(tot[t, j] for j in range(4))))
        u_hi, u_lo = split(weight * dot_stacked(tb("x4"), r_hi, r_lo))
        term = dot3(tb(f"by{t}_hi"), tb(f"by{t}_lo"), u_hi, u_lo, dot_nt)
        out = term if out is None else out + term
    half = is_upper()
    for t in range(2):
        at = slice(HALF * t, HALF * t + HALF)
        top, low = out[CORE * t : CORE * t + HALF], out[CORE * t + HALF : CORE * t + CORE]
        keep_ref[at] = jnp.where(half, low, top)
        send_ref[at] = jnp.where(half, top, low)


def join(mine_ref, peer_ref, t):
    at = slice(HALF * t, HALF * t + HALF)
    mine, peer, half = mine_ref[at], peer_ref[at], is_upper()
    return jnp.concatenate([jnp.where(half, peer, mine), jnp.where(half, mine, peer)], axis=0)


def first_kernel(
    kern, last, w_ref, thr_ref, mask_ref, target_ref, a_ref, b_ref, h_ref, tb,
    keep_ref, send_ref, f_ref, tgt_ref, fld, inten, tot,
):
    m_hi, m_lo = split(mask_ref[...])
    v, left, right = sides(a_ref, b_ref, tb)
    v = v + dot3(tb("cx_own_hi"), tb("cx_own_lo"), m_hi, m_lo, dot_nt)
    to_spectrum(v, tb, f_ref, None)
    tgt_ref[...] = (
        dot_nt(tb("sel_own"), target_ref[...].astype(f32).astype(bf16))
        + dot(tb("sel_halo", 0)[:, :EDGE], left)
        + dot(tb("sel_halo", 1)[:, :EDGE], right)
    )
    refs = (w_ref, thr_ref, tb, keep_ref, send_ref, fld, inten, tot)
    gradient_body(kern, last, f_ref, tgt_ref, h_ref, *refs)


def later_kernel(
    kern, last, w_ref, thr_ref, mine_ref, peer_ref, rim_ref, far_ref, f_in_ref, tgt_ref, h_ref,
    tb, keep_ref, send_ref, f_ref, fld, inten, tot,
):
    own = [join(mine_ref, peer_ref, t) for t in range(2)]
    s_hi, s_lo = split(jnp.concatenate(own, axis=0))
    half = is_upper()
    rim, far = rim_ref[...], far_ref[...]
    first, second = jnp.where(half, far, rim), jnp.where(half, rim, far)
    low = lax.broadcasted_iota(jnp.int32, rim.shape, 1) < HALF
    tile0 = jnp.where(low, first, pltpu.roll(second, HALF, 1))
    tile1 = jnp.where(low, pltpu.roll(first, HALF, 1), second)
    rims = jnp.concatenate([tile0, tile1], axis=1)
    v, _, _ = sides(rims[:WIDE_PAD], rims[WIDE_PAD:], tb)
    v = v + dot3(tb("cx_own_hi"), tb("cx_own_lo"), s_hi, s_lo, dot_nt)
    to_spectrum(v, tb, f_ref, f_in_ref)
    refs = (w_ref, thr_ref, tb, keep_ref, send_ref, fld, inten, tot)
    gradient_body(kern, last, f_ref, tgt_ref, h_ref, *refs)


def match_kernel(n_got, edges, table_ref, own_ref, *refs):
    got_refs, (tb, out_ref, *edge_refs) = refs[:n_got], refs[n_got:]
    device = lax.axis_index("tile")
    own = own_ref[...]
    mine, other = [], []
    for t in range(2):
        rows = slice(HALF * t, HALF * t + HALF)
        mine.append(own[rows])
        bit = lax.bitwise_xor(table_ref[t], 2 * device + t)
        value = jnp.where(bit == 1, own[HALF * (1 - t) : HALF * (1 - t) + HALF], mine[t])
        for b, got in enumerate(got_refs):
            value = jnp.where(bit == 2 << b, got[rows], value)
        other.append(value)
    hi, lo = split(jnp.concatenate(other, axis=0))
    turned = dot(hi, tb("flip")) + dot(lo, tb("flip"))
    tiles = []
    for t in range(2):
        flipped = turned[HALF * t : HALF * t + HALF]
        tiles.append(0.5 * (mine[t] + jnp.where(table_ref[2 + t] == 1, flipped, other[t])))
    matched = jnp.concatenate(tiles, axis=0)
    out_ref[...] = matched
    if edges:
        hi, lo = split(matched)
        right, left = tb("edge0")[:WIDE_PAD], tb("edge2")[:WIDE_PAD]
        right = dot_nt(right, hi) + dot_nt(right, lo)
        left = dot_nt(left, hi) + dot_nt(left, lo)
        send_edges(right, left, *edge_refs)


def final_kernel(n_moves, mask_ref, *refs):
    moves, (mask_out, grad_out) = refs[: 2 * n_moves], refs[2 * n_moves :]
    for t in range(2):
        now = mask_ref[t]
        for mine, peer in zip(moves[::2], moves[1::2]):
            step = join(mine, peer, t)
            now = now - STEP_RATE * step
        grad_out[t] = step
        mask_out[t] = now


def per_device(
    n_tile, n_depth, mask_tiles, target_tiles, kernels, socs_weights, thresholds,
    partner_table, mirror_flags,
):
    tiles_dev, core, _ = mask_tiles.shape
    kern = kernels.shape[2]
    assert tiles_dev == 2 and core == CORE
    pairs_a = [(i, i ^ 1) for i in range(n_tile)]
    pairs_b = [p for i in range(1, n_tile - 1, 2) for p in ((i, i + 1), (i + 1, i))]

    def swap_edges(send_a, send_b):
        return lax.ppermute(send_b, "tile", pairs_b), lax.ppermute(send_a, "tile", pairs_a)

    def peer_of(x, bit):
        return lax.ppermute(x, "depth", [(i, i ^ bit) for i in range(n_depth)])

    def gather_sum(keep, send):
        total = keep + peer_of(send, 1)
        bit = 2
        while bit < n_depth:
            total = total + peer_of(total, bit)
            bit *= 2
        bits = [1 << b for b in range(n_tile.bit_length() - 1)]
        got = [
            lax.ppermute(total, "tile", [(i, i ^ bit) for i in range(n_tile)])
            for bit in reversed(bits)
        ]
        return total, got[::-1]

    mask_rows = mask_tiles.reshape(tiles_dev * core, core)
    target_rows = target_tiles.reshape(tiles_dev * core, core)
    strip = jax.ShapeDtypeStruct((core, core), f32)
    side = jax.ShapeDtypeStruct((WIDE_PAD, core), f32)
    freq = jax.ShapeDtypeStruct((2, 4, XB, YB), f32)
    goal = jax.ShapeDtypeStruct((ROWS, 2 * CORE), f32)
    tiles = jax.ShapeDtypeStruct((tiles_dev, core, core), f32)
    scratch = [
        pltpu.VMEM((2, kern, 2 * ROWS, CORE), f32),
        pltpu.VMEM((2, ROWS, CORE), f32),
        pltpu.VMEM((2, 4, XB, YB), f32),
    ]

    send_a, send_b, kernels, spec_table = send_first_edges(mask_rows, target_rows, kernels)
    from_b, from_a = swap_edges(send_a, send_b)
    table = jnp.concatenate([partner_table, mirror_flags])
    spectra = call(
        functools.partial(spectra_kernel, kern),
        "spec",
        [kernels],
        jax.ShapeDtypeStruct((2 * kern, 4, XB, YB), f32),
        [pltpu.VMEM((32 * 2 * kern, 128), f32)],
        flops=3 * 10**9,
        nbytes=4 * 10**6,
        given=spec_table,
    )
    keep, send, freq_now, goals = call(
        functools.partial(first_kernel, kern, n_tile - 1),
        "grad",
        [socs_weights, thresholds, mask_rows, target_rows, from_a, from_b, spectra],
        [strip, strip, freq, goal],
        scratch,
        smem=(0, 1),
    )
    moves = []
    for step in range(1, STEPS + 1):
        more = step < STEPS
        total, got = gather_sum(keep, send)
        outs = call(
            functools.partial(match_kernel, len(got), more),
            "edge",
            [table, total, *got],
            [strip, side, side] if more else [strip],
            smem=(0,),
        )
        mine = outs[0]
        peer = peer_of(mine, 1)
        moves += [mine, peer]
        if more:
            from_b, from_a = swap_edges(*outs[1:])
            rim = jnp.concatenate([from_a, from_b])
            far = peer_of(rim, 1)
            keep, send, freq_now = call(
                functools.partial(later_kernel, kern, n_tile - 1),
                "grad",
                [socs_weights, thresholds, mine, peer, rim, far, freq_now, goals, spectra],
                [strip, strip, freq],
                scratch,
                smem=(0, 1),
            )
    final = functools.partial(final_kernel, STEPS)
    return tuple(call(final, None, [mask_tiles, *moves], [tiles, tiles]))


def solution(mesh):
    return jax.shard_map(
        functools.partial(per_device, mesh.shape["tile"], mesh.shape["depth"]),
        mesh=mesh,
        in_specs=(
            P("tile", None, None),
            P("tile", None, None),
            P(None, "depth", None, None, None),
            P("depth", None),
            P("depth"),
            P("tile"),
            P("tile"),
        ),
        out_specs=(P("tile", None, None), P("tile", None, None)),
        check_vma=False,
    )
```

```python
import functools

import jax
import jax.numpy as jnp
import ml_dtypes
import numpy as np
from jax import lax
from jax.experimental import pallas as pl
from jax.experimental.pallas import tpu as pltpu
from jax.sharding import PartitionSpec as P

HALO = 12
KSIZE = 25
STEPS = 2
STEEPNESS = 3.0
STEP_RATE = 0.05

CORE = 128
NY = 152
NX = 176
WIDE = 2 * HALO
XB = 96
YB = 128
NU = NY // 2 + 1
NV = NX // 2 + 1
ROWS = 160
ROW0 = 8
EDGE = 48
WIDE_PAD = 32
VMEM_LIMIT = 24 * 1024 * 1024

f32 = jnp.float32
bf16 = jnp.bfloat16


def np_split(a):
    hi = np.asarray(a, np.float32).astype(ml_dtypes.bfloat16)
    lo = (np.asarray(a, np.float64) - hi.astype(np.float64)).astype(ml_dtypes.bfloat16)
    return hi, lo


def x_rows(cols):
    out = np.zeros((2 * XB, len(cols)))
    ang = 2 * np.pi * np.outer(np.arange(NV), cols) / NX
    out[:NV] = np.cos(ang)
    out[XB : XB + NV] = np.sin(ang)
    out[XB] = 0.0
    out[XB + NV - 1] = 0.0
    return out


def y_lanes(rows):
    out = np.zeros((len(rows), 2 * YB))
    ang = 2 * np.pi * np.outer(rows, np.arange(NU)) / NY
    out[:, :NU] = np.cos(ang)
    out[:, YB : YB + NU] = np.sin(ang)
    out[:, YB] = 0.0
    out[:, YB + NU - 1] = 0.0
    return out


def half_weights(bins):
    weights = np.full(bins, 2.0)
    weights[0] = weights[-1] = 1.0
    return weights


def x_back(cols):
    kappa = np.zeros(2 * XB)
    kappa[:NV] = half_weights(NV) / 2
    kappa[XB : XB + NV] = half_weights(NV) / 2
    return x_rows(cols).T * kappa


def y_back(rows):
    weight = np.zeros(2 * YB)
    weight[:NU] = half_weights(NU)
    weight[YB : YB + NU] = -half_weights(NU)
    return (y_lanes(rows) * weight).T / (NX * NY)


def pack(parts):
    rows, where, at = [], {}, 0
    for name, a in parts:
        height = -(-a.shape[0] // 16) * 16
        block = np.zeros((height, 256), np.float64)
        block[: a.shape[0], : a.shape[1]] = a
        rows.append(block)
        where[name] = (at, a.shape[0], a.shape[1])
        at += height
    return np.concatenate(rows), where


def pack_split(parts):
    both = []
    for name, a in parts:
        hi, lo = np_split(a)
        if name in ("x2", "x3", "x4"):
            both.append((name, np.concatenate([hi.astype(np.float64), lo.astype(np.float64)])))
            continue
        both += [(name + "_hi", hi.astype(np.float64)), (name + "_lo", lo.astype(np.float64))]
    return both


@functools.lru_cache(None)
def tables():
    core_rows = np.arange(HALO, HALO + CORE)
    field_cols = np.arange(ROW0, ROW0 + ROWS)
    own_cols = np.arange(WIDE, WIDE + CORE)
    sides = np.zeros((2 * XB, 256))
    sides[:, :WIDE] = x_rows(np.arange(WIDE))
    sides[:, CORE : CORE + WIDE] = x_rows(np.arange(WIDE + CORE, NX))
    parts = [("cx_own", x_rows(own_cols)), ("cx_side", sides)]
    for t in range(2):
        pos = np.arange(2 * CORE) - t * CORE + HALO
        inside = (pos >= 0) & (pos < NY)
        parts.append((f"by{t}", y_lanes(pos) * inside[:, None]))
    parts += [("x2", x_back(field_cols)), ("x3", x_rows(field_cols)), ("x4", x_back(own_cols))]
    y2_hi, y2_lo = (a.astype(np.float64) for a in np_split(y_back(core_rows)))
    y3_hi, y3_lo = (a.astype(np.float64) for a in np_split(y_lanes(core_rows)))
    grad = pack_split(parts)
    grad += [("y2", np.concatenate([y2_hi, y2_lo], axis=1))]
    grad += [("y3_dup", np.concatenate([y3_hi, y3_hi])), ("y3_lo", y3_lo)]
    own = np.zeros((ROWS, CORE))
    own[np.arange(CORE) + WIDE - ROW0, np.arange(CORE)] = 1
    halo = np.zeros((ROWS, 256))
    for r in range(HALO):
        halo[HALO + r - ROW0, WIDE + r] = 1
        halo[WIDE + CORE + r - ROW0, CORE + WIDE + r] = 1
    grad += [("sel_own", own), ("sel_halo", halo)]
    offs = np.arange(KSIZE) - HALO
    kx = np.zeros((2 * XB, 128))
    kx[:, :KSIZE] = x_rows(offs)
    spec = [("kx", kx)]
    for m in range(4):
        ky = np.zeros((128, 2 * YB))
        ky[32 * m : 32 * m + KSIZE] = y_lanes(offs)
        spec.append((f"ky{m}", ky))
    return {"grad": pack(grad), "spec": pack(pack_split(spec))}


def split(x):
    hi = x.astype(bf16)
    return hi, (x - hi.astype(f32)).astype(bf16)


def dot(a, b):
    return lax.dot_general(a, b, (((1,), (0,)), ((), ())), preferred_element_type=f32)


def dot_nt(a, b):
    return lax.dot_general(a, b, (((1,), (1,)), ((), ())), preferred_element_type=f32)


def dot3(a_hi, a_lo, b_hi, b_lo, mul=dot):
    return mul(a_hi, b_hi) + (mul(a_lo, b_hi) + mul(a_hi, b_lo))


def dot_stacked(table, b_hi, b_lo):
    rows = table.shape[0] // 2
    both = dot(table, b_hi)
    return both[:rows] + (both[rows:] + dot(table[:rows], b_lo))


def signed(spec):
    cc, cs = spec[:XB, :YB], spec[:XB, YB:]
    sc, ss = spec[XB:, :YB], spec[XB:, YB:]
    return cc - ss, -(cs + sc), cc + ss, sc - cs


def even_odd(pr, pi, mr, mi):
    top = jnp.concatenate([pr + mr, pi + mi], axis=1)
    low = jnp.concatenate([mi - pi, pr - mr], axis=1)
    return jnp.concatenate([top, low], axis=0)


def table_array(group):
    return jnp.asarray(tables()[group][0].astype(ml_dtypes.bfloat16))


def table_reader(group, ref):
    where = tables()[group][1]

    def table(name, half=None):
        at, height, width = where[name]
        lanes = slice(0, width) if half is None else slice(128 * half, 128 * half + 128)
        return ref[at : at + height, lanes]

    return table


def call(body, group, args, out_shape, scratch=(), smem=(), flops=0, nbytes=0):
    vm = pl.BlockSpec(memory_space=pltpu.VMEM)
    sm = pl.BlockSpec(memory_space=pltpu.SMEM)
    n_in = len(args)
    if group is not None:
        args = [*args, table_array(group)]

    def wrapped(*refs):
        if group is not None:
            refs = [*refs[:n_in], table_reader(group, refs[n_in]), *refs[n_in + 1 :]]
        body(*refs)

    return pl.pallas_call(
        wrapped,
        out_shape=out_shape,
        in_specs=[sm if i in smem else vm for i in range(len(args))],
        out_specs=[vm] * len(out_shape),
        scratch_shapes=list(scratch),
        compiler_params=pltpu.CompilerParams(vmem_limit_bytes=VMEM_LIMIT),
        cost_estimate=pl.CostEstimate(flops=flops, bytes_accessed=nbytes, transcendentals=0),
    )(*args)


def is_even():
    return lax.rem(lax.axis_index("tile"), 2) == 0


def send_edges(right, left, a_ref, b_ref):
    even = is_even()
    a_ref[...] = jnp.where(even, right, left)
    b_ref[...] = jnp.where(even, left, right)


def picker(rows, first, count, col):
    row = lax.broadcasted_iota(jnp.int32, (rows, CORE), 0)
    lane = lax.broadcasted_iota(jnp.int32, (rows, CORE), 1)
    hit = (row - first == lane - col) & (row >= first) & (row < first + count)
    return jnp.where(hit, 1.0, 0.0).astype(bf16)


def edges_of(rows, strip, extra=None):
    hi, lo = split(strip)
    both = []
    for col, more in ((CORE - WIDE, CORE - HALO), (0, 0)):
        pick = picker(rows, 0, WIDE, col)
        edge = dot_nt(pick, hi) + dot_nt(pick, lo)
        if extra is not None:
            edge = edge + dot_nt(picker(rows, WIDE, HALO, more), extra)
        both.append(edge)
    return both


def edges_kernel(mask_ref, target_ref, a_ref, b_ref):
    target = target_ref[...].astype(f32).astype(bf16)
    send_edges(*edges_of(EDGE, mask_ref[...], target), a_ref, b_ref)


def spectra_kernel(kern, ker_ref, tb, h_ref, hs_ref):
    hs_ref[...] = jnp.zeros_like(hs_ref)
    for k in range(kern):
        for part in range(2):
            row = 32 * (2 * k + part)
            hs_ref[row : row + KSIZE, :KSIZE] = ker_ref[part, k, :, 0, :]
    s_hi, s_lo = split(hs_ref[...])
    z = dot3(tb("kx_hi"), tb("kx_lo"), s_hi, s_lo, dot_nt)
    z_hi, z_lo = split(z)
    for c in range(2 * kern):
        lanes = slice(128 * (c // 4), 128 * (c // 4) + 128)
        spec = dot3(z_hi[:, lanes], z_lo[:, lanes], tb(f"ky{c % 4}_hi"), tb(f"ky{c % 4}_lo"))
        for j, comp in enumerate(signed(spec)):
            h_ref[c, j] = comp


def sides(a_ref, b_ref, tb):
    even = is_even()
    from_a, from_b = a_ref[...], b_ref[...]
    l_hi, l_lo = split(jnp.where(even, from_b, from_a))
    r_hi, r_lo = split(jnp.where(even, from_a, from_b))
    height = l_hi.shape[0]
    v = None
    for half, hi, lo in ((0, l_hi, l_lo), (1, r_hi, r_lo)):
        c_hi, c_lo = tb("cx_side_hi", half), tb("cx_side_lo", half)
        term = dot3(c_hi[:, :height], c_lo[:, :height], hi, lo)
        v = term if v is None else v + term
    return v, l_hi, r_hi


def to_spectrum(v, tb, f_ref, base):
    v_hi, v_lo = split(v)
    for t in range(2):
        spec = dot3(v_hi, v_lo, tb(f"by{t}_hi"), tb(f"by{t}_lo"))
        for j, comp in enumerate(signed(spec)):
            f_ref[t, j] = comp if base is None else base[t, j] - STEP_RATE * comp


def gradient_body(kern, last, f_ref, tgt_ref, h_ref, w_ref, thr_ref, tb, g_ref, fld, inten, tot):
    inten[...] = jnp.zeros_like(inten)

    @pl.loop(0, kern, unroll=True)
    def _(k):
        for t in range(2):
            parts = []
            for part in range(2):
                hpr, hpi, hmr, hmi = (h_ref[2 * k + part, j] for j in range(4))
                fpr, fpi, fmr, fmi = (f_ref[t, j] for j in range(4))
                pr, pi = hpr * fpr - hpi * fpi, hpr * fpi + hpi * fpr
                mr, mi = hmr * fmr - hmi * fmi, hmr * fmi + hmi * fmr
                parts.append(even_odd(pr, pi, mr, mi))
            p_hi, p_lo = split(jnp.concatenate(parts, axis=0))
            z = dot(p_hi, tb("y2"))
            z = z[:, :CORE] + (z[:, CORE:] + dot(p_lo, tb("y2", 0)))
            z_hi, z_lo = split(jnp.concatenate([z[: 2 * XB], z[2 * XB :]], axis=1))
            field = dot_stacked(tb("x2"), z_hi, z_lo)
            fld[t, k] = field
            re, im = field[:, :CORE], field[:, CORE:]
            inten[t] += w_ref[0, k] * (re * re + im * im)

    tile = lax.axis_index("tile")
    first = jnp.where(tile == 0, WIDE, HALO) - ROW0
    end = jnp.where(tile == last, WIDE + CORE, WIDE + CORE + HALO) - ROW0
    row = lax.broadcasted_iota(jnp.int32, (ROWS, CORE), 0)
    inside = (row >= first) & (row < end)
    for t in range(2):
        resist = jax.nn.sigmoid(STEEPNESS * (inten[t] - thr_ref[0]))
        target = tgt_ref[:, CORE * t : CORE * t + CORE]
        slope = 2.0 * (resist - target) * STEEPNESS * resist * (1.0 - resist)
        inten[t] = jnp.where(inside, 2.0 * slope, 0.0)
    tot[...] = jnp.zeros_like(tot)

    @pl.loop(0, kern, unroll=True)
    def _(k):
        for t in range(2):
            scaled = w_ref[0, k] * inten[t]
            field = fld[t, k]
            r_hi, r_lo = split(
                jnp.concatenate([scaled * field[:, :CORE], scaled * field[:, CORE:]], axis=1)
            )
            w_hi, w_lo = split(dot_stacked(tb("x3"), r_hi, r_lo))
            his = [w_hi[:, :CORE], w_hi[:, CORE:]]
            los = [w_lo[:, :CORE], w_lo[:, CORE:]]
            both = [jnp.concatenate([his[p], los[p]], axis=1) for p in range(2)]
            specs = dot(jnp.concatenate(both, axis=0), tb("y3_dup"))
            specs = specs + dot(jnp.concatenate(his, axis=0), tb("y3_lo"))
            acc = [tot[t, j] for j in range(4)]
            for part in range(2):
                spec = specs[2 * XB * part : 2 * XB * part + 2 * XB]
                cc, cs = spec[:XB, :YB], spec[:XB, YB:]
                sc, ss = spec[XB:, :YB], spec[XB:, YB:]
                bpr, neg, bmr, bmi = cc - ss, cs + sc, cc + ss, sc - cs
                hpr, hpi, hmr, hmi = (h_ref[2 * k + part, j] for j in range(4))
                acc[0] = acc[0] + (hpr * bpr - hpi * neg)
                acc[1] = acc[1] - (hpr * neg + hpi * bpr)
                acc[2] = acc[2] + (hmr * bmr + hmi * bmi)
                acc[3] = acc[3] + (hmr * bmi - hmi * bmr)
            for j in range(4):
                tot[t, j] = acc[j]

    lane = lax.broadcasted_iota(jnp.int32, (1, 2 * YB), 1)
    bin_at = lax.rem(lane, YB)
    weight = jnp.where((bin_at == 0) | (bin_at == NU - 1), 1.0, 2.0) / (NX * NY)
    weight = jnp.where(lane < YB, weight, -weight)
    out = None
    for t in range(2):
        r_hi, r_lo = split(even_odd(*(tot[t, j] for j in range(4))))
        u_hi, u_lo = split(weight * dot_stacked(tb("x4"), r_hi, r_lo))
        term = dot3(tb(f"by{t}_hi"), tb(f"by{t}_lo"), u_hi, u_lo, dot_nt)
        out = term if out is None else out + term
    g_ref[...] = out


def first_kernel(
    kern, last, w_ref, thr_ref, mask_ref, target_ref, a_ref, b_ref, h_ref, tb,
    g_ref, f_ref, tgt_ref, fld, inten, tot,
):
    m_hi, m_lo = split(mask_ref[...])
    v, left, right = sides(a_ref, b_ref, tb)
    v = v + dot3(tb("cx_own_hi"), tb("cx_own_lo"), m_hi, m_lo, dot_nt)
    to_spectrum(v, tb, f_ref, None)
    tgt_ref[...] = (
        dot_nt(tb("sel_own"), target_ref[...].astype(f32).astype(bf16))
        + dot(tb("sel_halo", 0)[:, :EDGE], left)
        + dot(tb("sel_halo", 1)[:, :EDGE], right)
    )
    gradient_body(kern, last, f_ref, tgt_ref, h_ref, w_ref, thr_ref, tb, g_ref, fld, inten, tot)


def later_kernel(
    kern, last, w_ref, thr_ref, mine_ref, peer_ref, rim_ref, far_ref, f_in_ref, tgt_ref, h_ref,
    tb, g_ref, f_ref, fld, inten, tot,
):
    s_hi, s_lo = split(mine_ref[...] + peer_ref[...])
    rims = rim_ref[...] + far_ref[...]
    v, _, _ = sides(rims[:WIDE_PAD], rims[WIDE_PAD:], tb)
    v = v + dot3(tb("cx_own_hi"), tb("cx_own_lo"), s_hi, s_lo, dot_nt)
    to_spectrum(v, tb, f_ref, f_in_ref)
    gradient_body(kern, last, f_ref, tgt_ref, h_ref, w_ref, thr_ref, tb, g_ref, fld, inten, tot)


def match_kernel(n_got, table_ref, own_ref, *refs):
    got_refs, (out_ref, *edge_refs) = refs[:n_got], refs[n_got:]
    device = lax.axis_index("tile")
    other = []
    for t in range(2):
        rows = slice(CORE * t, CORE * t + CORE)
        bit = lax.bitwise_xor(table_ref[t], 2 * device + t)
        value = jnp.where(bit == 1, own_ref[CORE * (1 - t) : CORE * (2 - t)], own_ref[rows])
        for b, got in enumerate(got_refs):
            value = jnp.where(bit == 2 << b, got[rows], value)
        other.append(value)
    row = lax.broadcasted_iota(jnp.int32, (CORE, CORE), 0)
    lane = lax.broadcasted_iota(jnp.int32, (CORE, CORE), 1)
    flip = jnp.where(row + lane == CORE - 1, 1.0, 0.0).astype(bf16)
    hi, lo = split(jnp.concatenate(other, axis=0))
    turned = dot(hi, flip) + dot(lo, flip)
    tiles = []
    for t in range(2):
        rows = slice(CORE * t, CORE * t + CORE)
        value = jnp.where(table_ref[2 + t] == 1, turned[rows], other[t])
        tiles.append(0.5 * (own_ref[rows] + value))
    matched = jnp.concatenate(tiles, axis=0)
    out_ref[...] = matched
    if edge_refs:
        send_edges(*edges_of(WIDE_PAD, matched), *edge_refs)


def final_kernel(n_moves, mask_ref, *refs):
    moves, (mask_out, grad_out) = refs[: 2 * n_moves], refs[2 * n_moves :]
    for t in range(2):
        rows = slice(CORE * t, CORE * t + CORE)
        now = mask_ref[t]
        for mine, peer in zip(moves[::2], moves[1::2]):
            step = mine[rows] + peer[rows]
            now = now - STEP_RATE * step
        grad_out[t] = step
        mask_out[t] = now


def per_device(
    n_tile, n_depth, mask_tiles, target_tiles, kernels, socs_weights, thresholds,
    partner_table, mirror_flags,
):
    tiles_dev, core, _ = mask_tiles.shape
    kern = kernels.shape[2]
    assert tiles_dev == 2 and core == CORE
    pairs_a = [(i, i ^ 1) for i in range(n_tile)]
    pairs_b = [p for i in range(1, n_tile - 1, 2) for p in ((i, i + 1), (i + 1, i))]

    def swap_edges(send_a, send_b):
        return lax.ppermute(send_b, "tile", pairs_b), lax.ppermute(send_a, "tile", pairs_a)

    def depth_pair(x):
        bit = 1
        while True:
            peer = lax.ppermute(x, "depth", [(i, i ^ bit) for i in range(n_depth)])
            bit *= 2
            if bit >= n_depth:
                return x, peer
            x = x + peer

    def from_partners(grad):
        bits = [1 << b for b in range(n_tile.bit_length() - 1)]
        got = [
            lax.ppermute(grad, "tile", [(i, i ^ bit) for i in range(n_tile)])
            for bit in reversed(bits)
        ]
        return got[::-1]

    mask_rows = mask_tiles.reshape(tiles_dev * core, core)
    target_rows = target_tiles.reshape(tiles_dev * core, core)
    strip = jax.ShapeDtypeStruct((tiles_dev * core, core), f32)
    side = jax.ShapeDtypeStruct((WIDE_PAD, tiles_dev * core), f32)
    freq = jax.ShapeDtypeStruct((2, 4, XB, YB), f32)
    goal = jax.ShapeDtypeStruct((ROWS, 2 * CORE), f32)
    tiles = jax.ShapeDtypeStruct((tiles_dev, core, core), f32)
    scratch = [
        pltpu.VMEM((2, kern, ROWS, 2 * CORE), f32),
        pltpu.VMEM((2, ROWS, CORE), f32),
        pltpu.VMEM((2, 4, XB, YB), f32),
    ]

    edge = jax.ShapeDtypeStruct((EDGE, tiles_dev * core), f32)
    send_a, send_b = call(
        edges_kernel, None, [mask_rows, target_rows], [edge, edge], flops=3 * 10**9
    )
    from_b, from_a = swap_edges(send_a, send_b)
    table = jnp.concatenate([partner_table, mirror_flags])
    (spectra,) = call(
        functools.partial(spectra_kernel, kern),
        "spec",
        [kernels.transpose(0, 2, 3, 1, 4)],
        [jax.ShapeDtypeStruct((2 * kern, 4, XB, YB), f32)],
        [pltpu.VMEM((32 * 2 * kern, 128), f32)],
        flops=3 * 10**9,
        nbytes=4 * 10**6,
    )
    grad, freq_now, goals = call(
        functools.partial(first_kernel, kern, n_tile - 1),
        "grad",
        [socs_weights, thresholds, mask_rows, target_rows, from_a, from_b, spectra],
        [strip, freq, goal],
        scratch,
        smem=(0, 1),
        flops=10**10,
    )
    moves = []
    for step in range(1, STEPS + 1):
        got = from_partners(grad)
        outs = call(
            functools.partial(match_kernel, len(got)),
            None,
            [table, grad, *got],
            [strip, side, side] if step < STEPS else [strip],
            smem=(0,),
        )
        if step == STEPS:
            moves += depth_pair(outs[0])
            break
        from_b, from_a = swap_edges(*outs[1:])
        moves += depth_pair(outs[0])
        rims = depth_pair(jnp.concatenate([from_a, from_b]))
        kept = step + 1 < STEPS
        grad, *rest = call(
            functools.partial(later_kernel, kern, n_tile - 1),
            "grad",
            [socs_weights, thresholds, *moves[-2:], *rims, freq_now, goals, spectra],
            [strip, freq] if kept else [strip],
            scratch if kept else [pltpu.VMEM(freq.shape, f32)] + scratch,
            smem=(0, 1),
            flops=10**10,
        )
        freq_now = rest[0] if kept else None
    final = functools.partial(final_kernel, STEPS)
    return tuple(call(final, None, [mask_tiles, *moves], [tiles, tiles]))


def solution(mesh):
    return jax.shard_map(
        functools.partial(per_device, mesh.shape["tile"], mesh.shape["depth"]),
        mesh=mesh,
        in_specs=(
            P("tile", None, None),
            P("tile", None, None),
            P(None, "depth", None, None, None),
            P("depth", None),
            P("depth"),
            P("tile"),
            P("tile"),
        ),
        out_specs=(P("tile", None, None), P("tile", None, None)),
        check_vma=False,
    )
```

```python
import functools

import jax
import jax.numpy as jnp
import ml_dtypes
import numpy as np
from jax import lax
from jax.experimental import pallas as pl
from jax.experimental.pallas import tpu as pltpu
from jax.sharding import PartitionSpec as P

HALO = 12
KSIZE = 25
STEPS = 2
STEEPNESS = 3.0
STEP_RATE = 0.05

CORE = 128
NY = 152
NX = 176
WIDE = 2 * HALO
XB = 96
YB = 128
NU = NY // 2 + 1
NV = NX // 2 + 1
ROWS = 160
ROW0 = 8
EDGE = 48
WIDE_PAD = 32
VMEM_LIMIT = 24 * 1024 * 1024

f32 = jnp.float32
bf16 = jnp.bfloat16


def np_split(a):
    hi = np.asarray(a, np.float32).astype(ml_dtypes.bfloat16)
    lo = (np.asarray(a, np.float64) - hi.astype(np.float64)).astype(ml_dtypes.bfloat16)
    return hi, lo


def x_rows(cols):
    out = np.zeros((2 * XB, len(cols)))
    ang = 2 * np.pi * np.outer(np.arange(NV), cols) / NX
    out[:NV] = np.cos(ang)
    out[XB : XB + NV] = np.sin(ang)
    out[XB] = 0.0
    out[XB + NV - 1] = 0.0
    return out


def y_lanes(rows):
    out = np.zeros((len(rows), 2 * YB))
    ang = 2 * np.pi * np.outer(rows, np.arange(NU)) / NY
    out[:, :NU] = np.cos(ang)
    out[:, YB : YB + NU] = np.sin(ang)
    out[:, YB] = 0.0
    out[:, YB + NU - 1] = 0.0
    return out


def half_weights(bins):
    weights = np.full(bins, 2.0)
    weights[0] = weights[-1] = 1.0
    return weights


def x_back(cols):
    kappa = np.zeros(2 * XB)
    kappa[:NV] = half_weights(NV) / 2
    kappa[XB : XB + NV] = half_weights(NV) / 2
    return x_rows(cols).T * kappa


def y_back(rows):
    weight = np.zeros(2 * YB)
    weight[:NU] = half_weights(NU)
    weight[YB : YB + NU] = -half_weights(NU)
    return (y_lanes(rows) * weight).T / (NX * NY)


def pack(parts):
    rows, where, at = [], {}, 0
    for name, a in parts:
        height = -(-a.shape[0] // 16) * 16
        block = np.zeros((height, 256), np.float64)
        block[: a.shape[0], : a.shape[1]] = a
        rows.append(block)
        where[name] = (at, a.shape[0], a.shape[1])
        at += height
    return np.concatenate(rows), where


def pack_split(parts):
    both = []
    for name, a in parts:
        hi, lo = np_split(a)
        if name in ("x2", "x3", "x4"):
            both.append((name, np.concatenate([hi.astype(np.float64), lo.astype(np.float64)])))
            continue
        both += [(name + "_hi", hi.astype(np.float64)), (name + "_lo", lo.astype(np.float64))]
    return both


@functools.lru_cache(None)
def tables():
    core_rows = np.arange(HALO, HALO + CORE)
    field_cols = np.arange(ROW0, ROW0 + ROWS)
    own_cols = np.arange(WIDE, WIDE + CORE)
    sides = np.zeros((2 * XB, 256))
    sides[:, :WIDE] = x_rows(np.arange(WIDE))
    sides[:, CORE : CORE + WIDE] = x_rows(np.arange(WIDE + CORE, NX))
    parts = [("cx_own", x_rows(own_cols)), ("cx_side", sides)]
    for t in range(2):
        pos = np.arange(2 * CORE) - t * CORE + HALO
        inside = (pos >= 0) & (pos < NY)
        parts.append((f"by{t}", y_lanes(pos) * inside[:, None]))
    parts += [("x2", x_back(field_cols)), ("x3", x_rows(field_cols)), ("x4", x_back(own_cols))]
    y2_hi, y2_lo = (a.astype(np.float64) for a in np_split(y_back(core_rows)))
    y3_hi, y3_lo = (a.astype(np.float64) for a in np_split(y_lanes(core_rows)))
    grad = pack_split(parts)
    grad += [("y2", np.concatenate([y2_hi, y2_lo], axis=1))]
    grad += [("y3_dup", np.concatenate([y3_hi, y3_hi])), ("y3_lo", y3_lo)]
    own = np.zeros((ROWS, CORE))
    own[np.arange(CORE) + WIDE - ROW0, np.arange(CORE)] = 1
    halo = np.zeros((ROWS, 256))
    for r in range(HALO):
        halo[HALO + r - ROW0, WIDE + r] = 1
        halo[WIDE + CORE + r - ROW0, CORE + WIDE + r] = 1
    grad += [("sel_own", own), ("sel_halo", halo)]
    offs = np.arange(KSIZE) - HALO
    kx = np.zeros((2 * XB, 128))
    kx[:, :KSIZE] = x_rows(offs)
    spec = [("kx", kx)]
    for m in range(4):
        ky = np.zeros((128, 2 * YB))
        ky[32 * m : 32 * m + KSIZE] = y_lanes(offs)
        spec.append((f"ky{m}", ky))
    return {"grad": pack(grad), "spec": pack(pack_split(spec))}


def split(x):
    hi = x.astype(bf16)
    return hi, (x - hi.astype(f32)).astype(bf16)


def dot(a, b):
    return lax.dot_general(a, b, (((1,), (0,)), ((), ())), preferred_element_type=f32)


def dot_nt(a, b):
    return lax.dot_general(a, b, (((1,), (1,)), ((), ())), preferred_element_type=f32)


def dot3(a_hi, a_lo, b_hi, b_lo, mul=dot):
    return mul(a_hi, b_hi) + (mul(a_lo, b_hi) + mul(a_hi, b_lo))


def dot_stacked(table, b_hi, b_lo):
    rows = table.shape[0] // 2
    both = dot(table, b_hi)
    return both[:rows] + (both[rows:] + dot(table[:rows], b_lo))


def signed(spec):
    cc, cs = spec[:XB, :YB], spec[:XB, YB:]
    sc, ss = spec[XB:, :YB], spec[XB:, YB:]
    return cc - ss, -(cs + sc), cc + ss, sc - cs


def even_odd(pr, pi, mr, mi):
    top = jnp.concatenate([pr + mr, pi + mi], axis=1)
    low = jnp.concatenate([mi - pi, pr - mr], axis=1)
    return jnp.concatenate([top, low], axis=0)


def table_array(group):
    return jnp.asarray(tables()[group][0].astype(ml_dtypes.bfloat16))


def table_reader(group, ref):
    where = tables()[group][1]

    def table(name, half=None):
        at, height, width = where[name]
        lanes = slice(0, width) if half is None else slice(128 * half, 128 * half + 128)
        return ref[at : at + height, lanes]

    return table


def call(body, group, args, out_shape, scratch=(), smem=(), flops=0, nbytes=0):
    vm = pl.BlockSpec(memory_space=pltpu.VMEM)
    sm = pl.BlockSpec(memory_space=pltpu.SMEM)
    n_in = len(args)
    if group is not None:
        args = [*args, table_array(group)]

    def wrapped(*refs):
        if group is not None:
            refs = [*refs[:n_in], table_reader(group, refs[n_in]), *refs[n_in + 1 :]]
        body(*refs)

    return pl.pallas_call(
        wrapped,
        out_shape=out_shape,
        in_specs=[sm if i in smem else vm for i in range(len(args))],
        out_specs=[vm] * len(out_shape),
        scratch_shapes=list(scratch),
        compiler_params=pltpu.CompilerParams(vmem_limit_bytes=VMEM_LIMIT),
        cost_estimate=pl.CostEstimate(flops=flops, bytes_accessed=nbytes, transcendentals=0),
    )(*args)


def is_even():
    return lax.rem(lax.axis_index("tile"), 2) == 0


def send_edges(right, left, a_ref, b_ref):
    even = is_even()
    a_ref[...] = jnp.where(even, right, left)
    b_ref[...] = jnp.where(even, left, right)


def picker(rows, first, count, col):
    row = lax.broadcasted_iota(jnp.int32, (rows, CORE), 0)
    lane = lax.broadcasted_iota(jnp.int32, (rows, CORE), 1)
    hit = (row - first == lane - col) & (row >= first) & (row < first + count)
    return jnp.where(hit, 1.0, 0.0).astype(bf16)


def edges_of(rows, strip, extra=None):
    hi, lo = split(strip)
    both = []
    for col, more in ((CORE - WIDE, CORE - HALO), (0, 0)):
        pick = picker(rows, 0, WIDE, col)
        edge = dot_nt(pick, hi) + dot_nt(pick, lo)
        if extra is not None:
            edge = edge + dot_nt(picker(rows, WIDE, HALO, more), extra)
        both.append(edge)
    return both


def edges_kernel(mask_ref, target_ref, a_ref, b_ref):
    target = target_ref[...].astype(f32).astype(bf16)
    send_edges(*edges_of(EDGE, mask_ref[...], target), a_ref, b_ref)


def spectra_kernel(kern, ker_ref, tb, h_ref, hs_ref):
    hs_ref[...] = jnp.zeros_like(hs_ref)
    for k in range(kern):
        for part in range(2):
            row = 32 * (2 * k + part)
            hs_ref[row : row + KSIZE, :KSIZE] = ker_ref[part, k, :, 0, :]
    s_hi, s_lo = split(hs_ref[...])
    z = dot3(tb("kx_hi"), tb("kx_lo"), s_hi, s_lo, dot_nt)
    z_hi, z_lo = split(z)
    for c in range(2 * kern):
        lanes = slice(128 * (c // 4), 128 * (c // 4) + 128)
        spec = dot3(z_hi[:, lanes], z_lo[:, lanes], tb(f"ky{c % 4}_hi"), tb(f"ky{c % 4}_lo"))
        for j, comp in enumerate(signed(spec)):
            h_ref[c, j] = comp


def sides(from_a, from_b, tb):
    even = is_even()
    l_hi, l_lo = split(jnp.where(even, from_b, from_a))
    r_hi, r_lo = split(jnp.where(even, from_a, from_b))
    height = l_hi.shape[0]
    v = None
    for half, hi, lo in ((0, l_hi, l_lo), (1, r_hi, r_lo)):
        c_hi, c_lo = tb("cx_side_hi", half), tb("cx_side_lo", half)
        term = dot3(c_hi[:, :height], c_lo[:, :height], hi, lo)
        v = term if v is None else v + term
    return v, l_hi, r_hi


def to_spectrum(v, tb, f_ref, base):
    v_hi, v_lo = split(v)
    for t in range(2):
        spec = dot3(v_hi, v_lo, tb(f"by{t}_hi"), tb(f"by{t}_lo"))
        for j, comp in enumerate(signed(spec)):
            f_ref[t, j] = comp if base is None else base[t, j] - STEP_RATE * comp


def gradient_body(kern, last, f_ref, tgt_ref, h_ref, w_ref, thr_ref, tb, g_ref, work):
    fld, inten, tot, a_hi, a_lo, b_hi, b_lo = work
    chains = [(t, k) for t in range(2) for k in range(kern)]
    rounds = range(len(chains) + 2)

    def at(i):
        return chains[i] if 0 <= i < len(chains) else None

    for i in rounds:
        new, mid, old = at(i), at(i - 1), at(i - 2)
        if mid:
            slot = (i - 1) % 2
            z_one = dot(a_hi[slot], tb("y2"))
            z_two = dot(a_lo[slot], tb("y2", 0))
        if new:
            t, k = new
            slot = i % 2
            for part in range(2):
                hpr, hpi, hmr, hmi = (h_ref[2 * k + part, j] for j in range(4))
                fpr, fpi, fmr, fmi = (f_ref[t, j] for j in range(4))
                pr, pi = hpr * fpr - hpi * fpi, hpr * fpi + hpi * fpr
                mr, mi = hmr * fmr - hmi * fmi, hmr * fmi + hmi * fmr
                p_hi, p_lo = split(even_odd(pr, pi, mr, mi))
                rows = slice(2 * XB * part, 2 * XB * part + 2 * XB)
                a_hi[slot, rows] = p_hi
                a_lo[slot, rows] = p_lo
        if old:
            slot = (i - 2) % 2
            field = dot_stacked(tb("x2"), b_hi[slot], b_lo[slot])
            t, k = old
            fld[t, k] = field
            re, im = field[:, :CORE], field[:, CORE:]
            power = w_ref[0, k] * (re * re + im * im)
            inten[t] = power if k == 0 else inten[t] + power
        if mid:
            slot = (i - 1) % 2
            z = z_one[:, :CORE] + (z_one[:, CORE:] + z_two)
            z_hi, z_lo = split(jnp.concatenate([z[: 2 * XB], z[2 * XB :]], axis=1))
            b_hi[slot] = z_hi
            b_lo[slot] = z_lo

    tile = lax.axis_index("tile")
    first = jnp.where(tile == 0, WIDE, HALO) - ROW0
    end = jnp.where(tile == last, WIDE + CORE, WIDE + CORE + HALO) - ROW0
    row = lax.broadcasted_iota(jnp.int32, (ROWS, CORE), 0)
    inside = (row >= first) & (row < end)
    for t in range(2):
        resist = jax.nn.sigmoid(STEEPNESS * (inten[t] - thr_ref[0]))
        target = tgt_ref[:, CORE * t : CORE * t + CORE]
        slope = 2.0 * (resist - target) * STEEPNESS * resist * (1.0 - resist)
        inten[t] = jnp.where(inside, 2.0 * slope, 0.0)
    for i in rounds:
        new, mid, old = at(i), at(i - 1), at(i - 2)
        if mid:
            slot = (i - 1) % 2
            w_now = dot_stacked(tb("x3"), b_hi[slot, :ROWS], b_lo[slot, :ROWS])
        if new:
            t, k = new
            slot = i % 2
            scaled = w_ref[0, k] * inten[t]
            field = fld[t, k]
            r_hi, r_lo = split(
                jnp.concatenate([scaled * field[:, :CORE], scaled * field[:, CORE:]], axis=1)
            )
            b_hi[slot, :ROWS] = r_hi
            b_lo[slot, :ROWS] = r_lo
        if old:
            slot = (i - 2) % 2
            t, k = old
            cat = a_hi[slot]
            specs = dot(cat, tb("y3_dup")) + dot(cat[:, :CORE], tb("y3_lo"))
            acc = [0.0] * 4 if k == 0 else [tot[t, j] for j in range(4)]
            for part in range(2):
                spec = specs[2 * XB * part : 2 * XB * part + 2 * XB]
                cc, cs = spec[:XB, :YB], spec[:XB, YB:]
                sc, ss = spec[XB:, :YB], spec[XB:, YB:]
                bpr, neg, bmr, bmi = cc - ss, cs + sc, cc + ss, sc - cs
                hpr, hpi, hmr, hmi = (h_ref[2 * k + part, j] for j in range(4))
                acc[0] = acc[0] + (hpr * bpr - hpi * neg)
                acc[1] = acc[1] - (hpr * neg + hpi * bpr)
                acc[2] = acc[2] + (hmr * bmr + hmi * bmi)
                acc[3] = acc[3] + (hmr * bmi - hmi * bmr)
            for j in range(4):
                tot[t, j] = acc[j]
        if mid:
            slot = (i - 1) % 2
            w_hi, w_lo = split(w_now)
            for part in range(2):
                rows = slice(2 * XB * part, 2 * XB * part + 2 * XB)
                lanes = slice(CORE * part, CORE * part + CORE)
                a_hi[slot, rows, :CORE] = w_hi[:, lanes]
                a_hi[slot, rows, CORE:] = w_lo[:, lanes]

    lane = lax.broadcasted_iota(jnp.int32, (1, 2 * YB), 1)
    bin_at = lax.rem(lane, YB)
    weight = jnp.where((bin_at == 0) | (bin_at == NU - 1), 1.0, 2.0) / (NX * NY)
    weight = jnp.where(lane < YB, weight, -weight)
    out = None
    for t in range(2):
        r_hi, r_lo = split(even_odd(*(tot[t, j] for j in range(4))))
        u_hi, u_lo = split(weight * dot_stacked(tb("x4"), r_hi, r_lo))
        term = dot3(tb(f"by{t}_hi"), tb(f"by{t}_lo"), u_hi, u_lo, dot_nt)
        out = term if out is None else out + term
    g_ref[...] = out


def first_kernel(
    kern, last, w_ref, thr_ref, mask_ref, target_ref, a_ref, b_ref, h_ref, tb,
    g_ref, f_ref, tgt_ref, *work,
):
    m_hi, m_lo = split(mask_ref[...])
    v, left, right = sides(a_ref[...], b_ref[...], tb)
    v = v + dot3(tb("cx_own_hi"), tb("cx_own_lo"), m_hi, m_lo, dot_nt)
    to_spectrum(v, tb, f_ref, None)
    tgt_ref[...] = (
        dot_nt(tb("sel_own"), target_ref[...].astype(f32).astype(bf16))
        + dot(tb("sel_halo", 0)[:, :EDGE], left)
        + dot(tb("sel_halo", 1)[:, :EDGE], right)
    )
    gradient_body(kern, last, f_ref, tgt_ref, h_ref, w_ref, thr_ref, tb, g_ref, work)


def later_kernel(
    kern, last, w_ref, thr_ref, mine_ref, peer_ref, a_ref, a2_ref, b_ref, b2_ref, f_in_ref, tgt_ref,
    h_ref, tb, g_ref, f_ref, *work,
):
    s_hi, s_lo = split(mine_ref[...] + peer_ref[...])
    from_a = a_ref[...] + a2_ref[...]
    from_b = b_ref[...] + b2_ref[...]
    v, _, _ = sides(from_a, from_b, tb)
    v = v + dot3(tb("cx_own_hi"), tb("cx_own_lo"), s_hi, s_lo, dot_nt)
    to_spectrum(v, tb, f_ref, f_in_ref)
    gradient_body(kern, last, f_ref, tgt_ref, h_ref, w_ref, thr_ref, tb, g_ref, work)


def match_kernel(n_got, table_ref, own_ref, *refs):
    got_refs, (out_ref, *edge_refs) = refs[:n_got], refs[n_got:]
    device = lax.axis_index("tile")
    other = []
    for t in range(2):
        rows = slice(CORE * t, CORE * t + CORE)
        bit = lax.bitwise_xor(table_ref[t], 2 * device + t)
        value = jnp.where(bit == 1, own_ref[CORE * (1 - t) : CORE * (2 - t)], own_ref[rows])
        for b, got in enumerate(got_refs):
            value = jnp.where(bit == 2 << b, got[rows], value)
        other.append(value)
    row = lax.broadcasted_iota(jnp.int32, (CORE, CORE), 0)
    lane = lax.broadcasted_iota(jnp.int32, (CORE, CORE), 1)
    flip = jnp.where(row + lane == CORE - 1, 1.0, 0.0).astype(bf16)
    hi, lo = split(jnp.concatenate(other, axis=0))
    turned = dot(hi, flip) + dot(lo, flip)
    tiles = []
    for t in range(2):
        rows = slice(CORE * t, CORE * t + CORE)
        value = jnp.where(table_ref[2 + t] == 1, turned[rows], other[t])
        tiles.append(0.5 * (own_ref[rows] + value))
    matched = jnp.concatenate(tiles, axis=0)
    out_ref[...] = matched
    if edge_refs:
        send_edges(*edges_of(WIDE_PAD, matched), *edge_refs)


def final_kernel(n_moves, mask_ref, *refs):
    moves, (mask_out, grad_out) = refs[: 2 * n_moves], refs[2 * n_moves :]
    for t in range(2):
        rows = slice(CORE * t, CORE * t + CORE)
        now = mask_ref[t]
        for mine, peer in zip(moves[::2], moves[1::2]):
            step = mine[rows] + peer[rows]
            now = now - STEP_RATE * step
        grad_out[t] = step
        mask_out[t] = now


def per_device(
    n_tile, n_depth, mask_tiles, target_tiles, kernels, socs_weights, thresholds,
    partner_table, mirror_flags,
):
    tiles_dev, core, _ = mask_tiles.shape
    kern = kernels.shape[2]
    assert tiles_dev == 2 and core == CORE
    pairs_a = [(i, i ^ 1) for i in range(n_tile)]
    pairs_b = [p for i in range(1, n_tile - 1, 2) for p in ((i, i + 1), (i + 1, i))]

    def swap_edges(send_a, send_b, cross=False):
        def move(x, pairs):
            if not cross:
                return lax.ppermute(x, "tile", pairs)
            both = [(2 * i + p, 2 * j + 1 - p) for i, j in pairs for p in range(2)]
            return lax.ppermute(x, ("tile", "depth"), both)

        return move(send_b, pairs_b), move(send_a, pairs_a)

    def depth_pair(x):
        bit = 1
        while True:
            peer = lax.ppermute(x, "depth", [(i, i ^ bit) for i in range(n_depth)])
            bit *= 2
            if bit >= n_depth:
                return x, peer
            x = x + peer

    def from_partners(grad):
        bits = [1 << b for b in range(n_tile.bit_length() - 1)]
        got = [
            lax.ppermute(grad, "tile", [(i, i ^ bit) for i in range(n_tile)])
            for bit in reversed(bits)
        ]
        return got[::-1]

    mask_rows = mask_tiles.reshape(tiles_dev * core, core)
    target_rows = target_tiles.reshape(tiles_dev * core, core)
    strip = jax.ShapeDtypeStruct((tiles_dev * core, core), f32)
    side = jax.ShapeDtypeStruct((WIDE_PAD, tiles_dev * core), f32)
    freq = jax.ShapeDtypeStruct((2, 4, XB, YB), f32)
    goal = jax.ShapeDtypeStruct((ROWS, 2 * CORE), f32)
    tiles = jax.ShapeDtypeStruct((tiles_dev, core, core), f32)
    scratch = [
        pltpu.VMEM((2, kern, ROWS, 2 * CORE), f32),
        pltpu.VMEM((2, ROWS, CORE), f32),
        pltpu.VMEM((2, 4, XB, YB), f32),
        pltpu.VMEM((2, 4 * XB, 2 * YB), bf16),
        pltpu.VMEM((2, 4 * XB, 2 * YB), bf16),
        pltpu.VMEM((2, 2 * XB, 2 * CORE), bf16),
        pltpu.VMEM((2, 2 * XB, 2 * CORE), bf16),
    ]

    edge = jax.ShapeDtypeStruct((EDGE, tiles_dev * core), f32)
    send_a, send_b = call(
        edges_kernel, None, [mask_rows, target_rows], [edge, edge], flops=3 * 10**9
    )
    from_b, from_a = swap_edges(send_a, send_b)
    table = jnp.concatenate([partner_table, mirror_flags])
    (spectra,) = call(
        functools.partial(spectra_kernel, kern),
        "spec",
        [kernels.transpose(0, 2, 3, 1, 4)],
        [jax.ShapeDtypeStruct((2 * kern, 4, XB, YB), f32)],
        [pltpu.VMEM((32 * 2 * kern, 128), f32)],
        flops=3 * 10**9,
        nbytes=4 * 10**6,
    )
    grad, freq_now, goals = call(
        functools.partial(first_kernel, kern, n_tile - 1),
        "grad",
        [socs_weights, thresholds, mask_rows, target_rows, from_a, from_b, spectra],
        [strip, freq, goal],
        scratch,
        smem=(0, 1),
        flops=10**10,
    )
    moves = []
    for step in range(1, STEPS + 1):
        got = from_partners(grad)
        outs = call(
            functools.partial(match_kernel, len(got)),
            None,
            [table, grad, *got],
            [strip, side, side] if step < STEPS else [strip],
            smem=(0,),
        )
        if step == STEPS:
            moves += depth_pair(outs[0])
            break
        if n_depth == 2:
            from_b, from_a = swap_edges(*outs[1:])
            far_b, far_a = swap_edges(*outs[1:], cross=True)
            rims = (from_a, far_a, from_b, far_b)
        else:
            from_b, from_a = swap_edges(*outs[1:])
            rims = depth_pair(from_a) + depth_pair(from_b)
        moves += depth_pair(outs[0])
        kept = step + 1 < STEPS
        grad, *rest = call(
            functools.partial(later_kernel, kern, n_tile - 1),
            "grad",
            [socs_weights, thresholds, *moves[-2:], *rims, freq_now, goals, spectra],
            [strip, freq] if kept else [strip],
            scratch if kept else [pltpu.VMEM(freq.shape, f32)] + scratch,
            smem=(0, 1),
            flops=10**10,
        )
        freq_now = rest[0] if kept else None
    final = functools.partial(final_kernel, STEPS)
    return tuple(call(final, None, [mask_tiles, *moves], [tiles, tiles]))


def solution(mesh):
    return jax.shard_map(
        functools.partial(per_device, mesh.shape["tile"], mesh.shape["depth"]),
        mesh=mesh,
        in_specs=(
            P("tile", None, None),
            P("tile", None, None),
            P(None, "depth", None, None, None),
            P("depth", None),
            P("depth"),
            P("tile"),
            P("tile"),
        ),
        out_specs=(P("tile", None, None), P("tile", None, None)),
        check_vma=False,
    )
```

```python
import functools

import jax
import jax.numpy as jnp
import ml_dtypes
import numpy as np
from jax import lax
from jax.experimental import pallas as pl
from jax.experimental.pallas import tpu as pltpu
from jax.sharding import PartitionSpec as P

HALO = 12
KSIZE = 25
STEPS = 2
STEEPNESS = 3.0
STEP_RATE = 0.05

CORE = 128
NY = 152
NX = 176
WIDE = 2 * HALO
XB = 96
YB = 128
NU = NY // 2 + 1
NV = NX // 2 + 1
ROWS = 160
ROW0 = 8
EDGE = 48
WIDE_PAD = 32
VMEM_LIMIT = 24 * 1024 * 1024

f32 = jnp.float32
bf16 = jnp.bfloat16


def np_split(a):
    hi = np.asarray(a, np.float32).astype(ml_dtypes.bfloat16)
    lo = (np.asarray(a, np.float64) - hi.astype(np.float64)).astype(ml_dtypes.bfloat16)
    return hi, lo


def x_rows(cols):
    out = np.zeros((2 * XB, len(cols)))
    ang = 2 * np.pi * np.outer(np.arange(NV), cols) / NX
    out[:NV] = np.cos(ang)
    out[XB : XB + NV] = np.sin(ang)
    out[XB] = 0.0
    out[XB + NV - 1] = 0.0
    return out


def y_lanes(rows):
    out = np.zeros((len(rows), 2 * YB))
    ang = 2 * np.pi * np.outer(rows, np.arange(NU)) / NY
    out[:, :NU] = np.cos(ang)
    out[:, YB : YB + NU] = np.sin(ang)
    out[:, YB] = 0.0
    out[:, YB + NU - 1] = 0.0
    return out


def half_weights(bins):
    weights = np.full(bins, 2.0)
    weights[0] = weights[-1] = 1.0
    return weights


def x_back(cols):
    kappa = np.zeros(2 * XB)
    kappa[:NV] = half_weights(NV) / 2
    kappa[XB : XB + NV] = half_weights(NV) / 2
    return x_rows(cols).T * kappa


def y_back(rows):
    weight = np.zeros(2 * YB)
    weight[:NU] = half_weights(NU)
    weight[YB : YB + NU] = -half_weights(NU)
    return (y_lanes(rows) * weight).T / (NX * NY)


def pack(parts):
    rows, where, at = [], {}, 0
    pieces = []
    for name, a in parts:
        if a.shape[1] <= 256:
            pieces.append((name, a))
            continue
        cuts = range(0, a.shape[1], 256)
        where[name] = len(cuts)
        pieces += [(f"{name}.{i}", a[:, c : c + 256]) for i, c in enumerate(cuts)]
    for name, a in pieces:
        height = -(-a.shape[0] // 16) * 16
        block = np.zeros((height, 256), np.float64)
        block[: a.shape[0], : a.shape[1]] = a
        rows.append(block)
        where[name] = (at, a.shape[0], a.shape[1])
        at += height
    return np.concatenate(rows), where


def pack_split(parts):
    both = []
    for name, a in parts:
        hi, lo = np_split(a)
        if name in ("x2", "x3", "x4"):
            hi, lo = hi.astype(np.float64), lo.astype(np.float64)
            both.append((name, np.concatenate([hi, lo, hi], axis=1)))
            continue
        both += [(name + "_hi", hi.astype(np.float64)), (name + "_lo", lo.astype(np.float64))]
    return both


@functools.lru_cache(None)
def tables():
    core_rows = np.arange(HALO, HALO + CORE)
    field_cols = np.arange(ROW0, ROW0 + ROWS)
    own_cols = np.arange(WIDE, WIDE + CORE)
    sides = np.zeros((2 * XB, 256))
    sides[:, :WIDE] = x_rows(np.arange(WIDE))
    sides[:, CORE : CORE + WIDE] = x_rows(np.arange(WIDE + CORE, NX))
    parts = [("cx_own", x_rows(own_cols)), ("cx_side", sides)]
    for t in range(2):
        pos = np.arange(2 * CORE) - t * CORE + HALO
        inside = (pos >= 0) & (pos < NY)
        parts.append((f"by{t}", y_lanes(pos) * inside[:, None]))
    parts += [("x2", x_back(field_cols)), ("x3", x_rows(field_cols)), ("x4", x_back(own_cols))]
    y2_hi, y2_lo = (a.astype(np.float64) for a in np_split(y_back(core_rows)))
    y3_hi, y3_lo = (a.astype(np.float64) for a in np_split(y_lanes(core_rows)))
    grad = pack_split(parts)
    grad += [("y2", np.concatenate([y2_hi, y2_lo], axis=1))]
    grad += [("y3", np.concatenate([y3_hi, y3_hi, y3_lo]))]
    own = np.zeros((ROWS, CORE))
    own[np.arange(CORE) + WIDE - ROW0, np.arange(CORE)] = 1
    halo = np.zeros((ROWS, 256))
    for r in range(HALO):
        halo[HALO + r - ROW0, WIDE + r] = 1
        halo[WIDE + CORE + r - ROW0, CORE + WIDE + r] = 1
    grad += [("sel_own", own), ("sel_halo", halo)]
    offs = np.arange(KSIZE) - HALO
    kx = np.zeros((2 * XB, 128))
    kx[:, :KSIZE] = x_rows(offs)
    spec = [("kx", kx)]
    for m in range(4):
        ky = np.zeros((128, 2 * YB))
        ky[32 * m : 32 * m + KSIZE] = y_lanes(offs)
        spec.append((f"ky{m}", ky))
    return {"grad": pack(grad), "spec": pack(pack_split(spec))}


def split(x):
    hi = x.astype(bf16)
    return hi, (x - hi.astype(f32)).astype(bf16)


def dot(a, b):
    return lax.dot_general(a, b, (((1,), (0,)), ((), ())), preferred_element_type=f32)


def dot_nt(a, b):
    return lax.dot_general(a, b, (((1,), (1,)), ((), ())), preferred_element_type=f32)


def dot3(a_hi, a_lo, b_hi, b_lo, mul=dot):
    return mul(a_hi, b_hi) + (mul(a_lo, b_hi) + mul(a_hi, b_lo))


def signed(spec):
    cc, cs = spec[:XB, :YB], spec[:XB, YB:]
    sc, ss = spec[XB:, :YB], spec[XB:, YB:]
    return cc - ss, -(cs + sc), cc + ss, sc - cs


def even_odd(pr, pi, mr, mi):
    top = jnp.concatenate([pr + mr, pi + mi], axis=1)
    low = jnp.concatenate([mi - pi, pr - mr], axis=1)
    return jnp.concatenate([top, low], axis=0)


def table_array(group):
    return jnp.asarray(tables()[group][0].astype(ml_dtypes.bfloat16))


def table_reader(group, ref):
    where = tables()[group][1]

    def table(name, half=None):
        if isinstance(where[name], int):
            return jnp.concatenate([table(f"{name}.{i}") for i in range(where[name])], axis=1)
        at, height, width = where[name]
        lanes = slice(0, width) if half is None else slice(128 * half, 128 * half + 128)
        return ref[at : at + height, lanes]

    return table


def call(body, group, args, out_shape, scratch=(), smem=(), flops=0, nbytes=0):
    vm = pl.BlockSpec(memory_space=pltpu.VMEM)
    sm = pl.BlockSpec(memory_space=pltpu.SMEM)
    n_in = len(args)
    if group is not None:
        args = [*args, table_array(group)]

    def wrapped(*refs):
        if group is not None:
            refs = [*refs[:n_in], table_reader(group, refs[n_in]), *refs[n_in + 1 :]]
        body(*refs)

    return pl.pallas_call(
        wrapped,
        out_shape=out_shape,
        in_specs=[sm if i in smem else vm for i in range(len(args))],
        out_specs=[vm] * len(out_shape),
        scratch_shapes=list(scratch),
        compiler_params=pltpu.CompilerParams(vmem_limit_bytes=VMEM_LIMIT),
        cost_estimate=pl.CostEstimate(flops=flops, bytes_accessed=nbytes, transcendentals=0),
    )(*args)


def is_even():
    return lax.rem(lax.axis_index("tile"), 2) == 0


def send_edges(right, left, a_ref, b_ref):
    even = is_even()
    a_ref[...] = jnp.where(even, right, left)
    b_ref[...] = jnp.where(even, left, right)


def picker(rows, first, count, col):
    row = lax.broadcasted_iota(jnp.int32, (rows, CORE), 0)
    lane = lax.broadcasted_iota(jnp.int32, (rows, CORE), 1)
    hit = (row - first == lane - col) & (row >= first) & (row < first + count)
    return jnp.where(hit, 1.0, 0.0).astype(bf16)


def edges_of(rows, strip, extra=None):
    hi, lo = split(strip)
    both = []
    for col, more in ((CORE - WIDE, CORE - HALO), (0, 0)):
        pick = picker(rows, 0, WIDE, col)
        edge = dot_nt(pick, hi) + dot_nt(pick, lo)
        if extra is not None:
            edge = edge + dot_nt(picker(rows, WIDE, HALO, more), extra)
        both.append(edge)
    return both


def edges_kernel(mask_ref, target_ref, a_ref, b_ref):
    target = target_ref[...].astype(f32).astype(bf16)
    send_edges(*edges_of(EDGE, mask_ref[...], target), a_ref, b_ref)


def spectra_kernel(kern, ker_ref, tb, h_ref, hs_ref):
    hs_ref[...] = jnp.zeros_like(hs_ref)
    for k in range(kern):
        for part in range(2):
            row = 32 * (2 * k + part)
            hs_ref[row : row + KSIZE, :KSIZE] = ker_ref[part, k, :, 0, :]
    s_hi, s_lo = split(hs_ref[...])
    z = dot3(tb("kx_hi"), tb("kx_lo"), s_hi, s_lo, dot_nt)
    z_hi, z_lo = split(z)
    for c in range(2 * kern):
        lanes = slice(128 * (c // 4), 128 * (c // 4) + 128)
        spec = dot3(z_hi[:, lanes], z_lo[:, lanes], tb(f"ky{c % 4}_hi"), tb(f"ky{c % 4}_lo"))
        for j, comp in enumerate(signed(spec)):
            h_ref[c, j] = comp


def sides(from_a, from_b, tb):
    even = is_even()
    l_hi, l_lo = split(jnp.where(even, from_b, from_a))
    r_hi, r_lo = split(jnp.where(even, from_a, from_b))
    height = l_hi.shape[0]
    v = None
    for half, hi, lo in ((0, l_hi, l_lo), (1, r_hi, r_lo)):
        c_hi, c_lo = tb("cx_side_hi", half), tb("cx_side_lo", half)
        term = dot3(c_hi[:, :height], c_lo[:, :height], hi, lo)
        v = term if v is None else v + term
    return v, l_hi, r_hi


def to_spectrum(v, tb, f_ref, base):
    v_hi, v_lo = split(v)
    for t in range(2):
        spec = dot3(v_hi, v_lo, tb(f"by{t}_hi"), tb(f"by{t}_lo"))
        for j, comp in enumerate(signed(spec)):
            f_ref[t, j] = comp if base is None else base[t, j] - STEP_RATE * comp


def gradient_body(kern, last, f_ref, tgt_ref, h_ref, w_ref, thr_ref, tb, g_ref, work):
    fld, inten, tot, a_hi, a_lo, b_cat, c_cat = work
    chains = [(t, k) for t in range(2) for k in range(kern)]
    rounds = range(len(chains) + 2)

    def at(i):
        return chains[i] if 0 <= i < len(chains) else None

    for i in rounds:
        new, mid, old = at(i), at(i - 1), at(i - 2)
        if mid:
            slot = (i - 1) % 2
            z_one = dot(a_hi[slot], tb("y2"))
            z_two = dot(a_lo[slot], tb("y2", 0))
        if new:
            t, k = new
            slot = i % 2
            for part in range(2):
                hpr, hpi, hmr, hmi = (h_ref[2 * k + part, j] for j in range(4))
                fpr, fpi, fmr, fmi = (f_ref[t, j] for j in range(4))
                pr, pi = hpr * fpr - hpi * fpi, hpr * fpi + hpi * fpr
                mr, mi = hmr * fmr - hmi * fmi, hmr * fmi + hmi * fmr
                p_hi, p_lo = split(even_odd(pr, pi, mr, mi))
                rows = slice(2 * XB * part, 2 * XB * part + 2 * XB)
                a_hi[slot, rows] = p_hi
                a_lo[slot, rows] = p_lo
        if old:
            slot = (i - 2) % 2
            field = dot(tb("x2"), b_cat[slot])
            t, k = old
            fld[t, k] = field
            re, im = field[:, :CORE], field[:, CORE:]
            power = w_ref[0, k] * (re * re + im * im)
            inten[t] = power if k == 0 else inten[t] + power
        if mid:
            slot = (i - 1) % 2
            z = z_one[:, :CORE] + (z_one[:, CORE:] + z_two)
            z_hi, z_lo = split(jnp.concatenate([z[: 2 * XB], z[2 * XB :]], axis=1))
            for j, piece in enumerate((z_hi, z_hi, z_lo)):
                b_cat[slot, 2 * XB * j : 2 * XB * j + 2 * XB] = piece

    tile = lax.axis_index("tile")
    first = jnp.where(tile == 0, WIDE, HALO) - ROW0
    end = jnp.where(tile == last, WIDE + CORE, WIDE + CORE + HALO) - ROW0
    row = lax.broadcasted_iota(jnp.int32, (ROWS, CORE), 0)
    inside = (row >= first) & (row < end)
    for t in range(2):
        resist = jax.nn.sigmoid(STEEPNESS * (inten[t] - thr_ref[0]))
        target = tgt_ref[:, CORE * t : CORE * t + CORE]
        slope = 2.0 * (resist - target) * STEEPNESS * resist * (1.0 - resist)
        inten[t] = jnp.where(inside, 2.0 * slope, 0.0)
    for i in rounds:
        new, mid, old = at(i), at(i - 1), at(i - 2)
        if mid:
            slot = (i - 1) % 2
            w_now = dot(tb("x3"), b_cat[slot, : 3 * ROWS])
        if new:
            t, k = new
            slot = i % 2
            scaled = w_ref[0, k] * inten[t]
            field = fld[t, k]
            r_hi, r_lo = split(
                jnp.concatenate([scaled * field[:, :CORE], scaled * field[:, CORE:]], axis=1)
            )
            for j, piece in enumerate((r_hi, r_hi, r_lo)):
                b_cat[slot, ROWS * j : ROWS * j + ROWS] = piece
        if old:
            slot = (i - 2) % 2
            t, k = old
            specs = dot(c_cat[slot], tb("y3"))
            acc = [0.0] * 4 if k == 0 else [tot[t, j] for j in range(4)]
            for part in range(2):
                spec = specs[2 * XB * part : 2 * XB * part + 2 * XB]
                cc, cs = spec[:XB, :YB], spec[:XB, YB:]
                sc, ss = spec[XB:, :YB], spec[XB:, YB:]
                bpr, neg, bmr, bmi = cc - ss, cs + sc, cc + ss, sc - cs
                hpr, hpi, hmr, hmi = (h_ref[2 * k + part, j] for j in range(4))
                acc[0] = acc[0] + (hpr * bpr - hpi * neg)
                acc[1] = acc[1] - (hpr * neg + hpi * bpr)
                acc[2] = acc[2] + (hmr * bmr + hmi * bmi)
                acc[3] = acc[3] + (hmr * bmi - hmi * bmr)
            for j in range(4):
                tot[t, j] = acc[j]
        if mid:
            slot = (i - 1) % 2
            w_hi, w_lo = split(w_now)
            for part in range(2):
                rows = slice(2 * XB * part, 2 * XB * part + 2 * XB)
                lanes = slice(CORE * part, CORE * part + CORE)
                for j, piece in enumerate((w_hi, w_lo, w_hi)):
                    c_cat[slot, rows, CORE * j : CORE * j + CORE] = piece[:, lanes]

    lane = lax.broadcasted_iota(jnp.int32, (1, 2 * YB), 1)
    bin_at = lax.rem(lane, YB)
    weight = jnp.where((bin_at == 0) | (bin_at == NU - 1), 1.0, 2.0) / (NX * NY)
    weight = jnp.where(lane < YB, weight, -weight)
    out = None
    for t in range(2):
        r_hi, r_lo = split(even_odd(*(tot[t, j] for j in range(4))))
        u_hi, u_lo = split(weight * dot(tb("x4"), jnp.concatenate([r_hi, r_hi, r_lo], axis=0)))
        term = dot3(tb(f"by{t}_hi"), tb(f"by{t}_lo"), u_hi, u_lo, dot_nt)
        out = term if out is None else out + term
    g_ref[...] = out


def first_kernel(
    kern, last, w_ref, thr_ref, mask_ref, target_ref, a_ref, b_ref, h_ref, tb,
    g_ref, f_ref, tgt_ref, *work,
):
    m_hi, m_lo = split(mask_ref[...])
    v, left, right = sides(a_ref[...], b_ref[...], tb)
    v = v + dot3(tb("cx_own_hi"), tb("cx_own_lo"), m_hi, m_lo, dot_nt)
    to_spectrum(v, tb, f_ref, None)
    tgt_ref[...] = (
        dot_nt(tb("sel_own"), target_ref[...].astype(f32).astype(bf16))
        + dot(tb("sel_halo", 0)[:, :EDGE], left)
        + dot(tb("sel_halo", 1)[:, :EDGE], right)
    )
    gradient_body(kern, last, f_ref, tgt_ref, h_ref, w_ref, thr_ref, tb, g_ref, work)


def later_kernel(
    kern, last, w_ref, thr_ref, mine_ref, peer_ref, a_ref, a2_ref, b_ref, b2_ref, f_in_ref, tgt_ref,
    h_ref, tb, g_ref, f_ref, *work,
):
    s_hi, s_lo = split(mine_ref[...] + peer_ref[...])
    from_a = a_ref[...] + a2_ref[...]
    from_b = b_ref[...] + b2_ref[...]
    v, _, _ = sides(from_a, from_b, tb)
    v = v + dot3(tb("cx_own_hi"), tb("cx_own_lo"), s_hi, s_lo, dot_nt)
    to_spectrum(v, tb, f_ref, f_in_ref)
    gradient_body(kern, last, f_ref, tgt_ref, h_ref, w_ref, thr_ref, tb, g_ref, work)


def match_kernel(n_got, table_ref, own_ref, *refs):
    got_refs, (out_ref, *edge_refs) = refs[:n_got], refs[n_got:]
    device = lax.axis_index("tile")
    other = []
    for t in range(2):
        rows = slice(CORE * t, CORE * t + CORE)
        bit = lax.bitwise_xor(table_ref[t], 2 * device + t)
        value = jnp.where(bit == 1, own_ref[CORE * (1 - t) : CORE * (2 - t)], own_ref[rows])
        for b, got in enumerate(got_refs):
            value = jnp.where(bit == 2 << b, got[rows], value)
        other.append(value)
    row = lax.broadcasted_iota(jnp.int32, (CORE, CORE), 0)
    lane = lax.broadcasted_iota(jnp.int32, (CORE, CORE), 1)
    flip = jnp.where(row + lane == CORE - 1, 1.0, 0.0).astype(bf16)
    hi, lo = split(jnp.concatenate(other, axis=0))
    turned = dot(hi, flip) + dot(lo, flip)
    tiles = []
    for t in range(2):
        rows = slice(CORE * t, CORE * t + CORE)
        value = jnp.where(table_ref[2 + t] == 1, turned[rows], other[t])
        tiles.append(0.5 * (own_ref[rows] + value))
    matched = jnp.concatenate(tiles, axis=0)
    out_ref[...] = matched
    if edge_refs:
        send_edges(*edges_of(WIDE_PAD, matched), *edge_refs)


def final_kernel(n_moves, mask_ref, *refs):
    moves, (mask_out, grad_out) = refs[: 2 * n_moves], refs[2 * n_moves :]
    for t in range(2):
        rows = slice(CORE * t, CORE * t + CORE)
        now = mask_ref[t]
        for mine, peer in zip(moves[::2], moves[1::2]):
            step = mine[rows] + peer[rows]
            now = now - STEP_RATE * step
        grad_out[t] = step
        mask_out[t] = now


def per_device(
    n_tile, n_depth, mask_tiles, target_tiles, kernels, socs_weights, thresholds,
    partner_table, mirror_flags,
):
    tiles_dev, core, _ = mask_tiles.shape
    kern = kernels.shape[2]
    assert tiles_dev == 2 and core == CORE
    pairs_a = [(i, i ^ 1) for i in range(n_tile)]
    pairs_b = [p for i in range(1, n_tile - 1, 2) for p in ((i, i + 1), (i + 1, i))]

    def swap_edges(send_a, send_b, cross=False):
        def move(x, pairs):
            if not cross:
                return lax.ppermute(x, "tile", pairs)
            both = [(2 * i + p, 2 * j + 1 - p) for i, j in pairs for p in range(2)]
            return lax.ppermute(x, ("tile", "depth"), both)

        return move(send_b, pairs_b), move(send_a, pairs_a)

    def depth_pair(x):
        bit = 1
        while True:
            peer = lax.ppermute(x, "depth", [(i, i ^ bit) for i in range(n_depth)])
            bit *= 2
            if bit >= n_depth:
                return x, peer
            x = x + peer

    def from_partners(grad):
        bits = [1 << b for b in range(n_tile.bit_length() - 1)]
        got = [
            lax.ppermute(grad, "tile", [(i, i ^ bit) for i in range(n_tile)])
            for bit in reversed(bits)
        ]
        return got[::-1]

    mask_rows = mask_tiles.reshape(tiles_dev * core, core)
    target_rows = target_tiles.reshape(tiles_dev * core, core)
    strip = jax.ShapeDtypeStruct((tiles_dev * core, core), f32)
    side = jax.ShapeDtypeStruct((WIDE_PAD, tiles_dev * core), f32)
    freq = jax.ShapeDtypeStruct((2, 4, XB, YB), f32)
    goal = jax.ShapeDtypeStruct((ROWS, 2 * CORE), f32)
    tiles = jax.ShapeDtypeStruct((tiles_dev, core, core), f32)
    scratch = [
        pltpu.VMEM((2, kern, ROWS, 2 * CORE), f32),
        pltpu.VMEM((2, ROWS, CORE), f32),
        pltpu.VMEM((2, 4, XB, YB), f32),
        pltpu.VMEM((2, 4 * XB, 2 * YB), bf16),
        pltpu.VMEM((2, 4 * XB, 2 * YB), bf16),
        pltpu.VMEM((2, 6 * XB, 2 * CORE), bf16),
        pltpu.VMEM((2, 4 * XB, 3 * CORE), bf16),
    ]

    edge = jax.ShapeDtypeStruct((EDGE, tiles_dev * core), f32)
    send_a, send_b = call(
        edges_kernel, None, [mask_rows, target_rows], [edge, edge], flops=3 * 10**9
    )
    from_b, from_a = swap_edges(send_a, send_b)
    table = jnp.concatenate([partner_table, mirror_flags])
    (spectra,) = call(
        functools.partial(spectra_kernel, kern),
        "spec",
        [kernels.transpose(0, 2, 3, 1, 4)],
        [jax.ShapeDtypeStruct((2 * kern, 4, XB, YB), f32)],
        [pltpu.VMEM((32 * 2 * kern, 128), f32)],
        flops=3 * 10**9,
        nbytes=4 * 10**6,
    )
    grad, freq_now, goals = call(
        functools.partial(first_kernel, kern, n_tile - 1),
        "grad",
        [socs_weights, thresholds, mask_rows, target_rows, from_a, from_b, spectra],
        [strip, freq, goal],
        scratch,
        smem=(0, 1),
        flops=10**10,
    )
    moves = []
    for step in range(1, STEPS + 1):
        got = from_partners(grad)
        outs = call(
            functools.partial(match_kernel, len(got)),
            None,
            [table, grad, *got],
            [strip, side, side] if step < STEPS else [strip],
            smem=(0,),
        )
        if step == STEPS:
            moves += depth_pair(outs[0])
            break
        if n_depth == 2:
            from_b, from_a = swap_edges(*outs[1:])
            far_b, far_a = swap_edges(*outs[1:], cross=True)
            rims = (from_a, far_a, from_b, far_b)
        else:
            from_b, from_a = swap_edges(*outs[1:])
            rims = depth_pair(from_a) + depth_pair(from_b)
        moves += depth_pair(outs[0])
        kept = step + 1 < STEPS
        grad, *rest = call(
            functools.partial(later_kernel, kern, n_tile - 1),
            "grad",
            [socs_weights, thresholds, *moves[-2:], *rims, freq_now, goals, spectra],
            [strip, freq] if kept else [strip],
            scratch if kept else [pltpu.VMEM(freq.shape, f32)] + scratch,
            smem=(0, 1),
            flops=10**10,
        )
        freq_now = rest[0] if kept else None
    final = functools.partial(final_kernel, STEPS)
    return tuple(call(final, None, [mask_tiles, *moves], [tiles, tiles]))


def solution(mesh):
    return jax.shard_map(
        functools.partial(per_device, mesh.shape["tile"], mesh.shape["depth"]),
        mesh=mesh,
        in_specs=(
            P("tile", None, None),
            P("tile", None, None),
            P(None, "depth", None, None, None),
            P("depth", None),
            P("depth"),
            P("tile"),
            P("tile"),
        ),
        out_specs=(P("tile", None, None), P("tile", None, None)),
        check_vma=False,
    )
```

```python
import functools

import jax
import jax.numpy as jnp
import ml_dtypes
import numpy as np
from jax import lax
from jax.experimental import pallas as pl
from jax.experimental.pallas import tpu as pltpu
from jax.sharding import PartitionSpec as P

HALO = 12
KSIZE = 25
STEPS = 2
STEEPNESS = 3.0
STEP_RATE = 0.05

CORE = 128
NY = 152
NX = 176
WIDE = 2 * HALO
XB = 96
YB = 128
NU = NY // 2 + 1
NV = NX // 2 + 1
ROWS = 160
ROW0 = 8
EDGE = 48
WIDE_PAD = 32
VMEM_LIMIT = 24 * 1024 * 1024

f32 = jnp.float32
bf16 = jnp.bfloat16


def np_split(a):
    hi = np.asarray(a, np.float32).astype(ml_dtypes.bfloat16)
    lo = (np.asarray(a, np.float64) - hi.astype(np.float64)).astype(ml_dtypes.bfloat16)
    return hi, lo


def x_rows(cols):
    out = np.zeros((2 * XB, len(cols)))
    ang = 2 * np.pi * np.outer(np.arange(NV), cols) / NX
    out[:NV] = np.cos(ang)
    out[XB : XB + NV] = np.sin(ang)
    out[XB] = 0.0
    out[XB + NV - 1] = 0.0
    return out


def y_lanes(rows):
    out = np.zeros((len(rows), 2 * YB))
    ang = 2 * np.pi * np.outer(rows, np.arange(NU)) / NY
    out[:, :NU] = np.cos(ang)
    out[:, YB : YB + NU] = np.sin(ang)
    out[:, YB] = 0.0
    out[:, YB + NU - 1] = 0.0
    return out


def half_weights(bins):
    weights = np.full(bins, 2.0)
    weights[0] = weights[-1] = 1.0
    return weights


def x_back(cols):
    kappa = np.zeros(2 * XB)
    kappa[:NV] = half_weights(NV) / 2
    kappa[XB : XB + NV] = half_weights(NV) / 2
    return x_rows(cols).T * kappa


def y_back(rows):
    weight = np.zeros(2 * YB)
    weight[:NU] = half_weights(NU)
    weight[YB : YB + NU] = -half_weights(NU)
    return (y_lanes(rows) * weight).T / (NX * NY)


def pack(parts):
    rows, where, at = [], {}, 0
    pieces = []
    for name, a in parts:
        if a.shape[1] <= 256:
            pieces.append((name, a))
            continue
        cuts = range(0, a.shape[1], 256)
        where[name] = len(cuts)
        pieces += [(f"{name}.{i}", a[:, c : c + 256]) for i, c in enumerate(cuts)]
    for name, a in pieces:
        height = -(-a.shape[0] // 16) * 16
        block = np.zeros((height, 256), np.float64)
        block[: a.shape[0], : a.shape[1]] = a
        rows.append(block)
        where[name] = (at, a.shape[0], a.shape[1])
        at += height
    return np.concatenate(rows), where


def pack_split(parts):
    both = []
    for name, a in parts:
        hi, lo = np_split(a)
        if name in ("x2", "x3", "x4"):
            hi, lo = hi.astype(np.float64), lo.astype(np.float64)
            both.append((name, np.concatenate([hi, lo, hi], axis=1)))
            continue
        both += [(name + "_hi", hi.astype(np.float64)), (name + "_lo", lo.astype(np.float64))]
    return both


@functools.lru_cache(None)
def tables():
    core_rows = np.arange(HALO, HALO + CORE)
    field_cols = np.arange(ROW0, ROW0 + ROWS)
    own_cols = np.arange(WIDE, WIDE + CORE)
    sides = np.zeros((2 * XB, 256))
    sides[:, :WIDE] = x_rows(np.arange(WIDE))
    sides[:, CORE : CORE + WIDE] = x_rows(np.arange(WIDE + CORE, NX))
    parts = [("cx_own", x_rows(own_cols)), ("cx_side", sides)]
    for t in range(2):
        pos = np.arange(2 * CORE) - t * CORE + HALO
        inside = (pos >= 0) & (pos < NY)
        parts.append((f"by{t}", y_lanes(pos) * inside[:, None]))
    parts += [("x2", x_back(field_cols)), ("x3", x_rows(field_cols)), ("x4", x_back(own_cols))]
    y2_hi, y2_lo = (a.astype(np.float64) for a in np_split(y_back(core_rows)))
    y3_hi, y3_lo = (a.astype(np.float64) for a in np_split(y_lanes(core_rows)))
    grad = pack_split(parts)
    grad += [("y2", np.concatenate([y2_hi, y2_lo], axis=1))]
    grad += [("y3", np.concatenate([y3_hi, y3_hi, y3_lo]))]
    own = np.zeros((ROWS, CORE))
    own[np.arange(CORE) + WIDE - ROW0, np.arange(CORE)] = 1
    halo = np.zeros((ROWS, 256))
    for r in range(HALO):
        halo[HALO + r - ROW0, WIDE + r] = 1
        halo[WIDE + CORE + r - ROW0, CORE + WIDE + r] = 1
    grad += [("sel_own", own), ("sel_halo", halo)]
    offs = np.arange(KSIZE) - HALO
    kx = np.zeros((2 * XB, 128))
    kx[:, :KSIZE] = x_rows(offs)
    spec = [("kx", kx)]
    for m in range(4):
        ky = np.zeros((128, 2 * YB))
        ky[32 * m : 32 * m + KSIZE] = y_lanes(offs)
        spec.append((f"ky{m}", ky))
    return {"grad": pack(grad), "spec": pack(pack_split(spec))}


def split(x):
    hi = x.astype(bf16)
    return hi, (x - hi.astype(f32)).astype(bf16)


def dot(a, b):
    return lax.dot_general(a, b, (((1,), (0,)), ((), ())), preferred_element_type=f32)


def dot_nt(a, b):
    return lax.dot_general(a, b, (((1,), (1,)), ((), ())), preferred_element_type=f32)


def dot3(a_hi, a_lo, b_hi, b_lo, mul=dot):
    return mul(a_hi, b_hi) + (mul(a_lo, b_hi) + mul(a_hi, b_lo))


def signed(spec):
    cc, cs = spec[:XB, :YB], spec[:XB, YB:]
    sc, ss = spec[XB:, :YB], spec[XB:, YB:]
    return cc - ss, -(cs + sc), cc + ss, sc - cs


def even_odd(pr, pi, mr, mi):
    top = jnp.concatenate([pr + mr, pi + mi], axis=1)
    low = jnp.concatenate([mi - pi, pr - mr], axis=1)
    return jnp.concatenate([top, low], axis=0)


def table_array(group):
    return jnp.asarray(tables()[group][0].astype(ml_dtypes.bfloat16))


def table_reader(group, ref):
    where = tables()[group][1]

    def table(name, half=None):
        if isinstance(where[name], int):
            return jnp.concatenate([table(f"{name}.{i}") for i in range(where[name])], axis=1)
        at, height, width = where[name]
        lanes = slice(0, width) if half is None else slice(128 * half, 128 * half + 128)
        return ref[at : at + height, lanes]

    return table


def call(body, group, args, out_shape, scratch=(), smem=(), flops=0, nbytes=0):
    vm = pl.BlockSpec(memory_space=pltpu.VMEM)
    sm = pl.BlockSpec(memory_space=pltpu.SMEM)
    n_in = len(args)
    if group is not None:
        args = [*args, table_array(group)]

    def wrapped(*refs):
        if group is not None:
            refs = [*refs[:n_in], table_reader(group, refs[n_in]), *refs[n_in + 1 :]]
        body(*refs)

    return pl.pallas_call(
        wrapped,
        out_shape=out_shape,
        in_specs=[sm if i in smem else vm for i in range(len(args))],
        out_specs=[vm] * len(out_shape),
        scratch_shapes=list(scratch),
        compiler_params=pltpu.CompilerParams(vmem_limit_bytes=VMEM_LIMIT),
        cost_estimate=pl.CostEstimate(flops=flops, bytes_accessed=nbytes, transcendentals=0),
    )(*args)


def is_even():
    return lax.rem(lax.axis_index("tile"), 2) == 0


def send_edges(right, left, a_ref, b_ref):
    even = is_even()
    a_ref[...] = jnp.where(even, right, left)
    b_ref[...] = jnp.where(even, left, right)


def picker(rows, first, count, col):
    row = lax.broadcasted_iota(jnp.int32, (rows, CORE), 0)
    lane = lax.broadcasted_iota(jnp.int32, (rows, CORE), 1)
    hit = (row - first == lane - col) & (row >= first) & (row < first + count)
    return jnp.where(hit, 1.0, 0.0).astype(bf16)


def edges_of(rows, strip, extra=None):
    hi, lo = split(strip)
    both = []
    for col, more in ((CORE - WIDE, CORE - HALO), (0, 0)):
        pick = picker(rows, 0, WIDE, col)
        edge = dot_nt(pick, hi) + dot_nt(pick, lo)
        if extra is not None:
            edge = edge + dot_nt(picker(rows, WIDE, HALO, more), extra)
        both.append(edge)
    return both


def edges_kernel(mask_ref, target_ref, a_ref, b_ref):
    target = target_ref[...].astype(f32).astype(bf16)
    send_edges(*edges_of(EDGE, mask_ref[...], target), a_ref, b_ref)


def spectra_kernel(kern, w_ref, ker_ref, tb, h_ref, hs_ref):
    hs_ref[...] = jnp.zeros_like(hs_ref)
    for k in range(kern):
        for part in range(2):
            row = 32 * (2 * k + part)
            hs_ref[row : row + KSIZE, :KSIZE] = ker_ref[part, k, :, 0, :]
    s_hi, s_lo = split(hs_ref[...])
    z = dot3(tb("kx_hi"), tb("kx_lo"), s_hi, s_lo, dot_nt)
    z_hi, z_lo = split(z)
    for c in range(2 * kern):
        lanes = slice(128 * (c // 4), 128 * (c // 4) + 128)
        spec = dot3(z_hi[:, lanes], z_lo[:, lanes], tb(f"ky{c % 4}_hi"), tb(f"ky{c % 4}_lo"))
        root = jnp.sqrt(jnp.full((1, YB), w_ref[0, c // 2], f32))
        for j, comp in enumerate(signed(spec)):
            h_ref[c, j] = root * comp


def sides(from_a, from_b, tb):
    even = is_even()
    l_hi, l_lo = split(jnp.where(even, from_b, from_a))
    r_hi, r_lo = split(jnp.where(even, from_a, from_b))
    height = l_hi.shape[0]
    v = None
    for half, hi, lo in ((0, l_hi, l_lo), (1, r_hi, r_lo)):
        c_hi, c_lo = tb("cx_side_hi", half), tb("cx_side_lo", half)
        term = dot3(c_hi[:, :height], c_lo[:, :height], hi, lo)
        v = term if v is None else v + term
    return v, l_hi, r_hi


def to_spectrum(v, tb, f_ref, base):
    v_hi, v_lo = split(v)
    for t in range(2):
        spec = dot3(v_hi, v_lo, tb(f"by{t}_hi"), tb(f"by{t}_lo"))
        for j, comp in enumerate(signed(spec)):
            f_ref[t, j] = comp if base is None else base[t, j] - STEP_RATE * comp


def gradient_body(kern, last, f_ref, tgt_ref, h_ref, thr_ref, tb, g_ref, work):
    fld, inten, tot, a_hi, a_lo, b_cat, r_cat, w_cat = work
    chains = [(t, k) for t in range(2) for k in range(kern)]
    lag = kern + 2

    def at(i):
        return chains[i] if 0 <= i < len(chains) else None

    tile = lax.axis_index("tile")
    first = jnp.where(tile == 0, WIDE, HALO) - ROW0
    end = jnp.where(tile == last, WIDE + CORE, WIDE + CORE + HALO) - ROW0
    row = lax.broadcasted_iota(jnp.int32, (ROWS, CORE), 0)
    inside = (row >= first) & (row < end)
    lane = lax.broadcasted_iota(jnp.int32, (1, 2 * YB), 1)
    bin_at = lax.rem(lane, YB)
    weight = jnp.where((bin_at == 0) | (bin_at == NU - 1), 1.0, 2.0) / (NX * NY)
    weight = jnp.where(lane < YB, weight, -weight)

    def spectra_of(t, k, part):
        return [h_ref[2 * k + part, j] for j in range(4)], [f_ref[t, j] for j in range(4)]

    def products(t, k, slot):
        for part in range(2):
            (hpr, hpi, hmr, hmi), (fpr, fpi, fmr, fmi) = spectra_of(t, k, part)
            pr, pi = hpr * fpr - hpi * fpi, hpr * fpi + hpi * fpr
            mr, mi = hmr * fmr - hmi * fmi, hmr * fmi + hmi * fmr
            p_hi, p_lo = split(even_odd(pr, pi, mr, mi))
            rows = slice(2 * XB * part, 2 * XB * part + 2 * XB)
            a_hi[slot, rows] = p_hi
            a_lo[slot, rows] = p_lo

    def store_three(ref, slot, pieces, height):
        for j, piece in enumerate(pieces):
            ref[slot, height * j : height * j + height] = piece

    def field_of(t, k, slot):
        field = dot(tb("x2"), b_cat[slot])
        fld[t, k] = field
        re, im = field[:, :CORE], field[:, CORE:]
        power = re * re + im * im
        inten[t] = power if k == 0 else inten[t] + power

    def slope_of(t):
        resist = jax.nn.sigmoid(STEEPNESS * (inten[t] - thr_ref[0]))
        target = tgt_ref[:, CORE * t : CORE * t + CORE]
        slope = 2.0 * (resist - target) * STEEPNESS * resist * (1.0 - resist)
        inten[t] = jnp.where(inside, 2.0 * slope, 0.0)

    def scaled_field(t, k, slot):
        slope, field = inten[t], fld[t, k]
        r_hi, r_lo = split(
            jnp.concatenate([slope * field[:, :CORE], slope * field[:, CORE:]], axis=1)
        )
        store_three(r_cat, slot, (r_hi, r_hi, r_lo), ROWS)

    def add_back(t, k, slot):
        specs = dot(w_cat[slot], tb("y3"))
        acc = [0.0] * 4 if k == 0 else [tot[t, j] for j in range(4)]
        for part in range(2):
            spec = specs[2 * XB * part : 2 * XB * part + 2 * XB]
            cc, cs = spec[:XB, :YB], spec[:XB, YB:]
            sc, ss = spec[XB:, :YB], spec[XB:, YB:]
            bpr, neg, bmr, bmi = cc - ss, cs + sc, cc + ss, sc - cs
            hpr, hpi, hmr, hmi = (h_ref[2 * k + part, j] for j in range(4))
            acc[0] = acc[0] + (hpr * bpr - hpi * neg)
            acc[1] = acc[1] - (hpr * neg + hpi * bpr)
            acc[2] = acc[2] + (hmr * bmr + hmi * bmi)
            acc[3] = acc[3] + (hmr * bmi - hmi * bmr)
        for j in range(4):
            tot[t, j] = acc[j]

    def finish(t):
        r_hi, r_lo = split(even_odd(*(tot[t, j] for j in range(4))))
        u = dot(tb("x4"), jnp.concatenate([r_hi, r_hi, r_lo], axis=0))
        u_hi, u_lo = split(weight * u)
        term = dot3(tb(f"by{t}_hi"), tb(f"by{t}_lo"), u_hi, u_lo, dot_nt)
        g_ref[...] = term if t == 0 else g_ref[...] + term

    for i in range(len(chains) + lag + 2):
        new, mid, old = at(i), at(i - 1), at(i - 2)
        back, back_mid, back_old = at(i - lag), at(i - lag - 1), at(i - lag - 2)
        slot, other = i % 2, (i + 1) % 2
        if mid:
            z_one = dot(a_hi[other], tb("y2"))
            z_two = dot(a_lo[other], tb("y2", 0))
        if new:
            products(*new, slot)
        if back_mid:
            w_now = dot(tb("x3"), r_cat[other])
        if back:
            scaled_field(*back, slot)
        if old:
            field_of(*old, slot)
        if back_old:
            add_back(*back_old, slot)
        if mid:
            z = z_one[:, :CORE] + (z_one[:, CORE:] + z_two)
            z_hi, z_lo = split(jnp.concatenate([z[: 2 * XB], z[2 * XB :]], axis=1))
            store_three(b_cat, other, (z_hi, z_hi, z_lo), 2 * XB)
        if back_mid:
            w_hi, w_lo = split(w_now)
            for part in range(2):
                rows = slice(2 * XB * part, 2 * XB * part + 2 * XB)
                lanes = slice(CORE * part, CORE * part + CORE)
                for j, piece in enumerate((w_hi, w_lo, w_hi)):
                    w_cat[other, rows, CORE * j : CORE * j + CORE] = piece[:, lanes]
        if old and old[1] == kern - 1:
            slope_of(old[0])
        if back_old and back_old[1] == kern - 1:
            finish(back_old[0])


def first_kernel(
    kern, last, thr_ref, mask_ref, target_ref, a_ref, b_ref, h_ref, tb,
    g_ref, f_ref, tgt_ref, *work,
):
    m_hi, m_lo = split(mask_ref[...])
    v, left, right = sides(a_ref[...], b_ref[...], tb)
    v = v + dot3(tb("cx_own_hi"), tb("cx_own_lo"), m_hi, m_lo, dot_nt)
    to_spectrum(v, tb, f_ref, None)
    tgt_ref[...] = (
        dot_nt(tb("sel_own"), target_ref[...].astype(f32).astype(bf16))
        + dot(tb("sel_halo", 0)[:, :EDGE], left)
        + dot(tb("sel_halo", 1)[:, :EDGE], right)
    )
    gradient_body(kern, last, f_ref, tgt_ref, h_ref, thr_ref, tb, g_ref, work)


def later_kernel(
    kern, last, thr_ref, mine_ref, peer_ref, a_ref, a2_ref, b_ref, b2_ref, f_in_ref, tgt_ref,
    h_ref, tb, g_ref, f_ref, *work,
):
    s_hi, s_lo = split(mine_ref[...] + peer_ref[...])
    from_a = a_ref[...] + a2_ref[...]
    from_b = b_ref[...] + b2_ref[...]
    v, _, _ = sides(from_a, from_b, tb)
    v = v + dot3(tb("cx_own_hi"), tb("cx_own_lo"), s_hi, s_lo, dot_nt)
    to_spectrum(v, tb, f_ref, f_in_ref)
    gradient_body(kern, last, f_ref, tgt_ref, h_ref, thr_ref, tb, g_ref, work)


def match_kernel(n_got, table_ref, own_ref, *refs):
    got_refs, (out_ref, *edge_refs) = refs[:n_got], refs[n_got:]
    device = lax.axis_index("tile")
    other = []
    for t in range(2):
        rows = slice(CORE * t, CORE * t + CORE)
        bit = lax.bitwise_xor(table_ref[t], 2 * device + t)
        value = jnp.where(bit == 1, own_ref[CORE * (1 - t) : CORE * (2 - t)], own_ref[rows])
        for b, got in enumerate(got_refs):
            value = jnp.where(bit == 2 << b, got[rows], value)
        other.append(value)
    row = lax.broadcasted_iota(jnp.int32, (CORE, CORE), 0)
    lane = lax.broadcasted_iota(jnp.int32, (CORE, CORE), 1)
    flip = jnp.where(row + lane == CORE - 1, 1.0, 0.0).astype(bf16)
    hi, lo = split(jnp.concatenate(other, axis=0))
    turned = dot(hi, flip) + dot(lo, flip)
    tiles = []
    for t in range(2):
        rows = slice(CORE * t, CORE * t + CORE)
        value = jnp.where(table_ref[2 + t] == 1, turned[rows], other[t])
        tiles.append(0.5 * (own_ref[rows] + value))
    matched = jnp.concatenate(tiles, axis=0)
    out_ref[...] = matched
    if edge_refs:
        send_edges(*edges_of(WIDE_PAD, matched), *edge_refs)


def final_kernel(n_moves, mask_ref, *refs):
    moves, (mask_out, grad_out) = refs[: 2 * n_moves], refs[2 * n_moves :]
    for t in range(2):
        rows = slice(CORE * t, CORE * t + CORE)
        now = mask_ref[t]
        for mine, peer in zip(moves[::2], moves[1::2]):
            step = mine[rows] + peer[rows]
            now = now - STEP_RATE * step
        grad_out[t] = step
        mask_out[t] = now


def per_device(
    n_tile, n_depth, mask_tiles, target_tiles, kernels, socs_weights, thresholds,
    partner_table, mirror_flags,
):
    tiles_dev, core, _ = mask_tiles.shape
    kern = kernels.shape[2]
    assert tiles_dev == 2 and core == CORE
    pairs_a = [(i, i ^ 1) for i in range(n_tile)]
    pairs_b = [p for i in range(1, n_tile - 1, 2) for p in ((i, i + 1), (i + 1, i))]

    def swap_edges(send_a, send_b, cross=False):
        def move(x, pairs):
            if not cross:
                return lax.ppermute(x, "tile", pairs)
            both = [(2 * i + p, 2 * j + 1 - p) for i, j in pairs for p in range(2)]
            return lax.ppermute(x, ("tile", "depth"), both)

        return move(send_b, pairs_b), move(send_a, pairs_a)

    def depth_pair(x):
        bit = 1
        while True:
            peer = lax.ppermute(x, "depth", [(i, i ^ bit) for i in range(n_depth)])
            bit *= 2
            if bit >= n_depth:
                return x, peer
            x = x + peer

    def from_partners(grad):
        bits = [1 << b for b in range(n_tile.bit_length() - 1)]
        got = [
            lax.ppermute(grad, "tile", [(i, i ^ bit) for i in range(n_tile)])
            for bit in reversed(bits)
        ]
        return got[::-1]

    mask_rows = mask_tiles.reshape(tiles_dev * core, core)
    target_rows = target_tiles.reshape(tiles_dev * core, core)
    strip = jax.ShapeDtypeStruct((tiles_dev * core, core), f32)
    side = jax.ShapeDtypeStruct((WIDE_PAD, tiles_dev * core), f32)
    freq = jax.ShapeDtypeStruct((2, 4, XB, YB), f32)
    goal = jax.ShapeDtypeStruct((ROWS, 2 * CORE), f32)
    tiles = jax.ShapeDtypeStruct((tiles_dev, core, core), f32)
    scratch = [
        pltpu.VMEM((2, kern, ROWS, 2 * CORE), f32),
        pltpu.VMEM((2, ROWS, CORE), f32),
        pltpu.VMEM((2, 4, XB, YB), f32),
        pltpu.VMEM((2, 4 * XB, 2 * YB), bf16),
        pltpu.VMEM((2, 4 * XB, 2 * YB), bf16),
        pltpu.VMEM((2, 6 * XB, 2 * CORE), bf16),
        pltpu.VMEM((2, 3 * ROWS, 2 * CORE), bf16),
        pltpu.VMEM((2, 4 * XB, 3 * CORE), bf16),
    ]

    edge = jax.ShapeDtypeStruct((EDGE, tiles_dev * core), f32)
    send_a, send_b = call(
        edges_kernel, None, [mask_rows, target_rows], [edge, edge], flops=3 * 10**9
    )
    from_b, from_a = swap_edges(send_a, send_b)
    table = jnp.concatenate([partner_table, mirror_flags])
    (spectra,) = call(
        functools.partial(spectra_kernel, kern),
        "spec",
        [socs_weights, kernels.transpose(0, 2, 3, 1, 4)],
        [jax.ShapeDtypeStruct((2 * kern, 4, XB, YB), f32)],
        [pltpu.VMEM((32 * 2 * kern, 128), f32)],
        smem=(0,),
        flops=3 * 10**9,
        nbytes=4 * 10**6,
    )
    grad, freq_now, goals = call(
        functools.partial(first_kernel, kern, n_tile - 1),
        "grad",
        [thresholds, mask_rows, target_rows, from_a, from_b, spectra],
        [strip, freq, goal],
        scratch,
        smem=(0,),
        flops=10**10,
    )
    moves = []
    for step in range(1, STEPS + 1):
        got = from_partners(grad)
        outs = call(
            functools.partial(match_kernel, len(got)),
            None,
            [table, grad, *got],
            [strip, side, side] if step < STEPS else [strip],
            smem=(0,),
        )
        if step == STEPS:
            moves += depth_pair(outs[0])
            break
        if n_depth == 2:
            from_b, from_a = swap_edges(*outs[1:])
            far_b, far_a = swap_edges(*outs[1:], cross=True)
            rims = (from_a, far_a, from_b, far_b)
        else:
            from_b, from_a = swap_edges(*outs[1:])
            rims = depth_pair(from_a) + depth_pair(from_b)
        moves += depth_pair(outs[0])
        kept = step + 1 < STEPS
        grad, *rest = call(
            functools.partial(later_kernel, kern, n_tile - 1),
            "grad",
            [thresholds, *moves[-2:], *rims, freq_now, goals, spectra],
            [strip, freq] if kept else [strip],
            scratch if kept else [pltpu.VMEM(freq.shape, f32)] + scratch,
            smem=(0,),
            flops=10**10,
        )
        freq_now = rest[0] if kept else None
    final = functools.partial(final_kernel, STEPS)
    return tuple(call(final, None, [mask_tiles, *moves], [tiles, tiles]))


def solution(mesh):
    return jax.shard_map(
        functools.partial(per_device, mesh.shape["tile"], mesh.shape["depth"]),
        mesh=mesh,
        in_specs=(
            P("tile", None, None),
            P("tile", None, None),
            P(None, "depth", None, None, None),
            P("depth", None),
            P("depth"),
            P("tile"),
            P("tile"),
        ),
        out_specs=(P("tile", None, None), P("tile", None, None)),
        check_vma=False,
    )
```

```python
import functools

import jax
import jax.numpy as jnp
import ml_dtypes
import numpy as np
from jax import lax
from jax.experimental import pallas as pl
from jax.experimental.pallas import tpu as pltpu
from jax.sharding import PartitionSpec as P

HALO = 12
KSIZE = 25
STEPS = 2
STEEPNESS = 3.0
STEP_RATE = 0.05

CORE = 128
NY = 152
NX = 176
WIDE = 2 * HALO
XB = 96
YB = 128
NU = NY // 2 + 1
NV = NX // 2 + 1
ROWS = 160
ROW0 = 8
CHUNK = 16
EDGE = 48
WIDE_PAD = 32
VMEM_LIMIT = 24 * 1024 * 1024

f32 = jnp.float32
bf16 = jnp.bfloat16


def np_split(a):
    hi = np.asarray(a, np.float32).astype(ml_dtypes.bfloat16)
    lo = (np.asarray(a, np.float64) - hi.astype(np.float64)).astype(ml_dtypes.bfloat16)
    return hi, lo


def x_rows(cols):
    out = np.zeros((2 * XB, len(cols)))
    ang = 2 * np.pi * np.outer(np.arange(NV), cols) / NX
    out[:NV] = np.cos(ang)
    out[XB : XB + NV] = np.sin(ang)
    out[XB] = 0.0
    out[XB + NV - 1] = 0.0
    return out


def y_lanes(rows):
    out = np.zeros((len(rows), 2 * YB))
    ang = 2 * np.pi * np.outer(rows, np.arange(NU)) / NY
    out[:, :NU] = np.cos(ang)
    out[:, YB : YB + NU] = np.sin(ang)
    out[:, YB] = 0.0
    out[:, YB + NU - 1] = 0.0
    return out


def half_weights(bins):
    weights = np.full(bins, 2.0)
    weights[0] = weights[-1] = 1.0
    return weights


def x_back(cols):
    kappa = np.zeros(2 * XB)
    kappa[:NV] = half_weights(NV) / 2
    kappa[XB : XB + NV] = half_weights(NV) / 2
    return x_rows(cols).T * kappa


def y_back(rows):
    weight = np.zeros(2 * YB)
    weight[:NU] = half_weights(NU)
    weight[YB : YB + NU] = -half_weights(NU)
    return (y_lanes(rows) * weight).T / (NX * NY)


def pack(parts):
    rows, where, at = [], {}, 0
    pieces = []
    for name, a in parts:
        if a.shape[1] <= 256:
            pieces.append((name, a))
            continue
        cuts = range(0, a.shape[1], 256)
        where[name] = len(cuts)
        pieces += [(f"{name}.{i}", a[:, c : c + 256]) for i, c in enumerate(cuts)]
    for name, a in pieces:
        height = -(-a.shape[0] // 16) * 16
        block = np.zeros((height, 256), np.float64)
        block[: a.shape[0], : a.shape[1]] = a
        rows.append(block)
        where[name] = (at, a.shape[0], a.shape[1])
        at += height
    return np.concatenate(rows), where


def pack_split(parts):
    both = []
    for name, a in parts:
        hi, lo = np_split(a)
        if name in ("x2", "x3", "x4"):
            hi, lo = hi.astype(np.float64), lo.astype(np.float64)
            both.append((name, np.concatenate([hi, lo, hi], axis=1)))
            continue
        both += [(name + "_hi", hi.astype(np.float64)), (name + "_lo", lo.astype(np.float64))]
    return both


@functools.lru_cache(None)
def tables():
    core_rows = np.arange(HALO, HALO + CORE)
    field_cols = np.arange(ROW0, ROW0 + ROWS)
    own_cols = np.arange(WIDE, WIDE + CORE)
    sides = np.zeros((2 * XB, 256))
    sides[:, :WIDE] = x_rows(np.arange(WIDE))
    sides[:, CORE : CORE + WIDE] = x_rows(np.arange(WIDE + CORE, NX))
    parts = [("cx_own", x_rows(own_cols)), ("cx_side", sides)]
    for t in range(2):
        pos = np.arange(2 * CORE) - t * CORE + HALO
        inside = (pos >= 0) & (pos < NY)
        parts.append((f"by{t}", y_lanes(pos) * inside[:, None]))
    parts += [("x2", x_back(field_cols)), ("x3", x_rows(field_cols)), ("x4", x_back(own_cols))]
    y2_hi, y2_lo = (a.astype(np.float64) for a in np_split(y_back(core_rows)))
    y3_hi, y3_lo = (a.astype(np.float64) for a in np_split(y_lanes(core_rows)))
    grad = pack_split(parts)
    grad += [("y2", np.concatenate([y2_hi, y2_lo], axis=1))]
    grad += [("y3", np.concatenate([y3_hi, y3_hi, y3_lo]))]
    own = np.zeros((ROWS, CORE))
    own[np.arange(CORE) + WIDE - ROW0, np.arange(CORE)] = 1
    halo = np.zeros((ROWS, 256))
    for r in range(HALO):
        halo[HALO + r - ROW0, WIDE + r] = 1
        halo[WIDE + CORE + r - ROW0, CORE + WIDE + r] = 1
    grad += [("sel_own", own), ("sel_halo", halo)]
    offs = np.arange(KSIZE) - HALO
    kx = np.zeros((2 * XB, 128))
    kx[:, :KSIZE] = x_rows(offs)
    spec = [("kx", kx)]
    for m in range(4):
        ky = np.zeros((128, 2 * YB))
        ky[32 * m : 32 * m + KSIZE] = y_lanes(offs)
        spec.append((f"ky{m}", ky))
    return {"grad": pack(grad), "spec": pack(pack_split(spec))}


def split(x):
    hi = x.astype(bf16)
    return hi, (x - hi.astype(f32)).astype(bf16)


def dot(a, b):
    return lax.dot_general(a, b, (((1,), (0,)), ((), ())), preferred_element_type=f32)


def dot_nt(a, b):
    return lax.dot_general(a, b, (((1,), (1,)), ((), ())), preferred_element_type=f32)


def dot3(a_hi, a_lo, b_hi, b_lo, mul=dot):
    return mul(a_hi, b_hi) + (mul(a_lo, b_hi) + mul(a_hi, b_lo))


def signed(spec):
    cc, cs = spec[:XB, :YB], spec[:XB, YB:]
    sc, ss = spec[XB:, :YB], spec[XB:, YB:]
    return cc - ss, -(cs + sc), cc + ss, sc - cs


def even_odd(pr, pi, mr, mi):
    top = jnp.concatenate([pr + mr, pi + mi], axis=1)
    low = jnp.concatenate([mi - pi, pr - mr], axis=1)
    return jnp.concatenate([top, low], axis=0)


def table_array(group):
    return jnp.asarray(tables()[group][0].astype(ml_dtypes.bfloat16))


def table_reader(group, ref):
    where = tables()[group][1]

    def table(name, half=None):
        if isinstance(where[name], int):
            return jnp.concatenate([table(f"{name}.{i}") for i in range(where[name])], axis=1)
        at, height, width = where[name]
        lanes = slice(0, width) if half is None else slice(128 * half, 128 * half + 128)
        return ref[at : at + height, lanes]

    return table


def call(body, group, args, out_shape, scratch=(), smem=(), flops=0, nbytes=0):
    vm = pl.BlockSpec(memory_space=pltpu.VMEM)
    sm = pl.BlockSpec(memory_space=pltpu.SMEM)
    n_in = len(args)
    if group is not None:
        args = [*args, table_array(group)]

    def wrapped(*refs):
        if group is not None:
            refs = [*refs[:n_in], table_reader(group, refs[n_in]), *refs[n_in + 1 :]]
        body(*refs)

    return pl.pallas_call(
        wrapped,
        out_shape=out_shape,
        in_specs=[sm if i in smem else vm for i in range(len(args))],
        out_specs=[vm] * len(out_shape),
        scratch_shapes=list(scratch),
        compiler_params=pltpu.CompilerParams(vmem_limit_bytes=VMEM_LIMIT),
        cost_estimate=pl.CostEstimate(flops=flops, bytes_accessed=nbytes, transcendentals=0),
    )(*args)


def is_even():
    return lax.rem(lax.axis_index("tile"), 2) == 0


def send_edges(right, left, a_ref, b_ref):
    even = is_even()
    a_ref[...] = jnp.where(even, right, left)
    b_ref[...] = jnp.where(even, left, right)


def picker(rows, first, count, col):
    row = lax.broadcasted_iota(jnp.int32, (rows, CORE), 0)
    lane = lax.broadcasted_iota(jnp.int32, (rows, CORE), 1)
    hit = (row - first == lane - col) & (row >= first) & (row < first + count)
    return jnp.where(hit, 1.0, 0.0).astype(bf16)


def edges_of(rows, strip, extra=None):
    hi, lo = split(strip)
    both = []
    for col, more in ((CORE - WIDE, CORE - HALO), (0, 0)):
        pick = picker(rows, 0, WIDE, col)
        edge = dot_nt(pick, hi) + dot_nt(pick, lo)
        if extra is not None:
            edge = edge + dot_nt(picker(rows, WIDE, HALO, more), extra)
        both.append(edge)
    return both


def edges_kernel(mask_ref, target_ref, a_ref, b_ref):
    target = target_ref[...].astype(f32).astype(bf16)
    send_edges(*edges_of(EDGE, mask_ref[...], target), a_ref, b_ref)


def spectra_kernel(kern, w_ref, ker_ref, tb, h_ref, hs_ref):
    hs_ref[...] = jnp.zeros_like(hs_ref)
    for k in range(kern):
        for part in range(2):
            row = 32 * (2 * k + part)
            hs_ref[row : row + KSIZE, :KSIZE] = ker_ref[part, k, :, 0, :]
    s_hi, s_lo = split(hs_ref[...])
    z = dot3(tb("kx_hi"), tb("kx_lo"), s_hi, s_lo, dot_nt)
    z_hi, z_lo = split(z)
    for c in range(2 * kern):
        lanes = slice(128 * (c // 4), 128 * (c // 4) + 128)
        spec = dot3(z_hi[:, lanes], z_lo[:, lanes], tb(f"ky{c % 4}_hi"), tb(f"ky{c % 4}_lo"))
        root = jnp.sqrt(jnp.full((1, YB), w_ref[0, c // 2], f32))
        for j, comp in enumerate(signed(spec)):
            h_ref[c, j] = root * comp


def sides(from_a, from_b, tb):
    even = is_even()
    l_hi, l_lo = split(jnp.where(even, from_b, from_a))
    r_hi, r_lo = split(jnp.where(even, from_a, from_b))
    height = l_hi.shape[0]
    v = None
    for half, hi, lo in ((0, l_hi, l_lo), (1, r_hi, r_lo)):
        c_hi, c_lo = tb("cx_side_hi", half), tb("cx_side_lo", half)
        term = dot3(c_hi[:, :height], c_lo[:, :height], hi, lo)
        v = term if v is None else v + term
    return v, l_hi, r_hi


def to_spectrum(v, tb, f_ref, base):
    v_hi, v_lo = split(v)
    for t in range(2):
        spec = dot3(v_hi, v_lo, tb(f"by{t}_hi"), tb(f"by{t}_lo"))
        for j, comp in enumerate(signed(spec)):
            f_ref[t, j] = comp if base is None else base[t, j] - STEP_RATE * comp


def gradient_body(kern, last, f_ref, tgt_ref, h_ref, thr_ref, tb, g_ref, work):
    fld, inten, tot, a_hi, a_lo, b_cat, r_cat, w_cat = work
    chains = [(t, k) for t in range(2) for k in range(kern)]
    lag = kern + 2

    def at(i):
        return chains[i] if 0 <= i < len(chains) else None

    tile = lax.axis_index("tile")
    first = jnp.where(tile == 0, WIDE, HALO) - ROW0
    end = jnp.where(tile == last, WIDE + CORE, WIDE + CORE + HALO) - ROW0
    row = lax.broadcasted_iota(jnp.int32, (ROWS, CORE), 0)
    inside = (row >= first) & (row < end)
    lane = lax.broadcasted_iota(jnp.int32, (1, 2 * YB), 1)
    bin_at = lax.rem(lane, YB)
    weight = jnp.where((bin_at == 0) | (bin_at == NU - 1), 1.0, 2.0) / (NX * NY)
    weight = jnp.where(lane < YB, weight, -weight)

    def chunks(height):
        return [slice(r, r + CHUNK) for r in range(0, height, CHUNK)]

    def put(ref, slot, starts, pieces):
        for at_row, piece in zip(starts, pieces):
            ref[slot, at_row : at_row + CHUNK] = piece

    def products(t, k, slot):
        for part in range(2):
            for rows in chunks(XB):
                hpr, hpi, hmr, hmi = (h_ref[2 * k + part, j, rows] for j in range(4))
                fpr, fpi, fmr, fmi = (f_ref[t, j, rows] for j in range(4))
                pr, pi = hpr * fpr - hpi * fpi, hpr * fpi + hpi * fpr
                mr, mi = hmr * fmr - hmi * fmi, hmr * fmi + hmi * fmr
                starts = [2 * XB * part + rows.start, 2 * XB * part + XB + rows.start]
                top = split(jnp.concatenate([pr + mr, pi + mi], axis=1))
                low = split(jnp.concatenate([mi - pi, pr - mr], axis=1))
                put(a_hi, slot, starts, (top[0], low[0]))
                put(a_lo, slot, starts, (top[1], low[1]))

    def y_done(z_one, z_two, slot):
        for rows in chunks(2 * XB):
            z = []
            for part in range(2):
                here = slice(2 * XB * part + rows.start, 2 * XB * part + rows.stop)
                z.append(z_one[here, :CORE] + (z_one[here, CORE:] + z_two[here]))
            z_hi, z_lo = split(jnp.concatenate(z, axis=1))
            starts = [2 * XB * j + rows.start for j in range(3)]
            put(b_cat, slot, starts, (z_hi, z_hi, z_lo))

    def field_of(t, k, slot):
        whole = dot(tb("x2"), b_cat[slot])
        for rows in chunks(ROWS):
            field = whole[rows]
            fld[t, k, rows] = field
            re, im = field[:, :CORE], field[:, CORE:]
            power = re * re + im * im
            inten[t, rows] = power if k == 0 else inten[t, rows] + power

    def slope_of(t):
        resist = jax.nn.sigmoid(STEEPNESS * (inten[t] - thr_ref[0]))
        target = tgt_ref[:, CORE * t : CORE * t + CORE]
        slope = 2.0 * (resist - target) * STEEPNESS * resist * (1.0 - resist)
        inten[t] = jnp.where(inside, 2.0 * slope, 0.0)

    def scaled_field(t, k, slot):
        for rows in chunks(ROWS):
            slope, field = inten[t, rows], fld[t, k, rows]
            r_hi, r_lo = split(
                jnp.concatenate([slope * field[:, :CORE], slope * field[:, CORE:]], axis=1)
            )
            starts = [ROWS * j + rows.start for j in range(3)]
            put(r_cat, slot, starts, (r_hi, r_hi, r_lo))

    def x_back_done(w_now, slot):
        for rows in chunks(2 * XB):
            w_hi, w_lo = split(w_now[rows])
            for part in range(2):
                here = slice(2 * XB * part + rows.start, 2 * XB * part + rows.stop)
                lanes = slice(CORE * part, CORE * part + CORE)
                for j, piece in enumerate((w_hi, w_lo, w_hi)):
                    w_cat[slot, here, CORE * j : CORE * j + CORE] = piece[:, lanes]

    def add_back(t, k, slot):
        specs = dot(w_cat[slot], tb("y3"))
        for rows in chunks(XB):
            acc = [0.0] * 4 if k == 0 else [tot[t, j, rows] for j in range(4)]
            for part in range(2):
                base = 2 * XB * part + rows.start
                cos_rows, sin_rows = slice(base, base + CHUNK), slice(base + XB, base + XB + CHUNK)
                cc, cs = specs[cos_rows, :YB], specs[cos_rows, YB:]
                sc, ss = specs[sin_rows, :YB], specs[sin_rows, YB:]
                bpr, neg, bmr, bmi = cc - ss, cs + sc, cc + ss, sc - cs
                hpr, hpi, hmr, hmi = (h_ref[2 * k + part, j, rows] for j in range(4))
                acc[0] = acc[0] + (hpr * bpr - hpi * neg)
                acc[1] = acc[1] - (hpr * neg + hpi * bpr)
                acc[2] = acc[2] + (hmr * bmr + hmi * bmi)
                acc[3] = acc[3] + (hmr * bmi - hmi * bmr)
            for j in range(4):
                tot[t, j, rows] = acc[j]

    def finish(t):
        r_hi, r_lo = split(even_odd(*(tot[t, j] for j in range(4))))
        u = dot(tb("x4"), jnp.concatenate([r_hi, r_hi, r_lo], axis=0))
        u_hi, u_lo = split(weight * u)
        term = dot3(tb(f"by{t}_hi"), tb(f"by{t}_lo"), u_hi, u_lo, dot_nt)
        g_ref[...] = term if t == 0 else g_ref[...] + term

    for i in range(len(chains) + lag + 2):
        new, mid, old = at(i), at(i - 1), at(i - 2)
        back, back_mid, back_old = at(i - lag), at(i - lag - 1), at(i - lag - 2)
        slot, other = i % 2, (i + 1) % 2
        if mid:
            z_one = dot(a_hi[other], tb("y2"))
            z_two = dot(a_lo[other], tb("y2", 0))
        if new:
            products(*new, slot)
        if back_mid:
            w_now = dot(tb("x3"), r_cat[other])
        if back:
            scaled_field(*back, slot)
        if old:
            field_of(*old, slot)
        if back_old:
            add_back(*back_old, slot)
        if mid:
            y_done(z_one, z_two, other)
        if back_mid:
            x_back_done(w_now, other)
        if old and old[1] == kern - 1:
            slope_of(old[0])
        if back_old and back_old[1] == kern - 1:
            finish(back_old[0])


def first_kernel(
    kern, last, thr_ref, mask_ref, target_ref, a_ref, b_ref, h_ref, tb,
    g_ref, f_ref, tgt_ref, *work,
):
    m_hi, m_lo = split(mask_ref[...])
    v, left, right = sides(a_ref[...], b_ref[...], tb)
    v = v + dot3(tb("cx_own_hi"), tb("cx_own_lo"), m_hi, m_lo, dot_nt)
    to_spectrum(v, tb, f_ref, None)
    tgt_ref[...] = (
        dot_nt(tb("sel_own"), target_ref[...].astype(f32).astype(bf16))
        + dot(tb("sel_halo", 0)[:, :EDGE], left)
        + dot(tb("sel_halo", 1)[:, :EDGE], right)
    )
    gradient_body(kern, last, f_ref, tgt_ref, h_ref, thr_ref, tb, g_ref, work)


def later_kernel(
    kern, last, thr_ref, mine_ref, peer_ref, a_ref, a2_ref, b_ref, b2_ref, f_in_ref, tgt_ref,
    h_ref, tb, g_ref, f_ref, *work,
):
    s_hi, s_lo = split(mine_ref[...] + peer_ref[...])
    from_a = a_ref[...] + a2_ref[...]
    from_b = b_ref[...] + b2_ref[...]
    v, _, _ = sides(from_a, from_b, tb)
    v = v + dot3(tb("cx_own_hi"), tb("cx_own_lo"), s_hi, s_lo, dot_nt)
    to_spectrum(v, tb, f_ref, f_in_ref)
    gradient_body(kern, last, f_ref, tgt_ref, h_ref, thr_ref, tb, g_ref, work)


def match_kernel(n_got, table_ref, own_ref, *refs):
    got_refs, (out_ref, *edge_refs) = refs[:n_got], refs[n_got:]
    device = lax.axis_index("tile")
    other = []
    for t in range(2):
        rows = slice(CORE * t, CORE * t + CORE)
        bit = lax.bitwise_xor(table_ref[t], 2 * device + t)
        value = jnp.where(bit == 1, own_ref[CORE * (1 - t) : CORE * (2 - t)], own_ref[rows])
        for b, got in enumerate(got_refs):
            value = jnp.where(bit == 2 << b, got[rows], value)
        other.append(value)
    row = lax.broadcasted_iota(jnp.int32, (CORE, CORE), 0)
    lane = lax.broadcasted_iota(jnp.int32, (CORE, CORE), 1)
    flip = jnp.where(row + lane == CORE - 1, 1.0, 0.0).astype(bf16)
    hi, lo = split(jnp.concatenate(other, axis=0))
    turned = dot(hi, flip) + dot(lo, flip)
    tiles = []
    for t in range(2):
        rows = slice(CORE * t, CORE * t + CORE)
        value = jnp.where(table_ref[2 + t] == 1, turned[rows], other[t])
        tiles.append(0.5 * (own_ref[rows] + value))
    matched = jnp.concatenate(tiles, axis=0)
    out_ref[...] = matched
    if edge_refs:
        send_edges(*edges_of(WIDE_PAD, matched), *edge_refs)


def final_kernel(n_moves, mask_ref, *refs):
    moves, (mask_out, grad_out) = refs[: 2 * n_moves], refs[2 * n_moves :]
    for t in range(2):
        rows = slice(CORE * t, CORE * t + CORE)
        now = mask_ref[t]
        for mine, peer in zip(moves[::2], moves[1::2]):
            step = mine[rows] + peer[rows]
            now = now - STEP_RATE * step
        grad_out[t] = step
        mask_out[t] = now


def per_device(
    n_tile, n_depth, mask_tiles, target_tiles, kernels, socs_weights, thresholds,
    partner_table, mirror_flags,
):
    tiles_dev, core, _ = mask_tiles.shape
    kern = kernels.shape[2]
    assert tiles_dev == 2 and core == CORE
    pairs_a = [(i, i ^ 1) for i in range(n_tile)]
    pairs_b = [p for i in range(1, n_tile - 1, 2) for p in ((i, i + 1), (i + 1, i))]

    def swap_edges(send_a, send_b, cross=False):
        def move(x, pairs):
            if not cross:
                return lax.ppermute(x, "tile", pairs)
            both = [(2 * i + p, 2 * j + 1 - p) for i, j in pairs for p in range(2)]
            return lax.ppermute(x, ("tile", "depth"), both)

        return move(send_b, pairs_b), move(send_a, pairs_a)

    def depth_pair(x):
        bit = 1
        while True:
            peer = lax.ppermute(x, "depth", [(i, i ^ bit) for i in range(n_depth)])
            bit *= 2
            if bit >= n_depth:
                return x, peer
            x = x + peer

    def from_partners(grad):
        bits = [1 << b for b in range(n_tile.bit_length() - 1)]
        got = [
            lax.ppermute(grad, "tile", [(i, i ^ bit) for i in range(n_tile)])
            for bit in reversed(bits)
        ]
        return got[::-1]

    mask_rows = mask_tiles.reshape(tiles_dev * core, core)
    target_rows = target_tiles.reshape(tiles_dev * core, core)
    strip = jax.ShapeDtypeStruct((tiles_dev * core, core), f32)
    side = jax.ShapeDtypeStruct((WIDE_PAD, tiles_dev * core), f32)
    freq = jax.ShapeDtypeStruct((2, 4, XB, YB), f32)
    goal = jax.ShapeDtypeStruct((ROWS, 2 * CORE), f32)
    tiles = jax.ShapeDtypeStruct((tiles_dev, core, core), f32)
    scratch = [
        pltpu.VMEM((2, kern, ROWS, 2 * CORE), f32),
        pltpu.VMEM((2, ROWS, CORE), f32),
        pltpu.VMEM((2, 4, XB, YB), f32),
        pltpu.VMEM((2, 4 * XB, 2 * YB), bf16),
        pltpu.VMEM((2, 4 * XB, 2 * YB), bf16),
        pltpu.VMEM((2, 6 * XB, 2 * CORE), bf16),
        pltpu.VMEM((2, 3 * ROWS, 2 * CORE), bf16),
        pltpu.VMEM((2, 4 * XB, 3 * CORE), bf16),
    ]

    edge = jax.ShapeDtypeStruct((EDGE, tiles_dev * core), f32)
    send_a, send_b = call(
        edges_kernel, None, [mask_rows, target_rows], [edge, edge], flops=3 * 10**9
    )
    from_b, from_a = swap_edges(send_a, send_b)
    table = jnp.concatenate([partner_table, mirror_flags])
    (spectra,) = call(
        functools.partial(spectra_kernel, kern),
        "spec",
        [socs_weights, kernels.transpose(0, 2, 3, 1, 4)],
        [jax.ShapeDtypeStruct((2 * kern, 4, XB, YB), f32)],
        [pltpu.VMEM((32 * 2 * kern, 128), f32)],
        smem=(0,),
        flops=3 * 10**9,
        nbytes=4 * 10**6,
    )
    grad, freq_now, goals = call(
        functools.partial(first_kernel, kern, n_tile - 1),
        "grad",
        [thresholds, mask_rows, target_rows, from_a, from_b, spectra],
        [strip, freq, goal],
        scratch,
        smem=(0,),
        flops=10**10,
    )
    moves = []
    for step in range(1, STEPS + 1):
        got = from_partners(grad)
        outs = call(
            functools.partial(match_kernel, len(got)),
            None,
            [table, grad, *got],
            [strip, side, side] if step < STEPS else [strip],
            smem=(0,),
        )
        if step == STEPS:
            moves += depth_pair(outs[0])
            break
        if n_depth == 2:
            from_b, from_a = swap_edges(*outs[1:])
            far_b, far_a = swap_edges(*outs[1:], cross=True)
            rims = (from_a, far_a, from_b, far_b)
        else:
            from_b, from_a = swap_edges(*outs[1:])
            rims = depth_pair(from_a) + depth_pair(from_b)
        moves += depth_pair(outs[0])
        kept = step + 1 < STEPS
        grad, *rest = call(
            functools.partial(later_kernel, kern, n_tile - 1),
            "grad",
            [thresholds, *moves[-2:], *rims, freq_now, goals, spectra],
            [strip, freq] if kept else [strip],
            scratch if kept else [pltpu.VMEM(freq.shape, f32)] + scratch,
            smem=(0,),
            flops=10**10,
        )
        freq_now = rest[0] if kept else None
    final = functools.partial(final_kernel, STEPS)
    return tuple(call(final, None, [mask_tiles, *moves], [tiles, tiles]))


def solution(mesh):
    return jax.shard_map(
        functools.partial(per_device, mesh.shape["tile"], mesh.shape["depth"]),
        mesh=mesh,
        in_specs=(
            P("tile", None, None),
            P("tile", None, None),
            P(None, "depth", None, None, None),
            P("depth", None),
            P("depth"),
            P("tile"),
            P("tile"),
        ),
        out_specs=(P("tile", None, None), P("tile", None, None)),
        check_vma=False,
    )
```

```python
import functools

import jax
import jax.numpy as jnp
import ml_dtypes
import numpy as np
from jax import lax
from jax.experimental import pallas as pl
from jax.experimental.pallas import tpu as pltpu
from jax.sharding import PartitionSpec as P

HALO = 12
KSIZE = 25
STEPS = 2
STEEPNESS = 3.0
STEP_RATE = 0.05

CORE = 128
NY = 152
NX = 176
WIDE = 2 * HALO
XB = 96
YB = 128
NU = NY // 2 + 1
NV = NX // 2 + 1
ROWS = 160
ROW0 = 8
CHUNK = 16
EDGE = 48
WIDE_PAD = 32
VMEM_LIMIT = 24 * 1024 * 1024

f32 = jnp.float32
bf16 = jnp.bfloat16


def np_split(a):
    hi = np.asarray(a, np.float32).astype(ml_dtypes.bfloat16)
    lo = (np.asarray(a, np.float64) - hi.astype(np.float64)).astype(ml_dtypes.bfloat16)
    return hi, lo


def x_rows(cols):
    out = np.zeros((2 * XB, len(cols)))
    ang = 2 * np.pi * np.outer(np.arange(NV), cols) / NX
    out[:NV] = np.cos(ang)
    out[XB : XB + NV] = np.sin(ang)
    out[XB] = 0.0
    out[XB + NV - 1] = 0.0
    return out


def y_lanes(rows):
    out = np.zeros((len(rows), 2 * YB))
    ang = 2 * np.pi * np.outer(rows, np.arange(NU)) / NY
    out[:, :NU] = np.cos(ang)
    out[:, YB : YB + NU] = np.sin(ang)
    out[:, YB] = 0.0
    out[:, YB + NU - 1] = 0.0
    return out


def half_weights(bins):
    weights = np.full(bins, 2.0)
    weights[0] = weights[-1] = 1.0
    return weights


def x_back(cols):
    kappa = np.zeros(2 * XB)
    kappa[:NV] = half_weights(NV) / 2
    kappa[XB : XB + NV] = half_weights(NV) / 2
    return x_rows(cols).T * kappa


def y_back(rows):
    weight = np.zeros(2 * YB)
    weight[:NU] = half_weights(NU)
    weight[YB : YB + NU] = -half_weights(NU)
    return (y_lanes(rows) * weight).T / (NX * NY)


def pack(parts):
    rows, where, at = [], {}, 0
    pieces = []
    for name, a in parts:
        if a.shape[1] <= 256:
            pieces.append((name, a))
            continue
        cuts = range(0, a.shape[1], 256)
        where[name] = len(cuts)
        pieces += [(f"{name}.{i}", a[:, c : c + 256]) for i, c in enumerate(cuts)]
    for name, a in pieces:
        height = -(-a.shape[0] // 16) * 16
        block = np.zeros((height, 256), np.float64)
        block[: a.shape[0], : a.shape[1]] = a
        rows.append(block)
        where[name] = (at, a.shape[0], a.shape[1])
        at += height
    return np.concatenate(rows), where


def pack_split(parts):
    both = []
    for name, a in parts:
        hi, lo = np_split(a)
        if name in ("x2", "x3", "x4"):
            hi, lo = hi.astype(np.float64), lo.astype(np.float64)
            both.append((name, np.concatenate([hi, lo, hi], axis=1)))
            continue
        both += [(name + "_hi", hi.astype(np.float64)), (name + "_lo", lo.astype(np.float64))]
    return both


@functools.lru_cache(None)
def tables():
    core_rows = np.arange(HALO, HALO + CORE)
    field_cols = np.arange(ROW0, ROW0 + ROWS)
    own_cols = np.arange(WIDE, WIDE + CORE)
    sides = np.zeros((2 * XB, 256))
    sides[:, :WIDE] = x_rows(np.arange(WIDE))
    sides[:, CORE : CORE + WIDE] = x_rows(np.arange(WIDE + CORE, NX))
    parts = [("cx_own", x_rows(own_cols)), ("cx_side", sides)]
    for t in range(2):
        pos = np.arange(2 * CORE) - t * CORE + HALO
        inside = (pos >= 0) & (pos < NY)
        parts.append((f"by{t}", y_lanes(pos) * inside[:, None]))
    parts += [("x2", x_back(field_cols)), ("x3", x_rows(field_cols)), ("x4", x_back(own_cols))]
    y2_hi, y2_lo = (a.astype(np.float64) for a in np_split(y_back(core_rows)))
    y3_hi, y3_lo = (a.astype(np.float64) for a in np_split(y_lanes(core_rows)))
    grad = pack_split(parts)
    grad += [("y2", np.concatenate([y2_hi, y2_lo], axis=1))]
    grad += [("y3", np.concatenate([y3_hi, y3_hi, y3_lo]))]
    own = np.zeros((ROWS, CORE))
    own[np.arange(CORE) + WIDE - ROW0, np.arange(CORE)] = 1
    halo = np.zeros((ROWS, 256))
    for r in range(HALO):
        halo[HALO + r - ROW0, WIDE + r] = 1
        halo[WIDE + CORE + r - ROW0, CORE + WIDE + r] = 1
    grad += [("sel_own", own), ("sel_halo", halo)]
    offs = np.arange(KSIZE) - HALO
    kx = np.zeros((2 * XB, 128))
    kx[:, :KSIZE] = x_rows(offs)
    spec = [("kx", kx)]
    for m in range(4):
        ky = np.zeros((128, 2 * YB))
        ky[32 * m : 32 * m + KSIZE] = y_lanes(offs)
        spec.append((f"ky{m}", ky))
    return {"grad": pack(grad), "spec": pack(pack_split(spec))}


def split(x):
    hi = x.astype(bf16)
    return hi, (x - hi.astype(f32)).astype(bf16)


def dot(a, b):
    return lax.dot_general(a, b, (((1,), (0,)), ((), ())), preferred_element_type=f32)


def dot_nt(a, b):
    return lax.dot_general(a, b, (((1,), (1,)), ((), ())), preferred_element_type=f32)


def dot3(a_hi, a_lo, b_hi, b_lo, mul=dot):
    return mul(a_hi, b_hi) + (mul(a_lo, b_hi) + mul(a_hi, b_lo))


def signed(spec):
    cc, cs = spec[:XB, :YB], spec[:XB, YB:]
    sc, ss = spec[XB:, :YB], spec[XB:, YB:]
    return cc - ss, -(cs + sc), cc + ss, sc - cs


def even_odd(pr, pi, mr, mi):
    top = jnp.concatenate([pr + mr, pi + mi], axis=1)
    low = jnp.concatenate([mi - pi, pr - mr], axis=1)
    return jnp.concatenate([top, low], axis=0)


def table_array(group):
    return jnp.asarray(tables()[group][0].astype(ml_dtypes.bfloat16))


def table_reader(group, ref):
    where = tables()[group][1]

    def table(name, half=None):
        if isinstance(where[name], int):
            return jnp.concatenate([table(f"{name}.{i}") for i in range(where[name])], axis=1)
        at, height, width = where[name]
        lanes = slice(0, width) if half is None else slice(128 * half, 128 * half + 128)
        return ref[at : at + height, lanes]

    return table


def call(body, group, args, out_shape, scratch=(), smem=(), flops=0, nbytes=0):
    vm = pl.BlockSpec(memory_space=pltpu.VMEM)
    sm = pl.BlockSpec(memory_space=pltpu.SMEM)
    n_in = len(args)
    if group is not None:
        args = [*args, table_array(group)]

    def wrapped(*refs):
        if group is not None:
            refs = [*refs[:n_in], table_reader(group, refs[n_in]), *refs[n_in + 1 :]]
        body(*refs)

    return pl.pallas_call(
        wrapped,
        out_shape=out_shape,
        in_specs=[sm if i in smem else vm for i in range(len(args))],
        out_specs=[vm] * len(out_shape),
        scratch_shapes=list(scratch),
        compiler_params=pltpu.CompilerParams(vmem_limit_bytes=VMEM_LIMIT),
        cost_estimate=pl.CostEstimate(flops=flops, bytes_accessed=nbytes, transcendentals=0),
    )(*args)


def is_even():
    return lax.rem(lax.axis_index("tile"), 2) == 0


def send_edges(right, left, a_ref, b_ref):
    even = is_even()
    a_ref[...] = jnp.where(even, right, left)
    b_ref[...] = jnp.where(even, left, right)


def picker(rows, first, count, col):
    row = lax.broadcasted_iota(jnp.int32, (rows, CORE), 0)
    lane = lax.broadcasted_iota(jnp.int32, (rows, CORE), 1)
    hit = (row - first == lane - col) & (row >= first) & (row < first + count)
    return jnp.where(hit, 1.0, 0.0).astype(bf16)


def edges_of(rows, strip, extra=None):
    hi, lo = split(strip)
    both = []
    for col, more in ((CORE - WIDE, CORE - HALO), (0, 0)):
        pick = picker(rows, 0, WIDE, col)
        edge = dot_nt(pick, hi) + dot_nt(pick, lo)
        if extra is not None:
            edge = edge + dot_nt(picker(rows, WIDE, HALO, more), extra)
        both.append(edge)
    return both


def edges_kernel(mask_ref, target_ref, a_ref, b_ref):
    target = target_ref[...].astype(f32).astype(bf16)
    send_edges(*edges_of(EDGE, mask_ref[...], target), a_ref, b_ref)


def spectra_kernel(kern, w_ref, ker_ref, tb, h_ref, hs_ref):
    hs_ref[...] = jnp.zeros_like(hs_ref)
    for k in range(kern):
        for part in range(2):
            row = 32 * (2 * k + part)
            hs_ref[row : row + KSIZE, :KSIZE] = ker_ref[part, k, :, 0, :]
    s_hi, s_lo = split(hs_ref[...])
    z = dot3(tb("kx_hi"), tb("kx_lo"), s_hi, s_lo, dot_nt)
    z_hi, z_lo = split(z)
    for c in range(2 * kern):
        lanes = slice(128 * (c // 4), 128 * (c // 4) + 128)
        spec = dot3(z_hi[:, lanes], z_lo[:, lanes], tb(f"ky{c % 4}_hi"), tb(f"ky{c % 4}_lo"))
        root = jnp.sqrt(jnp.full((1, YB), w_ref[0, c // 2], f32))
        for j, comp in enumerate(signed(spec)):
            h_ref[c, j] = root * comp


def sides(from_a, from_b, tb):
    even = is_even()
    l_hi, l_lo = split(jnp.where(even, from_b, from_a))
    r_hi, r_lo = split(jnp.where(even, from_a, from_b))
    height = l_hi.shape[0]
    v = None
    for half, hi, lo in ((0, l_hi, l_lo), (1, r_hi, r_lo)):
        c_hi, c_lo = tb("cx_side_hi", half), tb("cx_side_lo", half)
        term = dot3(c_hi[:, :height], c_lo[:, :height], hi, lo)
        v = term if v is None else v + term
    return v, l_hi, r_hi


def to_spectrum(v, tb, f_ref, base):
    v_hi, v_lo = split(v)
    for t in range(2):
        spec = dot3(v_hi, v_lo, tb(f"by{t}_hi"), tb(f"by{t}_lo"))
        for j, comp in enumerate(signed(spec)):
            f_ref[t, j] = comp if base is None else base[t, j] - STEP_RATE * comp


def gradient_body(kern, last, f_ref, tgt_ref, h_ref, thr_ref, tb, g_ref, work):
    fld, inten, tot, a_hi, a_lo, b_cat, r_cat, w_cat = work
    group = 2 if kern % 2 == 0 else 1
    count = kern // group
    chains = [(t, c) for t in range(2) for c in range(count)]
    lag = count + 2

    def at(i):
        return chains[i] if 0 <= i < len(chains) else None

    tile = lax.axis_index("tile")
    first = jnp.where(tile == 0, WIDE, HALO) - ROW0
    end = jnp.where(tile == last, WIDE + CORE, WIDE + CORE + HALO) - ROW0
    row = lax.broadcasted_iota(jnp.int32, (ROWS, CORE), 0)
    inside = (row >= first) & (row < end)
    lane = lax.broadcasted_iota(jnp.int32, (1, 2 * YB), 1)
    bin_at = lax.rem(lane, YB)
    weight = jnp.where((bin_at == 0) | (bin_at == NU - 1), 1.0, 2.0) / (NX * NY)
    weight = jnp.where(lane < YB, weight, -weight)

    def chunks(height):
        return [slice(r, r + CHUNK) for r in range(0, height, CHUNK)]

    def put(ref, slot, starts, pieces):
        for at_row, piece in zip(starts, pieces):
            ref[slot, at_row : at_row + CHUNK] = piece

    def products(t, c, slot):
        for part in range(2 * group):
            for rows in chunks(XB):
                hpr, hpi, hmr, hmi = (h_ref[2 * group * c + part, j, rows] for j in range(4))
                fpr, fpi, fmr, fmi = (f_ref[t, j, rows] for j in range(4))
                pr, pi = hpr * fpr - hpi * fpi, hpr * fpi + hpi * fpr
                mr, mi = hmr * fmr - hmi * fmi, hmr * fmi + hmi * fmr
                starts = [2 * XB * part + rows.start, 2 * XB * part + XB + rows.start]
                top = split(jnp.concatenate([pr + mr, pi + mi], axis=1))
                low = split(jnp.concatenate([mi - pi, pr - mr], axis=1))
                put(a_hi, slot, starts, (top[0], low[0]))
                put(a_lo, slot, starts, (top[1], low[1]))

    def y_done(z_one, z_two, slot):
        for g in range(group):
            for rows in chunks(2 * XB):
                z = []
                for part in range(2 * g, 2 * g + 2):
                    here = slice(2 * XB * part + rows.start, 2 * XB * part + rows.stop)
                    z.append(z_one[here, :CORE] + (z_one[here, CORE:] + z_two[here]))
                z_hi, z_lo = split(jnp.concatenate(z, axis=1))
                starts = [2 * XB * j + rows.start for j in range(3)]
                put(b_cat, 2 * g + slot, starts, (z_hi, z_hi, z_lo))

    def field_of(t, c, slot):
        for g in range(group):
            k = group * c + g
            whole = dot(tb("x2"), b_cat[2 * g + slot])
            for rows in chunks(ROWS):
                field = whole[rows]
                fld[t, k, rows] = field
                re, im = field[:, :CORE], field[:, CORE:]
                power = re * re + im * im
                inten[t, rows] = power if k == 0 else inten[t, rows] + power

    def slope_of(t):
        resist = jax.nn.sigmoid(STEEPNESS * (inten[t] - thr_ref[0]))
        target = tgt_ref[:, CORE * t : CORE * t + CORE]
        slope = 2.0 * (resist - target) * STEEPNESS * resist * (1.0 - resist)
        inten[t] = jnp.where(inside, 2.0 * slope, 0.0)

    def scaled_field(t, c, slot):
        for g in range(group):
            for rows in chunks(ROWS):
                slope, field = inten[t, rows], fld[t, group * c + g, rows]
                r_hi, r_lo = split(
                    jnp.concatenate([slope * field[:, :CORE], slope * field[:, CORE:]], axis=1)
                )
                starts = [ROWS * j + rows.start for j in range(3)]
                put(r_cat, 2 * g + slot, starts, (r_hi, r_hi, r_lo))

    def x_back_done(w_now, g, slot):
        for rows in chunks(2 * XB):
            w_hi, w_lo = split(w_now[rows])
            for part in range(2):
                base = 2 * XB * (2 * g + part)
                here = slice(base + rows.start, base + rows.stop)
                lanes = slice(CORE * part, CORE * part + CORE)
                for j, piece in enumerate((w_hi, w_lo, w_hi)):
                    w_cat[slot, here, CORE * j : CORE * j + CORE] = piece[:, lanes]

    def add_back(t, c, slot):
        specs = dot(w_cat[slot], tb("y3"))
        for rows in chunks(XB):
            acc = [0.0] * 4 if c == 0 else [tot[t, j, rows] for j in range(4)]
            for part in range(2 * group):
                base = 2 * XB * part + rows.start
                cos_rows, sin_rows = slice(base, base + CHUNK), slice(base + XB, base + XB + CHUNK)
                cc, cs = specs[cos_rows, :YB], specs[cos_rows, YB:]
                sc, ss = specs[sin_rows, :YB], specs[sin_rows, YB:]
                bpr, neg, bmr, bmi = cc - ss, cs + sc, cc + ss, sc - cs
                hpr, hpi, hmr, hmi = (h_ref[2 * group * c + part, j, rows] for j in range(4))
                acc[0] = acc[0] + (hpr * bpr - hpi * neg)
                acc[1] = acc[1] - (hpr * neg + hpi * bpr)
                acc[2] = acc[2] + (hmr * bmr + hmi * bmi)
                acc[3] = acc[3] + (hmr * bmi - hmi * bmr)
            for j in range(4):
                tot[t, j, rows] = acc[j]

    def finish(t):
        r_hi, r_lo = split(even_odd(*(tot[t, j] for j in range(4))))
        u = dot(tb("x4"), jnp.concatenate([r_hi, r_hi, r_lo], axis=0))
        u_hi, u_lo = split(weight * u)
        term = dot3(tb(f"by{t}_hi"), tb(f"by{t}_lo"), u_hi, u_lo, dot_nt)
        g_ref[...] = term if t == 0 else g_ref[...] + term

    for i in range(len(chains) + lag + 2):
        new, mid, old = at(i), at(i - 1), at(i - 2)
        back, back_mid, back_old = at(i - lag), at(i - lag - 1), at(i - lag - 2)
        slot, other = i % 2, (i + 1) % 2
        if mid:
            z_one = dot(a_hi[other], tb("y2"))
            z_two = dot(a_lo[other], tb("y2", 0))
        if new:
            products(*new, slot)
        if back_mid:
            w_now = [dot(tb("x3"), r_cat[2 * g + other]) for g in range(group)]
        if back:
            scaled_field(*back, slot)
        if old:
            field_of(*old, slot)
        if back_old:
            add_back(*back_old, slot)
        if mid:
            y_done(z_one, z_two, other)
        if back_mid:
            for g in range(group):
                x_back_done(w_now[g], g, other)
        if old and old[1] == count - 1:
            slope_of(old[0])
        if back_old and back_old[1] == count - 1:
            finish(back_old[0])


def first_kernel(
    kern, last, thr_ref, mask_ref, target_ref, a_ref, b_ref, h_ref, tb,
    g_ref, f_ref, tgt_ref, *work,
):
    m_hi, m_lo = split(mask_ref[...])
    v, left, right = sides(a_ref[...], b_ref[...], tb)
    v = v + dot3(tb("cx_own_hi"), tb("cx_own_lo"), m_hi, m_lo, dot_nt)
    to_spectrum(v, tb, f_ref, None)
    tgt_ref[...] = (
        dot_nt(tb("sel_own"), target_ref[...].astype(f32).astype(bf16))
        + dot(tb("sel_halo", 0)[:, :EDGE], left)
        + dot(tb("sel_halo", 1)[:, :EDGE], right)
    )
    gradient_body(kern, last, f_ref, tgt_ref, h_ref, thr_ref, tb, g_ref, work)


def later_kernel(
    kern, last, thr_ref, mine_ref, peer_ref, a_ref, a2_ref, b_ref, b2_ref, f_in_ref, tgt_ref,
    h_ref, tb, g_ref, f_ref, *work,
):
    s_hi, s_lo = split(mine_ref[...] + peer_ref[...])
    from_a = a_ref[...] + a2_ref[...]
    from_b = b_ref[...] + b2_ref[...]
    v, _, _ = sides(from_a, from_b, tb)
    v = v + dot3(tb("cx_own_hi"), tb("cx_own_lo"), s_hi, s_lo, dot_nt)
    to_spectrum(v, tb, f_ref, f_in_ref)
    gradient_body(kern, last, f_ref, tgt_ref, h_ref, thr_ref, tb, g_ref, work)


def match_kernel(n_got, table_ref, own_ref, *refs):
    got_refs, (out_ref, *edge_refs) = refs[:n_got], refs[n_got:]
    device = lax.axis_index("tile")
    other = []
    for t in range(2):
        rows = slice(CORE * t, CORE * t + CORE)
        bit = lax.bitwise_xor(table_ref[t], 2 * device + t)
        value = jnp.where(bit == 1, own_ref[CORE * (1 - t) : CORE * (2 - t)], own_ref[rows])
        for b, got in enumerate(got_refs):
            value = jnp.where(bit == 2 << b, got[rows], value)
        other.append(value)
    row = lax.broadcasted_iota(jnp.int32, (CORE, CORE), 0)
    lane = lax.broadcasted_iota(jnp.int32, (CORE, CORE), 1)
    flip = jnp.where(row + lane == CORE - 1, 1.0, 0.0).astype(bf16)
    hi, lo = split(jnp.concatenate(other, axis=0))
    turned = dot(hi, flip) + dot(lo, flip)
    tiles = []
    for t in range(2):
        rows = slice(CORE * t, CORE * t + CORE)
        value = jnp.where(table_ref[2 + t] == 1, turned[rows], other[t])
        tiles.append(0.5 * (own_ref[rows] + value))
    matched = jnp.concatenate(tiles, axis=0)
    out_ref[...] = matched
    if edge_refs:
        send_edges(*edges_of(WIDE_PAD, matched), *edge_refs)


def final_kernel(n_moves, mask_ref, *refs):
    moves, (mask_out, grad_out) = refs[: 2 * n_moves], refs[2 * n_moves :]
    for t in range(2):
        rows = slice(CORE * t, CORE * t + CORE)
        now = mask_ref[t]
        for mine, peer in zip(moves[::2], moves[1::2]):
            step = mine[rows] + peer[rows]
            now = now - STEP_RATE * step
        grad_out[t] = step
        mask_out[t] = now


def per_device(
    n_tile, n_depth, mask_tiles, target_tiles, kernels, socs_weights, thresholds,
    partner_table, mirror_flags,
):
    tiles_dev, core, _ = mask_tiles.shape
    kern = kernels.shape[2]
    assert tiles_dev == 2 and core == CORE
    pairs_a = [(i, i ^ 1) for i in range(n_tile)]
    pairs_b = [p for i in range(1, n_tile - 1, 2) for p in ((i, i + 1), (i + 1, i))]

    def swap_edges(send_a, send_b, cross=False):
        def move(x, pairs):
            if not cross:
                return lax.ppermute(x, "tile", pairs)
            both = [(2 * i + p, 2 * j + 1 - p) for i, j in pairs for p in range(2)]
            return lax.ppermute(x, ("tile", "depth"), both)

        return move(send_b, pairs_b), move(send_a, pairs_a)

    def depth_pair(x):
        bit = 1
        while True:
            peer = lax.ppermute(x, "depth", [(i, i ^ bit) for i in range(n_depth)])
            bit *= 2
            if bit >= n_depth:
                return x, peer
            x = x + peer

    def from_partners(grad):
        bits = [1 << b for b in range(n_tile.bit_length() - 1)]
        got = [
            lax.ppermute(grad, "tile", [(i, i ^ bit) for i in range(n_tile)])
            for bit in reversed(bits)
        ]
        return got[::-1]

    mask_rows = mask_tiles.reshape(tiles_dev * core, core)
    target_rows = target_tiles.reshape(tiles_dev * core, core)
    strip = jax.ShapeDtypeStruct((tiles_dev * core, core), f32)
    side = jax.ShapeDtypeStruct((WIDE_PAD, tiles_dev * core), f32)
    freq = jax.ShapeDtypeStruct((2, 4, XB, YB), f32)
    goal = jax.ShapeDtypeStruct((ROWS, 2 * CORE), f32)
    tiles = jax.ShapeDtypeStruct((tiles_dev, core, core), f32)
    group = 2 if kern % 2 == 0 else 1
    scratch = [
        pltpu.VMEM((2, kern, ROWS, 2 * CORE), f32),
        pltpu.VMEM((2, ROWS, CORE), f32),
        pltpu.VMEM((2, 4, XB, YB), f32),
        pltpu.VMEM((2, group * 4 * XB, 2 * YB), bf16),
        pltpu.VMEM((2, group * 4 * XB, 2 * YB), bf16),
        pltpu.VMEM((2 * group, 6 * XB, 2 * CORE), bf16),
        pltpu.VMEM((2 * group, 3 * ROWS, 2 * CORE), bf16),
        pltpu.VMEM((2, group * 4 * XB, 3 * CORE), bf16),
    ]

    edge = jax.ShapeDtypeStruct((EDGE, tiles_dev * core), f32)
    send_a, send_b = call(
        edges_kernel, None, [mask_rows, target_rows], [edge, edge], flops=3 * 10**9
    )
    from_b, from_a = swap_edges(send_a, send_b)
    table = jnp.concatenate([partner_table, mirror_flags])
    (spectra,) = call(
        functools.partial(spectra_kernel, kern),
        "spec",
        [socs_weights, kernels.transpose(0, 2, 3, 1, 4)],
        [jax.ShapeDtypeStruct((2 * kern, 4, XB, YB), f32)],
        [pltpu.VMEM((32 * 2 * kern, 128), f32)],
        smem=(0,),
        flops=3 * 10**9,
        nbytes=4 * 10**6,
    )
    grad, freq_now, goals = call(
        functools.partial(first_kernel, kern, n_tile - 1),
        "grad",
        [thresholds, mask_rows, target_rows, from_a, from_b, spectra],
        [strip, freq, goal],
        scratch,
        smem=(0,),
        flops=10**10,
    )
    moves = []
    for step in range(1, STEPS + 1):
        got = from_partners(grad)
        outs = call(
            functools.partial(match_kernel, len(got)),
            None,
            [table, grad, *got],
            [strip, side, side] if step < STEPS else [strip],
            smem=(0,),
        )
        if step == STEPS:
            moves += depth_pair(outs[0])
            break
        if n_depth == 2:
            from_b, from_a = swap_edges(*outs[1:])
            far_b, far_a = swap_edges(*outs[1:], cross=True)
            rims = (from_a, far_a, from_b, far_b)
        else:
            from_b, from_a = swap_edges(*outs[1:])
            rims = depth_pair(from_a) + depth_pair(from_b)
        moves += depth_pair(outs[0])
        kept = step + 1 < STEPS
        grad, *rest = call(
            functools.partial(later_kernel, kern, n_tile - 1),
            "grad",
            [thresholds, *moves[-2:], *rims, freq_now, goals, spectra],
            [strip, freq] if kept else [strip],
            scratch if kept else [pltpu.VMEM(freq.shape, f32)] + scratch,
            smem=(0,),
            flops=10**10,
        )
        freq_now = rest[0] if kept else None
    final = functools.partial(final_kernel, STEPS)
    return tuple(call(final, None, [mask_tiles, *moves], [tiles, tiles]))


def solution(mesh):
    return jax.shard_map(
        functools.partial(per_device, mesh.shape["tile"], mesh.shape["depth"]),
        mesh=mesh,
        in_specs=(
            P("tile", None, None),
            P("tile", None, None),
            P(None, "depth", None, None, None),
            P("depth", None),
            P("depth"),
            P("tile"),
            P("tile"),
        ),
        out_specs=(P("tile", None, None), P("tile", None, None)),
        check_vma=False,
    )
```

```python
import functools

import jax
import jax.numpy as jnp
import ml_dtypes
import numpy as np
from jax import lax
from jax.experimental import pallas as pl
from jax.experimental.pallas import tpu as pltpu
from jax.sharding import PartitionSpec as P

HALO = 12
KSIZE = 25
STEPS = 2
STEEPNESS = 3.0
STEP_RATE = 0.05

CORE = 128
NY = 152
NX = 176
WIDE = 2 * HALO
XB = 96
YB = 128
NU = NY // 2 + 1
NV = NX // 2 + 1
ROWS = 160
ROW0 = 8
CHUNK = 16
EDGE = 48
WIDE_PAD = 32
VMEM_LIMIT = 24 * 1024 * 1024

f32 = jnp.float32
bf16 = jnp.bfloat16


def np_split(a):
    hi = np.asarray(a, np.float32).astype(ml_dtypes.bfloat16)
    lo = (np.asarray(a, np.float64) - hi.astype(np.float64)).astype(ml_dtypes.bfloat16)
    return hi, lo


def x_rows(cols):
    out = np.zeros((2 * XB, len(cols)))
    ang = 2 * np.pi * np.outer(np.arange(NV), cols) / NX
    out[:NV] = np.cos(ang)
    out[XB : XB + NV] = np.sin(ang)
    out[XB] = 0.0
    out[XB + NV - 1] = 0.0
    return out


def y_lanes(rows):
    out = np.zeros((len(rows), 2 * YB))
    ang = 2 * np.pi * np.outer(rows, np.arange(NU)) / NY
    out[:, :NU] = np.cos(ang)
    out[:, YB : YB + NU] = np.sin(ang)
    out[:, YB] = 0.0
    out[:, YB + NU - 1] = 0.0
    return out


def half_weights(bins):
    weights = np.full(bins, 2.0)
    weights[0] = weights[-1] = 1.0
    return weights


def x_back(cols):
    kappa = np.zeros(2 * XB)
    kappa[:NV] = half_weights(NV) / 2
    kappa[XB : XB + NV] = half_weights(NV) / 2
    return x_rows(cols).T * kappa


def y_back(rows):
    weight = np.zeros(2 * YB)
    weight[:NU] = half_weights(NU)
    weight[YB : YB + NU] = -half_weights(NU)
    return (y_lanes(rows) * weight).T / (NX * NY)


def pack(parts):
    rows, where, at = [], {}, 0
    pieces = []
    for name, a in parts:
        if a.shape[1] <= 256:
            pieces.append((name, a))
            continue
        cuts = range(0, a.shape[1], 256)
        where[name] = len(cuts)
        pieces += [(f"{name}.{i}", a[:, c : c + 256]) for i, c in enumerate(cuts)]
    for name, a in pieces:
        height = -(-a.shape[0] // 16) * 16
        block = np.zeros((height, 256), np.float64)
        block[: a.shape[0], : a.shape[1]] = a
        rows.append(block)
        where[name] = (at, a.shape[0], a.shape[1])
        at += height
    return np.concatenate(rows), where


def pack_split(parts):
    both = []
    for name, a in parts:
        hi, lo = np_split(a)
        if name in ("x2", "x3", "x4"):
            hi, lo = hi.astype(np.float64), lo.astype(np.float64)
            both.append((name, np.concatenate([hi, lo, hi], axis=1)))
            continue
        both += [(name + "_hi", hi.astype(np.float64)), (name + "_lo", lo.astype(np.float64))]
    return both


@functools.lru_cache(None)
def tables():
    core_rows = np.arange(HALO, HALO + CORE)
    field_cols = np.arange(ROW0, ROW0 + ROWS)
    own_cols = np.arange(WIDE, WIDE + CORE)
    sides = np.zeros((2 * XB, 256))
    sides[:, :WIDE] = x_rows(np.arange(WIDE))
    sides[:, CORE : CORE + WIDE] = x_rows(np.arange(WIDE + CORE, NX))
    parts = [("cx_own", x_rows(own_cols)), ("cx_side", sides)]
    for t in range(2):
        pos = np.arange(2 * CORE) - t * CORE + HALO
        inside = (pos >= 0) & (pos < NY)
        parts.append((f"by{t}", y_lanes(pos) * inside[:, None]))
    parts += [("x2", x_back(field_cols)), ("x3", x_rows(field_cols)), ("x4", x_back(own_cols))]
    y2_hi, y2_lo = (a.astype(np.float64) for a in np_split(y_back(core_rows)))
    y3_hi, y3_lo = (a.astype(np.float64) for a in np_split(y_lanes(core_rows)))
    grad = pack_split(parts)
    grad += [("y2", np.concatenate([y2_hi, y2_lo], axis=1))]
    grad += [("y3", np.concatenate([y3_hi, y3_hi, y3_lo]))]
    own = np.zeros((ROWS, CORE))
    own[np.arange(CORE) + WIDE - ROW0, np.arange(CORE)] = 1
    halo = np.zeros((ROWS, 256))
    for r in range(HALO):
        halo[HALO + r - ROW0, WIDE + r] = 1
        halo[WIDE + CORE + r - ROW0, CORE + WIDE + r] = 1
    grad += [("sel_own", own), ("sel_halo", halo)]
    offs = np.arange(KSIZE) - HALO
    kx = np.zeros((2 * XB, 128))
    kx[:, :KSIZE] = x_rows(offs)
    spec = [("kx", kx)]
    for m in range(4):
        ky = np.zeros((128, 2 * YB))
        ky[32 * m : 32 * m + KSIZE] = y_lanes(offs)
        spec.append((f"ky{m}", ky))
    return {"grad": pack(grad), "spec": pack(pack_split(spec))}


def split(x):
    hi = x.astype(bf16)
    return hi, (x - hi.astype(f32)).astype(bf16)


def dot(a, b):
    return lax.dot_general(a, b, (((1,), (0,)), ((), ())), preferred_element_type=f32)


def dot_nt(a, b):
    return lax.dot_general(a, b, (((1,), (1,)), ((), ())), preferred_element_type=f32)


def dot3(a_hi, a_lo, b_hi, b_lo, mul=dot):
    return mul(a_hi, b_hi) + (mul(a_lo, b_hi) + mul(a_hi, b_lo))


def signed(spec):
    cc, cs = spec[:XB, :YB], spec[:XB, YB:]
    sc, ss = spec[XB:, :YB], spec[XB:, YB:]
    return cc - ss, -(cs + sc), cc + ss, sc - cs


def even_odd(pr, pi, mr, mi):
    top = jnp.concatenate([pr + mr, pi + mi], axis=1)
    low = jnp.concatenate([mi - pi, pr - mr], axis=1)
    return jnp.concatenate([top, low], axis=0)


def table_array(group):
    return jnp.asarray(tables()[group][0].astype(ml_dtypes.bfloat16))


def table_reader(group, ref):
    where = tables()[group][1]

    def table(name, half=None):
        if isinstance(where[name], int):
            return jnp.concatenate([table(f"{name}.{i}") for i in range(where[name])], axis=1)
        at, height, width = where[name]
        lanes = slice(0, width) if half is None else slice(128 * half, 128 * half + 128)
        return ref[at : at + height, lanes]

    return table


def call(body, group, args, out_shape, scratch=(), smem=(), flops=0, nbytes=0):
    vm = pl.BlockSpec(memory_space=pltpu.VMEM)
    sm = pl.BlockSpec(memory_space=pltpu.SMEM)
    n_in = len(args)
    if group is not None:
        args = [*args, table_array(group)]

    def wrapped(*refs):
        if group is not None:
            refs = [*refs[:n_in], table_reader(group, refs[n_in]), *refs[n_in + 1 :]]
        body(*refs)

    return pl.pallas_call(
        wrapped,
        out_shape=out_shape,
        in_specs=[sm if i in smem else vm for i in range(len(args))],
        out_specs=[vm] * len(out_shape),
        scratch_shapes=list(scratch),
        compiler_params=pltpu.CompilerParams(vmem_limit_bytes=VMEM_LIMIT),
        cost_estimate=pl.CostEstimate(flops=flops, bytes_accessed=nbytes, transcendentals=0),
    )(*args)


def is_even():
    return lax.rem(lax.axis_index("tile"), 2) == 0


def send_edges(right, left, a_ref, b_ref):
    even = is_even()
    a_ref[...] = jnp.where(even, right, left)
    b_ref[...] = jnp.where(even, left, right)


def picker(rows, first, count, col):
    row = lax.broadcasted_iota(jnp.int32, (rows, CORE), 0)
    lane = lax.broadcasted_iota(jnp.int32, (rows, CORE), 1)
    hit = (row - first == lane - col) & (row >= first) & (row < first + count)
    return jnp.where(hit, 1.0, 0.0).astype(bf16)


def edges_of(rows, strip, extra=None):
    hi, lo = split(strip)
    both = []
    for col, more in ((CORE - WIDE, CORE - HALO), (0, 0)):
        pick = picker(rows, 0, WIDE, col)
        edge = dot_nt(pick, hi) + dot_nt(pick, lo)
        if extra is not None:
            edge = edge + dot_nt(picker(rows, WIDE, HALO, more), extra)
        both.append(edge)
    return both


def edges_kernel(mask_ref, target_ref, a_ref, b_ref):
    target = target_ref[...].astype(f32).astype(bf16)
    send_edges(*edges_of(EDGE, mask_ref[...], target), a_ref, b_ref)


def spectra_kernel(kern, w_ref, ker_ref, tb, h_ref, hs_ref):
    hs_ref[...] = jnp.zeros_like(hs_ref)
    for k in range(kern):
        for part in range(2):
            row = 32 * (2 * k + part)
            hs_ref[row : row + KSIZE, :KSIZE] = ker_ref[part, k, :, 0, :]
    s_hi, s_lo = split(hs_ref[...])
    z = dot3(tb("kx_hi"), tb("kx_lo"), s_hi, s_lo, dot_nt)
    z_hi, z_lo = split(z)
    for c in range(2 * kern):
        lanes = slice(128 * (c // 4), 128 * (c // 4) + 128)
        spec = dot3(z_hi[:, lanes], z_lo[:, lanes], tb(f"ky{c % 4}_hi"), tb(f"ky{c % 4}_lo"))
        root = jnp.sqrt(jnp.full((1, YB), w_ref[0, c // 2], f32))
        for j, comp in enumerate(signed(spec)):
            h_ref[c, j] = root * comp


def sides(last, from_a, from_b, tb):
    even = is_even()
    tile = lax.axis_index("tile")
    from_b = jnp.where((tile == 0) | (tile == last), 0.0, from_b)
    l_hi, l_lo = split(jnp.where(even, from_b, from_a))
    r_hi, r_lo = split(jnp.where(even, from_a, from_b))
    height = l_hi.shape[0]
    v = None
    for half, hi, lo in ((0, l_hi, l_lo), (1, r_hi, r_lo)):
        c_hi, c_lo = tb("cx_side_hi", half), tb("cx_side_lo", half)
        term = dot3(c_hi[:, :height], c_lo[:, :height], hi, lo)
        v = term if v is None else v + term
    return v, l_hi, r_hi


def to_spectrum(v, tb, f_ref, base):
    v_hi, v_lo = split(v)
    for t in range(2):
        spec = dot3(v_hi, v_lo, tb(f"by{t}_hi"), tb(f"by{t}_lo"))
        for j, comp in enumerate(signed(spec)):
            f_ref[t, j] = comp if base is None else base[t, j] - STEP_RATE * comp


def gradient_body(kern, last, f_ref, tgt_ref, h_ref, thr_ref, tb, g_ref, work):
    fld, inten, tot, a_hi, a_lo, b_cat, r_cat, w_cat = work
    group = 2 if kern % 2 == 0 else 1
    count = kern // group
    chains = [(t, c) for t in range(2) for c in range(count)]
    lag = count + 2

    def at(i):
        return chains[i] if 0 <= i < len(chains) else None

    tile = lax.axis_index("tile")
    first = jnp.where(tile == 0, WIDE, HALO) - ROW0
    end = jnp.where(tile == last, WIDE + CORE, WIDE + CORE + HALO) - ROW0
    row = lax.broadcasted_iota(jnp.int32, (ROWS, CORE), 0)
    inside = (row >= first) & (row < end)
    lane = lax.broadcasted_iota(jnp.int32, (1, 2 * YB), 1)
    bin_at = lax.rem(lane, YB)
    weight = jnp.where((bin_at == 0) | (bin_at == NU - 1), 1.0, 2.0) / (NX * NY)
    weight = jnp.where(lane < YB, weight, -weight)

    def chunks(height):
        return [slice(r, r + CHUNK) for r in range(0, height, CHUNK)]

    def put(ref, slot, starts, pieces):
        for at_row, piece in zip(starts, pieces):
            ref[slot, at_row : at_row + CHUNK] = piece

    def products(t, c, slot):
        for part in range(2 * group):
            for rows in chunks(XB):
                hpr, hpi, hmr, hmi = (h_ref[2 * group * c + part, j, rows] for j in range(4))
                fpr, fpi, fmr, fmi = (f_ref[t, j, rows] for j in range(4))
                pr, pi = hpr * fpr - hpi * fpi, hpr * fpi + hpi * fpr
                mr, mi = hmr * fmr - hmi * fmi, hmr * fmi + hmi * fmr
                starts = [2 * XB * part + rows.start, 2 * XB * part + XB + rows.start]
                top = split(jnp.concatenate([pr + mr, pi + mi], axis=1))
                low = split(jnp.concatenate([mi - pi, pr - mr], axis=1))
                put(a_hi, slot, starts, (top[0], low[0]))
                put(a_lo, slot, starts, (top[1], low[1]))

    def y_done(z_one, z_two, slot):
        for g in range(group):
            for rows in chunks(2 * XB):
                z = []
                for part in range(2 * g, 2 * g + 2):
                    here = slice(2 * XB * part + rows.start, 2 * XB * part + rows.stop)
                    z.append(z_one[here, :CORE] + (z_one[here, CORE:] + z_two[here]))
                z_hi, z_lo = split(jnp.concatenate(z, axis=1))
                starts = [2 * XB * j + rows.start for j in range(3)]
                put(b_cat, 2 * g + slot, starts, (z_hi, z_hi, z_lo))

    def field_of(t, c, slot):
        for g in range(group):
            k = group * c + g
            whole = dot(tb("x2"), b_cat[2 * g + slot])
            for rows in chunks(ROWS):
                field = whole[rows]
                fld[t, k, rows] = field
                re, im = field[:, :CORE], field[:, CORE:]
                power = re * re + im * im
                inten[t, rows] = power if k == 0 else inten[t, rows] + power

    def slope_of(t):
        resist = jax.nn.sigmoid(STEEPNESS * (inten[t] - thr_ref[0]))
        target = tgt_ref[:, CORE * t : CORE * t + CORE]
        slope = 2.0 * (resist - target) * STEEPNESS * resist * (1.0 - resist)
        inten[t] = jnp.where(inside, 2.0 * slope, 0.0)

    def scaled_field(t, c, slot):
        for g in range(group):
            for rows in chunks(ROWS):
                slope, field = inten[t, rows], fld[t, group * c + g, rows]
                r_hi, r_lo = split(
                    jnp.concatenate([slope * field[:, :CORE], slope * field[:, CORE:]], axis=1)
                )
                starts = [ROWS * j + rows.start for j in range(3)]
                put(r_cat, 2 * g + slot, starts, (r_hi, r_hi, r_lo))

    def x_back_done(w_now, g, slot):
        for rows in chunks(2 * XB):
            w_hi, w_lo = split(w_now[rows])
            for part in range(2):
                base = 2 * XB * (2 * g + part)
                here = slice(base + rows.start, base + rows.stop)
                lanes = slice(CORE * part, CORE * part + CORE)
                for j, piece in enumerate((w_hi, w_lo, w_hi)):
                    w_cat[slot, here, CORE * j : CORE * j + CORE] = piece[:, lanes]

    def add_back(t, c, slot):
        specs = dot(w_cat[slot], tb("y3"))
        for rows in chunks(XB):
            acc = [0.0] * 4 if c == 0 else [tot[t, j, rows] for j in range(4)]
            for part in range(2 * group):
                base = 2 * XB * part + rows.start
                cos_rows, sin_rows = slice(base, base + CHUNK), slice(base + XB, base + XB + CHUNK)
                cc, cs = specs[cos_rows, :YB], specs[cos_rows, YB:]
                sc, ss = specs[sin_rows, :YB], specs[sin_rows, YB:]
                bpr, neg, bmr, bmi = cc - ss, cs + sc, cc + ss, sc - cs
                hpr, hpi, hmr, hmi = (h_ref[2 * group * c + part, j, rows] for j in range(4))
                acc[0] = acc[0] + (hpr * bpr - hpi * neg)
                acc[1] = acc[1] - (hpr * neg + hpi * bpr)
                acc[2] = acc[2] + (hmr * bmr + hmi * bmi)
                acc[3] = acc[3] + (hmr * bmi - hmi * bmr)
            for j in range(4):
                tot[t, j, rows] = acc[j]

    def finish(t):
        r_hi, r_lo = split(even_odd(*(tot[t, j] for j in range(4))))
        u = dot(tb("x4"), jnp.concatenate([r_hi, r_hi, r_lo], axis=0))
        u_hi, u_lo = split(weight * u)
        term = dot3(tb(f"by{t}_hi"), tb(f"by{t}_lo"), u_hi, u_lo, dot_nt)
        g_ref[...] = term if t == 0 else g_ref[...] + term

    for i in range(len(chains) + lag + 2):
        new, mid, old = at(i), at(i - 1), at(i - 2)
        back, back_mid, back_old = at(i - lag), at(i - lag - 1), at(i - lag - 2)
        slot, other = i % 2, (i + 1) % 2
        if mid:
            z_one = dot(a_hi[other], tb("y2"))
            z_two = dot(a_lo[other], tb("y2", 0))
        if new:
            products(*new, slot)
        if back_mid:
            w_now = [dot(tb("x3"), r_cat[2 * g + other]) for g in range(group)]
        if back:
            scaled_field(*back, slot)
        if old:
            field_of(*old, slot)
        if back_old:
            add_back(*back_old, slot)
        if mid:
            y_done(z_one, z_two, other)
        if back_mid:
            for g in range(group):
                x_back_done(w_now[g], g, other)
        if old and old[1] == count - 1:
            slope_of(old[0])
        if back_old and back_old[1] == count - 1:
            finish(back_old[0])


def first_kernel(
    kern, last, thr_ref, mask_ref, target_ref, a_ref, b_ref, h_ref, tb,
    g_ref, f_ref, tgt_ref, *work,
):
    m_hi, m_lo = split(mask_ref[...])
    v, left, right = sides(last, a_ref[...], b_ref[...], tb)
    v = v + dot3(tb("cx_own_hi"), tb("cx_own_lo"), m_hi, m_lo, dot_nt)
    to_spectrum(v, tb, f_ref, None)
    tgt_ref[...] = (
        dot_nt(tb("sel_own"), target_ref[...].astype(f32).astype(bf16))
        + dot(tb("sel_halo", 0)[:, :EDGE], left)
        + dot(tb("sel_halo", 1)[:, :EDGE], right)
    )
    gradient_body(kern, last, f_ref, tgt_ref, h_ref, thr_ref, tb, g_ref, work)


def later_kernel(
    kern, last, thr_ref, mine_ref, peer_ref, a_ref, a2_ref, b_ref, b2_ref, f_in_ref, tgt_ref,
    h_ref, tb, g_ref, f_ref, *work,
):
    s_hi, s_lo = split(mine_ref[...] + peer_ref[...])
    from_a = a_ref[...] + a2_ref[...]
    from_b = b_ref[...] + b2_ref[...]
    v, _, _ = sides(last, from_a, from_b, tb)
    v = v + dot3(tb("cx_own_hi"), tb("cx_own_lo"), s_hi, s_lo, dot_nt)
    to_spectrum(v, tb, f_ref, f_in_ref)
    gradient_body(kern, last, f_ref, tgt_ref, h_ref, thr_ref, tb, g_ref, work)


def match_kernel(n_got, table_ref, own_ref, *refs):
    got_refs, (out_ref, *edge_refs) = refs[:n_got], refs[n_got:]
    device = lax.axis_index("tile")
    other = []
    for t in range(2):
        rows = slice(CORE * t, CORE * t + CORE)
        bit = lax.bitwise_xor(table_ref[t], 2 * device + t)
        value = jnp.where(bit == 1, own_ref[CORE * (1 - t) : CORE * (2 - t)], own_ref[rows])
        for b, got in enumerate(got_refs):
            value = jnp.where(bit == 2 << b, got[rows], value)
        other.append(value)
    row = lax.broadcasted_iota(jnp.int32, (CORE, CORE), 0)
    lane = lax.broadcasted_iota(jnp.int32, (CORE, CORE), 1)
    flip = jnp.where(row + lane == CORE - 1, 1.0, 0.0).astype(bf16)
    hi, lo = split(jnp.concatenate(other, axis=0))
    turned = dot(hi, flip) + dot(lo, flip)
    tiles = []
    for t in range(2):
        rows = slice(CORE * t, CORE * t + CORE)
        value = jnp.where(table_ref[2 + t] == 1, turned[rows], other[t])
        tiles.append(0.5 * (own_ref[rows] + value))
    matched = jnp.concatenate(tiles, axis=0)
    out_ref[...] = matched
    if edge_refs:
        send_edges(*edges_of(WIDE_PAD, matched), *edge_refs)


def final_kernel(n_moves, mask_ref, *refs):
    moves, (mask_out, grad_out) = refs[: 2 * n_moves], refs[2 * n_moves :]
    for t in range(2):
        rows = slice(CORE * t, CORE * t + CORE)
        now = mask_ref[t]
        for mine, peer in zip(moves[::2], moves[1::2]):
            step = mine[rows] + peer[rows]
            now = now - STEP_RATE * step
        grad_out[t] = step
        mask_out[t] = now


def per_device(
    n_tile, n_depth, mask_tiles, target_tiles, kernels, socs_weights, thresholds,
    partner_table, mirror_flags,
):
    tiles_dev, core, _ = mask_tiles.shape
    kern = kernels.shape[2]
    assert tiles_dev == 2 and core == CORE
    pairs_a = [(i, i ^ 1) for i in range(n_tile)]
    pairs_b = [p for i in range(1, n_tile - 1, 2) for p in ((i, i + 1), (i + 1, i))]
    pairs_b += [(0, 0), (n_tile - 1, n_tile - 1)]

    def swap_edges(send_a, send_b, cross=False):
        def move(x, pairs):
            if not cross:
                return lax.ppermute(x, "tile", pairs)
            both = [(2 * i + p, 2 * j + 1 - p) for i, j in pairs for p in range(2)]
            return lax.ppermute(x, ("tile", "depth"), both)

        return move(send_b, pairs_b), move(send_a, pairs_a)

    def depth_pair(x):
        bit = 1
        while True:
            peer = lax.ppermute(x, "depth", [(i, i ^ bit) for i in range(n_depth)])
            bit *= 2
            if bit >= n_depth:
                return x, peer
            x = x + peer

    def from_partners(grad):
        bits = [1 << b for b in range(n_tile.bit_length() - 1)]
        got = [
            lax.ppermute(grad, "tile", [(i, i ^ bit) for i in range(n_tile)])
            for bit in reversed(bits)
        ]
        return got[::-1]

    mask_rows = mask_tiles.reshape(tiles_dev * core, core)
    target_rows = target_tiles.reshape(tiles_dev * core, core)
    strip = jax.ShapeDtypeStruct((tiles_dev * core, core), f32)
    side = jax.ShapeDtypeStruct((WIDE_PAD, tiles_dev * core), f32)
    freq = jax.ShapeDtypeStruct((2, 4, XB, YB), f32)
    goal = jax.ShapeDtypeStruct((ROWS, 2 * CORE), f32)
    tiles = jax.ShapeDtypeStruct((tiles_dev, core, core), f32)
    group = 2 if kern % 2 == 0 else 1
    scratch = [
        pltpu.VMEM((2, kern, ROWS, 2 * CORE), f32),
        pltpu.VMEM((2, ROWS, CORE), f32),
        pltpu.VMEM((2, 4, XB, YB), f32),
        pltpu.VMEM((2, group * 4 * XB, 2 * YB), bf16),
        pltpu.VMEM((2, group * 4 * XB, 2 * YB), bf16),
        pltpu.VMEM((2 * group, 6 * XB, 2 * CORE), bf16),
        pltpu.VMEM((2 * group, 3 * ROWS, 2 * CORE), bf16),
        pltpu.VMEM((2, group * 4 * XB, 3 * CORE), bf16),
    ]

    edge = jax.ShapeDtypeStruct((EDGE, tiles_dev * core), f32)
    send_a, send_b = call(
        edges_kernel, None, [mask_rows, target_rows], [edge, edge], flops=3 * 10**9
    )
    from_b, from_a = swap_edges(send_a, send_b)
    table = jnp.concatenate([partner_table, mirror_flags])
    (spectra,) = call(
        functools.partial(spectra_kernel, kern),
        "spec",
        [socs_weights, kernels.transpose(0, 2, 3, 1, 4)],
        [jax.ShapeDtypeStruct((2 * kern, 4, XB, YB), f32)],
        [pltpu.VMEM((32 * 2 * kern, 128), f32)],
        smem=(0,),
        flops=3 * 10**9,
        nbytes=4 * 10**6,
    )
    grad, freq_now, goals = call(
        functools.partial(first_kernel, kern, n_tile - 1),
        "grad",
        [thresholds, mask_rows, target_rows, from_a, from_b, spectra],
        [strip, freq, goal],
        scratch,
        smem=(0,),
        flops=10**10,
    )
    moves = []
    for step in range(1, STEPS + 1):
        got = from_partners(grad)
        outs = call(
            functools.partial(match_kernel, len(got)),
            None,
            [table, grad, *got],
            [strip, side, side] if step < STEPS else [strip],
            smem=(0,),
        )
        if step == STEPS:
            moves += depth_pair(outs[0])
            break
        if n_depth == 2:
            from_b, from_a = swap_edges(*outs[1:])
            far_b, far_a = swap_edges(*outs[1:], cross=True)
            rims = (from_a, far_a, from_b, far_b)
        else:
            from_b, from_a = swap_edges(*outs[1:])
            rims = depth_pair(from_a) + depth_pair(from_b)
        moves += depth_pair(outs[0])
        kept = step + 1 < STEPS
        grad, *rest = call(
            functools.partial(later_kernel, kern, n_tile - 1),
            "grad",
            [thresholds, *moves[-2:], *rims, freq_now, goals, spectra],
            [strip, freq] if kept else [strip],
            scratch if kept else [pltpu.VMEM(freq.shape, f32)] + scratch,
            smem=(0,),
            flops=10**10,
        )
        freq_now = rest[0] if kept else None
    final = functools.partial(final_kernel, STEPS)
    return tuple(call(final, None, [mask_tiles, *moves], [tiles, tiles]))


def solution(mesh):
    return jax.shard_map(
        functools.partial(per_device, mesh.shape["tile"], mesh.shape["depth"]),
        mesh=mesh,
        in_specs=(
            P("tile", None, None),
            P("tile", None, None),
            P(None, "depth", None, None, None),
            P("depth", None),
            P("depth"),
            P("tile"),
            P("tile"),
        ),
        out_specs=(P("tile", None, None), P("tile", None, None)),
        check_vma=False,
    )
```

```python
import functools

import jax
import jax.numpy as jnp
import ml_dtypes
import numpy as np
from jax import lax
from jax.experimental import pallas as pl
from jax.experimental.pallas import tpu as pltpu
from jax.sharding import PartitionSpec as P

HALO = 12
KSIZE = 25
STEPS = 2
STEEPNESS = 3.0
STEP_RATE = 0.05

CORE = 128
NY = 152
NX = 176
WIDE = 2 * HALO
XB = 96
YB = 128
NU = NY // 2 + 1
NV = NX // 2 + 1
ROWS = 160
ROW0 = 8
CHUNK = 16
EDGE = 48
WIDE_PAD = 32
VMEM_LIMIT = 24 * 1024 * 1024

f32 = jnp.float32
bf16 = jnp.bfloat16


def np_split(a):
    hi = np.asarray(a, np.float32).astype(ml_dtypes.bfloat16)
    lo = (np.asarray(a, np.float64) - hi.astype(np.float64)).astype(ml_dtypes.bfloat16)
    return hi, lo


def x_rows(cols):
    out = np.zeros((2 * XB, len(cols)))
    ang = 2 * np.pi * np.outer(np.arange(NV), cols) / NX
    out[:NV] = np.cos(ang)
    out[XB : XB + NV] = np.sin(ang)
    out[XB] = 0.0
    out[XB + NV - 1] = 0.0
    return out


def y_lanes(rows):
    out = np.zeros((len(rows), 2 * YB))
    ang = 2 * np.pi * np.outer(rows, np.arange(NU)) / NY
    out[:, :NU] = np.cos(ang)
    out[:, YB : YB + NU] = np.sin(ang)
    out[:, YB] = 0.0
    out[:, YB + NU - 1] = 0.0
    return out


def half_weights(bins):
    weights = np.full(bins, 2.0)
    weights[0] = weights[-1] = 1.0
    return weights


def x_back(cols):
    kappa = np.zeros(2 * XB)
    kappa[:NV] = half_weights(NV) / 2
    kappa[XB : XB + NV] = half_weights(NV) / 2
    return x_rows(cols).T * kappa


def y_back(rows):
    weight = np.zeros(2 * YB)
    weight[:NU] = half_weights(NU)
    weight[YB : YB + NU] = -half_weights(NU)
    return (y_lanes(rows) * weight).T / (NX * NY)


def pack(parts):
    rows, where, at = [], {}, 0
    pieces = []
    for name, a in parts:
        if a.shape[1] <= 256:
            pieces.append((name, a))
            continue
        cuts = range(0, a.shape[1], 256)
        where[name] = len(cuts)
        pieces += [(f"{name}.{i}", a[:, c : c + 256]) for i, c in enumerate(cuts)]
    for name, a in pieces:
        height = -(-a.shape[0] // 16) * 16
        block = np.zeros((height, 256), np.float64)
        block[: a.shape[0], : a.shape[1]] = a
        rows.append(block)
        where[name] = (at, a.shape[0], a.shape[1])
        at += height
    return np.concatenate(rows), where


def pack_split(parts):
    both = []
    for name, a in parts:
        hi, lo = np_split(a)
        if name in ("x2", "x3", "x4"):
            hi, lo = hi.astype(np.float64), lo.astype(np.float64)
            both.append((name, np.concatenate([hi, lo, hi], axis=1)))
            continue
        both += [(name + "_hi", hi.astype(np.float64)), (name + "_lo", lo.astype(np.float64))]
    return both


@functools.lru_cache(None)
def tables():
    core_rows = np.arange(HALO, HALO + CORE)
    field_cols = np.arange(ROW0, ROW0 + ROWS)
    own_cols = np.arange(WIDE, WIDE + CORE)
    sides = np.zeros((2 * XB, 256))
    sides[:, :WIDE] = x_rows(np.arange(WIDE))
    sides[:, CORE : CORE + WIDE] = x_rows(np.arange(WIDE + CORE, NX))
    parts = [("cx_own", x_rows(own_cols)), ("cx_side", sides)]
    for t in range(2):
        pos = np.arange(2 * CORE) - t * CORE + HALO
        inside = (pos >= 0) & (pos < NY)
        parts.append((f"by{t}", y_lanes(pos) * inside[:, None]))
    parts += [("x2", x_back(field_cols)), ("x3", x_rows(field_cols)), ("x4", x_back(own_cols))]
    y2_hi, y2_lo = (a.astype(np.float64) for a in np_split(y_back(core_rows)))
    y3_hi, y3_lo = (a.astype(np.float64) for a in np_split(y_lanes(core_rows)))
    grad = pack_split(parts)
    grad += [("y2", np.concatenate([y2_hi, y2_lo], axis=1))]
    grad += [("y3", np.concatenate([y3_hi, y3_hi, y3_lo]))]
    own = np.zeros((ROWS, CORE))
    own[np.arange(CORE) + WIDE - ROW0, np.arange(CORE)] = 1
    halo = np.zeros((ROWS, 256))
    for r in range(HALO):
        halo[HALO + r - ROW0, WIDE + r] = 1
        halo[WIDE + CORE + r - ROW0, CORE + WIDE + r] = 1
    grad += [("sel_own", own), ("sel_halo", halo)]
    offs = np.arange(KSIZE) - HALO
    kx = np.zeros((2 * XB, 128))
    kx[:, :KSIZE] = x_rows(offs)
    spec = [("kx", kx)]
    for m in range(4):
        ky = np.zeros((128, 2 * YB))
        ky[32 * m : 32 * m + KSIZE] = y_lanes(offs)
        spec.append((f"ky{m}", ky))
    return {"grad": pack(grad), "spec": pack(pack_split(spec))}


def split(x):
    hi = x.astype(bf16)
    return hi, (x - hi.astype(f32)).astype(bf16)


def dot(a, b):
    return lax.dot_general(a, b, (((1,), (0,)), ((), ())), preferred_element_type=f32)


def dot_nt(a, b):
    return lax.dot_general(a, b, (((1,), (1,)), ((), ())), preferred_element_type=f32)


def dot3(a_hi, a_lo, b_hi, b_lo, mul=dot):
    return mul(a_hi, b_hi) + (mul(a_lo, b_hi) + mul(a_hi, b_lo))


def signed(spec):
    cc, cs = spec[:XB, :YB], spec[:XB, YB:]
    sc, ss = spec[XB:, :YB], spec[XB:, YB:]
    return cc - ss, -(cs + sc), cc + ss, sc - cs


def even_odd(pr, pi, mr, mi):
    top = jnp.concatenate([pr + mr, pi + mi], axis=1)
    low = jnp.concatenate([mi - pi, pr - mr], axis=1)
    return jnp.concatenate([top, low], axis=0)


def table_array(group):
    return jnp.asarray(tables()[group][0].astype(ml_dtypes.bfloat16))


def table_reader(group, ref):
    where = tables()[group][1]

    def table(name, half=None):
        if isinstance(where[name], int):
            return jnp.concatenate([table(f"{name}.{i}") for i in range(where[name])], axis=1)
        at, height, width = where[name]
        lanes = slice(0, width) if half is None else slice(128 * half, 128 * half + 128)
        return ref[at : at + height, lanes]

    return table


def call(body, group, args, out_shape, scratch=(), smem=(), flops=0, nbytes=0):
    vm = pl.BlockSpec(memory_space=pltpu.VMEM)
    sm = pl.BlockSpec(memory_space=pltpu.SMEM)
    n_in = len(args)
    if group is not None:
        args = [*args, table_array(group)]

    def wrapped(*refs):
        if group is not None:
            refs = [*refs[:n_in], table_reader(group, refs[n_in]), *refs[n_in + 1 :]]
        body(*refs)

    return pl.pallas_call(
        wrapped,
        out_shape=out_shape,
        in_specs=[sm if i in smem else vm for i in range(len(args))],
        out_specs=[vm] * len(out_shape),
        scratch_shapes=list(scratch),
        compiler_params=pltpu.CompilerParams(vmem_limit_bytes=VMEM_LIMIT),
        cost_estimate=pl.CostEstimate(flops=flops, bytes_accessed=nbytes, transcendentals=0),
    )(*args)


def is_even():
    return lax.rem(lax.axis_index("tile"), 2) == 0


def send_edges(right, left, a_ref, b_ref):
    even = is_even()
    a_ref[...] = jnp.where(even, right, left)
    b_ref[...] = jnp.where(even, left, right)


def picker(rows, first, count, col):
    row = lax.broadcasted_iota(jnp.int32, (rows, CORE), 0)
    lane = lax.broadcasted_iota(jnp.int32, (rows, CORE), 1)
    hit = (row - first == lane - col) & (row >= first) & (row < first + count)
    return jnp.where(hit, 1.0, 0.0).astype(bf16)


def edges_of(rows, strip, extra=None):
    hi, lo = split(strip)
    both = []
    for col, more in ((CORE - WIDE, CORE - HALO), (0, 0)):
        pick = picker(rows, 0, WIDE, col)
        edge = dot_nt(pick, hi) + dot_nt(pick, lo)
        if extra is not None:
            edge = edge + dot_nt(picker(rows, WIDE, HALO, more), extra)
        both.append(edge)
    return both


def edges_kernel(mask_ref, target_ref, a_ref, b_ref):
    target = target_ref[...].astype(f32).astype(bf16)
    send_edges(*edges_of(EDGE, mask_ref[...], target), a_ref, b_ref)


def spectra_kernel(kern, w_ref, ker_ref, tb, h_ref, hs_ref):
    hs_ref[...] = jnp.zeros_like(hs_ref)
    for k in range(kern):
        for part in range(2):
            row = 32 * (2 * k + part)
            hs_ref[row : row + KSIZE, :KSIZE] = ker_ref[part, k, :, 0, :]
    s_hi, s_lo = split(hs_ref[...])
    z = dot3(tb("kx_hi"), tb("kx_lo"), s_hi, s_lo, dot_nt)
    z_hi, z_lo = split(z)
    for c in range(2 * kern):
        lanes = slice(128 * (c // 4), 128 * (c // 4) + 128)
        spec = dot3(z_hi[:, lanes], z_lo[:, lanes], tb(f"ky{c % 4}_hi"), tb(f"ky{c % 4}_lo"))
        root = jnp.sqrt(jnp.full((1, YB), w_ref[0, c // 2], f32))
        for j, comp in enumerate(signed(spec)):
            h_ref[c, j] = root * comp


def sides(masks, near, tb):
    even = is_even()
    tile = lax.axis_index("tile")
    differ = lax.bitwise_xor(tile, jnp.where(even, tile - 1, tile + 1))
    from_a, from_b = near[0], jnp.zeros_like(near[0])
    for mask, got in zip(masks, near[1:]):
        from_b = jnp.where(differ == mask, got, from_b)
    l_hi, l_lo = split(jnp.where(even, from_b, from_a))
    r_hi, r_lo = split(jnp.where(even, from_a, from_b))
    height = l_hi.shape[0]
    v = None
    for half, hi, lo in ((0, l_hi, l_lo), (1, r_hi, r_lo)):
        c_hi, c_lo = tb("cx_side_hi", half), tb("cx_side_lo", half)
        term = dot3(c_hi[:, :height], c_lo[:, :height], hi, lo)
        v = term if v is None else v + term
    return v, l_hi, r_hi


def to_spectrum(v, tb, f_ref, base):
    v_hi, v_lo = split(v)
    for t in range(2):
        spec = dot3(v_hi, v_lo, tb(f"by{t}_hi"), tb(f"by{t}_lo"))
        for j, comp in enumerate(signed(spec)):
            f_ref[t, j] = comp if base is None else base[t, j] - STEP_RATE * comp


def gradient_body(kern, last, f_ref, tgt_ref, h_ref, thr_ref, tb, g_ref, work):
    fld, inten, tot, a_hi, a_lo, b_cat, r_cat, w_cat = work
    group = 2 if kern % 2 == 0 else 1
    count = kern // group
    chains = [(t, c) for t in range(2) for c in range(count)]
    lag = count + 2

    def at(i):
        return chains[i] if 0 <= i < len(chains) else None

    tile = lax.axis_index("tile")
    first = jnp.where(tile == 0, WIDE, HALO) - ROW0
    end = jnp.where(tile == last, WIDE + CORE, WIDE + CORE + HALO) - ROW0
    row = lax.broadcasted_iota(jnp.int32, (ROWS, CORE), 0)
    inside = (row >= first) & (row < end)
    lane = lax.broadcasted_iota(jnp.int32, (1, 2 * YB), 1)
    bin_at = lax.rem(lane, YB)
    weight = jnp.where((bin_at == 0) | (bin_at == NU - 1), 1.0, 2.0) / (NX * NY)
    weight = jnp.where(lane < YB, weight, -weight)

    def chunks(height):
        return [slice(r, r + CHUNK) for r in range(0, height, CHUNK)]

    def put(ref, slot, starts, pieces):
        for at_row, piece in zip(starts, pieces):
            ref[slot, at_row : at_row + CHUNK] = piece

    def products(t, c, slot):
        for part in range(2 * group):
            for rows in chunks(XB):
                hpr, hpi, hmr, hmi = (h_ref[2 * group * c + part, j, rows] for j in range(4))
                fpr, fpi, fmr, fmi = (f_ref[t, j, rows] for j in range(4))
                pr, pi = hpr * fpr - hpi * fpi, hpr * fpi + hpi * fpr
                mr, mi = hmr * fmr - hmi * fmi, hmr * fmi + hmi * fmr
                starts = [2 * XB * part + rows.start, 2 * XB * part + XB + rows.start]
                top = split(jnp.concatenate([pr + mr, pi + mi], axis=1))
                low = split(jnp.concatenate([mi - pi, pr - mr], axis=1))
                put(a_hi, slot, starts, (top[0], low[0]))
                put(a_lo, slot, starts, (top[1], low[1]))

    def y_done(z_one, z_two, slot):
        for g in range(group):
            for rows in chunks(2 * XB):
                z = []
                for part in range(2 * g, 2 * g + 2):
                    here = slice(2 * XB * part + rows.start, 2 * XB * part + rows.stop)
                    z.append(z_one[here, :CORE] + (z_one[here, CORE:] + z_two[here]))
                z_hi, z_lo = split(jnp.concatenate(z, axis=1))
                starts = [2 * XB * j + rows.start for j in range(3)]
                put(b_cat, 2 * g + slot, starts, (z_hi, z_hi, z_lo))

    def field_of(t, c, slot):
        for g in range(group):
            k = group * c + g
            whole = dot(tb("x2"), b_cat[2 * g + slot])
            for rows in chunks(ROWS):
                field = whole[rows]
                fld[t, k, rows] = field
                re, im = field[:, :CORE], field[:, CORE:]
                power = re * re + im * im
                inten[t, rows] = power if k == 0 else inten[t, rows] + power

    def slope_of(t):
        resist = jax.nn.sigmoid(STEEPNESS * (inten[t] - thr_ref[0]))
        target = tgt_ref[:, CORE * t : CORE * t + CORE]
        slope = 2.0 * (resist - target) * STEEPNESS * resist * (1.0 - resist)
        inten[t] = jnp.where(inside, 2.0 * slope, 0.0)

    def scaled_field(t, c, slot):
        for g in range(group):
            for rows in chunks(ROWS):
                slope, field = inten[t, rows], fld[t, group * c + g, rows]
                r_hi, r_lo = split(
                    jnp.concatenate([slope * field[:, :CORE], slope * field[:, CORE:]], axis=1)
                )
                starts = [ROWS * j + rows.start for j in range(3)]
                put(r_cat, 2 * g + slot, starts, (r_hi, r_hi, r_lo))

    def x_back_done(w_now, g, slot):
        for rows in chunks(2 * XB):
            w_hi, w_lo = split(w_now[rows])
            for part in range(2):
                base = 2 * XB * (2 * g + part)
                here = slice(base + rows.start, base + rows.stop)
                lanes = slice(CORE * part, CORE * part + CORE)
                for j, piece in enumerate((w_hi, w_lo, w_hi)):
                    w_cat[slot, here, CORE * j : CORE * j + CORE] = piece[:, lanes]

    def add_back(t, c, slot):
        specs = dot(w_cat[slot], tb("y3"))
        for rows in chunks(XB):
            acc = [0.0] * 4 if c == 0 else [tot[t, j, rows] for j in range(4)]
            for part in range(2 * group):
                base = 2 * XB * part + rows.start
                cos_rows, sin_rows = slice(base, base + CHUNK), slice(base + XB, base + XB + CHUNK)
                cc, cs = specs[cos_rows, :YB], specs[cos_rows, YB:]
                sc, ss = specs[sin_rows, :YB], specs[sin_rows, YB:]
                bpr, neg, bmr, bmi = cc - ss, cs + sc, cc + ss, sc - cs
                hpr, hpi, hmr, hmi = (h_ref[2 * group * c + part, j, rows] for j in range(4))
                acc[0] = acc[0] + (hpr * bpr - hpi * neg)
                acc[1] = acc[1] - (hpr * neg + hpi * bpr)
                acc[2] = acc[2] + (hmr * bmr + hmi * bmi)
                acc[3] = acc[3] + (hmr * bmi - hmi * bmr)
            for j in range(4):
                tot[t, j, rows] = acc[j]

    def finish(t):
        r_hi, r_lo = split(even_odd(*(tot[t, j] for j in range(4))))
        u = dot(tb("x4"), jnp.concatenate([r_hi, r_hi, r_lo], axis=0))
        u_hi, u_lo = split(weight * u)
        term = dot3(tb(f"by{t}_hi"), tb(f"by{t}_lo"), u_hi, u_lo, dot_nt)
        g_ref[...] = term if t == 0 else g_ref[...] + term

    for i in range(len(chains) + lag + 2):
        new, mid, old = at(i), at(i - 1), at(i - 2)
        back, back_mid, back_old = at(i - lag), at(i - lag - 1), at(i - lag - 2)
        slot, other = i % 2, (i + 1) % 2
        if mid:
            z_one = dot(a_hi[other], tb("y2"))
            z_two = dot(a_lo[other], tb("y2", 0))
        if new:
            products(*new, slot)
        if back_mid:
            w_now = [dot(tb("x3"), r_cat[2 * g + other]) for g in range(group)]
        if back:
            scaled_field(*back, slot)
        if old:
            field_of(*old, slot)
        if back_old:
            add_back(*back_old, slot)
        if mid:
            y_done(z_one, z_two, other)
        if back_mid:
            for g in range(group):
                x_back_done(w_now[g], g, other)
        if old and old[1] == count - 1:
            slope_of(old[0])
        if back_old and back_old[1] == count - 1:
            finish(back_old[0])


def first_kernel(kern, last, masks, thr_ref, mask_ref, target_ref, *refs):
    near, refs = refs[: 1 + len(masks)], refs[1 + len(masks) :]
    h_ref, tb, g_ref, f_ref, tgt_ref, *work = refs
    m_hi, m_lo = split(mask_ref[...])
    v, left, right = sides(masks, [x[...] for x in near], tb)
    v = v + dot3(tb("cx_own_hi"), tb("cx_own_lo"), m_hi, m_lo, dot_nt)
    to_spectrum(v, tb, f_ref, None)
    tgt_ref[...] = (
        dot_nt(tb("sel_own"), target_ref[...].astype(f32).astype(bf16))
        + dot(tb("sel_halo", 0)[:, :EDGE], left)
        + dot(tb("sel_halo", 1)[:, :EDGE], right)
    )
    gradient_body(kern, last, f_ref, tgt_ref, h_ref, thr_ref, tb, g_ref, work)


def later_kernel(kern, last, masks, thr_ref, mine_ref, peer_ref, *refs):
    count = 1 + len(masks)
    near, far, refs = refs[:count], refs[count : 2 * count], refs[2 * count :]
    f_in_ref, tgt_ref, h_ref, tb, g_ref, f_ref, *work = refs
    s_hi, s_lo = split(mine_ref[...] + peer_ref[...])
    v, _, _ = sides(masks, [x[...] + y[...] for x, y in zip(near, far)], tb)
    v = v + dot3(tb("cx_own_hi"), tb("cx_own_lo"), s_hi, s_lo, dot_nt)
    to_spectrum(v, tb, f_ref, f_in_ref)
    gradient_body(kern, last, f_ref, tgt_ref, h_ref, thr_ref, tb, g_ref, work)


def match_kernel(n_got, table_ref, own_ref, *refs):
    got_refs, (out_ref, *edge_refs) = refs[:n_got], refs[n_got:]
    device = lax.axis_index("tile")
    other = []
    for t in range(2):
        rows = slice(CORE * t, CORE * t + CORE)
        bit = lax.bitwise_xor(table_ref[t], 2 * device + t)
        value = jnp.where(bit == 1, own_ref[CORE * (1 - t) : CORE * (2 - t)], own_ref[rows])
        for b, got in enumerate(got_refs):
            value = jnp.where(bit == 2 << b, got[rows], value)
        other.append(value)
    row = lax.broadcasted_iota(jnp.int32, (CORE, CORE), 0)
    lane = lax.broadcasted_iota(jnp.int32, (CORE, CORE), 1)
    flip = jnp.where(row + lane == CORE - 1, 1.0, 0.0).astype(bf16)
    hi, lo = split(jnp.concatenate(other, axis=0))
    turned = dot(hi, flip) + dot(lo, flip)
    tiles = []
    for t in range(2):
        rows = slice(CORE * t, CORE * t + CORE)
        value = jnp.where(table_ref[2 + t] == 1, turned[rows], other[t])
        tiles.append(0.5 * (own_ref[rows] + value))
    matched = jnp.concatenate(tiles, axis=0)
    out_ref[...] = matched
    if edge_refs:
        send_edges(*edges_of(WIDE_PAD, matched), *edge_refs)


def final_kernel(n_moves, mask_ref, *refs):
    moves, (mask_out, grad_out) = refs[: 2 * n_moves], refs[2 * n_moves :]
    for t in range(2):
        rows = slice(CORE * t, CORE * t + CORE)
        now = mask_ref[t]
        for mine, peer in zip(moves[::2], moves[1::2]):
            step = mine[rows] + peer[rows]
            now = now - STEP_RATE * step
        grad_out[t] = step
        mask_out[t] = now


def per_device(
    n_tile, n_depth, mask_tiles, target_tiles, kernels, socs_weights, thresholds,
    partner_table, mirror_flags,
):
    tiles_dev, core, _ = mask_tiles.shape
    kern = kernels.shape[2]
    assert tiles_dev == 2 and core == CORE
    bits = [1 << b for b in range(n_tile.bit_length() - 1)]
    masks = [2 * bit - 1 for bit in bits[1:]]

    def swap_edges(send_a, send_b, cross=False):
        def move(x, mask):
            if not cross:
                return lax.ppermute(x, "tile", [(i, i ^ mask) for i in range(n_tile)])
            both = [(2 * i + p, 2 * (i ^ mask) + 1 - p) for i in range(n_tile) for p in range(2)]
            return lax.ppermute(x, ("tile", "depth"), both)

        return [move(send_a, 1)] + [move(send_b, mask) for mask in masks]

    def depth_pair(x):
        bit = 1
        while True:
            peer = lax.ppermute(x, "depth", [(i, i ^ bit) for i in range(n_depth)])
            bit *= 2
            if bit >= n_depth:
                return x, peer
            x = x + peer

    def from_partners(grad):
        got = [
            lax.ppermute(grad, "tile", [(i, i ^ bit) for i in range(n_tile)])
            for bit in reversed(bits)
        ]
        return got[::-1]

    mask_rows = mask_tiles.reshape(tiles_dev * core, core)
    target_rows = target_tiles.reshape(tiles_dev * core, core)
    strip = jax.ShapeDtypeStruct((tiles_dev * core, core), f32)
    side = jax.ShapeDtypeStruct((WIDE_PAD, tiles_dev * core), f32)
    freq = jax.ShapeDtypeStruct((2, 4, XB, YB), f32)
    goal = jax.ShapeDtypeStruct((ROWS, 2 * CORE), f32)
    tiles = jax.ShapeDtypeStruct((tiles_dev, core, core), f32)
    group = 2 if kern % 2 == 0 else 1
    scratch = [
        pltpu.VMEM((2, kern, ROWS, 2 * CORE), f32),
        pltpu.VMEM((2, ROWS, CORE), f32),
        pltpu.VMEM((2, 4, XB, YB), f32),
        pltpu.VMEM((2, group * 4 * XB, 2 * YB), bf16),
        pltpu.VMEM((2, group * 4 * XB, 2 * YB), bf16),
        pltpu.VMEM((2 * group, 6 * XB, 2 * CORE), bf16),
        pltpu.VMEM((2 * group, 3 * ROWS, 2 * CORE), bf16),
        pltpu.VMEM((2, group * 4 * XB, 3 * CORE), bf16),
    ]

    edge = jax.ShapeDtypeStruct((EDGE, tiles_dev * core), f32)
    send_a, send_b = call(
        edges_kernel, None, [mask_rows, target_rows], [edge, edge], flops=3 * 10**9
    )
    near = swap_edges(send_a, send_b)
    table = jnp.concatenate([partner_table, mirror_flags])
    (spectra,) = call(
        functools.partial(spectra_kernel, kern),
        "spec",
        [socs_weights, kernels.transpose(0, 2, 3, 1, 4)],
        [jax.ShapeDtypeStruct((2 * kern, 4, XB, YB), f32)],
        [pltpu.VMEM((32 * 2 * kern, 128), f32)],
        smem=(0,),
        flops=3 * 10**9,
        nbytes=4 * 10**6,
    )
    grad, freq_now, goals = call(
        functools.partial(first_kernel, kern, n_tile - 1, masks),
        "grad",
        [thresholds, mask_rows, target_rows, *near, spectra],
        [strip, freq, goal],
        scratch,
        smem=(0,),
        flops=10**10,
    )
    moves = []
    for step in range(1, STEPS + 1):
        got = from_partners(grad)
        outs = call(
            functools.partial(match_kernel, len(got)),
            None,
            [table, grad, *got],
            [strip, side, side] if step < STEPS else [strip],
            smem=(0,),
        )
        if step == STEPS:
            moves += depth_pair(outs[0])
            break
        near = swap_edges(*outs[1:])
        if n_depth == 2:
            far = swap_edges(*outs[1:], cross=True)
        else:
            near, far = zip(*(depth_pair(x) for x in near))
        moves += depth_pair(outs[0])
        kept = step + 1 < STEPS
        grad, *rest = call(
            functools.partial(later_kernel, kern, n_tile - 1, masks),
            "grad",
            [thresholds, *moves[-2:], *near, *far, freq_now, goals, spectra],
            [strip, freq] if kept else [strip],
            scratch if kept else [pltpu.VMEM(freq.shape, f32)] + scratch,
            smem=(0,),
            flops=10**10,
        )
        freq_now = rest[0] if kept else None
    final = functools.partial(final_kernel, STEPS)
    return tuple(call(final, None, [mask_tiles, *moves], [tiles, tiles]))


def solution(mesh):
    return jax.shard_map(
        functools.partial(per_device, mesh.shape["tile"], mesh.shape["depth"]),
        mesh=mesh,
        in_specs=(
            P("tile", None, None),
            P("tile", None, None),
            P(None, "depth", None, None, None),
            P("depth", None),
            P("depth"),
            P("tile"),
            P("tile"),
        ),
        out_specs=(P("tile", None, None), P("tile", None, None)),
        check_vma=False,
    )
```

```python
import functools

import jax
import jax.numpy as jnp
import ml_dtypes
import numpy as np
from jax import lax
from jax.experimental import pallas as pl
from jax.experimental.pallas import tpu as pltpu
from jax.sharding import PartitionSpec as P

HALO = 12
KSIZE = 25
STEPS = 2
STEEPNESS = 3.0
STEP_RATE = 0.05

CORE = 128
NY = 152
NX = 176
WIDE = 2 * HALO
XB = 96
YB = 128
NU = NY // 2 + 1
NV = NX // 2 + 1
ROWS = 160
ROW0 = 8
CHUNK = 16
EDGE = 48
WIDE_PAD = 32
VMEM_LIMIT = 24 * 1024 * 1024

f32 = jnp.float32
bf16 = jnp.bfloat16


def np_split(a):
    hi = np.asarray(a, np.float32).astype(ml_dtypes.bfloat16)
    lo = (np.asarray(a, np.float64) - hi.astype(np.float64)).astype(ml_dtypes.bfloat16)
    return hi, lo


def x_rows(cols):
    out = np.zeros((2 * XB, len(cols)))
    ang = 2 * np.pi * np.outer(np.arange(NV), cols) / NX
    out[:NV] = np.cos(ang)
    out[XB : XB + NV] = np.sin(ang)
    out[XB] = 0.0
    out[XB + NV - 1] = 0.0
    return out


def y_lanes(rows):
    out = np.zeros((len(rows), 2 * YB))
    ang = 2 * np.pi * np.outer(rows, np.arange(NU)) / NY
    out[:, :NU] = np.cos(ang)
    out[:, YB : YB + NU] = np.sin(ang)
    out[:, YB] = 0.0
    out[:, YB + NU - 1] = 0.0
    return out


def half_weights(bins):
    weights = np.full(bins, 2.0)
    weights[0] = weights[-1] = 1.0
    return weights


def x_back(cols):
    kappa = np.zeros(2 * XB)
    kappa[:NV] = half_weights(NV) / 2
    kappa[XB : XB + NV] = half_weights(NV) / 2
    return x_rows(cols).T * kappa


def y_back(rows):
    weight = np.zeros(2 * YB)
    weight[:NU] = half_weights(NU)
    weight[YB : YB + NU] = -half_weights(NU)
    return (y_lanes(rows) * weight).T / (NX * NY)


def pack(parts):
    rows, where, at = [], {}, 0
    pieces = []
    for name, a in parts:
        if a.shape[1] <= 256:
            pieces.append((name, a))
            continue
        cuts = range(0, a.shape[1], 256)
        where[name] = len(cuts)
        pieces += [(f"{name}.{i}", a[:, c : c + 256]) for i, c in enumerate(cuts)]
    for name, a in pieces:
        height = -(-a.shape[0] // 16) * 16
        block = np.zeros((height, 256), np.float64)
        block[: a.shape[0], : a.shape[1]] = a
        rows.append(block)
        where[name] = (at, a.shape[0], a.shape[1])
        at += height
    return np.concatenate(rows), where


def pack_split(parts):
    both = []
    for name, a in parts:
        hi, lo = np_split(a)
        if name in ("x2", "x3", "x4"):
            hi, lo = hi.astype(np.float64), lo.astype(np.float64)
            both.append((name, np.concatenate([hi, lo, hi], axis=1)))
            continue
        both += [(name + "_hi", hi.astype(np.float64)), (name + "_lo", lo.astype(np.float64))]
    return both


@functools.lru_cache(None)
def tables():
    core_rows = np.arange(HALO, HALO + CORE)
    field_cols = np.arange(ROW0, ROW0 + ROWS)
    own_cols = np.arange(WIDE, WIDE + CORE)
    sides = np.zeros((2 * XB, 256))
    sides[:, :WIDE] = x_rows(np.arange(WIDE))
    sides[:, CORE : CORE + WIDE] = x_rows(np.arange(WIDE + CORE, NX))
    parts = [("cx_own", x_rows(own_cols)), ("cx_side", sides)]
    for t in range(2):
        pos = np.arange(2 * CORE) - t * CORE + HALO
        inside = (pos >= 0) & (pos < NY)
        parts.append((f"by{t}", y_lanes(pos) * inside[:, None]))
    parts += [("x2", x_back(field_cols)), ("x3", x_rows(field_cols)), ("x4", x_back(own_cols))]
    y2_hi, y2_lo = (a.astype(np.float64) for a in np_split(y_back(core_rows)))
    y3_hi, y3_lo = (a.astype(np.float64) for a in np_split(y_lanes(core_rows)))
    grad = pack_split(parts)
    grad += [("y2", np.concatenate([y2_hi, y2_lo], axis=1))]
    grad += [("y3", np.concatenate([y3_hi, y3_hi, y3_lo]))]
    own = np.zeros((ROWS, CORE))
    own[np.arange(CORE) + WIDE - ROW0, np.arange(CORE)] = 1
    halo = np.zeros((ROWS, 256))
    for r in range(HALO):
        halo[HALO + r - ROW0, WIDE + r] = 1
        halo[WIDE + CORE + r - ROW0, CORE + WIDE + r] = 1
    grad += [("sel_own", own), ("sel_halo", halo)]
    offs = np.arange(KSIZE) - HALO
    kx = np.zeros((2 * XB, 128))
    kx[:, :KSIZE] = x_rows(offs)
    spec = [("kx", kx)]
    for m in range(4):
        ky = np.zeros((128, 2 * YB))
        ky[32 * m : 32 * m + KSIZE] = y_lanes(offs)
        spec.append((f"ky{m}", ky))
    return {"grad": pack(grad), "spec": pack(pack_split(spec))}


def split(x):
    hi = x.astype(bf16)
    return hi, (x - hi.astype(f32)).astype(bf16)


def dot(a, b):
    return lax.dot_general(a, b, (((1,), (0,)), ((), ())), preferred_element_type=f32)


def dot_nt(a, b):
    return lax.dot_general(a, b, (((1,), (1,)), ((), ())), preferred_element_type=f32)


def dot3(a_hi, a_lo, b_hi, b_lo, mul=dot):
    return mul(a_hi, b_hi) + (mul(a_lo, b_hi) + mul(a_hi, b_lo))


def signed(spec):
    cc, cs = spec[:XB, :YB], spec[:XB, YB:]
    sc, ss = spec[XB:, :YB], spec[XB:, YB:]
    return cc - ss, -(cs + sc), cc + ss, sc - cs


def even_odd(pr, pi, mr, mi):
    top = jnp.concatenate([pr + mr, pi + mi], axis=1)
    low = jnp.concatenate([mi - pi, pr - mr], axis=1)
    return jnp.concatenate([top, low], axis=0)


def table_array(group):
    return jnp.asarray(tables()[group][0].astype(ml_dtypes.bfloat16))


def table_reader(group, ref):
    where = tables()[group][1]

    def table(name, half=None):
        if isinstance(where[name], int):
            return jnp.concatenate([table(f"{name}.{i}") for i in range(where[name])], axis=1)
        at, height, width = where[name]
        lanes = slice(0, width) if half is None else slice(128 * half, 128 * half + 128)
        return ref[at : at + height, lanes]

    return table


def call(body, group, args, out_shape, scratch=(), smem=(), flops=0, nbytes=0):
    vm = pl.BlockSpec(memory_space=pltpu.VMEM)
    sm = pl.BlockSpec(memory_space=pltpu.SMEM)
    n_in = len(args)
    if group is not None:
        args = [*args, table_array(group)]

    def wrapped(*refs):
        if group is not None:
            refs = [*refs[:n_in], table_reader(group, refs[n_in]), *refs[n_in + 1 :]]
        body(*refs)

    return pl.pallas_call(
        wrapped,
        out_shape=out_shape,
        in_specs=[sm if i in smem else vm for i in range(len(args))],
        out_specs=[vm] * len(out_shape),
        scratch_shapes=list(scratch),
        compiler_params=pltpu.CompilerParams(vmem_limit_bytes=VMEM_LIMIT),
        cost_estimate=pl.CostEstimate(flops=flops, bytes_accessed=nbytes, transcendentals=0),
    )(*args)


def is_even():
    return lax.rem(lax.axis_index("tile"), 2) == 0


def send_edges(right, left, a_ref, b_ref):
    even = is_even()
    a_ref[...] = jnp.where(even, right, left)
    b_ref[...] = jnp.where(even, left, right)


def picker(rows, first, count, col):
    row = lax.broadcasted_iota(jnp.int32, (rows, CORE), 0)
    lane = lax.broadcasted_iota(jnp.int32, (rows, CORE), 1)
    hit = (row - first == lane - col) & (row >= first) & (row < first + count)
    return jnp.where(hit, 1.0, 0.0).astype(bf16)


def edges_of(rows, strip, extra=None):
    hi, lo = split(strip)
    both = []
    for col, more in ((CORE - WIDE, CORE - HALO), (0, 0)):
        pick = picker(rows, 0, WIDE, col)
        edge = dot_nt(pick, hi) + dot_nt(pick, lo)
        if extra is not None:
            edge = edge + dot_nt(picker(rows, WIDE, HALO, more), extra)
        both.append(edge)
    return both


def edges_kernel(both_ref, a_ref, b_ref):
    both = both_ref[...]
    target = jnp.where(both >= 2.0, 1.0, 0.0)
    mask = both - 2.0 * target
    send_edges(*edges_of(EDGE, mask, target.astype(bf16)), a_ref, b_ref)


def spectra_kernel(kern, w_ref, ker_ref, tb, h_ref, hs_ref):
    hs_ref[...] = jnp.zeros_like(hs_ref)
    for k in range(kern):
        for part in range(2):
            row = 32 * (2 * k + part)
            hs_ref[row : row + KSIZE, :KSIZE] = ker_ref[part, k, :, 0, :]
    s_hi, s_lo = split(hs_ref[...])
    z = dot3(tb("kx_hi"), tb("kx_lo"), s_hi, s_lo, dot_nt)
    z_hi, z_lo = split(z)
    for c in range(2 * kern):
        lanes = slice(128 * (c // 4), 128 * (c // 4) + 128)
        spec = dot3(z_hi[:, lanes], z_lo[:, lanes], tb(f"ky{c % 4}_hi"), tb(f"ky{c % 4}_lo"))
        root = jnp.sqrt(jnp.full((1, YB), w_ref[0, c // 2], f32))
        for j, comp in enumerate(signed(spec)):
            h_ref[c, j] = root * comp


def sides(last, from_a, from_b, tb):
    even = is_even()
    tile = lax.axis_index("tile")
    from_b = jnp.where((tile == 0) | (tile == last), 0.0, from_b)
    l_hi, l_lo = split(jnp.where(even, from_b, from_a))
    r_hi, r_lo = split(jnp.where(even, from_a, from_b))
    height = l_hi.shape[0]
    v = None
    for half, hi, lo in ((0, l_hi, l_lo), (1, r_hi, r_lo)):
        c_hi, c_lo = tb("cx_side_hi", half), tb("cx_side_lo", half)
        term = dot3(c_hi[:, :height], c_lo[:, :height], hi, lo)
        v = term if v is None else v + term
    return v, l_hi, r_hi


def to_spectrum(v, tb, f_ref, base):
    v_hi, v_lo = split(v)
    for t in range(2):
        spec = dot3(v_hi, v_lo, tb(f"by{t}_hi"), tb(f"by{t}_lo"))
        for j, comp in enumerate(signed(spec)):
            f_ref[t, j] = comp if base is None else base[t, j] - STEP_RATE * comp


def gradient_body(kern, last, f_ref, tgt_ref, h_ref, thr_ref, tb, g_ref, work):
    fld, inten, tot, a_hi, a_lo, b_cat, r_cat, w_cat = work
    group = 2 if kern % 2 == 0 else 1
    count = kern // group
    chains = [(t, c) for t in range(2) for c in range(count)]
    lag = count + 2

    def at(i):
        return chains[i] if 0 <= i < len(chains) else None

    tile = lax.axis_index("tile")
    first = jnp.where(tile == 0, WIDE, HALO) - ROW0
    end = jnp.where(tile == last, WIDE + CORE, WIDE + CORE + HALO) - ROW0
    row = lax.broadcasted_iota(jnp.int32, (ROWS, CORE), 0)
    inside = (row >= first) & (row < end)
    lane = lax.broadcasted_iota(jnp.int32, (1, 2 * YB), 1)
    bin_at = lax.rem(lane, YB)
    weight = jnp.where((bin_at == 0) | (bin_at == NU - 1), 1.0, 2.0) / (NX * NY)
    weight = jnp.where(lane < YB, weight, -weight)

    def chunks(height):
        return [slice(r, r + CHUNK) for r in range(0, height, CHUNK)]

    def put(ref, slot, starts, pieces):
        for at_row, piece in zip(starts, pieces):
            ref[slot, at_row : at_row + CHUNK] = piece

    def products(t, c, slot):
        for part in range(2 * group):
            for rows in chunks(XB):
                hpr, hpi, hmr, hmi = (h_ref[2 * group * c + part, j, rows] for j in range(4))
                fpr, fpi, fmr, fmi = (f_ref[t, j, rows] for j in range(4))
                pr, pi = hpr * fpr - hpi * fpi, hpr * fpi + hpi * fpr
                mr, mi = hmr * fmr - hmi * fmi, hmr * fmi + hmi * fmr
                starts = [2 * XB * part + rows.start, 2 * XB * part + XB + rows.start]
                top = split(jnp.concatenate([pr + mr, pi + mi], axis=1))
                low = split(jnp.concatenate([mi - pi, pr - mr], axis=1))
                put(a_hi, slot, starts, (top[0], low[0]))
                put(a_lo, slot, starts, (top[1], low[1]))

    def y_done(z_one, z_two, slot):
        for g in range(group):
            for rows in chunks(2 * XB):
                z = []
                for part in range(2 * g, 2 * g + 2):
                    here = slice(2 * XB * part + rows.start, 2 * XB * part + rows.stop)
                    z.append(z_one[here, :CORE] + (z_one[here, CORE:] + z_two[here]))
                z_hi, z_lo = split(jnp.concatenate(z, axis=1))
                starts = [2 * XB * j + rows.start for j in range(3)]
                put(b_cat, 2 * g + slot, starts, (z_hi, z_hi, z_lo))

    def field_of(t, c, slot):
        for g in range(group):
            k = group * c + g
            whole = dot(tb("x2"), b_cat[2 * g + slot])
            for rows in chunks(ROWS):
                field = whole[rows]
                fld[t, k, rows] = field
                re, im = field[:, :CORE], field[:, CORE:]
                power = re * re + im * im
                inten[t, rows] = power if k == 0 else inten[t, rows] + power

    def slope_of(t):
        resist = jax.nn.sigmoid(STEEPNESS * (inten[t] - thr_ref[0]))
        target = tgt_ref[:, CORE * t : CORE * t + CORE]
        slope = 2.0 * (resist - target) * STEEPNESS * resist * (1.0 - resist)
        inten[t] = jnp.where(inside, 2.0 * slope, 0.0)

    def scaled_field(t, c, slot):
        for g in range(group):
            for rows in chunks(ROWS):
                slope, field = inten[t, rows], fld[t, group * c + g, rows]
                r_hi, r_lo = split(
                    jnp.concatenate([slope * field[:, :CORE], slope * field[:, CORE:]], axis=1)
                )
                starts = [ROWS * j + rows.start for j in range(3)]
                put(r_cat, 2 * g + slot, starts, (r_hi, r_hi, r_lo))

    def x_back_done(w_now, g, slot):
        for rows in chunks(2 * XB):
            w_hi, w_lo = split(w_now[rows])
            for part in range(2):
                base = 2 * XB * (2 * g + part)
                here = slice(base + rows.start, base + rows.stop)
                lanes = slice(CORE * part, CORE * part + CORE)
                for j, piece in enumerate((w_hi, w_lo, w_hi)):
                    w_cat[slot, here, CORE * j : CORE * j + CORE] = piece[:, lanes]

    def add_back(t, c, slot):
        specs = dot(w_cat[slot], tb("y3"))
        for rows in chunks(XB):
            acc = [0.0] * 4 if c == 0 else [tot[t, j, rows] for j in range(4)]
            for part in range(2 * group):
                base = 2 * XB * part + rows.start
                cos_rows, sin_rows = slice(base, base + CHUNK), slice(base + XB, base + XB + CHUNK)
                cc, cs = specs[cos_rows, :YB], specs[cos_rows, YB:]
                sc, ss = specs[sin_rows, :YB], specs[sin_rows, YB:]
                bpr, neg, bmr, bmi = cc - ss, cs + sc, cc + ss, sc - cs
                hpr, hpi, hmr, hmi = (h_ref[2 * group * c + part, j, rows] for j in range(4))
                acc[0] = acc[0] + (hpr * bpr - hpi * neg)
                acc[1] = acc[1] - (hpr * neg + hpi * bpr)
                acc[2] = acc[2] + (hmr * bmr + hmi * bmi)
                acc[3] = acc[3] + (hmr * bmi - hmi * bmr)
            for j in range(4):
                tot[t, j, rows] = acc[j]

    def finish(t):
        r_hi, r_lo = split(even_odd(*(tot[t, j] for j in range(4))))
        u = dot(tb("x4"), jnp.concatenate([r_hi, r_hi, r_lo], axis=0))
        u_hi, u_lo = split(weight * u)
        term = dot3(tb(f"by{t}_hi"), tb(f"by{t}_lo"), u_hi, u_lo, dot_nt)
        g_ref[...] = term if t == 0 else g_ref[...] + term

    for i in range(len(chains) + lag + 2):
        new, mid, old = at(i), at(i - 1), at(i - 2)
        back, back_mid, back_old = at(i - lag), at(i - lag - 1), at(i - lag - 2)
        slot, other = i % 2, (i + 1) % 2
        if mid:
            z_one = dot(a_hi[other], tb("y2"))
            z_two = dot(a_lo[other], tb("y2", 0))
        if new:
            products(*new, slot)
        if back_mid:
            w_now = [dot(tb("x3"), r_cat[2 * g + other]) for g in range(group)]
        if back:
            scaled_field(*back, slot)
        if old:
            field_of(*old, slot)
        if back_old:
            add_back(*back_old, slot)
        if mid:
            y_done(z_one, z_two, other)
        if back_mid:
            for g in range(group):
                x_back_done(w_now[g], g, other)
        if old and old[1] == count - 1:
            slope_of(old[0])
        if back_old and back_old[1] == count - 1:
            finish(back_old[0])


def first_kernel(
    kern, last, thr_ref, mask_ref, target_ref, a_ref, b_ref, h_ref, tb,
    g_ref, f_ref, tgt_ref, *work,
):
    m_hi, m_lo = split(mask_ref[...])
    v, left, right = sides(last, a_ref[...], b_ref[...], tb)
    v = v + dot3(tb("cx_own_hi"), tb("cx_own_lo"), m_hi, m_lo, dot_nt)
    to_spectrum(v, tb, f_ref, None)
    tgt_ref[...] = (
        dot_nt(tb("sel_own"), target_ref[...].astype(f32).astype(bf16))
        + dot(tb("sel_halo", 0)[:, :EDGE], left)
        + dot(tb("sel_halo", 1)[:, :EDGE], right)
    )
    gradient_body(kern, last, f_ref, tgt_ref, h_ref, thr_ref, tb, g_ref, work)


def later_kernel(
    kern, last, thr_ref, mine_ref, peer_ref, a_ref, a2_ref, b_ref, b2_ref, f_in_ref, tgt_ref,
    h_ref, tb, g_ref, f_ref, *work,
):
    s_hi, s_lo = split(mine_ref[...] + peer_ref[...])
    from_a = a_ref[...] + a2_ref[...]
    from_b = b_ref[...] + b2_ref[...]
    v, _, _ = sides(last, from_a, from_b, tb)
    v = v + dot3(tb("cx_own_hi"), tb("cx_own_lo"), s_hi, s_lo, dot_nt)
    to_spectrum(v, tb, f_ref, f_in_ref)
    gradient_body(kern, last, f_ref, tgt_ref, h_ref, thr_ref, tb, g_ref, work)


def match_kernel(n_got, table_ref, own_ref, *refs):
    got_refs, (out_ref, *edge_refs) = refs[:n_got], refs[n_got:]
    device = lax.axis_index("tile")
    other = []
    for t in range(2):
        rows = slice(CORE * t, CORE * t + CORE)
        bit = lax.bitwise_xor(table_ref[t], 2 * device + t)
        value = jnp.where(bit == 1, own_ref[CORE * (1 - t) : CORE * (2 - t)], own_ref[rows])
        for b, got in enumerate(got_refs):
            value = jnp.where(bit == 2 << b, got[rows], value)
        other.append(value)
    row = lax.broadcasted_iota(jnp.int32, (CORE, CORE), 0)
    lane = lax.broadcasted_iota(jnp.int32, (CORE, CORE), 1)
    flip = jnp.where(row + lane == CORE - 1, 1.0, 0.0).astype(bf16)
    hi, lo = split(jnp.concatenate(other, axis=0))
    turned = dot(hi, flip) + dot(lo, flip)
    tiles = []
    for t in range(2):
        rows = slice(CORE * t, CORE * t + CORE)
        value = jnp.where(table_ref[2 + t] == 1, turned[rows], other[t])
        tiles.append(0.5 * (own_ref[rows] + value))
    matched = jnp.concatenate(tiles, axis=0)
    out_ref[...] = matched
    if edge_refs:
        send_edges(*edges_of(WIDE_PAD, matched), *edge_refs)


def final_kernel(n_moves, mask_ref, *refs):
    moves, (mask_out, grad_out) = refs[: 2 * n_moves], refs[2 * n_moves :]
    for t in range(2):
        rows = slice(CORE * t, CORE * t + CORE)
        now = mask_ref[t]
        for mine, peer in zip(moves[::2], moves[1::2]):
            step = mine[rows] + peer[rows]
            now = now - STEP_RATE * step
        grad_out[t] = step
        mask_out[t] = now


def per_device(
    n_tile, n_depth, mask_tiles, target_tiles, kernels, socs_weights, thresholds,
    partner_table, mirror_flags,
):
    tiles_dev, core, _ = mask_tiles.shape
    kern = kernels.shape[2]
    assert tiles_dev == 2 and core == CORE
    pairs_a = [(i, i ^ 1) for i in range(n_tile)]
    pairs_b = [p for i in range(1, n_tile - 1, 2) for p in ((i, i + 1), (i + 1, i))]
    pairs_b += [(0, 0), (n_tile - 1, n_tile - 1)]

    def swap_edges(send_a, send_b, cross=False):
        def move(x, pairs):
            if not cross:
                return lax.ppermute(x, "tile", pairs)
            both = [(2 * i + p, 2 * j + 1 - p) for i, j in pairs for p in range(2)]
            return lax.ppermute(x, ("tile", "depth"), both)

        return move(send_b, pairs_b), move(send_a, pairs_a)

    def depth_pair(x):
        bit = 1
        while True:
            peer = lax.ppermute(x, "depth", [(i, i ^ bit) for i in range(n_depth)])
            bit *= 2
            if bit >= n_depth:
                return x, peer
            x = x + peer

    def from_partners(grad):
        bits = [1 << b for b in range(n_tile.bit_length() - 1)]
        got = [
            lax.ppermute(grad, "tile", [(i, i ^ bit) for i in range(n_tile)])
            for bit in reversed(bits)
        ]
        return got[::-1]

    mask_rows = mask_tiles.reshape(tiles_dev * core, core)
    target_rows = target_tiles.reshape(tiles_dev * core, core)
    strip = jax.ShapeDtypeStruct((tiles_dev * core, core), f32)
    side = jax.ShapeDtypeStruct((WIDE_PAD, tiles_dev * core), f32)
    freq = jax.ShapeDtypeStruct((2, 4, XB, YB), f32)
    goal = jax.ShapeDtypeStruct((ROWS, 2 * CORE), f32)
    tiles = jax.ShapeDtypeStruct((tiles_dev, core, core), f32)
    group = 2 if kern % 2 == 0 else 1
    scratch = [
        pltpu.VMEM((2, kern, ROWS, 2 * CORE), f32),
        pltpu.VMEM((2, ROWS, CORE), f32),
        pltpu.VMEM((2, 4, XB, YB), f32),
        pltpu.VMEM((2, group * 4 * XB, 2 * YB), bf16),
        pltpu.VMEM((2, group * 4 * XB, 2 * YB), bf16),
        pltpu.VMEM((2 * group, 6 * XB, 2 * CORE), bf16),
        pltpu.VMEM((2 * group, 3 * ROWS, 2 * CORE), bf16),
        pltpu.VMEM((2, group * 4 * XB, 3 * CORE), bf16),
    ]

    edge = jax.ShapeDtypeStruct((EDGE, tiles_dev * core), f32)
    send_a, send_b = call(
        edges_kernel,
        None,
        [mask_rows + 2.0 * target_rows.astype(f32)],
        [edge, edge],
        flops=3 * 10**9,
    )
    from_b, from_a = swap_edges(send_a, send_b)
    table = jnp.concatenate([partner_table, mirror_flags])
    (spectra,) = call(
        functools.partial(spectra_kernel, kern),
        "spec",
        [socs_weights, kernels.transpose(0, 2, 3, 1, 4)],
        [jax.ShapeDtypeStruct((2 * kern, 4, XB, YB), f32)],
        [pltpu.VMEM((32 * 2 * kern, 128), f32)],
        smem=(0,),
        flops=3 * 10**9,
        nbytes=4 * 10**6,
    )
    grad, freq_now, goals = call(
        functools.partial(first_kernel, kern, n_tile - 1),
        "grad",
        [thresholds, mask_rows, target_rows, from_a, from_b, spectra],
        [strip, freq, goal],
        scratch,
        smem=(0,),
        flops=10**10,
    )
    moves = []
    for step in range(1, STEPS + 1):
        got = from_partners(grad)
        outs = call(
            functools.partial(match_kernel, len(got)),
            None,
            [table, grad, *got],
            [strip, side, side] if step < STEPS else [strip],
            smem=(0,),
        )
        if step == STEPS:
            moves += depth_pair(outs[0])
            break
        if n_depth == 2:
            from_b, from_a = swap_edges(*outs[1:])
            far_b, far_a = swap_edges(*outs[1:], cross=True)
            rims = (from_a, far_a, from_b, far_b)
        else:
            from_b, from_a = swap_edges(*outs[1:])
            rims = depth_pair(from_a) + depth_pair(from_b)
        moves += depth_pair(outs[0])
        kept = step + 1 < STEPS
        grad, *rest = call(
            functools.partial(later_kernel, kern, n_tile - 1),
            "grad",
            [thresholds, *moves[-2:], *rims, freq_now, goals, spectra],
            [strip, freq] if kept else [strip],
            scratch if kept else [pltpu.VMEM(freq.shape, f32)] + scratch,
            smem=(0,),
            flops=10**10,
        )
        freq_now = rest[0] if kept else None
    final = functools.partial(final_kernel, STEPS)
    return tuple(call(final, None, [mask_tiles, *moves], [tiles, tiles]))


def solution(mesh):
    return jax.shard_map(
        functools.partial(per_device, mesh.shape["tile"], mesh.shape["depth"]),
        mesh=mesh,
        in_specs=(
            P("tile", None, None),
            P("tile", None, None),
            P(None, "depth", None, None, None),
            P("depth", None),
            P("depth"),
            P("tile"),
            P("tile"),
        ),
        out_specs=(P("tile", None, None), P("tile", None, None)),
        check_vma=False,
    )
```

```python
import functools

import jax
import jax.numpy as jnp
import ml_dtypes
import numpy as np
from jax import lax
from jax.experimental import pallas as pl
from jax.experimental.pallas import tpu as pltpu
from jax.sharding import PartitionSpec as P

HALO = 12
KSIZE = 25
STEPS = 2
STEEPNESS = 3.0
STEP_RATE = 0.05

CORE = 128
NY = 152
NX = 176
WIDE = 2 * HALO
XB = 96
YB = 128
NU = NY // 2 + 1
NV = NX // 2 + 1
ROWS = 160
ROW0 = 8
CHUNK = 16
SPILL = 16
EDGE = 48
WIDE_PAD = 32
VMEM_LIMIT = 24 * 1024 * 1024

f32 = jnp.float32
bf16 = jnp.bfloat16


def np_split(a):
    hi = np.asarray(a, np.float32).astype(ml_dtypes.bfloat16)
    lo = (np.asarray(a, np.float64) - hi.astype(np.float64)).astype(ml_dtypes.bfloat16)
    return hi, lo


def x_rows(cols):
    out = np.zeros((2 * XB, len(cols)))
    ang = 2 * np.pi * np.outer(np.arange(NV), cols) / NX
    out[:NV] = np.cos(ang)
    out[XB : XB + NV] = np.sin(ang)
    out[XB] = 0.0
    out[XB + NV - 1] = 0.0
    return out


def y_lanes(rows):
    out = np.zeros((len(rows), 2 * YB))
    ang = 2 * np.pi * np.outer(rows, np.arange(NU)) / NY
    out[:, :NU] = np.cos(ang)
    out[:, YB : YB + NU] = np.sin(ang)
    out[:, YB] = 0.0
    out[:, YB + NU - 1] = 0.0
    return out


def half_weights(bins):
    weights = np.full(bins, 2.0)
    weights[0] = weights[-1] = 1.0
    return weights


def x_back(cols):
    kappa = np.zeros(2 * XB)
    kappa[:NV] = half_weights(NV) / 2
    kappa[XB : XB + NV] = half_weights(NV) / 2
    return x_rows(cols).T * kappa


def y_back(rows):
    weight = np.zeros(2 * YB)
    weight[:NU] = half_weights(NU)
    weight[YB : YB + NU] = -half_weights(NU)
    return (y_lanes(rows) * weight).T / (NX * NY)


def pack(parts):
    rows, where, at = [], {}, 0
    pieces = []
    for name, a in parts:
        if a.shape[1] <= 256:
            pieces.append((name, a))
            continue
        cuts = range(0, a.shape[1], 256)
        where[name] = len(cuts)
        pieces += [(f"{name}.{i}", a[:, c : c + 256]) for i, c in enumerate(cuts)]
    for name, a in pieces:
        height = -(-a.shape[0] // 16) * 16
        block = np.zeros((height, 256), np.float64)
        block[: a.shape[0], : a.shape[1]] = a
        rows.append(block)
        where[name] = (at, a.shape[0], a.shape[1])
        at += height
    return np.concatenate(rows), where


def pack_split(parts):
    both = []
    for name, a in parts:
        hi, lo = np_split(a)
        if name in ("x2", "x3", "x4"):
            hi, lo = hi.astype(np.float64), lo.astype(np.float64)
            both.append((name, np.concatenate([hi, lo, hi], axis=1)))
            continue
        both += [(name + "_hi", hi.astype(np.float64)), (name + "_lo", lo.astype(np.float64))]
    return both


@functools.lru_cache(None)
def tables():
    core_rows = np.arange(HALO, HALO + CORE)
    field_cols = np.arange(ROW0, ROW0 + ROWS)
    own_cols = np.arange(WIDE, WIDE + CORE)
    sides = np.zeros((2 * XB, 256))
    sides[:, :WIDE] = x_rows(np.arange(WIDE))
    sides[:, CORE : CORE + WIDE] = x_rows(np.arange(WIDE + CORE, NX))
    parts = [("cx_own", x_rows(own_cols)), ("cx_side", sides)]
    for t in range(2):
        pos = np.arange(2 * CORE) - t * CORE + HALO
        inside = (pos >= 0) & (pos < NY)
        parts.append((f"by{t}", y_lanes(pos) * inside[:, None]))
    parts += [("x2", x_back(field_cols)), ("x3", x_rows(field_cols)), ("x4", x_back(own_cols))]
    y2_hi, y2_lo = (a.astype(np.float64) for a in np_split(y_back(core_rows)))
    y3_hi, y3_lo = (a.astype(np.float64) for a in np_split(y_lanes(core_rows)))
    grad = pack_split(parts)
    grad += [("y2", np.concatenate([y2_hi, y2_lo], axis=1))]
    grad += [("y3", np.concatenate([y3_hi, y3_hi, y3_lo]))]
    own = np.zeros((ROWS, CORE))
    own[np.arange(CORE) + WIDE - ROW0, np.arange(CORE)] = 1
    halo = np.zeros((ROWS, 256))
    for r in range(HALO):
        halo[HALO + r - ROW0, WIDE + r] = 1
        halo[WIDE + CORE + r - ROW0, CORE + WIDE + r] = 1
    grad += [("sel_own", own), ("sel_halo", halo)]
    offs = np.arange(KSIZE) - HALO
    kx = np.zeros((2 * XB, 128))
    kx[:, :KSIZE] = x_rows(offs)
    spec = [("kx", kx)]
    for m in range(4):
        ky = np.zeros((128, 2 * YB))
        ky[32 * m : 32 * m + KSIZE] = y_lanes(offs)
        spec.append((f"ky{m}", ky))
    return {"grad": pack(grad), "spec": pack(pack_split(spec))}


def split(x):
    hi = x.astype(bf16)
    return hi, (x - hi.astype(f32)).astype(bf16)


def dot(a, b):
    return lax.dot_general(a, b, (((1,), (0,)), ((), ())), preferred_element_type=f32)


def dot_nt(a, b):
    return lax.dot_general(a, b, (((1,), (1,)), ((), ())), preferred_element_type=f32)


def dot3(a_hi, a_lo, b_hi, b_lo, mul=dot):
    return mul(a_hi, b_hi) + (mul(a_lo, b_hi) + mul(a_hi, b_lo))


def signed(spec):
    cc, cs = spec[:XB, :YB], spec[:XB, YB:]
    sc, ss = spec[XB:, :YB], spec[XB:, YB:]
    return cc - ss, -(cs + sc), cc + ss, sc - cs


def even_odd(pr, pi, mr, mi):
    top = jnp.concatenate([pr + mr, pi + mi], axis=1)
    low = jnp.concatenate([mi - pi, pr - mr], axis=1)
    return jnp.concatenate([top, low], axis=0)


def table_array(group):
    return jnp.asarray(tables()[group][0].astype(ml_dtypes.bfloat16))


def table_reader(group, ref):
    where = tables()[group][1]

    def table(name, half=None):
        if isinstance(where[name], int):
            return jnp.concatenate([table(f"{name}.{i}") for i in range(where[name])], axis=1)
        at, height, width = where[name]
        lanes = slice(0, width) if half is None else slice(128 * half, 128 * half + 128)
        return ref[at : at + height, lanes]

    return table


def call(body, group, args, out_shape, scratch=(), smem=(), flops=0, nbytes=0):
    vm = pl.BlockSpec(memory_space=pltpu.VMEM)
    sm = pl.BlockSpec(memory_space=pltpu.SMEM)
    n_in = len(args)
    if group is not None:
        args = [*args, table_array(group)]

    def wrapped(*refs):
        if group is not None:
            refs = [*refs[:n_in], table_reader(group, refs[n_in]), *refs[n_in + 1 :]]
        body(*refs)

    return pl.pallas_call(
        wrapped,
        out_shape=out_shape,
        in_specs=[sm if i in smem else vm for i in range(len(args))],
        out_specs=[vm] * len(out_shape),
        scratch_shapes=list(scratch),
        compiler_params=pltpu.CompilerParams(vmem_limit_bytes=VMEM_LIMIT),
        cost_estimate=pl.CostEstimate(flops=flops, bytes_accessed=nbytes, transcendentals=0),
    )(*args)


def is_even():
    return lax.rem(lax.axis_index("tile"), 2) == 0


def send_edges(right, left, a_ref, b_ref):
    even = is_even()
    a_ref[...] = jnp.where(even, right, left)
    b_ref[...] = jnp.where(even, left, right)


def picker(rows, first, count, col):
    row = lax.broadcasted_iota(jnp.int32, (rows, CORE), 0)
    lane = lax.broadcasted_iota(jnp.int32, (rows, CORE), 1)
    hit = (row - first == lane - col) & (row >= first) & (row < first + count)
    return jnp.where(hit, 1.0, 0.0).astype(bf16)


def edges_of(rows, strip, extra=None):
    hi, lo = split(strip)
    both = []
    for col, more in ((CORE - WIDE, CORE - HALO), (0, 0)):
        pick = picker(rows, 0, WIDE, col)
        edge = dot_nt(pick, hi) + dot_nt(pick, lo)
        if extra is not None:
            edge = edge + dot_nt(picker(rows, WIDE, HALO, more), extra)
        both.append(edge)
    return both


def edges_kernel(both_ref, a_ref, b_ref):
    both = both_ref[...]
    target = jnp.where(both >= 2.0, 1.0, 0.0)
    mask = both - 2.0 * target
    send_edges(*edges_of(EDGE, mask, target.astype(bf16)), a_ref, b_ref)


def spectra_kernel(kern, w_ref, ker_ref, tb, h_ref, hs_ref):
    hs_ref[...] = jnp.zeros_like(hs_ref)
    for k in range(kern):
        for part in range(2):
            row = 32 * (2 * k + part)
            hs_ref[row : row + KSIZE, :KSIZE] = ker_ref[part, k, :, 0, :]
    s_hi, s_lo = split(hs_ref[...])
    z = dot3(tb("kx_hi"), tb("kx_lo"), s_hi, s_lo, dot_nt)
    z_hi, z_lo = split(z)
    for c in range(2 * kern):
        lanes = slice(128 * (c // 4), 128 * (c // 4) + 128)
        spec = dot3(z_hi[:, lanes], z_lo[:, lanes], tb(f"ky{c % 4}_hi"), tb(f"ky{c % 4}_lo"))
        root = jnp.sqrt(jnp.full((1, YB), w_ref[0, c // 2], f32))
        for j, comp in enumerate(signed(spec)):
            h_ref[c, j] = root * comp


def sides(last, from_a, from_b, tb):
    even = is_even()
    tile = lax.axis_index("tile")
    from_b = jnp.where((tile == 0) | (tile == last), 0.0, from_b)
    l_hi, l_lo = split(jnp.where(even, from_b, from_a))
    r_hi, r_lo = split(jnp.where(even, from_a, from_b))
    height = l_hi.shape[0]
    v = None
    for half, hi, lo in ((0, l_hi, l_lo), (1, r_hi, r_lo)):
        c_hi, c_lo = tb("cx_side_hi", half), tb("cx_side_lo", half)
        term = dot3(c_hi[:, :height], c_lo[:, :height], hi, lo)
        v = term if v is None else v + term
    return v, l_hi, r_hi


def to_spectrum(v, tb, f_ref, base):
    v_hi, v_lo = split(v)
    for t in range(2):
        spec = dot3(v_hi, v_lo, tb(f"by{t}_hi"), tb(f"by{t}_lo"))
        for j, comp in enumerate(signed(spec)):
            f_ref[t, j] = comp if base is None else base[t, j] - STEP_RATE * comp


def group_of(kern):
    return 2 if kern % 2 == 0 else 1


def gradient_body(kern, field_tiles, back_tiles, field_refs, back_refs, fld, inten, h_ref, tb):
    if field_tiles:
        last, f_ref, tgt_ref, thr_ref, a_hi, a_lo, b_cat = field_refs
    finish, tot, r_cat, w_cat = back_refs
    group = group_of(kern)
    count = kern // group
    chains = [(t, c) for t in field_tiles for c in range(count)]
    backs = [(t, c) for t in back_tiles for c in range(count)]
    lag = count + 2 if field_tiles else 0

    def pick(i, listed):
        return listed[i] if 0 <= i < len(listed) else None

    if field_tiles:
        tile = lax.axis_index("tile")
        first = jnp.where(tile == 0, WIDE, HALO) - ROW0
        end = jnp.where(tile == last, WIDE + CORE, WIDE + CORE + HALO) - ROW0
        row = lax.broadcasted_iota(jnp.int32, (ROWS, CORE), 0)
        inside = (row >= first) & (row < end)

    def chunks(height):
        return [slice(r, r + CHUNK) for r in range(0, height, CHUNK)]

    def put(ref, slot, starts, pieces):
        for at_row, piece in zip(starts, pieces):
            ref[slot, at_row : at_row + CHUNK] = piece

    def products(t, c, slot):
        for part in range(2 * group):
            for rows in chunks(XB):
                hpr, hpi, hmr, hmi = (h_ref[2 * group * c + part, j, rows] for j in range(4))
                fpr, fpi, fmr, fmi = (f_ref[t, j, rows] for j in range(4))
                pr, pi = hpr * fpr - hpi * fpi, hpr * fpi + hpi * fpr
                mr, mi = hmr * fmr - hmi * fmi, hmr * fmi + hmi * fmr
                starts = [2 * XB * part + rows.start, 2 * XB * part + XB + rows.start]
                top = split(jnp.concatenate([pr + mr, pi + mi], axis=1))
                low = split(jnp.concatenate([mi - pi, pr - mr], axis=1))
                put(a_hi, slot, starts, (top[0], low[0]))
                put(a_lo, slot, starts, (top[1], low[1]))

    def y_done(z_one, z_two, slot):
        for g in range(group):
            for rows in chunks(2 * XB):
                z = []
                for part in range(2 * g, 2 * g + 2):
                    here = slice(2 * XB * part + rows.start, 2 * XB * part + rows.stop)
                    z.append(z_one[here, :CORE] + (z_one[here, CORE:] + z_two[here]))
                z_hi, z_lo = split(jnp.concatenate(z, axis=1))
                starts = [2 * XB * j + rows.start for j in range(3)]
                put(b_cat, 2 * g + slot, starts, (z_hi, z_hi, z_lo))

    def field_of(t, c, slot):
        for g in range(group):
            k = group * c + g
            whole = dot(tb("x2"), b_cat[2 * g + slot])
            for rows in chunks(ROWS):
                field = whole[rows]
                fld[t][k, rows] = field
                re, im = field[:, :CORE], field[:, CORE:]
                power = re * re + im * im
                inten[t][rows] = power if k == 0 else inten[t][rows] + power

    def slope_of(t):
        resist = jax.nn.sigmoid(STEEPNESS * (inten[t][...] - thr_ref[0]))
        target = tgt_ref[:, CORE * t : CORE * t + CORE]
        slope = 2.0 * (resist - target) * STEEPNESS * resist * (1.0 - resist)
        inten[t][...] = jnp.where(inside, 2.0 * slope, 0.0)

    def scaled_field(t, c, slot):
        for g in range(group):
            for rows in chunks(ROWS):
                slope, field = inten[t][rows], fld[t][group * c + g, rows]
                r_hi, r_lo = split(
                    jnp.concatenate([slope * field[:, :CORE], slope * field[:, CORE:]], axis=1)
                )
                starts = [ROWS * j + rows.start for j in range(3)]
                put(r_cat, 2 * g + slot, starts, (r_hi, r_hi, r_lo))

    def x_back_done(w_now, g, slot):
        for rows in chunks(2 * XB):
            w_hi, w_lo = split(w_now[rows])
            for part in range(2):
                base = 2 * XB * (2 * g + part)
                here = slice(base + rows.start, base + rows.stop)
                lanes = slice(CORE * part, CORE * part + CORE)
                for j, piece in enumerate((w_hi, w_lo, w_hi)):
                    w_cat[slot, here, CORE * j : CORE * j + CORE] = piece[:, lanes]

    def add_back(t, c, slot):
        specs = dot(w_cat[slot], tb("y3"))
        for rows in chunks(XB):
            acc = [0.0] * 4 if c == 0 else [tot[j, rows] for j in range(4)]
            for part in range(2 * group):
                base = 2 * XB * part + rows.start
                cos_rows, sin_rows = slice(base, base + CHUNK), slice(base + XB, base + XB + CHUNK)
                cc, cs = specs[cos_rows, :YB], specs[cos_rows, YB:]
                sc, ss = specs[sin_rows, :YB], specs[sin_rows, YB:]
                bpr, neg, bmr, bmi = cc - ss, cs + sc, cc + ss, sc - cs
                hpr, hpi, hmr, hmi = (h_ref[2 * group * c + part, j, rows] for j in range(4))
                acc[0] = acc[0] + (hpr * bpr - hpi * neg)
                acc[1] = acc[1] - (hpr * neg + hpi * bpr)
                acc[2] = acc[2] + (hmr * bmr + hmi * bmi)
                acc[3] = acc[3] + (hmr * bmi - hmi * bmr)
            for j in range(4):
                tot[j, rows] = acc[j]

    for i in range(max(len(chains) + 2, len(backs) + lag + 2)):
        new, mid, old = (pick(i - j, chains) for j in range(3))
        back, back_mid, back_old = (pick(i - lag - j, backs) for j in range(3))
        slot, other = i % 2, (i + 1) % 2
        if mid:
            z_one = dot(a_hi[other], tb("y2"))
            z_two = dot(a_lo[other], tb("y2", 0))
        if new:
            products(*new, slot)
        if back_mid:
            w_now = [dot(tb("x3"), r_cat[2 * g + other]) for g in range(group)]
        if back:
            scaled_field(*back, slot)
        if old:
            field_of(*old, slot)
        if back_old:
            add_back(*back_old, slot)
        if mid:
            y_done(z_one, z_two, other)
        if back_mid:
            for g in range(group):
                x_back_done(w_now[g], g, other)
        if old and old[1] == count - 1:
            slope_of(old[0])
        if back_old and back_old[1] == count - 1:
            finish()


def strip_part(t, rows, tot, tb):
    lane = lax.broadcasted_iota(jnp.int32, (1, 2 * YB), 1)
    bin_at = lax.rem(lane, YB)
    weight = jnp.where((bin_at == 0) | (bin_at == NU - 1), 1.0, 2.0) / (NX * NY)
    weight = jnp.where(lane < YB, weight, -weight)
    r_hi, r_lo = split(even_odd(*(tot[j] for j in range(4))))
    u = dot(tb("x4"), jnp.concatenate([r_hi, r_hi, r_lo], axis=0))
    u_hi, u_lo = split(weight * u)
    return dot3(tb(f"by{t}_hi")[rows], tb(f"by{t}_lo")[rows], u_hi, u_lo, dot_nt)


def upper_part(kern, last, f_ref, tgt_ref, h_ref, thr_ref, tb, outs, work):
    own_ref, spill_ref, fld1, slope1 = outs
    fld0, slope0, tot, a_hi, a_lo, b_cat, r_cat, w_cat = work

    def finish():
        term = strip_part(0, slice(0, CORE + SPILL), tot, tb)
        own_ref[...] = term[:CORE]
        spill_ref[...] = term[CORE:]

    field_refs = (last, f_ref, tgt_ref, thr_ref, a_hi, a_lo, b_cat)
    back_refs = (finish, tot, r_cat, w_cat)
    fld, inten = (fld0, fld1), (slope0, slope1)
    gradient_body(kern, (0, 1), (0,), field_refs, back_refs, fld, inten, h_ref, tb)


def lower_kernel(
    kern, own_ref, spill_ref, fld1, slope1, h_ref, tb, all_ref, late_ref, tot, r_cat, w_cat
):
    def finish():
        term = strip_part(1, slice(CORE - SPILL, 2 * CORE), tot, tb)
        join = term[SPILL : 2 * SPILL] + spill_ref[...]
        late_ref[...] = jnp.concatenate([term[:SPILL], join, term[2 * SPILL :]], axis=0)
        all_ref[: CORE - SPILL] = own_ref[: CORE - SPILL]
        all_ref[CORE - SPILL : CORE] = own_ref[CORE - SPILL :] + term[:SPILL]
        all_ref[CORE : CORE + SPILL] = join
        all_ref[CORE + SPILL :] = term[2 * SPILL :]

    back_refs = (finish, tot, r_cat, w_cat)
    gradient_body(kern, (), (1,), None, back_refs, (None, fld1), (None, slope1), h_ref, tb)


def first_kernel(
    kern, last, thr_ref, mask_ref, target_ref, a_ref, b_ref, h_ref, tb,
    own_ref, spill_ref, fld1, slope1, f_ref, tgt_ref, *work,
):
    m_hi, m_lo = split(mask_ref[...])
    v, left, right = sides(last, a_ref[...], b_ref[...], tb)
    v = v + dot3(tb("cx_own_hi"), tb("cx_own_lo"), m_hi, m_lo, dot_nt)
    to_spectrum(v, tb, f_ref, None)
    tgt_ref[...] = (
        dot_nt(tb("sel_own"), target_ref[...].astype(f32).astype(bf16))
        + dot(tb("sel_halo", 0)[:, :EDGE], left)
        + dot(tb("sel_halo", 1)[:, :EDGE], right)
    )
    outs = (own_ref, spill_ref, fld1, slope1)
    upper_part(kern, last, f_ref, tgt_ref, h_ref, thr_ref, tb, outs, work)


def later_kernel(
    kern, last, thr_ref, mine_ref, peer_ref, a_ref, a2_ref, b_ref, b2_ref, f_in_ref, tgt_ref,
    h_ref, tb, own_ref, spill_ref, fld1, slope1, f_ref, *work,
):
    s_hi, s_lo = split(mine_ref[...] + peer_ref[...])
    from_a = a_ref[...] + a2_ref[...]
    from_b = b_ref[...] + b2_ref[...]
    v, _, _ = sides(last, from_a, from_b, tb)
    v = v + dot3(tb("cx_own_hi"), tb("cx_own_lo"), s_hi, s_lo, dot_nt)
    to_spectrum(v, tb, f_ref, f_in_ref)
    outs = (own_ref, spill_ref, fld1, slope1)
    upper_part(kern, last, f_ref, tgt_ref, h_ref, thr_ref, tb, outs, work)


def match_kernel(n_got, n_split, table_ref, own_ref, *refs):
    got_refs, refs = refs[:n_got], refs[n_got:]
    split_refs, (out_ref, *edge_refs) = refs[: 2 * n_split], refs[2 * n_split :]

    def received(b, t):
        if b < n_got:
            return got_refs[b][CORE * t : CORE * t + CORE]
        early, late = split_refs[2 * (b - n_got) : 2 * (b - n_got) + 2]
        if t == 1:
            return late[SPILL:]
        tail = early[CORE - SPILL :] + late[:SPILL]
        return jnp.concatenate([early[: CORE - SPILL], tail], axis=0)

    device = lax.axis_index("tile")
    other = []
    for t in range(2):
        rows = slice(CORE * t, CORE * t + CORE)
        bit = lax.bitwise_xor(table_ref[t], 2 * device + t)
        value = jnp.where(bit == 1, own_ref[CORE * (1 - t) : CORE * (2 - t)], own_ref[rows])
        for b in range(n_got + n_split):
            value = jnp.where(bit == 2 << b, received(b, t), value)
        other.append(value)
    row = lax.broadcasted_iota(jnp.int32, (CORE, CORE), 0)
    lane = lax.broadcasted_iota(jnp.int32, (CORE, CORE), 1)
    flip = jnp.where(row + lane == CORE - 1, 1.0, 0.0).astype(bf16)
    hi, lo = split(jnp.concatenate(other, axis=0))
    turned = dot(hi, flip) + dot(lo, flip)
    tiles = []
    for t in range(2):
        rows = slice(CORE * t, CORE * t + CORE)
        value = jnp.where(table_ref[2 + t] == 1, turned[rows], other[t])
        tiles.append(0.5 * (own_ref[rows] + value))
    matched = jnp.concatenate(tiles, axis=0)
    out_ref[...] = matched
    if edge_refs:
        send_edges(*edges_of(WIDE_PAD, matched), *edge_refs)


def final_kernel(n_moves, mask_ref, *refs):
    moves, (mask_out, grad_out) = refs[: 2 * n_moves], refs[2 * n_moves :]
    for t in range(2):
        rows = slice(CORE * t, CORE * t + CORE)
        now = mask_ref[t]
        for mine, peer in zip(moves[::2], moves[1::2]):
            step = mine[rows] + peer[rows]
            now = now - STEP_RATE * step
        grad_out[t] = step
        mask_out[t] = now


def per_device(
    n_tile, n_depth, mask_tiles, target_tiles, kernels, socs_weights, thresholds,
    partner_table, mirror_flags,
):
    tiles_dev, core, _ = mask_tiles.shape
    kern = kernels.shape[2]
    assert tiles_dev == 2 and core == CORE
    pairs_a = [(i, i ^ 1) for i in range(n_tile)]
    pairs_b = [p for i in range(1, n_tile - 1, 2) for p in ((i, i + 1), (i + 1, i))]
    pairs_b += [(0, 0), (n_tile - 1, n_tile - 1)]

    def swap_edges(send_a, send_b, cross=False):
        def move(x, pairs):
            if not cross:
                return lax.ppermute(x, "tile", pairs)
            both = [(2 * i + p, 2 * j + 1 - p) for i, j in pairs for p in range(2)]
            return lax.ppermute(x, ("tile", "depth"), both)

        return move(send_b, pairs_b), move(send_a, pairs_a)

    def depth_pair(x):
        bit = 1
        while True:
            peer = lax.ppermute(x, "depth", [(i, i ^ bit) for i in range(n_depth)])
            bit *= 2
            if bit >= n_depth:
                return x, peer
            x = x + peer

    bits = [1 << b for b in range(n_tile.bit_length() - 1)]
    n_split = min(2, len(bits))

    def swap(x, bit):
        return lax.ppermute(x, "tile", [(i, i ^ bit) for i in range(n_tile)])

    def rest_of(own, spill, fields, slope):
        far_bits = bits[len(bits) - n_split :]
        early = [swap(own, bit) for bit in far_bits[::-1]][::-1]
        grad, late = call(
            functools.partial(lower_kernel, kern),
            "grad",
            [own, spill, fields, slope, spectra],
            [strip, late_rows],
            back_scratch,
            flops=3 * 10**9,
        )
        late = [swap(late, bit) for bit in far_bits[::-1]][::-1]
        near = [swap(grad, bit) for bit in bits[: len(bits) - n_split][::-1]][::-1]
        return grad, near, [x for pair in zip(early, late) for x in pair]

    mask_rows = mask_tiles.reshape(tiles_dev * core, core)
    target_rows = target_tiles.reshape(tiles_dev * core, core)
    strip = jax.ShapeDtypeStruct((tiles_dev * core, core), f32)
    side = jax.ShapeDtypeStruct((WIDE_PAD, tiles_dev * core), f32)
    freq = jax.ShapeDtypeStruct((2, 4, XB, YB), f32)
    goal = jax.ShapeDtypeStruct((ROWS, 2 * CORE), f32)
    tiles = jax.ShapeDtypeStruct((tiles_dev, core, core), f32)
    late_rows = jax.ShapeDtypeStruct((core + SPILL, core), f32)
    group = group_of(kern)
    fields = (kern, ROWS, 2 * CORE)
    upper_outs = [
        jax.ShapeDtypeStruct(shape, f32)
        for shape in ((core, core), (SPILL, core), fields, (ROWS, CORE))
    ]
    back_scratch = [
        pltpu.VMEM((4, XB, YB), f32),
        pltpu.VMEM((2 * group, 3 * ROWS, 2 * CORE), bf16),
        pltpu.VMEM((2, group * 4 * XB, 3 * CORE), bf16),
    ]
    scratch = [
        pltpu.VMEM(fields, f32),
        pltpu.VMEM((ROWS, CORE), f32),
        back_scratch[0],
        pltpu.VMEM((2, group * 4 * XB, 2 * YB), bf16),
        pltpu.VMEM((2, group * 4 * XB, 2 * YB), bf16),
        pltpu.VMEM((2 * group, 6 * XB, 2 * CORE), bf16),
        *back_scratch[1:],
    ]

    edge = jax.ShapeDtypeStruct((EDGE, tiles_dev * core), f32)
    send_a, send_b = call(
        edges_kernel,
        None,
        [mask_rows + 2.0 * target_rows.astype(f32)],
        [edge, edge],
        flops=3 * 10**9,
    )
    from_b, from_a = swap_edges(send_a, send_b)
    table = jnp.concatenate([partner_table, mirror_flags])
    (spectra,) = call(
        functools.partial(spectra_kernel, kern),
        "spec",
        [socs_weights, kernels.transpose(0, 2, 3, 1, 4)],
        [jax.ShapeDtypeStruct((2 * kern, 4, XB, YB), f32)],
        [pltpu.VMEM((32 * 2 * kern, 128), f32)],
        smem=(0,),
        flops=3 * 10**9,
        nbytes=4 * 10**6,
    )
    *upper, freq_now, goals = call(
        functools.partial(first_kernel, kern, n_tile - 1),
        "grad",
        [thresholds, mask_rows, target_rows, from_a, from_b, spectra],
        [*upper_outs, freq, goal],
        scratch,
        smem=(0,),
        flops=10**10,
    )
    moves = []
    for step in range(1, STEPS + 1):
        grad, got, got_split = rest_of(*upper)
        outs = call(
            functools.partial(match_kernel, len(got), n_split),
            None,
            [table, grad, *got, *got_split],
            [strip, side, side] if step < STEPS else [strip],
            smem=(0,),
        )
        if step == STEPS:
            moves += depth_pair(outs[0])
            break
        if n_depth == 2:
            from_b, from_a = swap_edges(*outs[1:])
            far_b, far_a = swap_edges(*outs[1:], cross=True)
            rims = (from_a, far_a, from_b, far_b)
        else:
            from_b, from_a = swap_edges(*outs[1:])
            rims = depth_pair(from_a) + depth_pair(from_b)
        moves += depth_pair(outs[0])
        kept = step + 1 < STEPS
        outs = call(
            functools.partial(later_kernel, kern, n_tile - 1),
            "grad",
            [thresholds, *moves[-2:], *rims, freq_now, goals, spectra],
            [*upper_outs, freq] if kept else upper_outs,
            scratch if kept else [pltpu.VMEM(freq.shape, f32)] + scratch,
            smem=(0,),
            flops=10**10,
        )
        upper, freq_now = outs[:4], outs[-1]
    final = functools.partial(final_kernel, STEPS)
    return tuple(call(final, None, [mask_tiles, *moves], [tiles, tiles]))


def solution(mesh):
    return jax.shard_map(
        functools.partial(per_device, mesh.shape["tile"], mesh.shape["depth"]),
        mesh=mesh,
        in_specs=(
            P("tile", None, None),
            P("tile", None, None),
            P(None, "depth", None, None, None),
            P("depth", None),
            P("depth"),
            P("tile"),
            P("tile"),
        ),
        out_specs=(P("tile", None, None), P("tile", None, None)),
        check_vma=False,
    )
```

```python
import functools

import jax
import jax.numpy as jnp
import ml_dtypes
import numpy as np
from jax import lax
from jax.experimental import pallas as pl
from jax.experimental.pallas import tpu as pltpu
from jax.sharding import PartitionSpec as P

HALO = 12
KSIZE = 25
STEPS = 2
STEEPNESS = 3.0
STEP_RATE = 0.05

CORE = 128
NY = 152
NX = 176
WIDE = 2 * HALO
XB = 96
YB = 128
NU = NY // 2 + 1
NV = NX // 2 + 1
ROWS = 160
ROW0 = 8
CHUNK = 16
EDGE = 48
WIDE_PAD = 32
VMEM_LIMIT = 24 * 1024 * 1024

f32 = jnp.float32
bf16 = jnp.bfloat16


def np_split(a):
    hi = np.asarray(a, np.float32).astype(ml_dtypes.bfloat16)
    lo = (np.asarray(a, np.float64) - hi.astype(np.float64)).astype(ml_dtypes.bfloat16)
    return hi, lo


def x_rows(cols):
    out = np.zeros((2 * XB, len(cols)))
    ang = 2 * np.pi * np.outer(np.arange(NV), cols) / NX
    out[:NV] = np.cos(ang)
    out[XB : XB + NV] = np.sin(ang)
    out[XB] = 0.0
    out[XB + NV - 1] = 0.0
    return out


def y_lanes(rows):
    out = np.zeros((len(rows), 2 * YB))
    ang = 2 * np.pi * np.outer(rows, np.arange(NU)) / NY
    out[:, :NU] = np.cos(ang)
    out[:, YB : YB + NU] = np.sin(ang)
    out[:, YB] = 0.0
    out[:, YB + NU - 1] = 0.0
    return out


def half_weights(bins):
    weights = np.full(bins, 2.0)
    weights[0] = weights[-1] = 1.0
    return weights


def x_back(cols):
    kappa = np.zeros(2 * XB)
    kappa[:NV] = half_weights(NV) / 2
    kappa[XB : XB + NV] = half_weights(NV) / 2
    return x_rows(cols).T * kappa


def y_back(rows):
    weight = np.zeros(2 * YB)
    weight[:NU] = half_weights(NU)
    weight[YB : YB + NU] = -half_weights(NU)
    return (y_lanes(rows) * weight).T / (NX * NY)


def pack(parts):
    rows, where, at = [], {}, 0
    pieces = []
    for name, a in parts:
        if a.shape[1] <= 256:
            pieces.append((name, a))
            continue
        cuts = range(0, a.shape[1], 256)
        where[name] = len(cuts)
        pieces += [(f"{name}.{i}", a[:, c : c + 256]) for i, c in enumerate(cuts)]
    for name, a in pieces:
        height = -(-a.shape[0] // 16) * 16
        block = np.zeros((height, 256), np.float64)
        block[: a.shape[0], : a.shape[1]] = a
        rows.append(block)
        where[name] = (at, a.shape[0], a.shape[1])
        at += height
    return np.concatenate(rows), where


def pack_split(parts):
    both = []
    for name, a in parts:
        hi, lo = np_split(a)
        if name in ("x2", "x3", "x4"):
            hi, lo = hi.astype(np.float64), lo.astype(np.float64)
            both.append((name, np.concatenate([hi, lo, hi], axis=1)))
            continue
        both += [(name + "_hi", hi.astype(np.float64)), (name + "_lo", lo.astype(np.float64))]
    return both


@functools.lru_cache(None)
def tables():
    core_rows = np.arange(HALO, HALO + CORE)
    field_cols = np.arange(ROW0, ROW0 + ROWS)
    own_cols = np.arange(WIDE, WIDE + CORE)
    sides = np.zeros((2 * XB, 256))
    sides[:, :WIDE] = x_rows(np.arange(WIDE))
    sides[:, CORE : CORE + WIDE] = x_rows(np.arange(WIDE + CORE, NX))
    parts = [("cx_own", x_rows(own_cols)), ("cx_side", sides)]
    for t in range(2):
        pos = np.arange(2 * CORE) - t * CORE + HALO
        inside = (pos >= 0) & (pos < NY)
        parts.append((f"by{t}", y_lanes(pos) * inside[:, None]))
    parts += [("x2", x_back(field_cols)), ("x3", x_rows(field_cols)), ("x4", x_back(own_cols))]
    y2_hi, y2_lo = (a.astype(np.float64) for a in np_split(y_back(core_rows)))
    y3_hi, y3_lo = (a.astype(np.float64) for a in np_split(y_lanes(core_rows)))
    grad = pack_split(parts)
    grad += [("y2", np.concatenate([y2_hi, y2_lo], axis=1))]
    grad += [("y3", np.concatenate([y3_hi, y3_hi, y3_lo]))]
    own = np.zeros((ROWS, CORE))
    own[np.arange(CORE) + WIDE - ROW0, np.arange(CORE)] = 1
    halo = np.zeros((ROWS, 256))
    for r in range(HALO):
        halo[HALO + r - ROW0, WIDE + r] = 1
        halo[WIDE + CORE + r - ROW0, CORE + WIDE + r] = 1
    grad += [("sel_own", own), ("sel_halo", halo)]
    offs = np.arange(KSIZE) - HALO
    kx = np.zeros((2 * XB, 128))
    kx[:, :KSIZE] = x_rows(offs)
    spec = [("kx", kx)]
    for m in range(4):
        ky = np.zeros((128, 2 * YB))
        ky[32 * m : 32 * m + KSIZE] = y_lanes(offs)
        spec.append((f"ky{m}", ky))
    return {"grad": pack(grad), "spec": pack(pack_split(spec))}


def split(x):
    hi = x.astype(bf16)
    return hi, (x - hi.astype(f32)).astype(bf16)


def dot(a, b):
    return lax.dot_general(a, b, (((1,), (0,)), ((), ())), preferred_element_type=f32)


def dot_nt(a, b):
    return lax.dot_general(a, b, (((1,), (1,)), ((), ())), preferred_element_type=f32)


def dot3(a_hi, a_lo, b_hi, b_lo, mul=dot):
    return mul(a_hi, b_hi) + (mul(a_lo, b_hi) + mul(a_hi, b_lo))


def signed(spec):
    cc, cs = spec[:XB, :YB], spec[:XB, YB:]
    sc, ss = spec[XB:, :YB], spec[XB:, YB:]
    return cc - ss, -(cs + sc), cc + ss, sc - cs


def even_odd(pr, pi, mr, mi):
    top = jnp.concatenate([pr + mr, pi + mi], axis=1)
    low = jnp.concatenate([mi - pi, pr - mr], axis=1)
    return jnp.concatenate([top, low], axis=0)


def table_array(group):
    return jnp.asarray(tables()[group][0].astype(ml_dtypes.bfloat16))


def table_reader(group, ref):
    where = tables()[group][1]

    def table(name, half=None):
        if isinstance(where[name], int):
            return jnp.concatenate([table(f"{name}.{i}") for i in range(where[name])], axis=1)
        at, height, width = where[name]
        lanes = slice(0, width) if half is None else slice(128 * half, 128 * half + 128)
        return ref[at : at + height, lanes]

    return table


def call(body, group, args, out_shape, scratch=(), smem=(), flops=0, nbytes=0):
    vm = pl.BlockSpec(memory_space=pltpu.VMEM)
    sm = pl.BlockSpec(memory_space=pltpu.SMEM)
    n_in = len(args)
    if group is not None:
        args = [*args, table_array(group)]

    def wrapped(*refs):
        if group is not None:
            refs = [*refs[:n_in], table_reader(group, refs[n_in]), *refs[n_in + 1 :]]
        body(*refs)

    return pl.pallas_call(
        wrapped,
        out_shape=out_shape,
        in_specs=[sm if i in smem else vm for i in range(len(args))],
        out_specs=[vm] * len(out_shape),
        scratch_shapes=list(scratch),
        compiler_params=pltpu.CompilerParams(vmem_limit_bytes=VMEM_LIMIT),
        cost_estimate=pl.CostEstimate(flops=flops, bytes_accessed=nbytes, transcendentals=0),
    )(*args)


def is_even():
    return lax.rem(lax.axis_index("tile"), 2) == 0


def send_edges(right, left, a_ref, b_ref):
    even = is_even()
    a_ref[...] = jnp.where(even, right, left)
    b_ref[...] = jnp.where(even, left, right)


def picker(rows, first, count, col):
    row = lax.broadcasted_iota(jnp.int32, (rows, CORE), 0)
    lane = lax.broadcasted_iota(jnp.int32, (rows, CORE), 1)
    hit = (row - first == lane - col) & (row >= first) & (row < first + count)
    return jnp.where(hit, 1.0, 0.0).astype(bf16)


def edges_of(rows, strip, extra=None):
    hi, lo = split(strip)
    both = []
    for col, more in ((CORE - WIDE, CORE - HALO), (0, 0)):
        pick = picker(rows, 0, WIDE, col)
        edge = dot_nt(pick, hi) + dot_nt(pick, lo)
        if extra is not None:
            edge = edge + dot_nt(picker(rows, WIDE, HALO, more), extra)
        both.append(edge)
    return both


def edges_kernel(both_ref, a_ref, b_ref):
    both = both_ref[...]
    target = jnp.where(both >= 2.0, 1.0, 0.0)
    mask = both - 2.0 * target
    send_edges(*edges_of(EDGE, mask, target.astype(bf16)), a_ref, b_ref)


def spectra_kernel(kern, w_ref, ker_ref, tb, h_ref, hs_ref):
    hs_ref[...] = jnp.zeros_like(hs_ref)
    for k in range(kern):
        for part in range(2):
            row = 32 * (2 * k + part)
            hs_ref[row : row + KSIZE, :KSIZE] = ker_ref[part, k, :, 0, :]
    s_hi, s_lo = split(hs_ref[...])
    z = dot3(tb("kx_hi"), tb("kx_lo"), s_hi, s_lo, dot_nt)
    z_hi, z_lo = split(z)
    for c in range(2 * kern):
        lanes = slice(128 * (c // 4), 128 * (c // 4) + 128)
        spec = dot3(z_hi[:, lanes], z_lo[:, lanes], tb(f"ky{c % 4}_hi"), tb(f"ky{c % 4}_lo"))
        root = jnp.sqrt(jnp.full((1, YB), w_ref[0, c // 2], f32))
        for j, comp in enumerate(signed(spec)):
            h_ref[c, j] = root * comp


def sides(last, from_a, from_b, tb):
    even = is_even()
    tile = lax.axis_index("tile")
    from_b = jnp.where((tile == 0) | (tile == last), 0.0, from_b)
    l_hi, l_lo = split(jnp.where(even, from_b, from_a))
    r_hi, r_lo = split(jnp.where(even, from_a, from_b))
    height = l_hi.shape[0]
    v = None
    for half, hi, lo in ((0, l_hi, l_lo), (1, r_hi, r_lo)):
        c_hi, c_lo = tb("cx_side_hi", half), tb("cx_side_lo", half)
        term = dot3(c_hi[:, :height], c_lo[:, :height], hi, lo)
        v = term if v is None else v + term
    return v, l_hi, r_hi


def to_spectrum(v, tb, f_ref, base):
    v_hi, v_lo = split(v)
    for t in range(2):
        spec = dot3(v_hi, v_lo, tb(f"by{t}_hi"), tb(f"by{t}_lo"))
        for j, comp in enumerate(signed(spec)):
            f_ref[t, j] = comp if base is None else base[t, j] - STEP_RATE * comp


def gradient_body(kern, last, f_ref, tgt_ref, h_ref, thr_ref, tb, g_ref, work):
    fld, inten, tot, a_hi, a_lo, b_cat, r_cat, w_cat = work
    group = 2 if kern % 2 == 0 else 1
    count = kern // group
    chains = [(t, c) for t in range(2) for c in range(count)]
    lag = count + 2

    def at(i):
        return chains[i] if 0 <= i < len(chains) else None

    tile = lax.axis_index("tile")
    first = jnp.where(tile == 0, WIDE, HALO) - ROW0
    end = jnp.where(tile == last, WIDE + CORE, WIDE + CORE + HALO) - ROW0
    row = lax.broadcasted_iota(jnp.int32, (ROWS, CORE), 0)
    inside = (row >= first) & (row < end)
    lane = lax.broadcasted_iota(jnp.int32, (1, 2 * YB), 1)
    bin_at = lax.rem(lane, YB)
    weight = jnp.where((bin_at == 0) | (bin_at == NU - 1), 1.0, 2.0) / (NX * NY)
    weight = jnp.where(lane < YB, weight, -weight)

    def chunks(height):
        return [slice(r, r + CHUNK) for r in range(0, height, CHUNK)]

    def put(ref, slot, starts, pieces):
        for at_row, piece in zip(starts, pieces):
            ref[slot, at_row : at_row + CHUNK] = piece

    def products(t, c, slot):
        for part in range(2 * group):
            for rows in chunks(XB):
                hpr, hpi, hmr, hmi = (h_ref[2 * group * c + part, j, rows] for j in range(4))
                fpr, fpi, fmr, fmi = (f_ref[t, j, rows] for j in range(4))
                pr, pi = hpr * fpr - hpi * fpi, hpr * fpi + hpi * fpr
                mr, mi = hmr * fmr - hmi * fmi, hmr * fmi + hmi * fmr
                starts = [2 * XB * part + rows.start, 2 * XB * part + XB + rows.start]
                top = split(jnp.concatenate([pr + mr, pi + mi], axis=1))
                low = split(jnp.concatenate([mi - pi, pr - mr], axis=1))
                put(a_hi, slot, starts, (top[0], low[0]))
                put(a_lo, slot, starts, (top[1], low[1]))

    def y_done(z_one, z_two, slot):
        for g in range(group):
            for rows in chunks(2 * XB):
                z = []
                for part in range(2 * g, 2 * g + 2):
                    here = slice(2 * XB * part + rows.start, 2 * XB * part + rows.stop)
                    z.append(z_one[here, :CORE] + (z_one[here, CORE:] + z_two[here]))
                z_hi, z_lo = split(jnp.concatenate(z, axis=1))
                starts = [2 * XB * j + rows.start for j in range(3)]
                put(b_cat, 2 * g + slot, starts, (z_hi, z_hi, z_lo))

    def field_of(t, c, slot):
        for g in range(group):
            k = group * c + g
            whole = dot(tb("x2"), b_cat[2 * g + slot])
            for rows in chunks(ROWS):
                field = whole[rows]
                fld[t, k, rows] = field
                re, im = field[:, :CORE], field[:, CORE:]
                power = re * re + im * im
                inten[t, rows] = power if k == 0 else inten[t, rows] + power

    def slope_of(t):
        resist = jax.nn.sigmoid(STEEPNESS * (inten[t] - thr_ref[0]))
        target = tgt_ref[:, CORE * t : CORE * t + CORE]
        slope = 2.0 * (resist - target) * STEEPNESS * resist * (1.0 - resist)
        inten[t] = jnp.where(inside, 2.0 * slope, 0.0)

    def scaled_field(t, c, slot):
        for g in range(group):
            for rows in chunks(ROWS):
                slope, field = inten[t, rows], fld[t, group * c + g, rows]
                r_hi, r_lo = split(
                    jnp.concatenate([slope * field[:, :CORE], slope * field[:, CORE:]], axis=1)
                )
                starts = [ROWS * j + rows.start for j in range(3)]
                put(r_cat, 2 * g + slot, starts, (r_hi, r_hi, r_lo))

    def x_back_done(w_now, g, slot):
        for rows in chunks(2 * XB):
            w_hi, w_lo = split(w_now[rows])
            for part in range(2):
                base = 2 * XB * (2 * g + part)
                here = slice(base + rows.start, base + rows.stop)
                lanes = slice(CORE * part, CORE * part + CORE)
                for j, piece in enumerate((w_hi, w_lo, w_hi)):
                    w_cat[slot, here, CORE * j : CORE * j + CORE] = piece[:, lanes]

    def add_back(t, c, slot):
        specs = dot(w_cat[slot], tb("y3"))
        for rows in chunks(XB):
            acc = [0.0] * 4 if c == 0 else [tot[t, j, rows] for j in range(4)]
            for part in range(2 * group):
                base = 2 * XB * part + rows.start
                cos_rows, sin_rows = slice(base, base + CHUNK), slice(base + XB, base + XB + CHUNK)
                cc, cs = specs[cos_rows, :YB], specs[cos_rows, YB:]
                sc, ss = specs[sin_rows, :YB], specs[sin_rows, YB:]
                bpr, neg, bmr, bmi = cc - ss, cs + sc, cc + ss, sc - cs
                hpr, hpi, hmr, hmi = (h_ref[2 * group * c + part, j, rows] for j in range(4))
                acc[0] = acc[0] + (hpr * bpr - hpi * neg)
                acc[1] = acc[1] - (hpr * neg + hpi * bpr)
                acc[2] = acc[2] + (hmr * bmr + hmi * bmi)
                acc[3] = acc[3] + (hmr * bmi - hmi * bmr)
            for j in range(4):
                tot[t, j, rows] = acc[j]

    def finish(t):
        r_hi, r_lo = split(even_odd(*(tot[t, j] for j in range(4))))
        u = dot(tb("x4"), jnp.concatenate([r_hi, r_hi, r_lo], axis=0))
        u_hi, u_lo = split(weight * u)
        term = dot3(tb(f"by{t}_hi"), tb(f"by{t}_lo"), u_hi, u_lo, dot_nt)
        g_ref[...] = term if t == 0 else g_ref[...] + term

    for i in range(len(chains) + lag + 2):
        new, mid, old = at(i), at(i - 1), at(i - 2)
        back, back_mid, back_old = at(i - lag), at(i - lag - 1), at(i - lag - 2)
        slot, other = i % 2, (i + 1) % 2
        if mid:
            z_one = dot(a_hi[other], tb("y2"))
            z_two = dot(a_lo[other], tb("y2", 0))
        if new:
            products(*new, slot)
        if back_mid:
            w_now = [dot(tb("x3"), r_cat[2 * g + other]) for g in range(group)]
        if back:
            scaled_field(*back, slot)
        if old:
            field_of(*old, slot)
        if back_old:
            add_back(*back_old, slot)
        if mid:
            y_done(z_one, z_two, other)
        if back_mid:
            for g in range(group):
                x_back_done(w_now[g], g, other)
        if old and old[1] == count - 1:
            slope_of(old[0])
        if back_old and back_old[1] == count - 1:
            finish(back_old[0])


def first_kernel(
    kern, last, thr_ref, mask_ref, target_ref, a_ref, b_ref, h_ref, tb,
    g_ref, f_ref, tgt_ref, *work,
):
    m_hi, m_lo = split(mask_ref[...])
    v, left, right = sides(last, a_ref[...], b_ref[...], tb)
    v = v + dot3(tb("cx_own_hi"), tb("cx_own_lo"), m_hi, m_lo, dot_nt)
    to_spectrum(v, tb, f_ref, None)
    tgt_ref[...] = (
        dot_nt(tb("sel_own"), target_ref[...].astype(f32).astype(bf16))
        + dot(tb("sel_halo", 0)[:, :EDGE], left)
        + dot(tb("sel_halo", 1)[:, :EDGE], right)
    )
    gradient_body(kern, last, f_ref, tgt_ref, h_ref, thr_ref, tb, g_ref, work)


def later_kernel(
    kern, last, thr_ref, mine_ref, peer_ref, a_ref, a2_ref, b_ref, b2_ref, f_in_ref, tgt_ref,
    h_ref, tb, g_ref, f_ref, *work,
):
    s_hi, s_lo = split(mine_ref[...] + peer_ref[...])
    from_a = a_ref[...] + a2_ref[...]
    from_b = b_ref[...] + b2_ref[...]
    v, _, _ = sides(last, from_a, from_b, tb)
    v = v + dot3(tb("cx_own_hi"), tb("cx_own_lo"), s_hi, s_lo, dot_nt)
    to_spectrum(v, tb, f_ref, f_in_ref)
    gradient_body(kern, last, f_ref, tgt_ref, h_ref, thr_ref, tb, g_ref, work)


def match(table_ref, own_ref, got_refs):
    device = lax.axis_index("tile")
    other = []
    for t in range(2):
        rows = slice(CORE * t, CORE * t + CORE)
        bit = lax.bitwise_xor(table_ref[t], 2 * device + t)
        value = jnp.where(bit == 1, own_ref[CORE * (1 - t) : CORE * (2 - t)], own_ref[rows])
        for b, got in enumerate(got_refs):
            value = jnp.where(bit == 2 << b, got[rows], value)
        other.append(value)
    row = lax.broadcasted_iota(jnp.int32, (CORE, CORE), 0)
    lane = lax.broadcasted_iota(jnp.int32, (CORE, CORE), 1)
    flip = jnp.where(row + lane == CORE - 1, 1.0, 0.0).astype(bf16)
    hi, lo = split(jnp.concatenate(other, axis=0))
    turned = dot(hi, flip) + dot(lo, flip)
    tiles = []
    for t in range(2):
        rows = slice(CORE * t, CORE * t + CORE)
        value = jnp.where(table_ref[2 + t] == 1, turned[rows], other[t])
        tiles.append(0.5 * (own_ref[rows] + value))
    return tiles


def match_kernel(n_got, table_ref, own_ref, *refs):
    got_refs, (out_ref, *edge_refs) = refs[:n_got], refs[n_got:]
    matched = jnp.concatenate(match(table_ref, own_ref, got_refs), axis=0)
    out_ref[...] = matched
    send_edges(*edges_of(WIDE_PAD, matched), *edge_refs)


def final_kernel(n_got, n_moves, table_ref, own_ref, *refs):
    got_refs, mask_ref, refs = refs[:n_got], refs[n_got], refs[n_got + 1 :]
    moves, (mask_out, grad_out) = refs[: 2 * n_moves], refs[2 * n_moves :]
    for t, step in enumerate(match(table_ref, own_ref, got_refs)):
        rows = slice(CORE * t, CORE * t + CORE)
        now = mask_ref[t]
        for mine, peer in zip(moves[::2], moves[1::2]):
            now = now - STEP_RATE * (mine[rows] + peer[rows])
        grad_out[t] = step
        mask_out[t] = now - STEP_RATE * step


def per_device(
    n_tile, n_depth, mask_tiles, target_tiles, kernels, socs_weights, thresholds,
    partner_table, mirror_flags,
):
    tiles_dev, core, _ = mask_tiles.shape
    kern = kernels.shape[2]
    assert tiles_dev == 2 and core == CORE
    pairs_a = [(i, i ^ 1) for i in range(n_tile)]
    pairs_b = [p for i in range(1, n_tile - 1, 2) for p in ((i, i + 1), (i + 1, i))]
    pairs_b += [(0, 0), (n_tile - 1, n_tile - 1)]

    def swap_edges(send_a, send_b, cross=False):
        def move(x, pairs):
            if not cross:
                return lax.ppermute(x, "tile", pairs)
            both = [(2 * i + p, 2 * j + 1 - p) for i, j in pairs for p in range(2)]
            return lax.ppermute(x, ("tile", "depth"), both)

        return move(send_b, pairs_b), move(send_a, pairs_a)

    def depth_pair(x):
        bit = 1
        while True:
            peer = lax.ppermute(x, "depth", [(i, i ^ bit) for i in range(n_depth)])
            bit *= 2
            if bit >= n_depth:
                return x, peer
            x = x + peer

    def from_partners(grad):
        bits = [1 << b for b in range(n_tile.bit_length() - 1)]
        got = [
            lax.ppermute(grad, "tile", [(i, i ^ bit) for i in range(n_tile)])
            for bit in reversed(bits)
        ]
        return got[::-1]

    mask_rows = mask_tiles.reshape(tiles_dev * core, core)
    target_rows = target_tiles.reshape(tiles_dev * core, core)
    strip = jax.ShapeDtypeStruct((tiles_dev * core, core), f32)
    side = jax.ShapeDtypeStruct((WIDE_PAD, tiles_dev * core), f32)
    freq = jax.ShapeDtypeStruct((2, 4, XB, YB), f32)
    goal = jax.ShapeDtypeStruct((ROWS, 2 * CORE), f32)
    tiles = jax.ShapeDtypeStruct((tiles_dev, core, core), f32)
    group = 2 if kern % 2 == 0 else 1
    scratch = [
        pltpu.VMEM((2, kern, ROWS, 2 * CORE), f32),
        pltpu.VMEM((2, ROWS, CORE), f32),
        pltpu.VMEM((2, 4, XB, YB), f32),
        pltpu.VMEM((2, group * 4 * XB, 2 * YB), bf16),
        pltpu.VMEM((2, group * 4 * XB, 2 * YB), bf16),
        pltpu.VMEM((2 * group, 6 * XB, 2 * CORE), bf16),
        pltpu.VMEM((2 * group, 3 * ROWS, 2 * CORE), bf16),
        pltpu.VMEM((2, group * 4 * XB, 3 * CORE), bf16),
    ]

    edge = jax.ShapeDtypeStruct((EDGE, tiles_dev * core), f32)
    send_a, send_b = call(
        edges_kernel,
        None,
        [mask_rows + 2.0 * target_rows.astype(f32)],
        [edge, edge],
        flops=3 * 10**9,
    )
    from_b, from_a = swap_edges(send_a, send_b)
    table = jnp.concatenate([partner_table, mirror_flags])
    (spectra,) = call(
        functools.partial(spectra_kernel, kern),
        "spec",
        [socs_weights, kernels.transpose(0, 2, 3, 1, 4)],
        [jax.ShapeDtypeStruct((2 * kern, 4, XB, YB), f32)],
        [pltpu.VMEM((32 * 2 * kern, 128), f32)],
        smem=(0,),
        flops=3 * 10**9,
        nbytes=4 * 10**6,
    )
    grad, freq_now, goals = call(
        functools.partial(first_kernel, kern, n_tile - 1),
        "grad",
        [thresholds, mask_rows, target_rows, from_a, from_b, spectra],
        [strip, freq, goal],
        scratch,
        smem=(0,),
        flops=10**10,
    )
    moves = []
    for step in range(1, STEPS):
        got = from_partners(grad)
        move, *edges = call(
            functools.partial(match_kernel, len(got)),
            None,
            [table, grad, *got],
            [strip, side, side],
            smem=(0,),
        )
        from_b, from_a = swap_edges(*edges)
        if n_depth == 2:
            far_b, far_a = swap_edges(*edges, cross=True)
            rims = (from_a, far_a, from_b, far_b)
        else:
            rims = depth_pair(from_a) + depth_pair(from_b)
        moves += depth_pair(move)
        kept = step + 1 < STEPS
        grad, *rest = call(
            functools.partial(later_kernel, kern, n_tile - 1),
            "grad",
            [thresholds, *moves[-2:], *rims, freq_now, goals, spectra],
            [strip, freq] if kept else [strip],
            scratch if kept else [pltpu.VMEM(freq.shape, f32)] + scratch,
            smem=(0,),
            flops=10**10,
        )
        freq_now = rest[0] if kept else None
    mine, peer = depth_pair(grad)
    total = mine + peer
    got = from_partners(total)
    final = functools.partial(final_kernel, len(got), len(moves) // 2)
    args = [table, total, *got, mask_tiles, *moves]
    return tuple(call(final, None, args, [tiles, tiles], smem=(0,)))


def solution(mesh):
    return jax.shard_map(
        functools.partial(per_device, mesh.shape["tile"], mesh.shape["depth"]),
        mesh=mesh,
        in_specs=(
            P("tile", None, None),
            P("tile", None, None),
            P(None, "depth", None, None, None),
            P("depth", None),
            P("depth"),
            P("tile"),
            P("tile"),
        ),
        out_specs=(P("tile", None, None), P("tile", None, None)),
        check_vma=False,
    )
```

```python
import functools

import jax
import jax.numpy as jnp
import ml_dtypes
import numpy as np
from jax import lax
from jax.experimental import pallas as pl
from jax.experimental.pallas import tpu as pltpu
from jax.sharding import PartitionSpec as P

HALO = 12
KSIZE = 25
STEPS = 2
STEEPNESS = 3.0
STEP_RATE = 0.05

CORE = 128
NY = 152
NX = 176
WIDE = 2 * HALO
XB = 88
YB = 128
NU = NY // 2 + 1
ROWS = 160
ROW0 = 8
CHUNK = 16
EDGE = 48
WIDE_PAD = 32
VMEM_LIMIT = 24 * 1024 * 1024

f32 = jnp.float32
bf16 = jnp.bfloat16


def np_split(a):
    hi = np.asarray(a, np.float32).astype(ml_dtypes.bfloat16)
    lo = (np.asarray(a, np.float64) - hi.astype(np.float64)).astype(ml_dtypes.bfloat16)
    return hi, lo


def x_rows(cols):
    ang = 2 * np.pi * np.outer(np.arange(XB + 1), cols) / NX
    out = np.concatenate([np.cos(ang[:XB]), np.sin(ang[:XB])])
    out[XB] = np.cos(ang[XB])
    return out


def y_lanes(rows):
    out = np.zeros((len(rows), 2 * YB))
    ang = 2 * np.pi * np.outer(rows, np.arange(NU)) / NY
    out[:, :NU] = np.cos(ang)
    out[:, YB : YB + NU] = np.sin(ang)
    out[:, YB] = 0.0
    out[:, YB + NU - 1] = 0.0
    return out


def half_weights(bins):
    weights = np.full(bins, 2.0)
    weights[0] = weights[-1] = 1.0
    return weights


def x_back(cols):
    out = x_rows(cols).T
    sign = 1 - 2.0 * (np.asarray(cols) % 2)
    out[:, 0] = (1 + sign) / 2
    out[:, XB] = (1 - sign) / 2
    return out


def y_back(rows):
    weight = np.zeros(2 * YB)
    weight[:NU] = half_weights(NU)
    weight[YB : YB + NU] = -half_weights(NU)
    return (y_lanes(rows) * weight).T / (NX * NY)


def pack(parts):
    rows, where, at = [], {}, 0
    pieces = []
    for name, a in parts:
        if a.shape[1] <= 256:
            pieces.append((name, a))
            continue
        cuts = range(0, a.shape[1], 256)
        where[name] = len(cuts)
        pieces += [(f"{name}.{i}", a[:, c : c + 256]) for i, c in enumerate(cuts)]
    for name, a in pieces:
        height = -(-a.shape[0] // 16) * 16
        block = np.zeros((height, 256), np.float64)
        block[: a.shape[0], : a.shape[1]] = a
        rows.append(block)
        where[name] = (at, a.shape[0], a.shape[1])
        at += height
    return np.concatenate(rows), where


def pack_split(parts):
    both = []
    for name, a in parts:
        hi, lo = np_split(a)
        if name in ("x2", "x3", "x4"):
            hi, lo = hi.astype(np.float64), lo.astype(np.float64)
            both.append((name, np.concatenate([hi, lo, hi], axis=1)))
            continue
        both += [(name + "_hi", hi.astype(np.float64)), (name + "_lo", lo.astype(np.float64))]
    return both


@functools.lru_cache(None)
def tables():
    core_rows = np.arange(HALO, HALO + CORE)
    field_cols = np.arange(ROW0, ROW0 + ROWS)
    own_cols = np.arange(WIDE, WIDE + CORE)
    sides = np.zeros((2 * XB, 256))
    sides[:, :WIDE] = x_rows(np.arange(WIDE))
    sides[:, CORE : CORE + WIDE] = x_rows(np.arange(WIDE + CORE, NX))
    parts = [("cx_own", x_rows(own_cols)), ("cx_side", sides)]
    for t in range(2):
        pos = np.arange(2 * CORE) - t * CORE + HALO
        inside = (pos >= 0) & (pos < NY)
        parts.append((f"by{t}", y_lanes(pos) * inside[:, None]))
    parts += [("x2", x_back(field_cols)), ("x3", x_rows(field_cols)), ("x4", x_back(own_cols))]
    y2_hi, y2_lo = (a.astype(np.float64) for a in np_split(y_back(core_rows)))
    y3_hi, y3_lo = (a.astype(np.float64) for a in np_split(y_lanes(core_rows)))
    grad = pack_split(parts)
    grad += [("y2", np.concatenate([y2_hi, y2_lo], axis=1))]
    grad += [("y3", np.concatenate([y3_hi, y3_hi, y3_lo]))]
    own = np.zeros((ROWS, CORE))
    own[np.arange(CORE) + WIDE - ROW0, np.arange(CORE)] = 1
    halo = np.zeros((ROWS, 256))
    for r in range(HALO):
        halo[HALO + r - ROW0, WIDE + r] = 1
        halo[WIDE + CORE + r - ROW0, CORE + WIDE + r] = 1
    grad += [("sel_own", own), ("sel_halo", halo)]
    offs = np.arange(KSIZE) - HALO
    kx = np.zeros((2 * XB, 128))
    kx[:, :KSIZE] = x_rows(offs)
    spec = [("kx", kx)]
    for m in range(4):
        ky = np.zeros((128, 2 * YB))
        ky[32 * m : 32 * m + KSIZE] = y_lanes(offs)
        spec.append((f"ky{m}", ky))
    return {"grad": pack(grad), "spec": pack(pack_split(spec))}


def split(x):
    hi = x.astype(bf16)
    return hi, (x - hi.astype(f32)).astype(bf16)


def dot(a, b):
    return lax.dot_general(a, b, (((1,), (0,)), ((), ())), preferred_element_type=f32)


def dot_nt(a, b):
    return lax.dot_general(a, b, (((1,), (1,)), ((), ())), preferred_element_type=f32)


def dot3(a_hi, a_lo, b_hi, b_lo, mul=dot):
    return mul(a_hi, b_hi) + (mul(a_lo, b_hi) + mul(a_hi, b_lo))


def top_row(like):
    return lax.broadcasted_iota(jnp.int32, like.shape, 0) == 0


def signed_parts(cc, cs, sc, ss, special):
    out = cc - ss, cs + sc, cc + ss, sc - cs
    if special:
        row0 = top_row(cc)
        out = [jnp.where(row0, x, y) for x, y in zip((cc, cs, sc, -ss), out)]
    return out


def signed(spec):
    parts = (spec[:XB, :YB], spec[:XB, YB:], spec[XB:, :YB], spec[XB:, YB:])
    pr, neg, mr, mi = signed_parts(*parts, True)
    return pr, -neg, mr, mi


def even_odd(pr, pi, mr, mi, special=True):
    top = jnp.concatenate([pr + mr, pi + mi], axis=1)
    low = jnp.concatenate([mi - pi, pr - mr], axis=1)
    if special:
        low = jnp.where(top_row(low), jnp.concatenate([pr - mr, pi - mi], axis=1), low)
    return top, low


def table_array(group):
    return jnp.asarray(tables()[group][0].astype(ml_dtypes.bfloat16))


def table_reader(group, ref):
    where = tables()[group][1]

    def table(name, half=None):
        if isinstance(where[name], int):
            return jnp.concatenate([table(f"{name}.{i}") for i in range(where[name])], axis=1)
        at, height, width = where[name]
        lanes = slice(0, width) if half is None else slice(128 * half, 128 * half + 128)
        return ref[at : at + height, lanes]

    return table


def call(body, group, args, out_shape, scratch=(), smem=(), flops=0, nbytes=0):
    vm = pl.BlockSpec(memory_space=pltpu.VMEM)
    sm = pl.BlockSpec(memory_space=pltpu.SMEM)
    n_in = len(args)
    if group is not None:
        args = [*args, table_array(group)]

    def wrapped(*refs):
        if group is not None:
            refs = [*refs[:n_in], table_reader(group, refs[n_in]), *refs[n_in + 1 :]]
        body(*refs)

    return pl.pallas_call(
        wrapped,
        out_shape=out_shape,
        in_specs=[sm if i in smem else vm for i in range(len(args))],
        out_specs=[vm] * len(out_shape),
        scratch_shapes=list(scratch),
        compiler_params=pltpu.CompilerParams(vmem_limit_bytes=VMEM_LIMIT),
        cost_estimate=pl.CostEstimate(flops=flops, bytes_accessed=nbytes, transcendentals=0),
    )(*args)


def is_even():
    return lax.rem(lax.axis_index("tile"), 2) == 0


def send_edges(right, left, a_ref, b_ref):
    even = is_even()
    a_ref[...] = jnp.where(even, right, left)
    b_ref[...] = jnp.where(even, left, right)


def picker(rows, first, count, col):
    row = lax.broadcasted_iota(jnp.int32, (rows, CORE), 0)
    lane = lax.broadcasted_iota(jnp.int32, (rows, CORE), 1)
    hit = (row - first == lane - col) & (row >= first) & (row < first + count)
    return jnp.where(hit, 1.0, 0.0).astype(bf16)


def edges_of(rows, strip, extra=None):
    hi, lo = split(strip)
    both = []
    for col, more in ((CORE - WIDE, CORE - HALO), (0, 0)):
        pick = picker(rows, 0, WIDE, col)
        edge = dot_nt(pick, hi) + dot_nt(pick, lo)
        if extra is not None:
            edge = edge + dot_nt(picker(rows, WIDE, HALO, more), extra)
        both.append(edge)
    return both


def edges_kernel(both_ref, a_ref, b_ref):
    both = both_ref[...]
    target = jnp.where(both >= 2.0, 1.0, 0.0)
    mask = both - 2.0 * target
    send_edges(*edges_of(EDGE, mask, target.astype(bf16)), a_ref, b_ref)


def spectra_kernel(kern, w_ref, ker_ref, tb, h_ref, hs_ref):
    hs_ref[...] = jnp.zeros_like(hs_ref)
    for k in range(kern):
        for part in range(2):
            row = 32 * (2 * k + part)
            hs_ref[row : row + KSIZE, :KSIZE] = ker_ref[part, k, :, 0, :]
    s_hi, s_lo = split(hs_ref[...])
    z = dot3(tb("kx_hi"), tb("kx_lo"), s_hi, s_lo, dot_nt)
    z_hi, z_lo = split(z)
    for c in range(2 * kern):
        lanes = slice(128 * (c // 4), 128 * (c // 4) + 128)
        spec = dot3(z_hi[:, lanes], z_lo[:, lanes], tb(f"ky{c % 4}_hi"), tb(f"ky{c % 4}_lo"))
        root = jnp.sqrt(jnp.full((1, YB), w_ref[0, c // 2], f32))
        for j, comp in enumerate(signed(spec)):
            h_ref[c, j] = root * comp


def sides(last, from_a, from_b, tb):
    even = is_even()
    tile = lax.axis_index("tile")
    from_b = jnp.where((tile == 0) | (tile == last), 0.0, from_b)
    l_hi, l_lo = split(jnp.where(even, from_b, from_a))
    r_hi, r_lo = split(jnp.where(even, from_a, from_b))
    height = l_hi.shape[0]
    v = None
    for half, hi, lo in ((0, l_hi, l_lo), (1, r_hi, r_lo)):
        c_hi, c_lo = tb("cx_side_hi", half), tb("cx_side_lo", half)
        term = dot3(c_hi[:, :height], c_lo[:, :height], hi, lo)
        v = term if v is None else v + term
    return v, l_hi, r_hi


def to_spectrum(v, tb, f_ref, base):
    v_hi, v_lo = split(v)
    for t in range(2):
        spec = dot3(v_hi, v_lo, tb(f"by{t}_hi"), tb(f"by{t}_lo"))
        for j, comp in enumerate(signed(spec)):
            f_ref[t, j] = comp if base is None else base[t, j] - STEP_RATE * comp


def gradient_body(kern, last, f_ref, tgt_ref, h_ref, thr_ref, tb, g_ref, work):
    fld, inten, tot, a_hi, a_lo, b_cat, r_cat, w_cat = work
    group = 2 if kern % 2 == 0 else 1
    count = kern // group
    chains = [(t, c) for t in range(2) for c in range(count)]
    lag = count + 2

    def at(i):
        return chains[i] if 0 <= i < len(chains) else None

    tile = lax.axis_index("tile")
    first = jnp.where(tile == 0, WIDE, HALO) - ROW0
    end = jnp.where(tile == last, WIDE + CORE, WIDE + CORE + HALO) - ROW0
    row = lax.broadcasted_iota(jnp.int32, (ROWS, CORE), 0)
    inside = (row >= first) & (row < end)
    lane = lax.broadcasted_iota(jnp.int32, (1, 2 * YB), 1)
    bin_at = lax.rem(lane, YB)
    weight = jnp.where((bin_at == 0) | (bin_at == NU - 1), 1.0, 2.0) / (NX * NY)
    weight = jnp.where(lane < YB, weight, -weight)

    def chunks(height):
        return [slice(r, r + CHUNK) for r in range(0, height, CHUNK)]

    def put(ref, slot, starts, pieces):
        for at_row, piece in zip(starts, pieces):
            ref[slot, at_row : at_row + CHUNK] = piece

    def products(t, c, slot):
        for part in range(2 * group):

            def pieces(start, height):
                rows = slice(start, start + height)
                hpr, hpi, hmr, hmi = (h_ref[2 * group * c + part, j, rows] for j in range(4))
                fpr, fpi, fmr, fmi = (f_ref[t, j, rows] for j in range(4))
                pr, pi = hpr * fpr - hpi * fpi, hpr * fpi + hpi * fpr
                mr, mi = hmr * fmr - hmi * fmi, hmr * fmi + hmi * fmr
                return even_odd(pr, pi, mr, mi, start == 0)

            def store(start, value):
                p_hi, p_lo = split(value)
                put(a_hi, slot, [2 * XB * part + start], [p_hi])
                put(a_lo, slot, [2 * XB * part + start], [p_lo])

            carry, last_low = pieces(XB - 8, 8)
            for start in range(0, XB - 8, CHUNK):
                top, low = pieces(start, CHUNK)
                store(start, top)
                store(XB - 8 + start, jnp.concatenate([carry, low[:8]], axis=0))
                carry = low[8:]
            store(2 * XB - CHUNK, jnp.concatenate([carry, last_low], axis=0))

    def y_done(z_one, z_two, slot):
        for g in range(group):
            for rows in chunks(2 * XB):
                z = []
                for part in range(2 * g, 2 * g + 2):
                    here = slice(2 * XB * part + rows.start, 2 * XB * part + rows.stop)
                    z.append(z_one[here, :CORE] + (z_one[here, CORE:] + z_two[here]))
                z_hi, z_lo = split(jnp.concatenate(z, axis=1))
                starts = [2 * XB * j + rows.start for j in range(3)]
                put(b_cat, 2 * g + slot, starts, (z_hi, z_hi, z_lo))

    def field_of(t, c, slot):
        for g in range(group):
            k = group * c + g
            whole = dot(tb("x2"), b_cat[2 * g + slot])
            for rows in chunks(ROWS):
                field = whole[rows]
                fld[t, k, rows] = field
                re, im = field[:, :CORE], field[:, CORE:]
                power = re * re + im * im
                inten[t, rows] = power if k == 0 else inten[t, rows] + power

    def slope_of(t):
        resist = jax.nn.sigmoid(STEEPNESS * (inten[t] - thr_ref[0]))
        target = tgt_ref[:, CORE * t : CORE * t + CORE]
        slope = 2.0 * (resist - target) * STEEPNESS * resist * (1.0 - resist)
        inten[t] = jnp.where(inside, 2.0 * slope, 0.0)

    def scaled_field(t, c, slot):
        for g in range(group):
            for rows in chunks(ROWS):
                slope, field = inten[t, rows], fld[t, group * c + g, rows]
                r_hi, r_lo = split(
                    jnp.concatenate([slope * field[:, :CORE], slope * field[:, CORE:]], axis=1)
                )
                starts = [ROWS * j + rows.start for j in range(3)]
                put(r_cat, 2 * g + slot, starts, (r_hi, r_hi, r_lo))

    def x_back_done(w_now, g, slot):
        for rows in chunks(2 * XB):
            w_hi, w_lo = split(w_now[rows])
            for part in range(2):
                base = 2 * XB * (2 * g + part)
                here = slice(base + rows.start, base + rows.stop)
                lanes = slice(CORE * part, CORE * part + CORE)
                for j, piece in enumerate((w_hi, w_lo, w_hi)):
                    w_cat[slot, here, CORE * j : CORE * j + CORE] = piece[:, lanes]

    def add_back(t, c, slot):
        specs = dot(w_cat[slot], tb("y3"))
        for start in range(0, XB, 8):
            rows = slice(start, start + 8)
            acc = [0.0] * 4 if c == 0 else [tot[t, j, rows] for j in range(4)]
            for part in range(2 * group):
                base = 2 * XB * part + start
                cos, sin = specs[base : base + 8], specs[base + XB : base + XB + 8]
                bpr, neg, bmr, bmi = signed_parts(
                    cos[:, :YB], cos[:, YB:], sin[:, :YB], sin[:, YB:], start == 0
                )
                hpr, hpi, hmr, hmi = (h_ref[2 * group * c + part, j, rows] for j in range(4))
                acc[0] = acc[0] + (hpr * bpr - hpi * neg)
                acc[1] = acc[1] - (hpr * neg + hpi * bpr)
                acc[2] = acc[2] + (hmr * bmr + hmi * bmi)
                acc[3] = acc[3] + (hmr * bmi - hmi * bmr)
            for j in range(4):
                tot[t, j, rows] = acc[j]

    def finish(t):
        sums = even_odd(*(tot[t, j] for j in range(4)))
        r_hi, r_lo = split(jnp.concatenate(sums, axis=0))
        u = dot(tb("x4"), jnp.concatenate([r_hi, r_hi, r_lo], axis=0))
        u_hi, u_lo = split(weight * u)
        term = dot3(tb(f"by{t}_hi"), tb(f"by{t}_lo"), u_hi, u_lo, dot_nt)
        g_ref[...] = term if t == 0 else g_ref[...] + term

    for i in range(len(chains) + lag + 2):
        new, mid, old = at(i), at(i - 1), at(i - 2)
        back, back_mid, back_old = at(i - lag), at(i - lag - 1), at(i - lag - 2)
        slot, other = i % 2, (i + 1) % 2
        if mid:
            z_one = dot(a_hi[other], tb("y2"))
            z_two = dot(a_lo[other], tb("y2", 0))
        if new:
            products(*new, slot)
        if back_mid:
            w_now = [dot(tb("x3"), r_cat[2 * g + other]) for g in range(group)]
        if back:
            scaled_field(*back, slot)
        if old:
            field_of(*old, slot)
        if back_old:
            add_back(*back_old, slot)
        if mid:
            y_done(z_one, z_two, other)
        if back_mid:
            for g in range(group):
                x_back_done(w_now[g], g, other)
        if old and old[1] == count - 1:
            slope_of(old[0])
        if back_old and back_old[1] == count - 1:
            finish(back_old[0])


def first_kernel(
    kern, last, thr_ref, mask_ref, target_ref, a_ref, b_ref, h_ref, tb,
    g_ref, f_ref, tgt_ref, *work,
):
    m_hi, m_lo = split(mask_ref[...])
    v, left, right = sides(last, a_ref[...], b_ref[...], tb)
    v = v + dot3(tb("cx_own_hi"), tb("cx_own_lo"), m_hi, m_lo, dot_nt)
    to_spectrum(v, tb, f_ref, None)
    tgt_ref[...] = (
        dot_nt(tb("sel_own"), target_ref[...].astype(f32).astype(bf16))
        + dot(tb("sel_halo", 0)[:, :EDGE], left)
        + dot(tb("sel_halo", 1)[:, :EDGE], right)
    )
    gradient_body(kern, last, f_ref, tgt_ref, h_ref, thr_ref, tb, g_ref, work)


def later_kernel(
    kern, last, thr_ref, mine_ref, peer_ref, a_ref, a2_ref, b_ref, b2_ref, f_in_ref, tgt_ref,
    h_ref, tb, g_ref, f_ref, *work,
):
    s_hi, s_lo = split(mine_ref[...] + peer_ref[...])
    from_a = a_ref[...] + a2_ref[...]
    from_b = b_ref[...] + b2_ref[...]
    v, _, _ = sides(last, from_a, from_b, tb)
    v = v + dot3(tb("cx_own_hi"), tb("cx_own_lo"), s_hi, s_lo, dot_nt)
    to_spectrum(v, tb, f_ref, f_in_ref)
    gradient_body(kern, last, f_ref, tgt_ref, h_ref, thr_ref, tb, g_ref, work)


def match(table_ref, own_ref, got_refs):
    device = lax.axis_index("tile")
    other = []
    for t in range(2):
        rows = slice(CORE * t, CORE * t + CORE)
        bit = lax.bitwise_xor(table_ref[t], 2 * device + t)
        value = jnp.where(bit == 1, own_ref[CORE * (1 - t) : CORE * (2 - t)], own_ref[rows])
        for b, got in enumerate(got_refs):
            value = jnp.where(bit == 2 << b, got[rows], value)
        other.append(value)
    row = lax.broadcasted_iota(jnp.int32, (CORE, CORE), 0)
    lane = lax.broadcasted_iota(jnp.int32, (CORE, CORE), 1)
    flip = jnp.where(row + lane == CORE - 1, 1.0, 0.0).astype(bf16)
    hi, lo = split(jnp.concatenate(other, axis=0))
    turned = dot(hi, flip) + dot(lo, flip)
    tiles = []
    for t in range(2):
        rows = slice(CORE * t, CORE * t + CORE)
        value = jnp.where(table_ref[2 + t] == 1, turned[rows], other[t])
        tiles.append(0.5 * (own_ref[rows] + value))
    return tiles


def match_kernel(n_got, table_ref, own_ref, *refs):
    got_refs, (out_ref, *edge_refs) = refs[:n_got], refs[n_got:]
    matched = jnp.concatenate(match(table_ref, own_ref, got_refs), axis=0)
    out_ref[...] = matched
    send_edges(*edges_of(WIDE_PAD, matched), *edge_refs)


def final_kernel(n_got, n_moves, table_ref, own_ref, *refs):
    got_refs, mask_ref, refs = refs[:n_got], refs[n_got], refs[n_got + 1 :]
    moves, (mask_out, grad_out) = refs[: 2 * n_moves], refs[2 * n_moves :]
    for t, step in enumerate(match(table_ref, own_ref, got_refs)):
        rows = slice(CORE * t, CORE * t + CORE)
        now = mask_ref[t]
        for mine, peer in zip(moves[::2], moves[1::2]):
            now = now - STEP_RATE * (mine[rows] + peer[rows])
        grad_out[t] = step
        mask_out[t] = now - STEP_RATE * step


def per_device(
    n_tile, n_depth, mask_tiles, target_tiles, kernels, socs_weights, thresholds,
    partner_table, mirror_flags,
):
    tiles_dev, core, _ = mask_tiles.shape
    kern = kernels.shape[2]
    assert tiles_dev == 2 and core == CORE
    pairs_a = [(i, i ^ 1) for i in range(n_tile)]
    pairs_b = [p for i in range(1, n_tile - 1, 2) for p in ((i, i + 1), (i + 1, i))]
    pairs_b += [(0, 0), (n_tile - 1, n_tile - 1)]

    def swap_edges(send_a, send_b, cross=False):
        def move(x, pairs):
            if not cross:
                return lax.ppermute(x, "tile", pairs)
            both = [(2 * i + p, 2 * j + 1 - p) for i, j in pairs for p in range(2)]
            return lax.ppermute(x, ("tile", "depth"), both)

        return move(send_b, pairs_b), move(send_a, pairs_a)

    def depth_pair(x):
        bit = 1
        while True:
            peer = lax.ppermute(x, "depth", [(i, i ^ bit) for i in range(n_depth)])
            bit *= 2
            if bit >= n_depth:
                return x, peer
            x = x + peer

    def from_partners(grad):
        bits = [1 << b for b in range(n_tile.bit_length() - 1)]
        got = [
            lax.ppermute(grad, "tile", [(i, i ^ bit) for i in range(n_tile)])
            for bit in reversed(bits)
        ]
        return got[::-1]

    mask_rows = mask_tiles.reshape(tiles_dev * core, core)
    target_rows = target_tiles.reshape(tiles_dev * core, core)
    strip = jax.ShapeDtypeStruct((tiles_dev * core, core), f32)
    side = jax.ShapeDtypeStruct((WIDE_PAD, tiles_dev * core), f32)
    freq = jax.ShapeDtypeStruct((2, 4, XB, YB), f32)
    goal = jax.ShapeDtypeStruct((ROWS, 2 * CORE), f32)
    tiles = jax.ShapeDtypeStruct((tiles_dev, core, core), f32)
    group = 2 if kern % 2 == 0 else 1
    scratch = [
        pltpu.VMEM((2, kern, ROWS, 2 * CORE), f32),
        pltpu.VMEM((2, ROWS, CORE), f32),
        pltpu.VMEM((2, 4, XB, YB), f32),
        pltpu.VMEM((2, group * 4 * XB, 2 * YB), bf16),
        pltpu.VMEM((2, group * 4 * XB, 2 * YB), bf16),
        pltpu.VMEM((2 * group, 6 * XB, 2 * CORE), bf16),
        pltpu.VMEM((2 * group, 3 * ROWS, 2 * CORE), bf16),
        pltpu.VMEM((2, group * 4 * XB, 3 * CORE), bf16),
    ]

    edge = jax.ShapeDtypeStruct((EDGE, tiles_dev * core), f32)
    send_a, send_b = call(
        edges_kernel,
        None,
        [mask_rows + 2.0 * target_rows.astype(f32)],
        [edge, edge],
        flops=3 * 10**9,
    )
    from_b, from_a = swap_edges(send_a, send_b)
    table = jnp.concatenate([partner_table, mirror_flags])
    (spectra,) = call(
        functools.partial(spectra_kernel, kern),
        "spec",
        [socs_weights, kernels.transpose(0, 2, 3, 1, 4)],
        [jax.ShapeDtypeStruct((2 * kern, 4, XB, YB), f32)],
        [pltpu.VMEM((32 * 2 * kern, 128), f32)],
        smem=(0,),
        flops=3 * 10**9,
        nbytes=4 * 10**6,
    )
    grad, freq_now, goals = call(
        functools.partial(first_kernel, kern, n_tile - 1),
        "grad",
        [thresholds, mask_rows, target_rows, from_a, from_b, spectra],
        [strip, freq, goal],
        scratch,
        smem=(0,),
        flops=10**10,
    )
    moves = []
    for step in range(1, STEPS):
        got = from_partners(grad)
        move, *edges = call(
            functools.partial(match_kernel, len(got)),
            None,
            [table, grad, *got],
            [strip, side, side],
            smem=(0,),
        )
        from_b, from_a = swap_edges(*edges)
        if n_depth == 2:
            far_b, far_a = swap_edges(*edges, cross=True)
            rims = (from_a, far_a, from_b, far_b)
        else:
            rims = depth_pair(from_a) + depth_pair(from_b)
        moves += depth_pair(move)
        kept = step + 1 < STEPS
        grad, *rest = call(
            functools.partial(later_kernel, kern, n_tile - 1),
            "grad",
            [thresholds, *moves[-2:], *rims, freq_now, goals, spectra],
            [strip, freq] if kept else [strip],
            scratch if kept else [pltpu.VMEM(freq.shape, f32)] + scratch,
            smem=(0,),
            flops=10**10,
        )
        freq_now = rest[0] if kept else None
    mine, peer = depth_pair(grad)
    total = mine + peer
    got = from_partners(total)
    final = functools.partial(final_kernel, len(got), len(moves) // 2)
    args = [table, total, *got, mask_tiles, *moves]
    return tuple(call(final, None, args, [tiles, tiles], smem=(0,)))


def solution(mesh):
    return jax.shard_map(
        functools.partial(per_device, mesh.shape["tile"], mesh.shape["depth"]),
        mesh=mesh,
        in_specs=(
            P("tile", None, None),
            P("tile", None, None),
            P(None, "depth", None, None, None),
            P("depth", None),
            P("depth"),
            P("tile"),
            P("tile"),
        ),
        out_specs=(P("tile", None, None), P("tile", None, None)),
        check_vma=False,
    )
```

```python
import functools

import jax
import jax.numpy as jnp
import ml_dtypes
import numpy as np
from jax import lax
from jax.experimental import pallas as pl
from jax.experimental.pallas import tpu as pltpu
from jax.sharding import PartitionSpec as P

HALO = 12
KSIZE = 25
STEPS = 2
STEEPNESS = 3.0
STEP_RATE = 0.05

CORE = 128
NY = 152
NX = 176
WIDE = 2 * HALO
XB = 88
YB = 128
NU = NY // 2 + 1
ROWS = 160
ROW0 = 8
CHUNK = 16
EDGE = 48
WIDE_PAD = 32
VMEM_LIMIT = 24 * 1024 * 1024

f32 = jnp.float32
bf16 = jnp.bfloat16


def np_split(a):
    hi = np.asarray(a, np.float32).astype(ml_dtypes.bfloat16)
    lo = (np.asarray(a, np.float64) - hi.astype(np.float64)).astype(ml_dtypes.bfloat16)
    return hi, lo


def x_rows(cols):
    ang = 2 * np.pi * np.outer(np.arange(XB + 1), cols) / NX
    out = np.concatenate([np.cos(ang[:XB]), np.sin(ang[:XB])])
    out[XB] = np.cos(ang[XB])
    return out


def y_lanes(rows):
    out = np.zeros((len(rows), 2 * YB))
    ang = 2 * np.pi * np.outer(rows, np.arange(NU)) / NY
    out[:, :NU] = np.cos(ang)
    out[:, YB : YB + NU] = np.sin(ang)
    out[:, YB] = 0.0
    out[:, YB + NU - 1] = 0.0
    return out


def half_weights(bins):
    weights = np.full(bins, 2.0)
    weights[0] = weights[-1] = 1.0
    return weights


def x_back(cols):
    out = x_rows(cols).T
    sign = 1 - 2.0 * (np.asarray(cols) % 2)
    out[:, 0] = (1 + sign) / 2
    out[:, XB] = (1 - sign) / 2
    return out


def y_back(rows):
    weight = np.zeros(2 * YB)
    weight[:NU] = half_weights(NU)
    weight[YB : YB + NU] = -half_weights(NU)
    return (y_lanes(rows) * weight).T / (NX * NY)


def pack(parts):
    rows, where, at = [], {}, 0
    pieces = []
    for name, a in parts:
        if a.shape[1] <= 256:
            pieces.append((name, a))
            continue
        cuts = range(0, a.shape[1], 256)
        where[name] = len(cuts)
        pieces += [(f"{name}.{i}", a[:, c : c + 256]) for i, c in enumerate(cuts)]
    for name, a in pieces:
        height = -(-a.shape[0] // 16) * 16
        block = np.zeros((height, 256), np.float64)
        block[: a.shape[0], : a.shape[1]] = a
        rows.append(block)
        where[name] = (at, a.shape[0], a.shape[1])
        at += height
    return np.concatenate(rows), where


def pack_split(parts):
    both = []
    for name, a in parts:
        hi, lo = np_split(a)
        if name in ("x2", "x3", "x4"):
            hi, lo = hi.astype(np.float64), lo.astype(np.float64)
            both.append((name, np.concatenate([hi, lo, hi], axis=1)))
            continue
        both += [(name + "_hi", hi.astype(np.float64)), (name + "_lo", lo.astype(np.float64))]
    return both


@functools.lru_cache(None)
def tables():
    core_rows = np.arange(HALO, HALO + CORE)
    field_cols = np.arange(ROW0, ROW0 + ROWS)
    own_cols = np.arange(WIDE, WIDE + CORE)
    sides = np.zeros((2 * XB, 256))
    sides[:, :WIDE] = x_rows(np.arange(WIDE))
    sides[:, CORE : CORE + WIDE] = x_rows(np.arange(WIDE + CORE, NX))
    parts = [("cx_own", x_rows(own_cols)), ("cx_side", sides)]
    for t in range(2):
        pos = np.arange(2 * CORE) - t * CORE + HALO
        inside = (pos >= 0) & (pos < NY)
        parts.append((f"by{t}", y_lanes(pos) * inside[:, None]))
    parts += [("x2", x_back(field_cols)), ("x3", x_rows(field_cols)), ("x4", x_back(own_cols))]
    y2_hi, y2_lo = (a.astype(np.float64) for a in np_split(y_back(core_rows)))
    y3_hi, y3_lo = (a.astype(np.float64) for a in np_split(y_lanes(core_rows)))
    grad = pack_split(parts)
    upper = np.concatenate([y2_hi, y2_lo], axis=1)
    lower = np.concatenate([y2_hi, np.zeros_like(y2_lo)], axis=1)
    grad += [("y2", np.concatenate([upper, lower]))]
    grad += [("y3", np.concatenate([y3_hi, y3_hi, y3_lo]))]
    own = np.zeros((ROWS, CORE))
    own[np.arange(CORE) + WIDE - ROW0, np.arange(CORE)] = 1
    halo = np.zeros((ROWS, 256))
    for r in range(HALO):
        halo[HALO + r - ROW0, WIDE + r] = 1
        halo[WIDE + CORE + r - ROW0, CORE + WIDE + r] = 1
    grad += [("sel_own", own), ("sel_halo", halo)]
    offs = np.arange(KSIZE) - HALO
    kx = np.zeros((2 * XB, 128))
    kx[:, :KSIZE] = x_rows(offs)
    spec = [("kx", kx)]
    for m in range(4):
        ky = np.zeros((128, 2 * YB))
        ky[32 * m : 32 * m + KSIZE] = y_lanes(offs)
        spec.append((f"ky{m}", ky))
    return {"grad": pack(grad), "spec": pack(pack_split(spec))}


def split(x):
    hi = x.astype(bf16)
    return hi, (x - hi.astype(f32)).astype(bf16)


def dot(a, b):
    return lax.dot_general(a, b, (((1,), (0,)), ((), ())), preferred_element_type=f32)


def dot_nt(a, b):
    return lax.dot_general(a, b, (((1,), (1,)), ((), ())), preferred_element_type=f32)


def dot3(a_hi, a_lo, b_hi, b_lo, mul=dot):
    return mul(a_hi, b_hi) + (mul(a_lo, b_hi) + mul(a_hi, b_lo))


def top_row(like):
    return lax.broadcasted_iota(jnp.int32, like.shape, 0) == 0


def signed_parts(cc, cs, sc, ss, special):
    out = cc - ss, cs + sc, cc + ss, sc - cs
    if special:
        row0 = top_row(cc)
        out = [jnp.where(row0, x, y) for x, y in zip((cc, cs, sc, -ss), out)]
    return out


def signed(spec):
    parts = (spec[:XB, :YB], spec[:XB, YB:], spec[XB:, :YB], spec[XB:, YB:])
    pr, neg, mr, mi = signed_parts(*parts, True)
    return pr, -neg, mr, mi


def even_odd(pr, pi, mr, mi, special=True):
    top = jnp.concatenate([pr + mr, pi + mi], axis=1)
    low = jnp.concatenate([mi - pi, pr - mr], axis=1)
    if special:
        low = jnp.where(top_row(low), jnp.concatenate([pr - mr, pi - mi], axis=1), low)
    return top, low


def table_array(group):
    return jnp.asarray(tables()[group][0].astype(ml_dtypes.bfloat16))


def table_reader(group, ref):
    where = tables()[group][1]

    def table(name, half=None):
        if isinstance(where[name], int):
            return jnp.concatenate([table(f"{name}.{i}") for i in range(where[name])], axis=1)
        at, height, width = where[name]
        lanes = slice(0, width) if half is None else slice(128 * half, 128 * half + 128)
        return ref[at : at + height, lanes]

    return table


def call(body, group, args, out_shape, scratch=(), smem=(), flops=0, nbytes=0):
    vm = pl.BlockSpec(memory_space=pltpu.VMEM)
    sm = pl.BlockSpec(memory_space=pltpu.SMEM)
    n_in = len(args)
    if group is not None:
        args = [*args, table_array(group)]

    def wrapped(*refs):
        if group is not None:
            refs = [*refs[:n_in], table_reader(group, refs[n_in]), *refs[n_in + 1 :]]
        body(*refs)

    return pl.pallas_call(
        wrapped,
        out_shape=out_shape,
        in_specs=[sm if i in smem else vm for i in range(len(args))],
        out_specs=[vm] * len(out_shape),
        scratch_shapes=list(scratch),
        compiler_params=pltpu.CompilerParams(vmem_limit_bytes=VMEM_LIMIT),
        cost_estimate=pl.CostEstimate(flops=flops, bytes_accessed=nbytes, transcendentals=0),
    )(*args)


def is_even():
    return lax.rem(lax.axis_index("tile"), 2) == 0


def send_edges(right, left, a_ref, b_ref):
    even = is_even()
    a_ref[...] = jnp.where(even, right, left)
    b_ref[...] = jnp.where(even, left, right)


def picker(rows, first, count, col):
    row = lax.broadcasted_iota(jnp.int32, (rows, CORE), 0)
    lane = lax.broadcasted_iota(jnp.int32, (rows, CORE), 1)
    hit = (row - first == lane - col) & (row >= first) & (row < first + count)
    return jnp.where(hit, 1.0, 0.0).astype(bf16)


def edges_of(rows, strip, extra=None):
    hi, lo = split(strip)
    both = []
    for col, more in ((CORE - WIDE, CORE - HALO), (0, 0)):
        pick = picker(rows, 0, WIDE, col)
        edge = dot_nt(pick, hi) + dot_nt(pick, lo)
        if extra is not None:
            edge = edge + dot_nt(picker(rows, WIDE, HALO, more), extra)
        both.append(edge)
    return both


def edges_kernel(both_ref, a_ref, b_ref):
    both = both_ref[...]
    target = jnp.where(both >= 2.0, 1.0, 0.0)
    mask = both - 2.0 * target
    send_edges(*edges_of(EDGE, mask, target.astype(bf16)), a_ref, b_ref)


def spectra_kernel(kern, w_ref, ker_ref, tb, h_ref, hs_ref):
    hs_ref[...] = jnp.zeros_like(hs_ref)
    for k in range(kern):
        for part in range(2):
            row = 32 * (2 * k + part)
            hs_ref[row : row + KSIZE, :KSIZE] = ker_ref[part, k, :, 0, :]
    s_hi, s_lo = split(hs_ref[...])
    z = dot3(tb("kx_hi"), tb("kx_lo"), s_hi, s_lo, dot_nt)
    z_hi, z_lo = split(z)
    for c in range(2 * kern):
        lanes = slice(128 * (c // 4), 128 * (c // 4) + 128)
        spec = dot3(z_hi[:, lanes], z_lo[:, lanes], tb(f"ky{c % 4}_hi"), tb(f"ky{c % 4}_lo"))
        root = jnp.sqrt(jnp.full((1, YB), w_ref[0, c // 2], f32))
        for j, comp in enumerate(signed(spec)):
            h_ref[c, j] = root * comp


def sides(last, from_a, from_b, tb):
    even = is_even()
    tile = lax.axis_index("tile")
    from_b = jnp.where((tile == 0) | (tile == last), 0.0, from_b)
    l_hi, l_lo = split(jnp.where(even, from_b, from_a))
    r_hi, r_lo = split(jnp.where(even, from_a, from_b))
    height = l_hi.shape[0]
    v = None
    for half, hi, lo in ((0, l_hi, l_lo), (1, r_hi, r_lo)):
        c_hi, c_lo = tb("cx_side_hi", half), tb("cx_side_lo", half)
        term = dot3(c_hi[:, :height], c_lo[:, :height], hi, lo)
        v = term if v is None else v + term
    return v, l_hi, r_hi


def to_spectrum(v, tb, f_ref, base):
    v_hi, v_lo = split(v)
    for t in range(2):
        spec = dot3(v_hi, v_lo, tb(f"by{t}_hi"), tb(f"by{t}_lo"))
        for j, comp in enumerate(signed(spec)):
            f_ref[t, j] = comp if base is None else base[t, j] - STEP_RATE * comp


def gradient_body(kern, last, f_ref, tgt_ref, h_ref, thr_ref, tb, g_ref, work):
    fld, inten, tot, a_cat, b_cat, r_cat, w_cat = work
    group = 2 if kern % 2 == 0 else 1
    count = kern // group
    chains = [(t, c) for t in range(2) for c in range(count)]
    lag = count + 2

    def at(i):
        return chains[i] if 0 <= i < len(chains) else None

    tile = lax.axis_index("tile")
    first = jnp.where(tile == 0, WIDE, HALO) - ROW0
    end = jnp.where(tile == last, WIDE + CORE, WIDE + CORE + HALO) - ROW0
    row = lax.broadcasted_iota(jnp.int32, (ROWS, CORE), 0)
    inside = (row >= first) & (row < end)
    lane = lax.broadcasted_iota(jnp.int32, (1, 2 * YB), 1)
    bin_at = lax.rem(lane, YB)
    weight = jnp.where((bin_at == 0) | (bin_at == NU - 1), 1.0, 2.0) / (NX * NY)
    weight = jnp.where(lane < YB, weight, -weight)

    def chunks(height):
        return [slice(r, r + CHUNK) for r in range(0, height, CHUNK)]

    def put(ref, slot, starts, pieces):
        for at_row, piece in zip(starts, pieces):
            ref[slot, at_row : at_row + CHUNK] = piece

    def products(t, c, slot):
        for part in range(2 * group):

            def pieces(start, height):
                rows = slice(start, start + height)
                hpr, hpi, hmr, hmi = (h_ref[2 * group * c + part, j, rows] for j in range(4))
                fpr, fpi, fmr, fmi = (f_ref[t, j, rows] for j in range(4))
                pr, pi = hpr * fpr - hpi * fpi, hpr * fpi + hpi * fpr
                mr, mi = hmr * fmr - hmi * fmi, hmr * fmi + hmi * fmr
                return even_odd(pr, pi, mr, mi, start == 0)

            def store(start, value):
                both = jnp.concatenate(split(value), axis=1)
                put(a_cat, slot, [2 * XB * part + start], [both])

            carry, last_low = pieces(XB - 8, 8)
            for start in range(0, XB - 8, CHUNK):
                top, low = pieces(start, CHUNK)
                store(start, top)
                store(XB - 8 + start, jnp.concatenate([carry, low[:8]], axis=0))
                carry = low[8:]
            store(2 * XB - CHUNK, jnp.concatenate([carry, last_low], axis=0))

    def y_done(z_now, slot):
        for g in range(group):
            for rows in chunks(2 * XB):
                z = []
                for part in range(2 * g, 2 * g + 2):
                    here = slice(2 * XB * part + rows.start, 2 * XB * part + rows.stop)
                    z.append(z_now[here, :CORE] + z_now[here, CORE:])
                z_hi, z_lo = split(jnp.concatenate(z, axis=1))
                starts = [2 * XB * j + rows.start for j in range(3)]
                put(b_cat, 2 * g + slot, starts, (z_hi, z_hi, z_lo))

    def field_of(t, c, slot):
        for g in range(group):
            k = group * c + g
            whole = dot(tb("x2"), b_cat[2 * g + slot])
            for rows in chunks(ROWS):
                field = whole[rows]
                fld[t, k, rows] = field
                re, im = field[:, :CORE], field[:, CORE:]
                power = re * re + im * im
                inten[t, rows] = power if k == 0 else inten[t, rows] + power

    def slope_of(t):
        resist = jax.nn.sigmoid(STEEPNESS * (inten[t] - thr_ref[0]))
        target = tgt_ref[:, CORE * t : CORE * t + CORE]
        slope = 2.0 * (resist - target) * STEEPNESS * resist * (1.0 - resist)
        inten[t] = jnp.where(inside, 2.0 * slope, 0.0)

    def scaled_field(t, c, slot):
        for g in range(group):
            for rows in chunks(ROWS):
                slope, field = inten[t, rows], fld[t, group * c + g, rows]
                r_hi, r_lo = split(
                    jnp.concatenate([slope * field[:, :CORE], slope * field[:, CORE:]], axis=1)
                )
                starts = [ROWS * j + rows.start for j in range(3)]
                put(r_cat, 2 * g + slot, starts, (r_hi, r_hi, r_lo))

    def x_back_done(w_now, g, slot):
        for rows in chunks(2 * XB):
            w_hi, w_lo = split(w_now[rows])
            for part in range(2):
                base = 2 * XB * (2 * g + part)
                here = slice(base + rows.start, base + rows.stop)
                lanes = slice(CORE * part, CORE * part + CORE)
                for j, piece in enumerate((w_hi, w_lo, w_hi)):
                    w_cat[slot, here, CORE * j : CORE * j + CORE] = piece[:, lanes]

    def add_back(t, c, slot):
        specs = dot(w_cat[slot], tb("y3"))
        for start in range(0, XB, 8):
            rows = slice(start, start + 8)
            acc = [0.0] * 4 if c == 0 else [tot[t, j, rows] for j in range(4)]
            for part in range(2 * group):
                base = 2 * XB * part + start
                cos, sin = specs[base : base + 8], specs[base + XB : base + XB + 8]
                bpr, neg, bmr, bmi = signed_parts(
                    cos[:, :YB], cos[:, YB:], sin[:, :YB], sin[:, YB:], start == 0
                )
                hpr, hpi, hmr, hmi = (h_ref[2 * group * c + part, j, rows] for j in range(4))
                acc[0] = acc[0] + (hpr * bpr - hpi * neg)
                acc[1] = acc[1] - (hpr * neg + hpi * bpr)
                acc[2] = acc[2] + (hmr * bmr + hmi * bmi)
                acc[3] = acc[3] + (hmr * bmi - hmi * bmr)
            for j in range(4):
                tot[t, j, rows] = acc[j]

    def finish(t):
        sums = even_odd(*(tot[t, j] for j in range(4)))
        r_hi, r_lo = split(jnp.concatenate(sums, axis=0))
        u = dot(tb("x4"), jnp.concatenate([r_hi, r_hi, r_lo], axis=0))
        u_hi, u_lo = split(weight * u)
        term = dot3(tb(f"by{t}_hi"), tb(f"by{t}_lo"), u_hi, u_lo, dot_nt)
        g_ref[...] = term if t == 0 else g_ref[...] + term

    for i in range(len(chains) + lag + 2):
        new, mid, old = at(i), at(i - 1), at(i - 2)
        back, back_mid, back_old = at(i - lag), at(i - lag - 1), at(i - lag - 2)
        slot, other = i % 2, (i + 1) % 2
        if mid:
            z_now = dot(a_cat[other], tb("y2"))
        if new:
            products(*new, slot)
        if back_mid:
            w_now = [dot(tb("x3"), r_cat[2 * g + other]) for g in range(group)]
        if back:
            scaled_field(*back, slot)
        if old:
            field_of(*old, slot)
        if back_old:
            add_back(*back_old, slot)
        if mid:
            y_done(z_now, other)
        if back_mid:
            for g in range(group):
                x_back_done(w_now[g], g, other)
        if old and old[1] == count - 1:
            slope_of(old[0])
        if back_old and back_old[1] == count - 1:
            finish(back_old[0])


def first_kernel(
    kern, last, thr_ref, mask_ref, target_ref, a_ref, b_ref, h_ref, tb,
    g_ref, f_ref, tgt_ref, *work,
):
    m_hi, m_lo = split(mask_ref[...])
    v, left, right = sides(last, a_ref[...], b_ref[...], tb)
    v = v + dot3(tb("cx_own_hi"), tb("cx_own_lo"), m_hi, m_lo, dot_nt)
    to_spectrum(v, tb, f_ref, None)
    tgt_ref[...] = (
        dot_nt(tb("sel_own"), target_ref[...].astype(f32).astype(bf16))
        + dot(tb("sel_halo", 0)[:, :EDGE], left)
        + dot(tb("sel_halo", 1)[:, :EDGE], right)
    )
    gradient_body(kern, last, f_ref, tgt_ref, h_ref, thr_ref, tb, g_ref, work)


def later_kernel(
    kern, last, thr_ref, mine_ref, peer_ref, a_ref, a2_ref, b_ref, b2_ref, f_in_ref, tgt_ref,
    h_ref, tb, g_ref, f_ref, *work,
):
    s_hi, s_lo = split(mine_ref[...] + peer_ref[...])
    from_a = a_ref[...] + a2_ref[...]
    from_b = b_ref[...] + b2_ref[...]
    v, _, _ = sides(last, from_a, from_b, tb)
    v = v + dot3(tb("cx_own_hi"), tb("cx_own_lo"), s_hi, s_lo, dot_nt)
    to_spectrum(v, tb, f_ref, f_in_ref)
    gradient_body(kern, last, f_ref, tgt_ref, h_ref, thr_ref, tb, g_ref, work)


def match(table_ref, own_ref, got_refs):
    device = lax.axis_index("tile")
    other = []
    for t in range(2):
        rows = slice(CORE * t, CORE * t + CORE)
        bit = lax.bitwise_xor(table_ref[t], 2 * device + t)
        value = jnp.where(bit == 1, own_ref[CORE * (1 - t) : CORE * (2 - t)], own_ref[rows])
        for b, got in enumerate(got_refs):
            value = jnp.where(bit == 2 << b, got[rows], value)
        other.append(value)
    row = lax.broadcasted_iota(jnp.int32, (CORE, CORE), 0)
    lane = lax.broadcasted_iota(jnp.int32, (CORE, CORE), 1)
    flip = jnp.where(row + lane == CORE - 1, 1.0, 0.0).astype(bf16)
    hi, lo = split(jnp.concatenate(other, axis=0))
    turned = dot(hi, flip) + dot(lo, flip)
    tiles = []
    for t in range(2):
        rows = slice(CORE * t, CORE * t + CORE)
        value = jnp.where(table_ref[2 + t] == 1, turned[rows], other[t])
        tiles.append(0.5 * (own_ref[rows] + value))
    return tiles, hi, lo


def matched_edges(table_ref, own_ref, hi, lo):
    row = lax.broadcasted_iota(jnp.int32, (WIDE_PAD, CORE), 0)
    lane = lax.broadcasted_iota(jnp.int32, (WIDE_PAD, CORE), 1)
    picks = [picker(WIDE_PAD, 0, WIDE, CORE - WIDE), picker(WIDE_PAD, 0, WIDE, 0)]
    for end in (WIDE - 1, CORE - 1):
        hit = (row + lane == end) & (row < WIDE)
        picks.append(jnp.where(hit, 1.0, 0.0).astype(bf16))
    picks = jnp.concatenate(picks, axis=0)
    own_hi, own_lo = split(own_ref[...])
    own = dot_nt(picks[: 2 * WIDE_PAD], own_hi) + dot_nt(picks[: 2 * WIDE_PAD], own_lo)
    other = dot_nt(picks, hi) + dot_nt(picks, lo)
    chosen = []
    for t in range(2):
        lanes = slice(CORE * t, CORE * t + CORE)
        plain, turned = other[: 2 * WIDE_PAD, lanes], other[2 * WIDE_PAD :, lanes]
        chosen.append(jnp.where(table_ref[2 + t] == 1, turned, plain))
    both = 0.5 * (own + jnp.concatenate(chosen, axis=1))
    return both[:WIDE_PAD], both[WIDE_PAD:]


def match_kernel(n_got, table_ref, own_ref, *refs):
    got_refs, (out_ref, *edge_refs) = refs[:n_got], refs[n_got:]
    tiles, hi, lo = match(table_ref, own_ref, got_refs)
    send_edges(*matched_edges(table_ref, own_ref, hi, lo), *edge_refs)
    out_ref[...] = jnp.concatenate(tiles, axis=0)


def final_kernel(n_got, n_moves, table_ref, own_ref, *refs):
    got_refs, mask_ref, refs = refs[:n_got], refs[n_got], refs[n_got + 1 :]
    moves, (mask_out, grad_out) = refs[: 2 * n_moves], refs[2 * n_moves :]
    for t, step in enumerate(match(table_ref, own_ref, got_refs)[0]):
        rows = slice(CORE * t, CORE * t + CORE)
        now = mask_ref[t]
        for mine, peer in zip(moves[::2], moves[1::2]):
            now = now - STEP_RATE * (mine[rows] + peer[rows])
        grad_out[t] = step
        mask_out[t] = now - STEP_RATE * step


def per_device(
    n_tile, n_depth, mask_tiles, target_tiles, kernels, socs_weights, thresholds,
    partner_table, mirror_flags,
):
    tiles_dev, core, _ = mask_tiles.shape
    kern = kernels.shape[2]
    assert tiles_dev == 2 and core == CORE
    pairs_a = [(i, i ^ 1) for i in range(n_tile)]
    pairs_b = [p for i in range(1, n_tile - 1, 2) for p in ((i, i + 1), (i + 1, i))]
    pairs_b += [(0, 0), (n_tile - 1, n_tile - 1)]

    def swap_edges(send_a, send_b, cross=False):
        def move(x, pairs):
            if not cross:
                return lax.ppermute(x, "tile", pairs)
            both = [(2 * i + p, 2 * j + 1 - p) for i, j in pairs for p in range(2)]
            return lax.ppermute(x, ("tile", "depth"), both)

        return move(send_b, pairs_b), move(send_a, pairs_a)

    def depth_pair(x):
        bit = 1
        while True:
            peer = lax.ppermute(x, "depth", [(i, i ^ bit) for i in range(n_depth)])
            bit *= 2
            if bit >= n_depth:
                return x, peer
            x = x + peer

    def from_partners(grad):
        bits = [1 << b for b in range(n_tile.bit_length() - 1)]
        got = [
            lax.ppermute(grad, "tile", [(i, i ^ bit) for i in range(n_tile)])
            for bit in reversed(bits)
        ]
        return got[::-1]

    mask_rows = mask_tiles.reshape(tiles_dev * core, core)
    target_rows = target_tiles.reshape(tiles_dev * core, core)
    strip = jax.ShapeDtypeStruct((tiles_dev * core, core), f32)
    side = jax.ShapeDtypeStruct((WIDE_PAD, tiles_dev * core), f32)
    freq = jax.ShapeDtypeStruct((2, 4, XB, YB), f32)
    goal = jax.ShapeDtypeStruct((ROWS, 2 * CORE), f32)
    tiles = jax.ShapeDtypeStruct((tiles_dev, core, core), f32)
    group = 2 if kern % 2 == 0 else 1
    scratch = [
        pltpu.VMEM((2, kern, ROWS, 2 * CORE), f32),
        pltpu.VMEM((2, ROWS, CORE), f32),
        pltpu.VMEM((2, 4, XB, YB), f32),
        pltpu.VMEM((2, group * 4 * XB, 4 * YB), bf16),
        pltpu.VMEM((2 * group, 6 * XB, 2 * CORE), bf16),
        pltpu.VMEM((2 * group, 3 * ROWS, 2 * CORE), bf16),
        pltpu.VMEM((2, group * 4 * XB, 3 * CORE), bf16),
    ]

    edge = jax.ShapeDtypeStruct((EDGE, tiles_dev * core), f32)
    send_a, send_b = call(
        edges_kernel,
        None,
        [mask_rows + 2.0 * target_rows.astype(f32)],
        [edge, edge],
        flops=3 * 10**9,
    )
    from_b, from_a = swap_edges(send_a, send_b)
    table = jnp.concatenate([partner_table, mirror_flags])
    (spectra,) = call(
        functools.partial(spectra_kernel, kern),
        "spec",
        [socs_weights, kernels.transpose(0, 2, 3, 1, 4)],
        [jax.ShapeDtypeStruct((2 * kern, 4, XB, YB), f32)],
        [pltpu.VMEM((32 * 2 * kern, 128), f32)],
        smem=(0,),
        flops=3 * 10**9,
        nbytes=4 * 10**6,
    )
    grad, freq_now, goals = call(
        functools.partial(first_kernel, kern, n_tile - 1),
        "grad",
        [thresholds, mask_rows, target_rows, from_a, from_b, spectra],
        [strip, freq, goal],
        scratch,
        smem=(0,),
        flops=10**10,
    )
    moves = []
    for step in range(1, STEPS):
        got = from_partners(grad)
        move, *edges = call(
            functools.partial(match_kernel, len(got)),
            None,
            [table, grad, *got],
            [strip, side, side],
            smem=(0,),
        )
        from_b, from_a = swap_edges(*edges)
        if n_depth == 2:
            far_b, far_a = swap_edges(*edges, cross=True)
            rims = (from_a, far_a, from_b, far_b)
        else:
            rims = depth_pair(from_a) + depth_pair(from_b)
        moves += depth_pair(move)
        kept = step + 1 < STEPS
        grad, *rest = call(
            functools.partial(later_kernel, kern, n_tile - 1),
            "grad",
            [thresholds, *moves[-2:], *rims, freq_now, goals, spectra],
            [strip, freq] if kept else [strip],
            scratch if kept else [pltpu.VMEM(freq.shape, f32)] + scratch,
            smem=(0,),
            flops=10**10,
        )
        freq_now = rest[0] if kept else None
    mine, peer = depth_pair(grad)
    total = mine + peer
    got = from_partners(total)
    final = functools.partial(final_kernel, len(got), len(moves) // 2)
    args = [table, total, *got, mask_tiles, *moves]
    return tuple(call(final, None, args, [tiles, tiles], smem=(0,)))


def solution(mesh):
    return jax.shard_map(
        functools.partial(per_device, mesh.shape["tile"], mesh.shape["depth"]),
        mesh=mesh,
        in_specs=(
            P("tile", None, None),
            P("tile", None, None),
            P(None, "depth", None, None, None),
            P("depth", None),
            P("depth"),
            P("tile"),
            P("tile"),
        ),
        out_specs=(P("tile", None, None), P("tile", None, None)),
        check_vma=False,
    )
```

```python
import functools

import jax
import jax.numpy as jnp
import ml_dtypes
import numpy as np
from jax import lax
from jax.experimental import pallas as pl
from jax.experimental.pallas import tpu as pltpu
from jax.sharding import PartitionSpec as P

HALO = 12
KSIZE = 25
STEPS = 2
STEEPNESS = 3.0
STEP_RATE = 0.05

CORE = 128
NY = 152
NX = 176
WIDE = 2 * HALO
XB = 88
YB = 128
NU = NY // 2 + 1
ROWS = 160
ROW0 = 8
CHUNK = 16
EDGE = 48
WIDE_PAD = 32
VMEM_LIMIT = 24 * 1024 * 1024

f32 = jnp.float32
bf16 = jnp.bfloat16


def np_split(a):
    hi = np.asarray(a, np.float32).astype(ml_dtypes.bfloat16)
    lo = (np.asarray(a, np.float64) - hi.astype(np.float64)).astype(ml_dtypes.bfloat16)
    return hi, lo


def x_rows(cols):
    ang = 2 * np.pi * np.outer(np.arange(XB + 1), cols) / NX
    out = np.concatenate([np.cos(ang[:XB]), np.sin(ang[:XB])])
    out[XB] = np.cos(ang[XB])
    return out


def y_lanes(rows):
    out = np.zeros((len(rows), 2 * YB))
    ang = 2 * np.pi * np.outer(rows, np.arange(NU)) / NY
    out[:, :NU] = np.cos(ang)
    out[:, YB : YB + NU] = np.sin(ang)
    out[:, YB] = 0.0
    out[:, YB + NU - 1] = 0.0
    return out


def half_weights(bins):
    weights = np.full(bins, 2.0)
    weights[0] = weights[-1] = 1.0
    return weights


def x_back(cols):
    out = x_rows(cols).T
    sign = 1 - 2.0 * (np.asarray(cols) % 2)
    out[:, 0] = (1 + sign) / 2
    out[:, XB] = (1 - sign) / 2
    return out


def y_back(rows):
    weight = np.zeros(2 * YB)
    weight[:NU] = half_weights(NU)
    weight[YB : YB + NU] = -half_weights(NU)
    return (y_lanes(rows) * weight).T / (NX * NY)


def pack(parts):
    rows, where, at = [], {}, 0
    pieces = []
    for name, a in parts:
        if a.shape[1] <= 256:
            pieces.append((name, a))
            continue
        cuts = range(0, a.shape[1], 256)
        where[name] = len(cuts)
        pieces += [(f"{name}.{i}", a[:, c : c + 256]) for i, c in enumerate(cuts)]
    for name, a in pieces:
        height = -(-a.shape[0] // 16) * 16
        block = np.zeros((height, 256), np.float64)
        block[: a.shape[0], : a.shape[1]] = a
        rows.append(block)
        where[name] = (at, a.shape[0], a.shape[1])
        at += height
    return np.concatenate(rows), where


def pack_split(parts):
    both = []
    for name, a in parts:
        hi, lo = np_split(a)
        if name in ("x2", "x3", "x4"):
            hi, lo = hi.astype(np.float64), lo.astype(np.float64)
            both.append((name, np.concatenate([hi, lo, hi], axis=1)))
            continue
        both += [(name + "_hi", hi.astype(np.float64)), (name + "_lo", lo.astype(np.float64))]
    return both


@functools.lru_cache(None)
def tables():
    core_rows = np.arange(HALO, HALO + CORE)
    field_cols = np.arange(ROW0, ROW0 + ROWS)
    own_cols = np.arange(WIDE, WIDE + CORE)
    sides = np.zeros((2 * XB, 256))
    sides[:, :WIDE] = x_rows(np.arange(WIDE))
    sides[:, CORE : CORE + WIDE] = x_rows(np.arange(WIDE + CORE, NX))
    parts = [("cx_own", x_rows(own_cols)), ("cx_side", sides)]
    for t in range(2):
        pos = np.arange(2 * CORE) - t * CORE + HALO
        inside = (pos >= 0) & (pos < NY)
        parts.append((f"by{t}", y_lanes(pos) * inside[:, None]))
    parts += [("x2", x_back(field_cols)), ("x3", x_rows(field_cols)), ("x4", x_back(own_cols))]
    y2_hi, y2_lo = (a.astype(np.float64) for a in np_split(y_back(core_rows)))
    y3_hi, y3_lo = (a.astype(np.float64) for a in np_split(y_lanes(core_rows)))
    grad = pack_split(parts)
    upper = np.concatenate([y2_hi, y2_lo], axis=1)
    lower = np.concatenate([y2_hi, np.zeros_like(y2_lo)], axis=1)
    grad += [("y2", np.concatenate([upper, lower]))]
    grad += [("y3", np.concatenate([y3_hi, y3_hi, y3_lo]))]
    own = np.zeros((ROWS, CORE))
    own[np.arange(CORE) + WIDE - ROW0, np.arange(CORE)] = 1
    halo = np.zeros((ROWS, 256))
    for r in range(HALO):
        halo[HALO + r - ROW0, WIDE + r] = 1
        halo[WIDE + CORE + r - ROW0, CORE + WIDE + r] = 1
    grad += [("sel_halo", halo)]
    offs = np.arange(KSIZE) - HALO
    kx = np.zeros((2 * XB, 128))
    kx[:, :KSIZE] = x_rows(offs)
    spec = [("kx", kx), ("cx_own", x_rows(own_cols))]
    for m in range(4):
        ky = np.zeros((128, 2 * YB))
        ky[32 * m : 32 * m + KSIZE] = y_lanes(offs)
        spec.append((f"ky{m}", ky))
    return {"grad": pack(grad), "spec": pack(pack_split(spec) + [("sel_own", own)])}


def split(x):
    hi = x.astype(bf16)
    return hi, (x - hi.astype(f32)).astype(bf16)


def dot(a, b):
    return lax.dot_general(a, b, (((1,), (0,)), ((), ())), preferred_element_type=f32)


def dot_nt(a, b):
    return lax.dot_general(a, b, (((1,), (1,)), ((), ())), preferred_element_type=f32)


def dot3(a_hi, a_lo, b_hi, b_lo, mul=dot):
    return mul(a_hi, b_hi) + (mul(a_lo, b_hi) + mul(a_hi, b_lo))


def top_row(like):
    return lax.broadcasted_iota(jnp.int32, like.shape, 0) == 0


def signed_parts(cc, cs, sc, ss, special):
    out = cc - ss, cs + sc, cc + ss, sc - cs
    if special:
        row0 = top_row(cc)
        out = [jnp.where(row0, x, y) for x, y in zip((cc, cs, sc, -ss), out)]
    return out


def signed(spec):
    parts = (spec[:XB, :YB], spec[:XB, YB:], spec[XB:, :YB], spec[XB:, YB:])
    pr, neg, mr, mi = signed_parts(*parts, True)
    return pr, -neg, mr, mi


def even_odd(pr, pi, mr, mi, special=True):
    top = jnp.concatenate([pr + mr, pi + mi], axis=1)
    low = jnp.concatenate([mi - pi, pr - mr], axis=1)
    if special:
        low = jnp.where(top_row(low), jnp.concatenate([pr - mr, pi - mi], axis=1), low)
    return top, low


def table_array(group):
    return jnp.asarray(tables()[group][0].astype(ml_dtypes.bfloat16))


def table_reader(group, ref):
    where = tables()[group][1]

    def table(name, half=None):
        if isinstance(where[name], int):
            return jnp.concatenate([table(f"{name}.{i}") for i in range(where[name])], axis=1)
        at, height, width = where[name]
        lanes = slice(0, width) if half is None else slice(128 * half, 128 * half + 128)
        return ref[at : at + height, lanes]

    return table


def call(body, group, args, out_shape, scratch=(), smem=(), flops=0, nbytes=0):
    vm = pl.BlockSpec(memory_space=pltpu.VMEM)
    sm = pl.BlockSpec(memory_space=pltpu.SMEM)
    n_in = len(args)
    if group is not None:
        args = [*args, table_array(group)]

    def wrapped(*refs):
        if group is not None:
            refs = [*refs[:n_in], table_reader(group, refs[n_in]), *refs[n_in + 1 :]]
        body(*refs)

    return pl.pallas_call(
        wrapped,
        out_shape=out_shape,
        in_specs=[sm if i in smem else vm for i in range(len(args))],
        out_specs=[vm] * len(out_shape),
        scratch_shapes=list(scratch),
        compiler_params=pltpu.CompilerParams(vmem_limit_bytes=VMEM_LIMIT),
        cost_estimate=pl.CostEstimate(flops=flops, bytes_accessed=nbytes, transcendentals=0),
    )(*args)


def is_even():
    return lax.rem(lax.axis_index("tile"), 2) == 0


def send_edges(right, left, a_ref, b_ref):
    even = is_even()
    a_ref[...] = jnp.where(even, right, left)
    b_ref[...] = jnp.where(even, left, right)


def picker(rows, first, count, col):
    row = lax.broadcasted_iota(jnp.int32, (rows, CORE), 0)
    lane = lax.broadcasted_iota(jnp.int32, (rows, CORE), 1)
    hit = (row - first == lane - col) & (row >= first) & (row < first + count)
    return jnp.where(hit, 1.0, 0.0).astype(bf16)


def edges_of(rows, strip, extra=None):
    hi, lo = split(strip)
    both = []
    for col, more in ((CORE - WIDE, CORE - HALO), (0, 0)):
        pick = picker(rows, 0, WIDE, col)
        edge = dot_nt(pick, hi) + dot_nt(pick, lo)
        if extra is not None:
            edge = edge + dot_nt(picker(rows, WIDE, HALO, more), extra)
        both.append(edge)
    return both


def edges_kernel(both_ref, a_ref, b_ref):
    both = both_ref[...]
    target = jnp.where(both >= 2.0, 1.0, 0.0)
    mask = both - 2.0 * target
    send_edges(*edges_of(EDGE, mask, target.astype(bf16)), a_ref, b_ref)


def spectra_kernel(
    kern, w_ref, ker_ref, mask_ref, target_ref, tb, h_ref, v_ref, tgt_ref, hs_ref
):
    m_hi, m_lo = split(mask_ref[...])
    v_ref[...] = dot3(tb("cx_own_hi"), tb("cx_own_lo"), m_hi, m_lo, dot_nt)
    tgt_ref[...] = dot_nt(tb("sel_own"), target_ref[...].astype(f32).astype(bf16))
    hs_ref[...] = jnp.zeros_like(hs_ref)
    for k in range(kern):
        for part in range(2):
            row = 32 * (2 * k + part)
            hs_ref[row : row + KSIZE, :KSIZE] = ker_ref[part, k, :, 0, :]
    s_hi, s_lo = split(hs_ref[...])
    z = dot3(tb("kx_hi"), tb("kx_lo"), s_hi, s_lo, dot_nt)
    z_hi, z_lo = split(z)
    for c in range(2 * kern):
        lanes = slice(128 * (c // 4), 128 * (c // 4) + 128)
        spec = dot3(z_hi[:, lanes], z_lo[:, lanes], tb(f"ky{c % 4}_hi"), tb(f"ky{c % 4}_lo"))
        root = jnp.sqrt(jnp.full((1, YB), w_ref[0, c // 2], f32))
        for j, comp in enumerate(signed(spec)):
            h_ref[c, j] = root * comp


def sides(last, from_a, from_b, tb):
    even = is_even()
    tile = lax.axis_index("tile")
    from_b = jnp.where((tile == 0) | (tile == last), 0.0, from_b)
    l_hi, l_lo = split(jnp.where(even, from_b, from_a))
    r_hi, r_lo = split(jnp.where(even, from_a, from_b))
    height = l_hi.shape[0]
    v = None
    for half, hi, lo in ((0, l_hi, l_lo), (1, r_hi, r_lo)):
        c_hi, c_lo = tb("cx_side_hi", half), tb("cx_side_lo", half)
        term = dot3(c_hi[:, :height], c_lo[:, :height], hi, lo)
        v = term if v is None else v + term
    return v, l_hi, r_hi


def to_spectrum(v, tb, f_ref, base):
    v_hi, v_lo = split(v)
    for t in range(2):
        spec = dot3(v_hi, v_lo, tb(f"by{t}_hi"), tb(f"by{t}_lo"))
        for j, comp in enumerate(signed(spec)):
            f_ref[t, j] = comp if base is None else base[t, j] - STEP_RATE * comp


def gradient_body(kern, last, f_ref, tgt_ref, h_ref, thr_ref, tb, g_ref, work):
    fld, inten, tot, a_cat, b_cat, r_cat, w_cat = work
    group = 2 if kern % 2 == 0 else 1
    count = kern // group
    chains = [(t, c) for t in range(2) for c in range(count)]
    lag = count + 2

    def at(i):
        return chains[i] if 0 <= i < len(chains) else None

    tile = lax.axis_index("tile")
    first = jnp.where(tile == 0, WIDE, HALO) - ROW0
    end = jnp.where(tile == last, WIDE + CORE, WIDE + CORE + HALO) - ROW0
    row = lax.broadcasted_iota(jnp.int32, (ROWS, CORE), 0)
    inside = (row >= first) & (row < end)
    lane = lax.broadcasted_iota(jnp.int32, (1, 2 * YB), 1)
    bin_at = lax.rem(lane, YB)
    weight = jnp.where((bin_at == 0) | (bin_at == NU - 1), 1.0, 2.0) / (NX * NY)
    weight = jnp.where(lane < YB, weight, -weight)

    def chunks(height):
        return [slice(r, r + CHUNK) for r in range(0, height, CHUNK)]

    def put(ref, slot, starts, pieces):
        for at_row, piece in zip(starts, pieces):
            ref[slot, at_row : at_row + CHUNK] = piece

    def products(t, c, slot):
        for part in range(2 * group):

            def pieces(start, height):
                rows = slice(start, start + height)
                hpr, hpi, hmr, hmi = (h_ref[2 * group * c + part, j, rows] for j in range(4))
                fpr, fpi, fmr, fmi = (f_ref[t, j, rows] for j in range(4))
                pr, pi = hpr * fpr - hpi * fpi, hpr * fpi + hpi * fpr
                mr, mi = hmr * fmr - hmi * fmi, hmr * fmi + hmi * fmr
                return even_odd(pr, pi, mr, mi, start == 0)

            def store(start, value):
                both = jnp.concatenate(split(value), axis=1)
                put(a_cat, slot, [2 * XB * part + start], [both])

            carry, last_low = pieces(XB - 8, 8)
            for start in range(0, XB - 8, CHUNK):
                top, low = pieces(start, CHUNK)
                store(start, top)
                store(XB - 8 + start, jnp.concatenate([carry, low[:8]], axis=0))
                carry = low[8:]
            store(2 * XB - CHUNK, jnp.concatenate([carry, last_low], axis=0))

    def y_done(z_now, slot):
        for g in range(group):
            for rows in chunks(2 * XB):
                z = []
                for part in range(2 * g, 2 * g + 2):
                    here = slice(2 * XB * part + rows.start, 2 * XB * part + rows.stop)
                    z.append(z_now[here, :CORE] + z_now[here, CORE:])
                z_hi, z_lo = split(jnp.concatenate(z, axis=1))
                starts = [2 * XB * j + rows.start for j in range(3)]
                put(b_cat, 2 * g + slot, starts, (z_hi, z_hi, z_lo))

    def field_of(t, c, slot):
        for g in range(group):
            k = group * c + g
            whole = dot(tb("x2"), b_cat[2 * g + slot])
            for rows in chunks(ROWS):
                field = whole[rows]
                fld[t, k, rows] = field
                re, im = field[:, :CORE], field[:, CORE:]
                power = re * re + im * im
                inten[t, rows] = power if k == 0 else inten[t, rows] + power

    def slope_of(t):
        resist = jax.nn.sigmoid(STEEPNESS * (inten[t] - thr_ref[...]))
        target = tgt_ref[:, CORE * t : CORE * t + CORE]
        slope = 2.0 * (resist - target) * STEEPNESS * resist * (1.0 - resist)
        inten[t] = jnp.where(inside, 2.0 * slope, 0.0)

    def scaled_field(t, c, slot):
        for g in range(group):
            for rows in chunks(ROWS):
                slope, field = inten[t, rows], fld[t, group * c + g, rows]
                r_hi, r_lo = split(
                    jnp.concatenate([slope * field[:, :CORE], slope * field[:, CORE:]], axis=1)
                )
                starts = [ROWS * j + rows.start for j in range(3)]
                put(r_cat, 2 * g + slot, starts, (r_hi, r_hi, r_lo))

    def x_back_done(w_now, g, slot):
        for rows in chunks(2 * XB):
            w_hi, w_lo = split(w_now[rows])
            for part in range(2):
                base = 2 * XB * (2 * g + part)
                here = slice(base + rows.start, base + rows.stop)
                lanes = slice(CORE * part, CORE * part + CORE)
                for j, piece in enumerate((w_hi, w_lo, w_hi)):
                    w_cat[slot, here, CORE * j : CORE * j + CORE] = piece[:, lanes]

    def add_back(t, c, slot):
        specs = dot(w_cat[slot], tb("y3"))
        for start in range(0, XB, 8):
            rows = slice(start, start + 8)
            acc = [0.0] * 4 if c == 0 else [tot[t, j, rows] for j in range(4)]
            for part in range(2 * group):
                base = 2 * XB * part + start
                cos, sin = specs[base : base + 8], specs[base + XB : base + XB + 8]
                bpr, neg, bmr, bmi = signed_parts(
                    cos[:, :YB], cos[:, YB:], sin[:, :YB], sin[:, YB:], start == 0
                )
                hpr, hpi, hmr, hmi = (h_ref[2 * group * c + part, j, rows] for j in range(4))
                acc[0] = acc[0] + (hpr * bpr - hpi * neg)
                acc[1] = acc[1] - (hpr * neg + hpi * bpr)
                acc[2] = acc[2] + (hmr * bmr + hmi * bmi)
                acc[3] = acc[3] + (hmr * bmi - hmi * bmr)
            for j in range(4):
                tot[t, j, rows] = acc[j]

    def finish(t):
        sums = even_odd(*(tot[t, j] for j in range(4)))
        r_hi, r_lo = split(jnp.concatenate(sums, axis=0))
        u = dot(tb("x4"), jnp.concatenate([r_hi, r_hi, r_lo], axis=0))
        u_hi, u_lo = split(weight * u)
        term = dot3(tb(f"by{t}_hi"), tb(f"by{t}_lo"), u_hi, u_lo, dot_nt)
        g_ref[...] = term if t == 0 else g_ref[...] + term

    for i in range(len(chains) + lag + 2):
        new, mid, old = at(i), at(i - 1), at(i - 2)
        back, back_mid, back_old = at(i - lag), at(i - lag - 1), at(i - lag - 2)
        slot, other = i % 2, (i + 1) % 2
        if mid:
            z_now = dot(a_cat[other], tb("y2"))
        if new:
            products(*new, slot)
        if back_mid:
            w_now = [dot(tb("x3"), r_cat[2 * g + other]) for g in range(group)]
        if back:
            scaled_field(*back, slot)
        if old:
            field_of(*old, slot)
        if back_old:
            add_back(*back_old, slot)
        if mid:
            y_done(z_now, other)
        if back_mid:
            for g in range(group):
                x_back_done(w_now[g], g, other)
        if old and old[1] == count - 1:
            slope_of(old[0])
        if back_old and back_old[1] == count - 1:
            finish(back_old[0])


def first_kernel(
    kern, last, thr_ref, v_ref, t_ref, a_ref, b_ref, h_ref, tb,
    g_ref, f_ref, tgt_ref, *work,
):
    v, left, right = sides(last, a_ref[...], b_ref[...], tb)
    v = v + v_ref[...]
    to_spectrum(v, tb, f_ref, None)
    tgt_ref[...] = (
        t_ref[...]
        + dot(tb("sel_halo", 0)[:, :EDGE], left)
        + dot(tb("sel_halo", 1)[:, :EDGE], right)
    )
    gradient_body(kern, last, f_ref, tgt_ref, h_ref, thr_ref, tb, g_ref, work)


def later_kernel(
    kern, last, thr_ref, mine_ref, peer_ref, a_ref, a2_ref, b_ref, b2_ref, f_in_ref, tgt_ref,
    h_ref, tb, g_ref, f_ref, *work,
):
    s_hi, s_lo = split(mine_ref[...] + peer_ref[...])
    from_a = a_ref[...] + a2_ref[...]
    from_b = b_ref[...] + b2_ref[...]
    v, _, _ = sides(last, from_a, from_b, tb)
    v = v + dot3(tb("cx_own_hi"), tb("cx_own_lo"), s_hi, s_lo, dot_nt)
    to_spectrum(v, tb, f_ref, f_in_ref)
    gradient_body(kern, last, f_ref, tgt_ref, h_ref, thr_ref, tb, g_ref, work)


def match(table_ref, own_ref, got_refs):
    device = lax.axis_index("tile")
    other = []
    for t in range(2):
        rows = slice(CORE * t, CORE * t + CORE)
        bit = lax.bitwise_xor(table_ref[t], 2 * device + t)
        value = jnp.where(bit == 1, own_ref[CORE * (1 - t) : CORE * (2 - t)], own_ref[rows])
        for b, got in enumerate(got_refs):
            value = jnp.where(bit == 2 << b, got[rows], value)
        other.append(value)
    row = lax.broadcasted_iota(jnp.int32, (CORE, CORE), 0)
    lane = lax.broadcasted_iota(jnp.int32, (CORE, CORE), 1)
    flip = jnp.where(row + lane == CORE - 1, 1.0, 0.0).astype(bf16)
    hi, lo = split(jnp.concatenate(other, axis=0))
    turned = dot(hi, flip) + dot(lo, flip)
    tiles = []
    for t in range(2):
        rows = slice(CORE * t, CORE * t + CORE)
        value = jnp.where(table_ref[2 + t] == 1, turned[rows], other[t])
        tiles.append(0.5 * (own_ref[rows] + value))
    return tiles, hi, lo


def matched_edges(table_ref, own_ref, hi, lo):
    row = lax.broadcasted_iota(jnp.int32, (WIDE_PAD, CORE), 0)
    lane = lax.broadcasted_iota(jnp.int32, (WIDE_PAD, CORE), 1)
    picks = [picker(WIDE_PAD, 0, WIDE, CORE - WIDE), picker(WIDE_PAD, 0, WIDE, 0)]
    for end in (WIDE - 1, CORE - 1):
        hit = (row + lane == end) & (row < WIDE)
        picks.append(jnp.where(hit, 1.0, 0.0).astype(bf16))
    picks = jnp.concatenate(picks, axis=0)
    own_hi, own_lo = split(own_ref[...])
    own = dot_nt(picks[: 2 * WIDE_PAD], own_hi) + dot_nt(picks[: 2 * WIDE_PAD], own_lo)
    other = dot_nt(picks, hi) + dot_nt(picks, lo)
    chosen = []
    for t in range(2):
        lanes = slice(CORE * t, CORE * t + CORE)
        plain, turned = other[: 2 * WIDE_PAD, lanes], other[2 * WIDE_PAD :, lanes]
        chosen.append(jnp.where(table_ref[2 + t] == 1, turned, plain))
    both = 0.5 * (own + jnp.concatenate(chosen, axis=1))
    return both[:WIDE_PAD], both[WIDE_PAD:]


def match_kernel(n_got, table_ref, own_ref, *refs):
    got_refs, (out_ref, *edge_refs) = refs[:n_got], refs[n_got:]
    tiles, hi, lo = match(table_ref, own_ref, got_refs)
    send_edges(*matched_edges(table_ref, own_ref, hi, lo), *edge_refs)
    out_ref[...] = jnp.concatenate(tiles, axis=0)


def final_kernel(n_got, n_moves, table_ref, own_ref, *refs):
    got_refs, mask_ref, refs = refs[:n_got], refs[n_got], refs[n_got + 1 :]
    moves, (mask_out, grad_out) = refs[: 2 * n_moves], refs[2 * n_moves :]
    for t, step in enumerate(match(table_ref, own_ref, got_refs)[0]):
        rows = slice(CORE * t, CORE * t + CORE)
        now = mask_ref[t]
        for mine, peer in zip(moves[::2], moves[1::2]):
            now = now - STEP_RATE * (mine[rows] + peer[rows])
        grad_out[t] = step
        mask_out[t] = now - STEP_RATE * step


def per_device(
    n_tile, n_depth, mask_tiles, target_tiles, kernels, socs_weights, thresholds,
    partner_table, mirror_flags,
):
    tiles_dev, core, _ = mask_tiles.shape
    kern = kernels.shape[2]
    assert tiles_dev == 2 and core == CORE
    pairs_a = [(i, i ^ 1) for i in range(n_tile)]
    pairs_b = [p for i in range(1, n_tile - 1, 2) for p in ((i, i + 1), (i + 1, i))]
    pairs_b += [(0, 0), (n_tile - 1, n_tile - 1)]

    def swap_edges(send_a, send_b, cross=False):
        def move(x, pairs):
            if not cross:
                return lax.ppermute(x, "tile", pairs)
            both = [(2 * i + p, 2 * j + 1 - p) for i, j in pairs for p in range(2)]
            return lax.ppermute(x, ("tile", "depth"), both)

        return move(send_b, pairs_b), move(send_a, pairs_a)

    def depth_pair(x):
        bit = 1
        while True:
            peer = lax.ppermute(x, "depth", [(i, i ^ bit) for i in range(n_depth)])
            bit *= 2
            if bit >= n_depth:
                return x, peer
            x = x + peer

    def from_partners(grad):
        bits = [1 << b for b in range(n_tile.bit_length() - 1)]
        got = [
            lax.ppermute(grad, "tile", [(i, i ^ bit) for i in range(n_tile)])
            for bit in reversed(bits)
        ]
        return got[::-1]

    mask_rows = mask_tiles.reshape(tiles_dev * core, core)
    target_rows = target_tiles.reshape(tiles_dev * core, core)
    strip = jax.ShapeDtypeStruct((tiles_dev * core, core), f32)
    side = jax.ShapeDtypeStruct((WIDE_PAD, tiles_dev * core), f32)
    freq = jax.ShapeDtypeStruct((2, 4, XB, YB), f32)
    goal = jax.ShapeDtypeStruct((ROWS, 2 * CORE), f32)
    tiles = jax.ShapeDtypeStruct((tiles_dev, core, core), f32)
    group = 2 if kern % 2 == 0 else 1
    scratch = [
        pltpu.VMEM((2, kern, ROWS, 2 * CORE), f32),
        pltpu.VMEM((2, ROWS, CORE), f32),
        pltpu.VMEM((2, 4, XB, YB), f32),
        pltpu.VMEM((2, group * 4 * XB, 4 * YB), bf16),
        pltpu.VMEM((2 * group, 6 * XB, 2 * CORE), bf16),
        pltpu.VMEM((2 * group, 3 * ROWS, 2 * CORE), bf16),
        pltpu.VMEM((2, group * 4 * XB, 3 * CORE), bf16),
    ]

    edge = jax.ShapeDtypeStruct((EDGE, tiles_dev * core), f32)
    send_a, send_b = call(
        edges_kernel,
        None,
        [mask_rows + 2.0 * target_rows.astype(f32)],
        [edge, edge],
        flops=3 * 10**9,
    )
    from_b, from_a = swap_edges(send_a, send_b)
    table = jnp.concatenate([partner_table, mirror_flags])
    level = thresholds.reshape(1, 1)
    spectra, own_v, own_goals = call(
        functools.partial(spectra_kernel, kern),
        "spec",
        [socs_weights, kernels.transpose(0, 2, 3, 1, 4), mask_rows, target_rows],
        [
            jax.ShapeDtypeStruct((2 * kern, 4, XB, YB), f32),
            jax.ShapeDtypeStruct((2 * XB, tiles_dev * core), f32),
            goal,
        ],
        [pltpu.VMEM((32 * 2 * kern, 128), f32)],
        smem=(0,),
        flops=3 * 10**9,
        nbytes=4 * 10**6,
    )
    grad, freq_now, goals = call(
        functools.partial(first_kernel, kern, n_tile - 1),
        "grad",
        [level, own_v, own_goals, from_a, from_b, spectra],
        [strip, freq, goal],
        scratch,
        flops=10**10,
    )
    moves = []
    for step in range(1, STEPS):
        got = from_partners(grad)
        move, *edges = call(
            functools.partial(match_kernel, len(got)),
            None,
            [table, grad, *got],
            [strip, side, side],
            smem=(0,),
        )
        from_b, from_a = swap_edges(*edges)
        if n_depth == 2:
            far_b, far_a = swap_edges(*edges, cross=True)
            rims = (from_a, far_a, from_b, far_b)
        else:
            rims = depth_pair(from_a) + depth_pair(from_b)
        moves += depth_pair(move)
        kept = step + 1 < STEPS
        grad, *rest = call(
            functools.partial(later_kernel, kern, n_tile - 1),
            "grad",
            [level, *moves[-2:], *rims, freq_now, goals, spectra],
            [strip, freq] if kept else [strip],
            scratch if kept else [pltpu.VMEM(freq.shape, f32)] + scratch,
            flops=10**10,
        )
        freq_now = rest[0] if kept else None
    mine, peer = depth_pair(grad)
    total = mine + peer
    got = from_partners(total)
    final = functools.partial(final_kernel, len(got), len(moves) // 2)
    args = [table, total, *got, mask_tiles, *moves]
    return tuple(call(final, None, args, [tiles, tiles], smem=(0,)))


def solution(mesh):
    return jax.shard_map(
        functools.partial(per_device, mesh.shape["tile"], mesh.shape["depth"]),
        mesh=mesh,
        in_specs=(
            P("tile", None, None),
            P("tile", None, None),
            P(None, "depth", None, None, None),
            P("depth", None),
            P("depth"),
            P("tile"),
            P("tile"),
        ),
        out_specs=(P("tile", None, None), P("tile", None, None)),
        check_vma=False,
    )
```

```python
import functools

import jax
import jax.numpy as jnp
import ml_dtypes
import numpy as np
from jax import lax
from jax.experimental import pallas as pl
from jax.experimental.pallas import tpu as pltpu
from jax.sharding import PartitionSpec as P

HALO = 12
KSIZE = 25
STEPS = 2
STEEPNESS = 3.0
STEP_RATE = 0.05

CORE = 128
NY = 152
NX = 176
WIDE = 2 * HALO
XB = 88
YB = 128
NU = NY // 2 + 1
ROWS = 160
ROW0 = 8
CHUNK = 16
EDGE = 48
WIDE_PAD = 32
VMEM_LIMIT = 24 * 1024 * 1024

f32 = jnp.float32
bf16 = jnp.bfloat16


def np_split(a):
    hi = np.asarray(a, np.float32).astype(ml_dtypes.bfloat16)
    lo = (np.asarray(a, np.float64) - hi.astype(np.float64)).astype(ml_dtypes.bfloat16)
    return hi, lo


def x_rows(cols):
    ang = 2 * np.pi * np.outer(np.arange(XB + 1), cols) / NX
    out = np.concatenate([np.cos(ang[:XB]), np.sin(ang[:XB])])
    out[XB] = np.cos(ang[XB])
    return out


def y_lanes(rows):
    out = np.zeros((len(rows), 2 * YB))
    ang = 2 * np.pi * np.outer(rows, np.arange(NU)) / NY
    out[:, :NU] = np.cos(ang)
    out[:, YB : YB + NU] = np.sin(ang)
    out[:, YB] = 0.0
    out[:, YB + NU - 1] = 0.0
    return out


def half_weights(bins):
    weights = np.full(bins, 2.0)
    weights[0] = weights[-1] = 1.0
    return weights


def x_back(cols):
    out = x_rows(cols).T
    sign = 1 - 2.0 * (np.asarray(cols) % 2)
    out[:, 0] = (1 + sign) / 2
    out[:, XB] = (1 - sign) / 2
    return out


def y_back(rows):
    weight = np.zeros(2 * YB)
    weight[:NU] = half_weights(NU)
    weight[YB : YB + NU] = -half_weights(NU)
    return (y_lanes(rows) * weight).T / (NX * NY)


def pack(parts):
    rows, where, at = [], {}, 0
    pieces = []
    for name, a in parts:
        if a.shape[1] <= 256:
            pieces.append((name, a))
            continue
        cuts = range(0, a.shape[1], 256)
        where[name] = len(cuts)
        pieces += [(f"{name}.{i}", a[:, c : c + 256]) for i, c in enumerate(cuts)]
    for name, a in pieces:
        height = -(-a.shape[0] // 16) * 16
        block = np.zeros((height, 256), np.float64)
        block[: a.shape[0], : a.shape[1]] = a
        rows.append(block)
        where[name] = (at, a.shape[0], a.shape[1])
        at += height
    return np.concatenate(rows), where


def pack_split(parts):
    both = []
    for name, a in parts:
        hi, lo = np_split(a)
        if name in ("x2", "x3", "x4"):
            hi, lo = hi.astype(np.float64), lo.astype(np.float64)
            both.append((name, np.concatenate([hi, lo, hi], axis=1)))
            continue
        both += [(name + "_hi", hi.astype(np.float64)), (name + "_lo", lo.astype(np.float64))]
    return both


@functools.lru_cache(None)
def tables():
    core_rows = np.arange(HALO, HALO + CORE)
    field_cols = np.arange(ROW0, ROW0 + ROWS)
    own_cols = np.arange(WIDE, WIDE + CORE)
    sides = np.zeros((2 * XB, 256))
    sides[:, :WIDE] = x_rows(np.arange(WIDE))
    sides[:, CORE : CORE + WIDE] = x_rows(np.arange(WIDE + CORE, NX))
    parts = [("cx_own", x_rows(own_cols)), ("cx_side", sides)]
    for t in range(2):
        pos = np.arange(2 * CORE) - t * CORE + HALO
        inside = (pos >= 0) & (pos < NY)
        parts.append((f"by{t}", y_lanes(pos) * inside[:, None]))
    parts += [("x2", x_back(field_cols)), ("x3", x_rows(field_cols)), ("x4", x_back(own_cols))]
    y2_hi, y2_lo = (a.astype(np.float64) for a in np_split(y_back(core_rows)))
    y3_hi, y3_lo = (a.astype(np.float64) for a in np_split(y_lanes(core_rows)))
    grad = pack_split(parts)
    upper = np.concatenate([y2_hi, y2_lo], axis=1)
    lower = np.concatenate([y2_hi, np.zeros_like(y2_lo)], axis=1)
    grad += [("y2", np.concatenate([upper, lower]))]
    grad += [("y3", np.concatenate([y3_hi, y3_hi, y3_lo]))]
    own = np.zeros((ROWS, CORE))
    own[np.arange(CORE) + WIDE - ROW0, np.arange(CORE)] = 1
    halo = np.zeros((ROWS, 256))
    for r in range(HALO):
        halo[HALO + r - ROW0, WIDE + r] = 1
        halo[WIDE + CORE + r - ROW0, CORE + WIDE + r] = 1
    grad += [("sel_own", own), ("sel_halo", halo)]
    offs = np.arange(KSIZE) - HALO
    kx = np.zeros((2 * XB, 128))
    kx[:, :KSIZE] = x_rows(offs)
    spec = [("kx", kx)]
    for m in range(4):
        ky = np.zeros((128, 2 * YB))
        ky[32 * m : 32 * m + KSIZE] = y_lanes(offs)
        spec.append((f"ky{m}", ky))
    return {"grad": pack(grad), "spec": pack(pack_split(spec))}


def split(x):
    hi = x.astype(bf16)
    return hi, (x - hi.astype(f32)).astype(bf16)


def dot(a, b):
    return lax.dot_general(a, b, (((1,), (0,)), ((), ())), preferred_element_type=f32)


def dot_nt(a, b):
    return lax.dot_general(a, b, (((1,), (1,)), ((), ())), preferred_element_type=f32)


def dot3(a_hi, a_lo, b_hi, b_lo, mul=dot):
    return mul(a_hi, b_hi) + (mul(a_lo, b_hi) + mul(a_hi, b_lo))


def top_row(like):
    return lax.broadcasted_iota(jnp.int32, like.shape, 0) == 0


def signed_parts(cc, cs, sc, ss, special):
    out = cc - ss, cs + sc, cc + ss, sc - cs
    if special:
        row0 = top_row(cc)
        out = [jnp.where(row0, x, y) for x, y in zip((cc, cs, sc, -ss), out)]
    return out


def signed(spec):
    parts = (spec[:XB, :YB], spec[:XB, YB:], spec[XB:, :YB], spec[XB:, YB:])
    pr, neg, mr, mi = signed_parts(*parts, True)
    return pr, -neg, mr, mi


def even_odd(pr, pi, mr, mi, special=True):
    top = jnp.concatenate([pr + mr, pi + mi], axis=1)
    low = jnp.concatenate([mi - pi, pr - mr], axis=1)
    if special:
        low = jnp.where(top_row(low), jnp.concatenate([pr - mr, pi - mi], axis=1), low)
    return top, low


def table_array(group):
    return jnp.asarray(tables()[group][0].astype(ml_dtypes.bfloat16))


def table_reader(group, ref):
    where = tables()[group][1]

    def table(name, half=None):
        if isinstance(where[name], int):
            return jnp.concatenate([table(f"{name}.{i}") for i in range(where[name])], axis=1)
        at, height, width = where[name]
        lanes = slice(0, width) if half is None else slice(128 * half, 128 * half + 128)
        return ref[at : at + height, lanes]

    return table


def call(body, group, args, out_shape, scratch=(), smem=(), flops=0, nbytes=0):
    vm = pl.BlockSpec(memory_space=pltpu.VMEM)
    sm = pl.BlockSpec(memory_space=pltpu.SMEM)
    n_in = len(args)
    if group is not None:
        args = [*args, table_array(group)]

    def wrapped(*refs):
        if group is not None:
            refs = [*refs[:n_in], table_reader(group, refs[n_in]), *refs[n_in + 1 :]]
        body(*refs)

    return pl.pallas_call(
        wrapped,
        out_shape=out_shape,
        in_specs=[sm if i in smem else vm for i in range(len(args))],
        out_specs=[vm] * len(out_shape),
        scratch_shapes=list(scratch),
        compiler_params=pltpu.CompilerParams(vmem_limit_bytes=VMEM_LIMIT),
        cost_estimate=pl.CostEstimate(flops=flops, bytes_accessed=nbytes, transcendentals=0),
    )(*args)


def is_even():
    return lax.rem(lax.axis_index("tile"), 2) == 0


def send_edges(right, left, a_ref, b_ref):
    even = is_even()
    a_ref[...] = jnp.where(even, right, left)
    b_ref[...] = jnp.where(even, left, right)


def picker(rows, first, count, col):
    row = lax.broadcasted_iota(jnp.int32, (rows, CORE), 0)
    lane = lax.broadcasted_iota(jnp.int32, (rows, CORE), 1)
    hit = (row - first == lane - col) & (row >= first) & (row < first + count)
    return jnp.where(hit, 1.0, 0.0).astype(bf16)


def edges_of(rows, strip, extra=None):
    hi, lo = split(strip)
    both = []
    for col, more in ((CORE - WIDE, CORE - HALO), (0, 0)):
        pick = picker(rows, 0, WIDE, col)
        edge = dot_nt(pick, hi) + dot_nt(pick, lo)
        if extra is not None:
            edge = edge + dot_nt(picker(rows, WIDE, HALO, more), extra)
        both.append(edge)
    return both


def edges_kernel(both_ref, a_ref, b_ref):
    both = both_ref[...]
    target = jnp.where(both >= 2.0, 1.0, 0.0)
    mask = both - 2.0 * target
    send_edges(*edges_of(EDGE, mask, target.astype(bf16)), a_ref, b_ref)


def spectra_kernel(kern, w_ref, ker_ref, tb, h_ref, hs_ref):
    hs_ref[...] = jnp.zeros_like(hs_ref)
    for k in range(kern):
        for part in range(2):
            row = 32 * (2 * k + part)
            hs_ref[row : row + KSIZE, :KSIZE] = ker_ref[part, k, :, 0, :]
    s_hi, s_lo = split(hs_ref[...])
    z = dot3(tb("kx_hi"), tb("kx_lo"), s_hi, s_lo, dot_nt)
    z_hi, z_lo = split(z)
    for c in range(2 * kern):
        lanes = slice(128 * (c // 4), 128 * (c // 4) + 128)
        spec = dot3(z_hi[:, lanes], z_lo[:, lanes], tb(f"ky{c % 4}_hi"), tb(f"ky{c % 4}_lo"))
        root = jnp.sqrt(jnp.full((1, YB), w_ref[0, c // 2], f32))
        for j, comp in enumerate(signed(spec)):
            h_ref[c, j] = root * comp


def sides(last, from_a, from_b, tb):
    even = is_even()
    tile = lax.axis_index("tile")
    from_b = jnp.where((tile == 0) | (tile == last), 0.0, from_b)
    l_hi, l_lo = split(jnp.where(even, from_b, from_a))
    r_hi, r_lo = split(jnp.where(even, from_a, from_b))
    height = l_hi.shape[0]
    v = None
    for half, hi, lo in ((0, l_hi, l_lo), (1, r_hi, r_lo)):
        c_hi, c_lo = tb("cx_side_hi", half), tb("cx_side_lo", half)
        term = dot3(c_hi[:, :height], c_lo[:, :height], hi, lo)
        v = term if v is None else v + term
    return v, l_hi, r_hi


def to_spectrum(v, tb, f_ref, base):
    v_hi, v_lo = split(v)
    for t in range(2):
        spec = dot3(v_hi, v_lo, tb(f"by{t}_hi"), tb(f"by{t}_lo"))
        for j, comp in enumerate(signed(spec)):
            f_ref[t, j] = comp if base is None else base[t, j] - STEP_RATE * comp


def gradient_body(kern, last, f_ref, tgt_ref, h_ref, thr_ref, tb, g_ref, work):
    fld, inten, tot, a_cat, b_cat, r_cat, w_cat = work
    group = 1
    count = kern // group
    chains = [(t, c) for t in range(2) for c in range(count)]
    lag = count + 2

    def at(i):
        return chains[i] if 0 <= i < len(chains) else None

    tile = lax.axis_index("tile")
    first = jnp.where(tile == 0, WIDE, HALO) - ROW0
    end = jnp.where(tile == last, WIDE + CORE, WIDE + CORE + HALO) - ROW0
    row = lax.broadcasted_iota(jnp.int32, (ROWS, CORE), 0)
    inside = (row >= first) & (row < end)
    lane = lax.broadcasted_iota(jnp.int32, (1, 2 * YB), 1)
    bin_at = lax.rem(lane, YB)
    weight = jnp.where((bin_at == 0) | (bin_at == NU - 1), 1.0, 2.0) / (NX * NY)
    weight = jnp.where(lane < YB, weight, -weight)

    def chunks(height):
        return [slice(r, r + CHUNK) for r in range(0, height, CHUNK)]

    def put(ref, slot, starts, pieces):
        for at_row, piece in zip(starts, pieces):
            ref[slot, at_row : at_row + CHUNK] = piece

    def products(t, c, slot):
        for part in range(2 * group):

            def pieces(start, height):
                rows = slice(start, start + height)
                hpr, hpi, hmr, hmi = (h_ref[2 * group * c + part, j, rows] for j in range(4))
                fpr, fpi, fmr, fmi = (f_ref[t, j, rows] for j in range(4))
                pr, pi = hpr * fpr - hpi * fpi, hpr * fpi + hpi * fpr
                mr, mi = hmr * fmr - hmi * fmi, hmr * fmi + hmi * fmr
                return even_odd(pr, pi, mr, mi, start == 0)

            def store(start, value):
                both = jnp.concatenate(split(value), axis=1)
                put(a_cat, slot, [2 * XB * part + start], [both])

            carry, last_low = pieces(XB - 8, 8)
            for start in range(0, XB - 8, CHUNK):
                top, low = pieces(start, CHUNK)
                store(start, top)
                store(XB - 8 + start, jnp.concatenate([carry, low[:8]], axis=0))
                carry = low[8:]
            store(2 * XB - CHUNK, jnp.concatenate([carry, last_low], axis=0))

    def y_done(z_now, slot):
        for g in range(group):
            for rows in chunks(2 * XB):
                z = []
                for part in range(2 * g, 2 * g + 2):
                    here = slice(2 * XB * part + rows.start, 2 * XB * part + rows.stop)
                    z.append(z_now[here, :CORE] + z_now[here, CORE:])
                z_hi, z_lo = split(jnp.concatenate(z, axis=1))
                starts = [2 * XB * j + rows.start for j in range(3)]
                put(b_cat, 2 * g + slot, starts, (z_hi, z_hi, z_lo))

    def field_of(t, c, slot):
        for g in range(group):
            k = group * c + g
            whole = dot(tb("x2"), b_cat[2 * g + slot])
            for rows in chunks(ROWS):
                field = whole[rows]
                fld[t, k, rows] = field
                re, im = field[:, :CORE], field[:, CORE:]
                power = re * re + im * im
                inten[t, rows] = power if k == 0 else inten[t, rows] + power

    def slope_of(t):
        resist = jax.nn.sigmoid(STEEPNESS * (inten[t] - thr_ref[0]))
        target = tgt_ref[:, CORE * t : CORE * t + CORE]
        slope = 2.0 * (resist - target) * STEEPNESS * resist * (1.0 - resist)
        inten[t] = jnp.where(inside, 2.0 * slope, 0.0)

    def scaled_field(t, c, slot):
        for g in range(group):
            for rows in chunks(ROWS):
                slope, field = inten[t, rows], fld[t, group * c + g, rows]
                r_hi, r_lo = split(
                    jnp.concatenate([slope * field[:, :CORE], slope * field[:, CORE:]], axis=1)
                )
                starts = [ROWS * j + rows.start for j in range(3)]
                put(r_cat, 2 * g + slot, starts, (r_hi, r_hi, r_lo))

    def x_back_done(w_now, g, slot):
        for rows in chunks(2 * XB):
            w_hi, w_lo = split(w_now[rows])
            for part in range(2):
                base = 2 * XB * (2 * g + part)
                here = slice(base + rows.start, base + rows.stop)
                lanes = slice(CORE * part, CORE * part + CORE)
                for j, piece in enumerate((w_hi, w_lo, w_hi)):
                    w_cat[slot, here, CORE * j : CORE * j + CORE] = piece[:, lanes]

    def add_back(t, c, slot):
        specs = dot(w_cat[slot], tb("y3"))
        for start in range(0, XB, 8):
            rows = slice(start, start + 8)
            acc = [0.0] * 4 if c == 0 else [tot[t, j, rows] for j in range(4)]
            for part in range(2 * group):
                base = 2 * XB * part + start
                cos, sin = specs[base : base + 8], specs[base + XB : base + XB + 8]
                bpr, neg, bmr, bmi = signed_parts(
                    cos[:, :YB], cos[:, YB:], sin[:, :YB], sin[:, YB:], start == 0
                )
                hpr, hpi, hmr, hmi = (h_ref[2 * group * c + part, j, rows] for j in range(4))
                acc[0] = acc[0] + (hpr * bpr - hpi * neg)
                acc[1] = acc[1] - (hpr * neg + hpi * bpr)
                acc[2] = acc[2] + (hmr * bmr + hmi * bmi)
                acc[3] = acc[3] + (hmr * bmi - hmi * bmr)
            for j in range(4):
                tot[t, j, rows] = acc[j]

    def finish(t):
        sums = even_odd(*(tot[t, j] for j in range(4)))
        r_hi, r_lo = split(jnp.concatenate(sums, axis=0))
        u = dot(tb("x4"), jnp.concatenate([r_hi, r_hi, r_lo], axis=0))
        u_hi, u_lo = split(weight * u)
        term = dot3(tb(f"by{t}_hi"), tb(f"by{t}_lo"), u_hi, u_lo, dot_nt)
        g_ref[...] = term if t == 0 else g_ref[...] + term

    for i in range(len(chains) + lag + 2):
        new, mid, old = at(i), at(i - 1), at(i - 2)
        back, back_mid, back_old = at(i - lag), at(i - lag - 1), at(i - lag - 2)
        slot, other = i % 2, (i + 1) % 2
        if mid:
            z_now = dot(a_cat[other], tb("y2"))
        if new:
            products(*new, slot)
        if back_mid:
            w_now = [dot(tb("x3"), r_cat[2 * g + other]) for g in range(group)]
        if back:
            scaled_field(*back, slot)
        if old:
            field_of(*old, slot)
        if back_old:
            add_back(*back_old, slot)
        if mid:
            y_done(z_now, other)
        if back_mid:
            for g in range(group):
                x_back_done(w_now[g], g, other)
        if old and old[1] == count - 1:
            slope_of(old[0])
        if back_old and back_old[1] == count - 1:
            finish(back_old[0])


def first_kernel(
    kern, last, thr_ref, mask_ref, target_ref, a_ref, b_ref, h_ref, tb,
    g_ref, f_ref, tgt_ref, *work,
):
    m_hi, m_lo = split(mask_ref[...])
    v, left, right = sides(last, a_ref[...], b_ref[...], tb)
    v = v + dot3(tb("cx_own_hi"), tb("cx_own_lo"), m_hi, m_lo, dot_nt)
    to_spectrum(v, tb, f_ref, None)
    tgt_ref[...] = (
        dot_nt(tb("sel_own"), target_ref[...].astype(f32).astype(bf16))
        + dot(tb("sel_halo", 0)[:, :EDGE], left)
        + dot(tb("sel_halo", 1)[:, :EDGE], right)
    )
    gradient_body(kern, last, f_ref, tgt_ref, h_ref, thr_ref, tb, g_ref, work)


def later_kernel(
    kern, last, thr_ref, mine_ref, peer_ref, a_ref, a2_ref, b_ref, b2_ref, f_in_ref, tgt_ref,
    h_ref, tb, g_ref, f_ref, *work,
):
    s_hi, s_lo = split(mine_ref[...] + peer_ref[...])
    from_a = a_ref[...] + a2_ref[...]
    from_b = b_ref[...] + b2_ref[...]
    v, _, _ = sides(last, from_a, from_b, tb)
    v = v + dot3(tb("cx_own_hi"), tb("cx_own_lo"), s_hi, s_lo, dot_nt)
    to_spectrum(v, tb, f_ref, f_in_ref)
    gradient_body(kern, last, f_ref, tgt_ref, h_ref, thr_ref, tb, g_ref, work)


def match(table_ref, own_ref, got_refs):
    device = lax.axis_index("tile")
    other = []
    for t in range(2):
        rows = slice(CORE * t, CORE * t + CORE)
        bit = lax.bitwise_xor(table_ref[t], 2 * device + t)
        value = jnp.where(bit == 1, own_ref[CORE * (1 - t) : CORE * (2 - t)], own_ref[rows])
        for b, got in enumerate(got_refs):
            value = jnp.where(bit == 2 << b, got[rows], value)
        other.append(value)
    row = lax.broadcasted_iota(jnp.int32, (CORE, CORE), 0)
    lane = lax.broadcasted_iota(jnp.int32, (CORE, CORE), 1)
    flip = jnp.where(row + lane == CORE - 1, 1.0, 0.0).astype(bf16)
    hi, lo = split(jnp.concatenate(other, axis=0))
    turned = dot(hi, flip) + dot(lo, flip)
    tiles = []
    for t in range(2):
        rows = slice(CORE * t, CORE * t + CORE)
        value = jnp.where(table_ref[2 + t] == 1, turned[rows], other[t])
        tiles.append(0.5 * (own_ref[rows] + value))
    return tiles, hi, lo


def matched_edges(table_ref, own_ref, hi, lo):
    row = lax.broadcasted_iota(jnp.int32, (WIDE_PAD, CORE), 0)
    lane = lax.broadcasted_iota(jnp.int32, (WIDE_PAD, CORE), 1)
    picks = [picker(WIDE_PAD, 0, WIDE, CORE - WIDE), picker(WIDE_PAD, 0, WIDE, 0)]
    for end in (WIDE - 1, CORE - 1):
        hit = (row + lane == end) & (row < WIDE)
        picks.append(jnp.where(hit, 1.0, 0.0).astype(bf16))
    picks = jnp.concatenate(picks, axis=0)
    own_hi, own_lo = split(own_ref[...])
    own = dot_nt(picks[: 2 * WIDE_PAD], own_hi) + dot_nt(picks[: 2 * WIDE_PAD], own_lo)
    other = dot_nt(picks, hi) + dot_nt(picks, lo)
    chosen = []
    for t in range(2):
        lanes = slice(CORE * t, CORE * t + CORE)
        plain, turned = other[: 2 * WIDE_PAD, lanes], other[2 * WIDE_PAD :, lanes]
        chosen.append(jnp.where(table_ref[2 + t] == 1, turned, plain))
    both = 0.5 * (own + jnp.concatenate(chosen, axis=1))
    return both[:WIDE_PAD], both[WIDE_PAD:]


def match_kernel(n_got, table_ref, own_ref, *refs):
    got_refs, (out_ref, *edge_refs) = refs[:n_got], refs[n_got:]
    tiles, hi, lo = match(table_ref, own_ref, got_refs)
    send_edges(*matched_edges(table_ref, own_ref, hi, lo), *edge_refs)
    out_ref[...] = jnp.concatenate(tiles, axis=0)


def final_kernel(n_got, n_moves, table_ref, own_ref, *refs):
    got_refs, mask_ref, refs = refs[:n_got], refs[n_got], refs[n_got + 1 :]
    moves, (mask_out, grad_out) = refs[: 2 * n_moves], refs[2 * n_moves :]
    for t, step in enumerate(match(table_ref, own_ref, got_refs)[0]):
        rows = slice(CORE * t, CORE * t + CORE)
        now = mask_ref[t]
        for mine, peer in zip(moves[::2], moves[1::2]):
            now = now - STEP_RATE * (mine[rows] + peer[rows])
        grad_out[t] = step
        mask_out[t] = now - STEP_RATE * step


def per_device(
    n_tile, n_depth, mask_tiles, target_tiles, kernels, socs_weights, thresholds,
    partner_table, mirror_flags,
):
    tiles_dev, core, _ = mask_tiles.shape
    kern = kernels.shape[2]
    assert tiles_dev == 2 and core == CORE
    pairs_a = [(i, i ^ 1) for i in range(n_tile)]
    pairs_b = [p for i in range(1, n_tile - 1, 2) for p in ((i, i + 1), (i + 1, i))]
    pairs_b += [(0, 0), (n_tile - 1, n_tile - 1)]

    def swap_edges(send_a, send_b, cross=False):
        def move(x, pairs):
            if not cross:
                return lax.ppermute(x, "tile", pairs)
            both = [(2 * i + p, 2 * j + 1 - p) for i, j in pairs for p in range(2)]
            return lax.ppermute(x, ("tile", "depth"), both)

        return move(send_b, pairs_b), move(send_a, pairs_a)

    def depth_pair(x):
        bit = 1
        while True:
            peer = lax.ppermute(x, "depth", [(i, i ^ bit) for i in range(n_depth)])
            bit *= 2
            if bit >= n_depth:
                return x, peer
            x = x + peer

    def from_partners(grad):
        bits = [1 << b for b in range(n_tile.bit_length() - 1)]
        got = [
            lax.ppermute(grad, "tile", [(i, i ^ bit) for i in range(n_tile)])
            for bit in reversed(bits)
        ]
        return got[::-1]

    mask_rows = mask_tiles.reshape(tiles_dev * core, core)
    target_rows = target_tiles.reshape(tiles_dev * core, core)
    strip = jax.ShapeDtypeStruct((tiles_dev * core, core), f32)
    side = jax.ShapeDtypeStruct((WIDE_PAD, tiles_dev * core), f32)
    freq = jax.ShapeDtypeStruct((2, 4, XB, YB), f32)
    goal = jax.ShapeDtypeStruct((ROWS, 2 * CORE), f32)
    tiles = jax.ShapeDtypeStruct((tiles_dev, core, core), f32)
    group = 1
    scratch = [
        pltpu.VMEM((2, kern, ROWS, 2 * CORE), f32),
        pltpu.VMEM((2, ROWS, CORE), f32),
        pltpu.VMEM((2, 4, XB, YB), f32),
        pltpu.VMEM((2, group * 4 * XB, 4 * YB), bf16),
        pltpu.VMEM((2 * group, 6 * XB, 2 * CORE), bf16),
        pltpu.VMEM((2 * group, 3 * ROWS, 2 * CORE), bf16),
        pltpu.VMEM((2, group * 4 * XB, 3 * CORE), bf16),
    ]

    edge = jax.ShapeDtypeStruct((EDGE, tiles_dev * core), f32)
    send_a, send_b = call(
        edges_kernel,
        None,
        [mask_rows + 2.0 * target_rows.astype(f32)],
        [edge, edge],
        flops=3 * 10**9,
    )
    from_b, from_a = swap_edges(send_a, send_b)
    table = jnp.concatenate([partner_table, mirror_flags])
    (spectra,) = call(
        functools.partial(spectra_kernel, kern),
        "spec",
        [socs_weights, kernels.transpose(0, 2, 3, 1, 4)],
        [jax.ShapeDtypeStruct((2 * kern, 4, XB, YB), f32)],
        [pltpu.VMEM((32 * 2 * kern, 128), f32)],
        smem=(0,),
        flops=3 * 10**9,
        nbytes=4 * 10**6,
    )
    grad, freq_now, goals = call(
        functools.partial(first_kernel, kern, n_tile - 1),
        "grad",
        [thresholds, mask_rows, target_rows, from_a, from_b, spectra],
        [strip, freq, goal],
        scratch,
        smem=(0,),
        flops=10**10,
    )
    moves = []
    for step in range(1, STEPS):
        got = from_partners(grad)
        move, *edges = call(
            functools.partial(match_kernel, len(got)),
            None,
            [table, grad, *got],
            [strip, side, side],
            smem=(0,),
        )
        from_b, from_a = swap_edges(*edges)
        if n_depth == 2:
            far_b, far_a = swap_edges(*edges, cross=True)
            rims = (from_a, far_a, from_b, far_b)
        else:
            rims = depth_pair(from_a) + depth_pair(from_b)
        moves += depth_pair(move)
        kept = step + 1 < STEPS
        grad, *rest = call(
            functools.partial(later_kernel, kern, n_tile - 1),
            "grad",
            [thresholds, *moves[-2:], *rims, freq_now, goals, spectra],
            [strip, freq] if kept else [strip],
            scratch if kept else [pltpu.VMEM(freq.shape, f32)] + scratch,
            smem=(0,),
            flops=10**10,
        )
        freq_now = rest[0] if kept else None
    mine, peer = depth_pair(grad)
    total = mine + peer
    got = from_partners(total)
    final = functools.partial(final_kernel, len(got), len(moves) // 2)
    args = [table, total, *got, mask_tiles, *moves]
    return tuple(call(final, None, args, [tiles, tiles], smem=(0,)))


def solution(mesh):
    return jax.shard_map(
        functools.partial(per_device, mesh.shape["tile"], mesh.shape["depth"]),
        mesh=mesh,
        in_specs=(
            P("tile", None, None),
            P("tile", None, None),
            P(None, "depth", None, None, None),
            P("depth", None),
            P("depth"),
            P("tile"),
            P("tile"),
        ),
        out_specs=(P("tile", None, None), P("tile", None, None)),
        check_vma=False,
    )
```
